32 devices in a mesh: context: 16 (over z, y, core), heads: 2 (over x).
Axes of the slice: x: 2, y: 2, z: 4, core: 2. Of those that a mesh axis runs over, the one named last changes fastest.
Arguments:
- upstream: bfloat16 [4096, 1024], P(('context', 'heads')), may hold values from -48 to 48
- out_weight: bfloat16 [1024, 1024], P('heads'), may hold values from -0.1875 to 0.1875
- query_rows: bfloat16 [4096, 1024], P('context', 'heads'), may hold values from -6 to 6
- key_rows: bfloat16 [4096, 1024], P('context', 'heads'), may hold values from -6 to 6
- value_rows: bfloat16 [4096, 1024], P('context', 'heads'), may hold values from -6 to 6
- head_offsets: int32 [16], replicated, may hold values from 0 to 15, each once
Outputs:
- query_grad: bfloat16 [4096, 1024], P('context', 'heads')
- key_grad: bfloat16 [4096, 1024], P('context', 'heads')
- value_grad: bfloat16 [4096, 1024], P('context', 'heads')
The draws below stay inside these ranges and needn't reach their ends.
Inputs may be any that keep to these rules, and one draw needn't show every extreme that they name: `head_offsets`: every value of 0 to 15 occurs once.
All inputs are finite; a program needn't handle non-finite values.
Results may differ from the reference program's by a relative error of at most 0.008.
Values may be sent and summed in bfloat16 or wider, within the bound.
No kernel may reach another device: no remote copies, remote signals or barrier semaphores. Data moves between devices by JAX's collectives and lax.ppermute only.
A program may use at most 128 MiB of HBM per device.

```python
import math
import jax
import jax.numpy as jnp
from jax import lax

D = 1024
H = 16
HEAD_SIZE = 64
DILATION_RATE = 16
FIRST_SEGMENT = 2048
SEQUENCE_TOKENS = 4096
SECOND_SEGMENT = 4096


def draw_query_rows(key, part):
    source = jax.random.fold_in(key, 1)
    value_tensor = jax.random.truncated_normal(source, -6.0, 6.0, (SEQUENCE_TOKENS, D), jnp.float32)
    return value_tensor.astype(jnp.bfloat16)


def draw_key_rows(key, part):
    source = jax.random.fold_in(key, 2)
    value_tensor = jax.random.truncated_normal(source, -6.0, 6.0, (SEQUENCE_TOKENS, D), jnp.float32)
    return value_tensor.astype(jnp.bfloat16)


def steps_of(own_key, shape, split, smallest, top_value):
    loudness, own = 1.0, jax.random.fold_in(own_key, 6)
    for axis_at, blocks in split:
        steps = jnp.exp(jax.random.uniform(jax.random.fold_in(own, axis_at), (blocks,), jnp.float32, smallest / len(split), top_value / len(split)))
        loudness = loudness * jnp.repeat(steps, shape[axis_at] // blocks).reshape([-1 if axis == axis_at else 1 for axis in range(len(shape))])
    return loudness


def bell_draw(stream_key, dims, scale, bound, cuts=(), kind=jnp.bfloat16):
    factor_of = steps_of(stream_key, dims, cuts, -0.22, 0.18) if cuts else 1.0
    entries = jax.random.normal(stream_key, dims, jnp.float32) * scale * factor_of
    return jnp.minimum(jnp.maximum(entries, -bound), bound).astype(kind)


def setup_inputs(seed: int = 0) -> dict:
    streams_of = jax.random.split(jax.random.key(seed), 7)
    return {
        "upstream": jnp.clip(jax.random.uniform(streams_of[0], (SEQUENCE_TOKENS, D), jnp.float32, -48.0, 48.0) * steps_of(streams_of[0], (SEQUENCE_TOKENS, D), ((0, 32),), -0.4, 0.0), -48.0, 48.0).astype(jnp.bfloat16),
        "out_weight": bell_draw(streams_of[1], (D, D), D ** -0.5, 0.1875, ((0, 2),)),
        "query_rows": draw_query_rows(jax.random.fold_in(streams_of[6], 71), 0),
        "key_rows": draw_key_rows(jax.random.fold_in(streams_of[6], 71), 0),
        "value_rows": bell_draw(streams_of[4], (SEQUENCE_TOKENS, D), 1.0, 6.0, ((0, 16), (1, 2))),
        "head_offsets": jax.random.permutation(streams_of[5], H).astype(jnp.int32),
    }


def spread_rows(value_tensor, head_shift):
    total_count = value_tensor.shape[0]
    matched_flag = jnp.arange(DILATION_RATE, dtype=jnp.int32)[None, :] == head_shift
    return jnp.where(matched_flag, value_tensor[:, None], jnp.zeros((), value_tensor.dtype)).reshape(total_count * DILATION_RATE)

def place_rows(value_tensor, head_shift):
    total_count = value_tensor.shape[0]
    matched_flag = (jnp.arange(DILATION_RATE, dtype=jnp.int32) == head_shift)[None, :, None]
    return jnp.where(matched_flag, value_tensor[:, None, :], jnp.zeros((), value_tensor.dtype)).reshape(total_count * DILATION_RATE, value_tensor.shape[1])

def batched(form, left, right):
    return jnp.einsum(form, left.astype(jnp.float32), right.astype(jnp.float32))

def head_grads(query_head, key_head, value_head, grad_head, head_shift):
    scale = 1.0 / math.sqrt(HEAD_SIZE)
    selected_count = SEQUENCE_TOKENS // DILATION_RATE

    def pick(payload_arrays):
        return lax.dynamic_index_in_dim(payload_arrays.reshape(selected_count, DILATION_RATE, HEAD_SIZE), head_shift, 1, keepdims=False)
    query_pick = pick(query_head)
    key_pick = pick(key_head)
    value_pick = pick(value_head)
    grad_pick = pick(grad_head)
    near_segs = SEQUENCE_TOKENS // FIRST_SEGMENT
    local_count = FIRST_SEGMENT // DILATION_RATE
    far_segs = SEQUENCE_TOKENS // SECOND_SEGMENT
    distant_count = SECOND_SEGMENT // DILATION_RATE
    near_keys = key_head.reshape(near_segs, FIRST_SEGMENT, HEAD_SIZE)
    near_values = value_head.reshape(near_segs, FIRST_SEGMENT, HEAD_SIZE)
    score_near = batched('sqd,skd->sqk', query_pick.reshape(near_segs, local_count, HEAD_SIZE), near_keys) * scale
    dprob_near = batched('sqd,skd->sqk', grad_pick.reshape(near_segs, local_count, HEAD_SIZE), near_values)
    score_near = score_near.reshape(selected_count, FIRST_SEGMENT)
    dprob_near = dprob_near.reshape(selected_count, FIRST_SEGMENT)
    query_far = query_pick.reshape(far_segs, distant_count, HEAD_SIZE)
    key_far = key_pick.reshape(far_segs, distant_count, HEAD_SIZE)
    value_far = value_pick.reshape(far_segs, distant_count, HEAD_SIZE)
    grad_far = grad_pick.reshape(far_segs, distant_count, HEAD_SIZE)
    score_far = (batched('sqd,skd->sqk', query_far, key_far) * scale).reshape(selected_count, distant_count)
    dprob_far = batched('sqd,skd->sqk', grad_far, value_far).reshape(selected_count, distant_count)
    row_max = jnp.maximum(lax.optimization_barrier(jnp.max(score_near, 1)), lax.optimization_barrier(jnp.max(score_far, 1)))
    row_sum = lax.optimization_barrier(jnp.sum(jnp.exp(score_near - row_max[:, None]), 1)) + lax.optimization_barrier(jnp.sum(jnp.exp(score_far - row_max[:, None]), 1))
    lse_pick = row_max + jnp.log(row_sum)
    prob_near = jnp.exp(score_near - lse_pick[:, None])
    prob_far = jnp.exp(score_far - lse_pick[:, None])
    delta_pick = lax.optimization_barrier(jnp.sum(prob_near * dprob_near, 1)) + lax.optimization_barrier(jnp.sum(prob_far * dprob_far, 1))
    dscore_far = (prob_far * (dprob_far - delta_pick[:, None])).astype(jnp.bfloat16).reshape(far_segs, distant_count, distant_count)
    prob_far16 = prob_far.astype(jnp.bfloat16).reshape(far_segs, distant_count, distant_count)
    dq_far = (batched('sqk,skd->sqd', dscore_far, key_far) * scale).reshape(selected_count, HEAD_SIZE)
    dk_far = (batched('sqk,sqd->skd', dscore_far, query_far) * scale).reshape(selected_count, HEAD_SIZE)
    dv_far = batched('sqk,sqd->skd', prob_far16, grad_far).reshape(selected_count, HEAD_SIZE)
    lse_rows = spread_rows(lse_pick, head_shift)
    delta_rows = spread_rows(delta_pick, head_shift)
    selected_rows = jnp.arange(SEQUENCE_TOKENS, dtype=jnp.int32) % DILATION_RATE == head_shift

    def segment(inputs):
        seg_query, seg_key, seg_value, seg_grad, seg_lse, seg_delta, seg_mask = inputs
        scores = jnp.dot(seg_query, seg_key.T, preferred_element_type=jnp.float32) * scale
        seg_max = lax.optimization_barrier(jnp.max(scores, 1))
        seg_sum = lax.optimization_barrier(jnp.sum(jnp.exp(scores - seg_max[:, None]), 1))
        lse_all = jnp.where(seg_mask, seg_lse, seg_max + jnp.log(seg_sum))
        probs = jnp.exp(scores - lse_all[:, None])
        dprobs = jnp.dot(seg_grad, seg_value.T, preferred_element_type=jnp.float32)
        delta_all = jnp.where(seg_mask, seg_delta, lax.optimization_barrier(jnp.sum(probs * dprobs, 1)))
        dscores = (probs * (dprobs - delta_all[:, None])).astype(jnp.bfloat16)
        probs16 = probs.astype(jnp.bfloat16)
        dq_seg = jnp.dot(dscores, seg_key, preferred_element_type=jnp.float32) * scale
        dk_seg = jnp.dot(dscores.T, seg_query, preferred_element_type=jnp.float32) * scale
        dv_seg = jnp.dot(probs16.T, seg_grad, preferred_element_type=jnp.float32)
        return (dq_seg, dk_seg, dv_seg)
    dq_near, dk_near, dv_near = lax.map(segment, (query_head.reshape(near_segs, FIRST_SEGMENT, HEAD_SIZE), near_keys, near_values, grad_head.reshape(near_segs, FIRST_SEGMENT, HEAD_SIZE), lse_rows.reshape(near_segs, FIRST_SEGMENT), delta_rows.reshape(near_segs, FIRST_SEGMENT), selected_rows.reshape(near_segs, FIRST_SEGMENT)))
    dq_all = dq_near.reshape(SEQUENCE_TOKENS, HEAD_SIZE) + place_rows(dq_far, head_shift)
    dk_all = dk_near.reshape(SEQUENCE_TOKENS, HEAD_SIZE) + place_rows(dk_far, head_shift)
    dv_all = dv_near.reshape(SEQUENCE_TOKENS, HEAD_SIZE) + place_rows(dv_far, head_shift)
    return (dq_all.astype(jnp.bfloat16), dk_all.astype(jnp.bfloat16), dv_all.astype(jnp.bfloat16))

def reference(upstream, out_weight, query_rows, key_rows, value_rows, head_offsets):
    attn_grad = jnp.dot(upstream, out_weight.T, preferred_element_type=jnp.float32).astype(jnp.bfloat16)

    def one_head(index):

        def columns(payload_arrays):
            return lax.dynamic_slice_in_dim(payload_arrays, index * HEAD_SIZE, HEAD_SIZE, 1)
        return head_grads(columns(query_rows), columns(key_rows), columns(value_rows), columns(attn_grad), head_offsets[index])
    dq_heads, dk_heads, dv_heads = lax.map(one_head, jnp.arange(H, dtype=jnp.int32))

    def merge_heads(payload_arrays):
        return jnp.transpose(payload_arrays, (1, 0, 2)).reshape(SEQUENCE_TOKENS, D)
    return (merge_heads(dq_heads), merge_heads(dk_heads), merge_heads(dv_heads))
```

```python
import functools
import math

import jax
import jax.numpy as jnp
from jax import lax
from jax.experimental import pallas as pl
from jax.experimental.pallas import tpu as pltpu
from jax.sharding import PartitionSpec as P

HEAD_SIZE = 64
PAIR = 2 * HEAD_SIZE
DILATION_RATE = 16
FIRST_SEGMENT = 2048
SCALE = 1.0 / math.sqrt(HEAD_SIZE)
LOG2E = math.log2(math.e)
NEG = -1e30

SMEM = pl.BlockSpec(memory_space=pltpu.SMEM)
VMEM = pl.BlockSpec(memory_space=pltpu.VMEM)


def dot_nt(left, right):
    return lax.dot_general(
        left, right, (((1,), (1,)), ((), ())), preferred_element_type=jnp.float32
    )


def dot_nn(left, right):
    return jnp.dot(left, right, preferred_element_type=jnp.float32)


def head_columns(ref, head):
    return ref[:, head * HEAD_SIZE : (head + 1) * HEAD_SIZE]


def pick_matrix(offset, picked, rows):
    source = lax.broadcasted_iota(jnp.int32, (picked, rows), 1)
    index = lax.broadcasted_iota(jnp.int32, (picked, rows), 0)
    return (source == index * DILATION_RATE + offset).astype(jnp.bfloat16)


def pack_kernel(head_count, place_ref, offset_ref, key_ref, value_ref, near_ref, far_ref):
    group = near_ref.shape[0]
    rows = near_ref.shape[1]
    picked = far_ref.shape[1]
    for head in range(head_count):
        pair = jnp.concatenate([head_columns(key_ref, head), head_columns(value_ref, head)], 1)
        offset = offset_ref[place_ref[1] * head_count + head]
        picks = dot_nn(pick_matrix(offset, picked, rows), pair).astype(jnp.bfloat16)
        for place in range(head, group, head_count):
            near_ref[place] = pair
        for place in range(head, far_ref.shape[0], head_count):
            far_ref[place] = picks


def project_kernel(head_count, place_ref, weight_ref, query_ref, *refs):
    upstream_refs, pair_ref, grad_ref = refs[:-2], refs[-2], refs[-1]
    shards = len(upstream_refs)
    rows = upstream_refs[0].shape[0]
    for step, upstream_ref in enumerate(upstream_refs):
        owner = lax.rem(place_ref[1] + (shards - step), shards)
        start = pl.multiple_of(owner * rows, rows)
        grad_ref[pl.ds(start, rows), :] = dot_nt(upstream_ref[...], weight_ref[...]).astype(
            jnp.bfloat16
        )
    for head in range(head_count):
        pair = jnp.concatenate([head_columns(query_ref, head), head_columns(grad_ref, head)], 1)
        for place in range(head, pair_ref.shape[0], head_count):
            pair_ref[place] = pair


def attend_kernel(
    head_count, place_ref, offset_ref, kv_ref, qg_ref, far_ref, near_out, far_out,
    score_ref, dprob_ref, key_t_ref, acc_ref,
):
    group, rows, _ = kv_ref.shape
    far_rows = far_ref.shape[0]
    far_chunks = far_rows // rows
    chunks = group + far_chunks
    half = rows // 2
    offset = offset_ref[place_ref[1] * head_count + lax.rem(place_ref[0], head_count)]
    lane = lax.broadcasted_iota(jnp.int32, (rows, PAIR), 1)
    left = lane < HEAD_SIZE
    row_lane = lax.broadcasted_iota(jnp.int32, (1, rows), 1)
    picked = lax.rem(row_lane, DILATION_RATE) == offset

    def pair_chunk(chunk):
        if chunk < group:
            return kv_ref[chunk]
        return far_ref[(chunk - group) * rows : (chunk - group + 1) * rows, :]

    for chunk in range(chunks):
        key_t_ref[chunk] = pair_chunk(chunk).astype(jnp.float32).T[:HEAD_SIZE].astype(jnp.bfloat16)
    acc_ref[...] = jnp.zeros_like(acc_ref)

    def block(index, carry):
        both = qg_ref[index]
        query = jnp.where(left, both, jnp.zeros((), both.dtype))
        grad = jnp.where(left, jnp.zeros((), both.dtype), both)
        weights = jnp.concatenate([query, grad], 0)
        top = jnp.full((1, rows), NEG, jnp.float32)
        for chunk in range(chunks):
            score = dot_nt(pair_chunk(chunk), query)
            if chunk >= group:
                score = jnp.where(picked, score, NEG)
            score_ref[chunk] = score
            top = jnp.maximum(top, jnp.max(score, 0, keepdims=True))
        total = jnp.zeros((1, rows), jnp.float32)
        delta = jnp.zeros((1, rows), jnp.float32)
        for chunk in range(chunks):
            prob = jnp.exp2((score_ref[chunk] - top) * (SCALE * LOG2E))
            dprob = dot_nt(pair_chunk(chunk), grad)
            total = total + jnp.sum(prob, 0, keepdims=True)
            delta = delta + jnp.sum(prob * dprob, 0, keepdims=True)
            score_ref[chunk] = prob
            dprob_ref[chunk] = dprob
        inverse = 1.0 / total
        delta = delta * inverse
        query_grad = jnp.zeros((HEAD_SIZE, rows), jnp.float32)
        for chunk in range(chunks):
            prob = score_ref[chunk] * inverse
            dscore = (prob * (dprob_ref[chunk] - delta)).astype(jnp.bfloat16)
            prob16 = prob.astype(jnp.bfloat16)
            acc_ref[chunk] += dot_nn(jnp.concatenate([dscore, prob16], 1), weights)
            query_grad = query_grad + dot_nn(key_t_ref[chunk], dscore)
        query_grad = (query_grad * SCALE).T.astype(jnp.bfloat16)
        near_out[index, rows : rows + half, :] = jnp.concatenate(
            [query_grad[:half], query_grad[half:]], 1
        )
        return carry

    lax.fori_loop(0, group, block, 0)
    factor = jnp.where(left, SCALE, 1.0)
    for chunk in range(chunks):
        terms = acc_ref[chunk] * factor
        if chunk < group:
            near_out[chunk, :rows, :] = terms.astype(jnp.bfloat16)
        else:
            far_out[(chunk - group) * rows : (chunk - group + 1) * rows, :] = terms


def unpack_kernel(
    head_count, place_ref, offset_ref, near_ref, far_ref, query_out, key_out, value_out
):
    rows = query_out.shape[0]
    half = rows // 2
    group = near_ref.shape[0]
    picked = far_ref.shape[1]
    for head in range(head_count):
        offset = offset_ref[place_ref[1] * head_count + head]
        spread = pick_matrix(offset, picked, rows)
        far = far_ref[head]
        for other in range(head + group, far_ref.shape[0], group):
            far = far + far_ref[other]
        high = far.astype(jnp.bfloat16)
        low = (far - high.astype(jnp.float32)).astype(jnp.bfloat16)
        placed = lax.dot_general(
            jnp.concatenate([spread, spread], 0),
            jnp.concatenate([high, low], 0),
            (((0,), (0,)), ((), ())),
            preferred_element_type=jnp.float32,
        )
        pair = (near_ref[head, :rows, :].astype(jnp.float32) + placed).astype(jnp.bfloat16)
        columns = slice(head * HEAD_SIZE, (head + 1) * HEAD_SIZE)
        key_out[:, columns] = pair[:, :HEAD_SIZE]
        value_out[:, columns] = pair[:, HEAD_SIZE:]
        packed = near_ref[head, rows : rows + half, :]
        query_out[:half, columns] = packed[:, :HEAD_SIZE]
        query_out[half:, columns] = packed[:, HEAD_SIZE:]


def params():
    return pltpu.CompilerParams(vmem_limit_bytes=40 * 1024 * 1024)


def body(upstream, out_weight, query_rows, key_rows, value_rows, head_offsets):
    rows, width = query_rows.shape
    head_count = width // HEAD_SIZE
    devices = lax.axis_size("context")
    shards = lax.axis_size("heads")
    group = FIRST_SEGMENT // rows
    picked = rows // DILATION_RATE
    place = jnp.stack(
        [lax.rem(lax.axis_index("context"), group), lax.axis_index("heads")]
    ).astype(jnp.int32)
    groups = [list(range(first, first + group)) for first in range(0, devices, group)]

    def swap(value):
        return lax.all_to_all(value, "context", 0, 0, axis_index_groups=groups)

    upstreams = [upstream]
    for step in range(1, shards):
        pairs = [(source, (source + step) % shards) for source in range(shards)]
        upstreams.append(lax.ppermute(upstream, "heads", pairs))

    kv_send, far_send = pl.pallas_call(
        functools.partial(pack_kernel, head_count),
        out_shape=(
            jax.ShapeDtypeStruct((group, rows, PAIR), jnp.bfloat16),
            jax.ShapeDtypeStruct((devices, picked, PAIR), jnp.bfloat16),
        ),
        in_specs=[SMEM, SMEM, VMEM, VMEM],
        out_specs=(VMEM, VMEM),
        compiler_params=params(),
        name="pack_keys_values",
    )(place, head_offsets, key_rows, value_rows)
    kv = swap(kv_send)
    far = lax.all_to_all(far_send, "context", 0, 0)

    qg_send = pl.pallas_call(
        functools.partial(project_kernel, head_count),
        out_shape=jax.ShapeDtypeStruct((group, rows, PAIR), jnp.bfloat16),
        in_specs=[SMEM] + [VMEM] * (2 + shards),
        out_specs=VMEM,
        scratch_shapes=[pltpu.VMEM((rows, width), jnp.bfloat16)],
        compiler_params=params(),
        name="project_pack",
    )(place, out_weight, query_rows, *upstreams)
    qg = swap(qg_send)

    far_rows = devices * picked
    chunks = group + far_rows // rows
    near_send, far_back = pl.pallas_call(
        functools.partial(attend_kernel, head_count),
        out_shape=(
            jax.ShapeDtypeStruct((group, rows + rows // 2, PAIR), jnp.bfloat16),
            jax.ShapeDtypeStruct((far_rows, PAIR), jnp.float32),
        ),
        in_specs=[SMEM, SMEM, VMEM, VMEM, VMEM],
        out_specs=(VMEM, VMEM),
        scratch_shapes=[
            pltpu.VMEM((chunks, rows, rows), jnp.float32),
            pltpu.VMEM((chunks, rows, rows), jnp.float32),
            pltpu.VMEM((chunks, HEAD_SIZE, rows), jnp.bfloat16),
            pltpu.VMEM((chunks, rows, PAIR), jnp.float32),
        ],
        compiler_params=params(),
        name="attend",
    )(place, head_offsets, kv, qg, far.reshape(far_rows, PAIR))
    near = swap(near_send)
    far_terms = lax.all_to_all(far_back.reshape(devices, picked, PAIR), "context", 0, 0)

    shape = jax.ShapeDtypeStruct((rows, width), jnp.bfloat16)
    return pl.pallas_call(
        functools.partial(unpack_kernel, head_count),
        out_shape=(shape, shape, shape),
        in_specs=[SMEM, SMEM, VMEM, VMEM],
        out_specs=(VMEM, VMEM, VMEM),
        compiler_params=params(),
        name="unpack",
    )(place, head_offsets, near, far_terms)


def solution(mesh):
    return jax.shard_map(
        body,
        mesh=mesh,
        in_specs=(
            P(("context", "heads"), None),
            P("heads", None),
            P("context", "heads"),
            P("context", "heads"),
            P("context", "heads"),
            P(),
        ),
        out_specs=(P("context", "heads"), P("context", "heads"), P("context", "heads")),
        check_vma=False,
    )
```

```python
import functools
import math

import jax
import jax.numpy as jnp
from jax import lax
from jax.experimental import pallas as pl
from jax.experimental.pallas import tpu as pltpu
from jax.sharding import PartitionSpec as P

HEAD_SIZE = 64
PAIR = 2 * HEAD_SIZE
DILATION_RATE = 16
FIRST_SEGMENT = 2048
SCALE = 1.0 / math.sqrt(HEAD_SIZE)
LOG2E = math.log2(math.e)
SCORE_FACTOR = SCALE * LOG2E
STRIP = 64
STAT_ROWS = 16

SMEM = pl.BlockSpec(memory_space=pltpu.SMEM)
VMEM = pl.BlockSpec(memory_space=pltpu.VMEM)


def dot_nt(left, right):
    return lax.dot_general(
        left, right, (((1,), (1,)), ((), ())), preferred_element_type=jnp.float32
    )


def dot_nn(left, right):
    return jnp.dot(left, right, preferred_element_type=jnp.float32)


def head_columns(ref, head):
    return ref[:, head * HEAD_SIZE : (head + 1) * HEAD_SIZE]


def pick_matrix(offset, picked, rows):
    source = lax.broadcasted_iota(jnp.int32, (picked, rows), 1)
    index = lax.broadcasted_iota(jnp.int32, (picked, rows), 0)
    return (source == index * DILATION_RATE + offset).astype(jnp.bfloat16)


def spread_matrix(offset, first, picked, rows, axis):
    shape = (picked, rows) if axis == 0 else (rows, picked)
    index = lax.broadcasted_iota(jnp.int32, shape, axis)
    source = lax.broadcasted_iota(jnp.int32, shape, 1 - axis)
    return (source == (index - first) * DILATION_RATE + offset).astype(jnp.bfloat16)


def split_two(value):
    high = value.astype(jnp.bfloat16)
    low = (value - high.astype(jnp.float32)).astype(jnp.bfloat16)
    return high, low


def split_three(value):
    high = value.astype(jnp.bfloat16)
    rest = value - high.astype(jnp.float32)
    middle = rest.astype(jnp.bfloat16)
    low = (rest - middle.astype(jnp.float32)).astype(jnp.bfloat16)
    return high, middle, low


def fold(value, combine):
    parts = [value[start : start + 8] for start in range(0, value.shape[0], 8)]
    while len(parts) > 1:
        merged = [combine(parts[i], parts[i + 1]) for i in range(0, len(parts) - 1, 2)]
        parts = merged + parts[len(merged) * 2 :]
    return parts[0]


def left_half(shape):
    return lax.broadcasted_iota(jnp.int32, shape, 1) < HEAD_SIZE


def halves(both):
    left = left_half(both.shape)
    zero = jnp.zeros((), both.dtype)
    return jnp.where(left, both, zero), jnp.where(left, zero, both)


def send_pairs(head_count, place, stage_ref, out_refs):
    for step, out_ref in enumerate(out_refs):
        target = lax.rem(lax.bitwise_xor(place, step), head_count)
        out_ref[: stage_ref.shape[1], :] = stage_ref[target]


def pack_kernel(head_count, group, place_ref, offset_ref, key_ref, value_ref, *refs):
    pair_refs, far_ref, stage_ref = refs[:group], refs[group], refs[group + 1]
    rows = key_ref.shape[0]
    picked = far_ref.shape[1]
    for head in range(head_count):
        pair = jnp.concatenate([head_columns(key_ref, head), head_columns(value_ref, head)], 1)
        offset = offset_ref[place_ref[1] * head_count + head]
        picks = dot_nn(pick_matrix(offset, picked, rows), pair).astype(jnp.bfloat16)
        stage_ref[head] = pair
        far_ref[head] = picks
    send_pairs(head_count, place_ref[0], stage_ref, pair_refs)


def project_kernel(head_count, group, shards, others, place_ref, weight_ref, query_ref, *refs):
    upstream_refs, refs = refs[:shards], refs[shards:]
    far_refs, refs = refs[:others], refs[others:]
    pair_refs, grad_ref, stage_ref = refs[:group], refs[group], refs[group + 1]
    shard_rows = upstream_refs[0].shape[0]
    rows = query_ref.shape[0]
    for step, upstream_ref in enumerate(upstream_refs):
        owner = lax.rem(place_ref[1] + (shards - step), shards)
        start = pl.multiple_of(owner * shard_rows, shard_rows)
        grad_ref[pl.ds(start, shard_rows), :] = dot_nt(
            upstream_ref[...], weight_ref[...]
        ).astype(jnp.bfloat16)
    for head in range(head_count):
        stage_ref[head, :rows, :] = jnp.concatenate(
            [head_columns(query_ref, head), head_columns(grad_ref, head)], 1
        )
        for other, far_ref in enumerate(far_refs):
            picked = far_ref.shape[1]
            first = rows + other * picked
            stage_ref[head, first : first + picked, :] = far_ref[head]
    send_pairs(head_count, place_ref[0], stage_ref, pair_refs)


def own_offset(head_count, place_ref, offset_ref):
    return offset_ref[place_ref[1] * head_count + lax.rem(place_ref[0], head_count)]


def far_kernel(head_count, group, others, place_ref, offset_ref, *refs):
    kv_refs, refs = refs[:group], refs[group:]
    qg_refs, refs = refs[:group], refs[group:]
    keys_out, key_t_out, extra_out, own_out, other_out, keys_ref, picked_ref = refs
    rows = kv_refs[0].shape[0]
    near = group * rows
    picked = rows // DILATION_RATE
    count = group * picked
    far = count * (1 + others)
    offset = own_offset(head_count, place_ref, offset_ref)
    pick = pick_matrix(offset, picked, rows)
    for step in range(group):
        pair = kv_refs[step][...]
        keys_ref[step * rows : (step + 1) * rows, :] = pair
        keys_out[step * rows : (step + 1) * rows, :] = pair
        first = near + step * picked
        keys_ref[first : first + picked, :] = dot_nn(pick, pair).astype(jnp.bfloat16)
        for other in range(others):
            first = near + (1 + other) * count + step * picked
            source = rows + other * picked
            keys_ref[first : first + picked, :] = qg_refs[step][source : source + picked, :]
        picked_ref[step * picked : (step + 1) * picked, :] = dot_nn(
            pick, qg_refs[step][:rows, :]
        ).astype(jnp.bfloat16)
    key_t = keys_ref[...].astype(jnp.float32).T[:HEAD_SIZE].astype(jnp.bfloat16)
    key_t_out[...] = key_t[:, :near]
    query, grad = halves(picked_ref[...])
    score = dot_nt(keys_ref[...], query)
    dprob = dot_nt(keys_ref[...], grad)
    top = jnp.max(score, 0, keepdims=True)
    prob = jnp.exp2((score - top) * SCORE_FACTOR)
    total = jnp.sum(prob, 0, keepdims=True)
    inverse = 1.0 / total
    delta = jnp.sum(prob * dprob, 0, keepdims=True) * inverse
    prob_far = prob[near:] * inverse
    dscore = (prob_far * (dprob[near:] - delta)).astype(jnp.bfloat16)
    terms = dot_nn(
        jnp.concatenate([dscore, prob_far.astype(jnp.bfloat16)], 1),
        jnp.concatenate([query, grad], 0),
    ) * jnp.where(left_half((far, PAIR)), SCALE, 1.0)
    own_out[...] = terms[:count]
    other_out[...] = terms[count:]
    query_grad = dot_nn(key_t[:, near:], dscore)
    lse = top * SCORE_FACTOR + jnp.log2(total)
    extra_out[:PAIR, :] = jnp.concatenate(split_two(query_grad), 0)
    blank = jnp.zeros((STAT_ROWS - 6, count), jnp.bfloat16)
    extra_out[PAIR:, :] = jnp.concatenate([*split_three(lse), *split_three(delta), blank], 0)


def near_block(
    first, offset, keys_ref, key_t_ref, qg_ref, extra_ref, score_ref, dprob_ref, work_ref, acc_ref
):
    near = keys_ref.shape[0]
    rows = score_ref.shape[1]
    count = extra_ref.shape[1]
    query, grad = halves(qg_ref[:rows, :])
    score_ref[...] = dot_nt(keys_ref[...], query)
    dprob_ref[...] = dot_nt(keys_ref[...], grad)
    extra = dot_nn(extra_ref[...], spread_matrix(offset, first, count, rows, 0))
    row_lane = lax.broadcasted_iota(jnp.int32, (1, rows), 1)
    picked = lax.rem(row_lane, DILATION_RATE) == offset
    lse_picked = extra[PAIR : PAIR + 1] + extra[PAIR + 1 : PAIR + 2] + extra[PAIR + 2 : PAIR + 3]
    delta_picked = (
        extra[PAIR + 3 : PAIR + 4] + extra[PAIR + 4 : PAIR + 5] + extra[PAIR + 5 : PAIR + 6]
    )
    strips = [slice(start, start + STRIP) for start in range(0, near, STRIP)]
    top = None
    for strip in strips:
        part = fold(score_ref[strip, :], jnp.maximum)
        top = part if top is None else jnp.maximum(top, part)
    top = jnp.max(top, 0, keepdims=True) * SCORE_FACTOR
    top = jnp.where(picked, lse_picked, top)
    total = jnp.zeros((8, rows), jnp.float32)
    delta = jnp.zeros((8, rows), jnp.float32)
    for strip in strips:
        prob = jnp.exp2(score_ref[strip, :] * SCORE_FACTOR - top)
        total = total + fold(prob, jnp.add)
        delta = delta + fold(prob * dprob_ref[strip, :], jnp.add)
        score_ref[strip, :] = prob
    inverse = jnp.where(picked, 1.0, 1.0 / jnp.sum(total, 0, keepdims=True))
    delta = jnp.where(picked, delta_picked, jnp.sum(delta, 0, keepdims=True) * inverse)
    for strip in strips:
        prob = score_ref[strip, :] * inverse
        work_ref[strip, :rows] = (prob * (dprob_ref[strip, :] - delta)).astype(jnp.bfloat16)
        work_ref[strip, rows:] = prob.astype(jnp.bfloat16)
    acc_ref[...] += dot_nn(work_ref[...], jnp.concatenate([query, grad], 0))
    query_grad = dot_nn(key_t_ref[...], work_ref[:, :rows])
    query_grad = query_grad + extra[:HEAD_SIZE] + extra[HEAD_SIZE:PAIR]
    query_grad = (query_grad * SCALE).T.astype(jnp.bfloat16)
    half = rows // 2
    return jnp.concatenate([query_grad[:half], query_grad[half:]], 1)


def first_kernel(head_count, steps, place_ref, offset_ref, keys_ref, key_t_ref, extra_ref, *refs):
    qg_refs, refs = refs[:steps], refs[steps:]
    acc_ref, query_out, *scratch = refs
    offset = own_offset(head_count, place_ref, offset_ref)
    picked = extra_ref.shape[1] // (keys_ref.shape[0] // scratch[0].shape[2])
    acc_ref[...] = jnp.zeros_like(acc_ref)
    for step, qg_ref in enumerate(qg_refs):
        query_out[step] = near_block(
            step * picked, offset, keys_ref, key_t_ref, qg_ref, extra_ref,
            *[ref.at[step % 2] for ref in scratch], acc_ref,
        )


def second_kernel(
    head_count, steps, others, place_ref, offset_ref, keys_ref, key_t_ref, extra_ref, start_ref,
    query_ref, own_ref, *refs,
):
    back_refs, refs = refs[:others], refs[others:]
    qg_refs, refs = refs[:steps], refs[steps:]
    rows = query_ref.shape[1] * 2
    group = keys_ref.shape[0] // rows
    out_refs, refs = refs[:group], refs[group:]
    acc_ref, *scratch = refs
    count = extra_ref.shape[1]
    picked = count // group
    offset = own_offset(head_count, place_ref, offset_ref)
    acc_ref[...] = start_ref[...]
    for step, qg_ref in enumerate(qg_refs):
        place = group - steps + step
        out_refs[place][rows:, :] = near_block(
            place * picked, offset, keys_ref, key_t_ref, qg_ref, extra_ref,
            *[ref.at[step % 2] for ref in scratch], acc_ref,
        )
    terms = own_ref[...]
    for back_ref in back_refs:
        terms = terms + back_ref[...]
    terms = jnp.concatenate(split_two(terms), 0)
    factor = jnp.where(left_half((rows, PAIR)), SCALE, 1.0)
    for place in range(group):
        spread = spread_matrix(offset, place * picked, count, rows, 1)
        placed = dot_nn(jnp.concatenate([spread, spread], 1), terms)
        summed = acc_ref[place * rows : (place + 1) * rows, :] * factor + placed
        out_refs[place][:rows, :] = summed.astype(jnp.bfloat16)
        if place < group - steps:
            out_refs[place][rows:, :] = query_ref[place]


def unpack_kernel(head_count, group, place_ref, *refs):
    near_refs, refs = refs[:group], refs[group:]
    query_out, key_out, value_out, stage_ref = refs
    rows = query_out.shape[0]
    half = rows // 2
    for step, near_ref in enumerate(near_refs):
        stage_ref[lax.bitwise_xor(place_ref[0], step)] = near_ref[...]
    for head in range(head_count):
        columns = slice(head * HEAD_SIZE, (head + 1) * HEAD_SIZE)
        key_out[:, columns] = stage_ref[head, :rows, :HEAD_SIZE]
        value_out[:, columns] = stage_ref[head, :rows, HEAD_SIZE:]
        query_out[:half, columns] = stage_ref[head, rows:, :HEAD_SIZE]
        query_out[half:, columns] = stage_ref[head, rows:, HEAD_SIZE:]


def call(kernel, name, out_shape, operands, scalars, scratch=(), flops=0):
    return pl.pallas_call(
        kernel,
        out_shape=tuple(jax.ShapeDtypeStruct(*shape) for shape in out_shape),
        in_specs=[SMEM] * scalars + [VMEM] * (len(operands) - scalars),
        out_specs=tuple(VMEM for _ in out_shape),
        scratch_shapes=[pltpu.VMEM(*shape) for shape in scratch],
        compiler_params=pltpu.CompilerParams(vmem_limit_bytes=40 * 1024 * 1024),
        cost_estimate=pl.CostEstimate(flops=flops, bytes_accessed=2**21, transcendentals=0),
        name=name,
    )(*operands)


def body(upstream, out_weight, query_rows, key_rows, value_rows, head_offsets):
    rows, width = query_rows.shape
    head_count = width // HEAD_SIZE
    devices = lax.axis_size("context")
    shards = lax.axis_size("heads")
    group = FIRST_SEGMENT // rows
    others = devices // group - 1
    picked = rows // DILATION_RATE
    count = group * picked
    near = group * rows
    place = jnp.stack(
        [lax.rem(lax.axis_index("context"), group), lax.axis_index("heads")]
    ).astype(jnp.int32)

    def swap(values):
        pairs = [[(source, source ^ step) for source in range(devices)] for step in range(group)]
        return [values[0]] + [
            lax.ppermute(values[step], "context", pairs[step]) for step in range(1, group)
        ]

    def segment_shift(value, shift):
        pairs = [(source, (source + shift * group) % devices) for source in range(devices)]
        return lax.ppermute(value, "context", pairs)

    upstreams = [upstream]
    for step in range(1, shards):
        pairs = [(source, (source + step) % shards) for source in range(shards)]
        upstreams.append(lax.ppermute(upstream, "heads", pairs))

    bf16, f32 = jnp.bfloat16, jnp.float32
    *kv_send, far_send = call(
        functools.partial(pack_kernel, head_count, group), "pack_keys_values",
        [((rows, PAIR), bf16)] * group + [((head_count, picked, PAIR), bf16)],
        [place, head_offsets, key_rows, value_rows], 2,
        [((head_count, rows, PAIR), bf16)],
    )
    far_in = [segment_shift(far_send, shift) for shift in range(1, others + 1)]
    kv = swap(kv_send)

    sent_rows = rows + others * picked
    qg_send = call(
        functools.partial(project_kernel, head_count, group, shards, others), "project_pack",
        [((sent_rows, PAIR), bf16)] * group,
        [place, out_weight, query_rows, *upstreams, *far_in], 1,
        [((rows, width), bf16), ((head_count, sent_rows, PAIR), bf16)],
        flops=2 * rows * width * upstream.shape[1],
    )
    qg = swap(qg_send)

    keys, key_t, extra, own_terms, other_terms = call(
        functools.partial(far_kernel, head_count, group, others), "picked_rows",
        [
            ((near, PAIR), bf16), ((HEAD_SIZE, near), bf16), ((PAIR + STAT_ROWS, count), bf16),
            ((count, PAIR), f32), ((others * count, PAIR), f32),
        ],
        [place, head_offsets, *kv, *qg], 2,
        [((near + count * (1 + others), PAIR), bf16), ((count, PAIR), bf16)],
        flops=8 * near * count * PAIR,
    )
    back = [
        segment_shift(other_terms[(shift - 1) * count : shift * count], -shift)
        for shift in range(1, others + 1)
    ]
    steps = group // 2
    scratch = [
        ((2, near, rows), f32), ((2, near, rows), f32), ((2, near, 2 * rows), bf16),
    ]
    half_flops = 10 * near * near // 2 * PAIR
    acc, query_half = call(
        functools.partial(first_kernel, head_count, steps), "first_rows",
        [((near, PAIR), f32), ((steps, rows // 2, PAIR), bf16)],
        [place, head_offsets, keys, key_t, extra, *qg[:steps]], 2, scratch, half_flops,
    )
    near_send = call(
        functools.partial(second_kernel, head_count, group - steps, others), "second_rows",
        [((rows + rows // 2, PAIR), bf16)] * group,
        [place, head_offsets, keys, key_t, extra, acc, query_half, own_terms, *back, *qg[steps:]],
        2, [((near, PAIR), f32)] + scratch, half_flops,
    )
    return tuple(
        call(
            functools.partial(unpack_kernel, head_count, group), "unpack",
            [((rows, width), bf16)] * 3,
            [place, *swap(near_send)], 1,
            [((group, rows + rows // 2, PAIR), bf16)],
        )
    )


def solution(mesh):
    return jax.shard_map(
        body,
        mesh=mesh,
        in_specs=(
            P(("context", "heads"), None),
            P("heads", None),
            P("context", "heads"),
            P("context", "heads"),
            P("context", "heads"),
            P(),
        ),
        out_specs=(P("context", "heads"), P("context", "heads"), P("context", "heads")),
        check_vma=False,
    )
```

```python
import functools
import math

import jax
import jax.numpy as jnp
from jax import lax
from jax.experimental import pallas as pl
from jax.experimental.pallas import tpu as pltpu
from jax.sharding import PartitionSpec as P

HEAD_SIZE = 64
PAIR = 2 * HEAD_SIZE
DILATION_RATE = 16
FIRST_SEGMENT = 2048
SCALE = 1.0 / math.sqrt(HEAD_SIZE)
LOG2E = math.log2(math.e)
SCORE_FACTOR = SCALE * LOG2E
STRIP = 64
STAT_ROWS = 16

SMEM = pl.BlockSpec(memory_space=pltpu.SMEM)
VMEM = pl.BlockSpec(memory_space=pltpu.VMEM)
ANY = pl.BlockSpec(memory_space=pl.ANY)


def dot_nt(left, right):
    return lax.dot_general(
        left, right, (((1,), (1,)), ((), ())), preferred_element_type=jnp.float32
    )


def dot_nn(left, right):
    return jnp.dot(left, right, preferred_element_type=jnp.float32)


def head_columns(ref, head):
    return ref[:, head * HEAD_SIZE : (head + 1) * HEAD_SIZE]


def pick_matrix(offset, picked, rows):
    source = lax.broadcasted_iota(jnp.int32, (picked, rows), 1)
    index = lax.broadcasted_iota(jnp.int32, (picked, rows), 0)
    return (source == index * DILATION_RATE + offset).astype(jnp.bfloat16)


def spread_matrix(offset, first, picked, rows, axis):
    shape = (picked, rows) if axis == 0 else (rows, picked)
    index = lax.broadcasted_iota(jnp.int32, shape, axis)
    source = lax.broadcasted_iota(jnp.int32, shape, 1 - axis)
    return (source == (index - first) * DILATION_RATE + offset).astype(jnp.bfloat16)


def split_two(value):
    high = value.astype(jnp.bfloat16)
    low = (value - high.astype(jnp.float32)).astype(jnp.bfloat16)
    return high, low


def split_three(value):
    high = value.astype(jnp.bfloat16)
    rest = value - high.astype(jnp.float32)
    middle = rest.astype(jnp.bfloat16)
    low = (rest - middle.astype(jnp.float32)).astype(jnp.bfloat16)
    return high, middle, low


def fold(value, combine):
    parts = [value[start : start + 8] for start in range(0, value.shape[0], 8)]
    while len(parts) > 1:
        merged = [combine(parts[i], parts[i + 1]) for i in range(0, len(parts) - 1, 2)]
        parts = merged + parts[len(merged) * 2 :]
    return parts[0]


def left_half(shape):
    return lax.broadcasted_iota(jnp.int32, shape, 1) < HEAD_SIZE


def side_by_side(block):
    half = block.shape[0] // 2
    return jnp.concatenate([block[:half], block[half:]], 1)


def pack_kernel(head_count, query_hbm, key_hbm, value_hbm, *refs):
    out_ref, query_ref, key_ref, value_ref, sems = refs
    rows = query_ref.shape[0]
    copies = [
        pltpu.make_async_copy(source, target, sems.at[index])
        for index, (source, target) in enumerate(
            [(key_hbm, key_ref), (value_hbm, value_ref), (query_hbm, query_ref)]
        )
    ]
    for copy in copies:
        copy.start()
    for copy in copies:
        copy.wait()
    for head in range(head_count):
        pair = jnp.concatenate([head_columns(key_ref, head), head_columns(value_ref, head)], 1)
        query = side_by_side(head_columns(query_ref, head))
        for place in range(head, out_ref.shape[0], head_count):
            out_ref[place, :rows, :] = pair
            out_ref[place, rows:, :] = query


def project_kernel(head_count, group, shards, place_ref, weight_ref, *refs):
    upstream_refs, refs = refs[:shards], refs[shards:]
    out_refs, grad_ref, stage_ref = refs[:group], refs[group], refs[group + 1]
    shard_rows = upstream_refs[0].shape[0]
    for step, upstream_ref in enumerate(upstream_refs):
        owner = lax.rem(place_ref[1] + (shards - step), shards)
        start = pl.multiple_of(owner * shard_rows, shard_rows)
        grad_ref[pl.ds(start, shard_rows), :] = dot_nt(
            upstream_ref[...], weight_ref[...]
        ).astype(jnp.bfloat16)
    for head in range(head_count):
        stage_ref[head] = side_by_side(head_columns(grad_ref, head))
    for step, out_ref in enumerate(out_refs):
        out_ref[...] = stage_ref[lax.rem(lax.bitwise_xor(place_ref[0], step), head_count)]


def own_offset(head_count, place_ref):
    return place_ref[2 + place_ref[1] * head_count + lax.rem(place_ref[0], head_count)]


def gather_kernel(head_count, place_ref, sent_ref, after_ref, keys_out, key_t_out, picks_out):
    group, sent_rows, _ = sent_ref.shape
    rows = keys_out.shape[0] // group
    picked = rows // DILATION_RATE
    pick = pick_matrix(own_offset(head_count, place_ref), picked, rows)
    for step in range(group):
        pair = sent_ref[lax.bitwise_xor(place_ref[0], step), :rows, :]
        keys_out[step * rows : (step + 1) * rows, :] = pair
        picks_out[step * picked : (step + 1) * picked, :] = dot_nn(pick, pair).astype(jnp.bfloat16)
        key_t_out[:, step * rows : (step + 1) * rows] = (
            pair.astype(jnp.float32).T[:HEAD_SIZE].astype(jnp.bfloat16)
        )


def queries_from(sent_ref, place_ref, step, rows):
    return sent_ref.at[lax.bitwise_xor(place_ref[0], step), rows:]


def query_and_grad(query_ref, grad_ref):
    query, grad = query_ref[...], grad_ref[...]
    zero = jnp.zeros((query.shape[0], HEAD_SIZE), query.dtype)
    return (
        jnp.concatenate(
            [
                jnp.concatenate([query[:, :HEAD_SIZE], zero], 1),
                jnp.concatenate([query[:, HEAD_SIZE:], zero], 1),
            ], 0,
        ),
        jnp.concatenate(
            [
                jnp.concatenate([zero, grad[:, :HEAD_SIZE]], 1),
                jnp.concatenate([zero, grad[:, HEAD_SIZE:]], 1),
            ], 0,
        ),
    )


def far_kernel(head_count, group, others, place_ref, near_ref, sent_ref, picks_ref, *refs):
    other_refs, refs = refs[:others], refs[others:]
    grad_refs, refs = refs[:group], refs[group:]
    extra_out, own_out, other_out, keys_ref, query_ref, grad_ref = refs
    near = near_ref.shape[0]
    rows = near // group
    picked = rows // DILATION_RATE
    count = group * picked
    far = count * (1 + others)
    pick = pick_matrix(own_offset(head_count, place_ref), picked, rows)
    keys_ref[:near, :] = near_ref[...]
    for index, ref in enumerate([picks_ref, *other_refs]):
        keys_ref[near + index * count : near + (index + 1) * count, :] = ref[...]
    for step in range(group):
        query, grad = query_and_grad(queries_from(sent_ref, place_ref, step, rows), grad_refs[step])
        span = slice(step * picked, (step + 1) * picked)
        query_ref[span, :] = dot_nn(pick, query).astype(jnp.bfloat16)
        grad_ref[span, :] = dot_nn(pick, grad).astype(jnp.bfloat16)
    far_t = keys_ref[near:, :].astype(jnp.float32).T[:HEAD_SIZE].astype(jnp.bfloat16)
    query, grad = query_ref[...], grad_ref[...]
    score = dot_nt(keys_ref[...], query)
    dprob = dot_nt(keys_ref[...], grad)
    top = jnp.max(score, 0, keepdims=True)
    prob = jnp.exp2((score - top) * SCORE_FACTOR)
    total = jnp.sum(prob, 0, keepdims=True)
    inverse = 1.0 / total
    delta = jnp.sum(prob * dprob, 0, keepdims=True) * inverse
    prob_far = prob[near:] * inverse
    dscore = (prob_far * (dprob[near:] - delta)).astype(jnp.bfloat16)
    terms = dot_nn(
        jnp.concatenate([dscore, prob_far.astype(jnp.bfloat16)], 1),
        jnp.concatenate([query, grad], 0),
    ) * jnp.where(left_half((far, PAIR)), SCALE, 1.0)
    own_out[...] = terms[:count]
    other_out[...] = terms[count:]
    query_grad = dot_nn(far_t, dscore)
    lse = top * SCORE_FACTOR + jnp.log2(total)
    extra_out[:PAIR, :] = jnp.concatenate(split_two(query_grad), 0)
    blank = jnp.zeros((STAT_ROWS - 6, count), jnp.bfloat16)
    extra_out[PAIR:, :] = jnp.concatenate([*split_three(lse), *split_three(delta), blank], 0)


def near_block(
    first, offset, keys_ref, key_t_ref, query_ref, grad_ref, extra_ref, score_ref, dprob_ref,
    work_ref, acc_ref,
):
    near = keys_ref.shape[0]
    rows = score_ref.shape[1]
    count = extra_ref.shape[1]
    query, grad = query_and_grad(query_ref, grad_ref)
    score_ref[...] = dot_nt(keys_ref[...], query)
    dprob_ref[...] = dot_nt(keys_ref[...], grad)
    extra = dot_nn(extra_ref[...], spread_matrix(offset, first, count, rows, 0))
    row_lane = lax.broadcasted_iota(jnp.int32, (1, rows), 1)
    picked = lax.rem(row_lane, DILATION_RATE) == offset
    lse_picked = extra[PAIR : PAIR + 1] + extra[PAIR + 1 : PAIR + 2] + extra[PAIR + 2 : PAIR + 3]
    delta_picked = (
        extra[PAIR + 3 : PAIR + 4] + extra[PAIR + 4 : PAIR + 5] + extra[PAIR + 5 : PAIR + 6]
    )
    strips = [slice(start, start + STRIP) for start in range(0, near, STRIP)]
    top = None
    for strip in strips:
        part = fold(score_ref[strip, :], jnp.maximum)
        top = part if top is None else jnp.maximum(top, part)
    top = jnp.max(top, 0, keepdims=True) * SCORE_FACTOR
    top = jnp.where(picked, lse_picked, top)
    total = jnp.zeros((8, rows), jnp.float32)
    delta = jnp.zeros((8, rows), jnp.float32)
    for strip in strips:
        prob = jnp.exp2(score_ref[strip, :] * SCORE_FACTOR - top)
        total = total + fold(prob, jnp.add)
        delta = delta + fold(prob * dprob_ref[strip, :], jnp.add)
        score_ref[strip, :] = prob
    inverse = jnp.where(picked, 1.0, 1.0 / jnp.sum(total, 0, keepdims=True))
    delta = jnp.where(picked, delta_picked, jnp.sum(delta, 0, keepdims=True) * inverse)
    for strip in strips:
        prob = score_ref[strip, :] * inverse
        work_ref[strip, :rows] = (prob * (dprob_ref[strip, :] - delta)).astype(jnp.bfloat16)
        work_ref[strip, rows:] = prob.astype(jnp.bfloat16)
    acc_ref[...] += dot_nn(work_ref[...], jnp.concatenate([query, grad], 0))
    query_grad = dot_nn(key_t_ref[...], work_ref[:, :rows])
    query_grad = query_grad + extra[:HEAD_SIZE] + extra[HEAD_SIZE:PAIR]
    query_grad = (query_grad * SCALE).T.astype(jnp.bfloat16)
    half = rows // 2
    return jnp.concatenate([query_grad[:half], query_grad[half:]], 1)


def first_kernel(head_count, place_ref, keys_ref, key_t_ref, sent_ref, extra_ref, *refs):
    acc_ref, query_out, *scratch = refs[-5:]
    grad_refs = refs[:-5]
    rows = scratch[0].shape[2]
    offset = own_offset(head_count, place_ref)
    acc_ref[...] = jnp.zeros_like(acc_ref)
    for step, grad_ref in enumerate(grad_refs):
        query_out[step] = near_block(
            step * (rows // DILATION_RATE), offset, keys_ref, key_t_ref,
            queries_from(sent_ref, place_ref, step, rows), grad_ref, extra_ref,
            *[ref.at[step % 2] for ref in scratch], acc_ref,
        )


def second_kernel(
    head_count, steps, others, place_ref, keys_ref, key_t_ref, sent_ref, extra_ref, start_ref,
    query_ref, own_ref, *refs,
):
    back_refs, refs = refs[:others], refs[others:]
    grad_refs, refs = refs[:steps], refs[steps:]
    rows = query_ref.shape[1] * 2
    group = keys_ref.shape[0] // rows
    out_refs, refs = refs[:group], refs[group:]
    acc_ref, *scratch = refs
    count = extra_ref.shape[1]
    picked = count // group
    offset = own_offset(head_count, place_ref)
    acc_ref[...] = start_ref[...]
    for step, grad_ref in enumerate(grad_refs):
        place = group - steps + step
        out_refs[place][rows:, :] = near_block(
            place * picked, offset, keys_ref, key_t_ref,
            queries_from(sent_ref, place_ref, place, rows), grad_ref, extra_ref,
            *[ref.at[step % 2] for ref in scratch], acc_ref,
        )
    terms = own_ref[...]
    for back_ref in back_refs:
        terms = terms + back_ref[...]
    terms = jnp.concatenate(split_two(terms), 0)
    factor = jnp.where(left_half((rows, PAIR)), SCALE, 1.0)
    for place in range(group):
        spread = spread_matrix(offset, place * picked, count, rows, 1)
        placed = dot_nn(jnp.concatenate([spread, spread], 1), terms)
        summed = acc_ref[place * rows : (place + 1) * rows, :] * factor + placed
        out_refs[place][:rows, :] = summed.astype(jnp.bfloat16)
        if place < group - steps:
            out_refs[place][rows:, :] = query_ref[place]


def unpack_kernel(head_count, group, place_ref, *refs):
    near_refs, refs = refs[:group], refs[group:]
    query_out, key_out, value_out, stage_ref = refs
    rows = query_out.shape[0]
    half = rows // 2
    for step, near_ref in enumerate(near_refs):
        stage_ref[lax.bitwise_xor(place_ref[0], step)] = near_ref[...]
    for head in range(head_count):
        columns = slice(head * HEAD_SIZE, (head + 1) * HEAD_SIZE)
        key_out[:, columns] = stage_ref[head, :rows, :HEAD_SIZE]
        value_out[:, columns] = stage_ref[head, :rows, HEAD_SIZE:]
        query_out[:half, columns] = stage_ref[head, rows:, :HEAD_SIZE]
        query_out[half:, columns] = stage_ref[head, rows:, HEAD_SIZE:]


def call(kernel, name, out_shape, operands, scratch=(), flops=0, hbm=0):
    specs = [ANY] * hbm if hbm else [SMEM] + [VMEM] * (len(operands) - 1)
    return pl.pallas_call(
        kernel,
        out_shape=tuple(jax.ShapeDtypeStruct(*shape) for shape in out_shape),
        in_specs=specs,
        out_specs=tuple(VMEM for _ in out_shape),
        scratch_shapes=[pltpu.VMEM(*shape) if isinstance(shape, tuple) else shape for shape in scratch],
        compiler_params=pltpu.CompilerParams(vmem_limit_bytes=(60 if hbm else 40) * 1024 * 1024),
        cost_estimate=pl.CostEstimate(flops=flops, bytes_accessed=2**21, transcendentals=0),
        name=name,
    )(*operands)


def swap_order(group):
    return sorted(range(1, group), key=lambda step: (-(step >> 1).bit_count(), step & 1, step))


def body(upstream, out_weight, query_rows, key_rows, value_rows, head_offsets):
    rows, width = query_rows.shape
    head_count = width // HEAD_SIZE
    devices = lax.axis_size("context")
    shards = lax.axis_size("heads")
    group = FIRST_SEGMENT // rows
    others = devices // group - 1
    half = rows // 2
    picked = rows // DILATION_RATE
    count = group * picked
    near = group * rows
    place = jnp.stack([lax.rem(lax.axis_index("context"), group), lax.axis_index("heads")])
    place = jnp.concatenate([place.astype(jnp.int32), head_offsets])

    def swap(values):
        result = list(values)
        for step in swap_order(group):
            pairs = [(source, source ^ step) for source in range(devices)]
            result[step] = lax.ppermute(values[step], "context", pairs)
        return result

    def segment_shift(value, shift):
        pairs = [(source, (source + shift * group) % devices) for source in range(devices)]
        return lax.ppermute(value, "context", pairs)

    upstreams = [upstream]
    for step in range(1, shards):
        pairs = [(source, (source + step) % shards) for source in range(shards)]
        upstreams.append(lax.ppermute(upstream, "heads", pairs))

    bf16, f32 = jnp.bfloat16, jnp.float32
    (sent,) = call(
        functools.partial(pack_kernel, head_count), "pack_rows",
        [((group, rows + half, PAIR), bf16)],
        [query_rows, key_rows, value_rows],
        [((rows, width), bf16)] * 3 + [pltpu.SemaphoreType.DMA((3,))], hbm=3,
    )
    groups = [list(range(first, first + group)) for first in range(0, devices, group)]
    sent = lax.all_to_all(sent, "context", 0, 0, axis_index_groups=groups)
    grads = swap(
        call(
            functools.partial(project_kernel, head_count, group, shards), "project_pack",
            [((half, PAIR), bf16)] * group,
            [place, out_weight, *upstreams],
            [((rows, width), bf16), ((head_count, half, PAIR), bf16)],
            flops=2 * rows * width * upstream.shape[1],
        )
    )
    keys, key_t, picks = call(
        functools.partial(gather_kernel, head_count), "gather_keys",
        [((near, PAIR), bf16), ((HEAD_SIZE, near), bf16), ((count, PAIR), bf16)],
        [place, sent, grads[0]],
    )
    other_picks = [segment_shift(picks, shift) for shift in range(1, others + 1)]
    extra, own_terms, other_terms = call(
        functools.partial(far_kernel, head_count, group, others), "picked_rows",
        [
            ((PAIR + STAT_ROWS, count), bf16),
            ((count, PAIR), f32), ((others * count, PAIR), f32),
        ],
        [place, keys, sent, picks, *other_picks, *grads],
        [((near + count * (1 + others), PAIR), bf16)] + [((count, PAIR), bf16)] * 2,
        flops=8 * near * count * PAIR,
    )
    back = [
        segment_shift(other_terms[(shift - 1) * count : shift * count], -shift)
        for shift in range(1, others + 1)
    ]
    steps = group // 2
    scratch = [
        ((2, near, rows), f32), ((2, near, rows), f32), ((2, near, 2 * rows), bf16),
    ]
    half_flops = 10 * near * near // 2 * PAIR
    acc, query_half = call(
        functools.partial(first_kernel, head_count), "first_rows",
        [((near, PAIR), f32), ((steps, half, PAIR), bf16)],
        [place, keys, key_t, sent, extra, *grads[:steps]], scratch, half_flops,
    )
    near_send = call(
        functools.partial(second_kernel, head_count, group - steps, others), "second_rows",
        [((rows + half, PAIR), bf16)] * group,
        [place, keys, key_t, sent, extra, acc, query_half, own_terms, *back, *grads[steps:]],
        [((near, PAIR), f32)] + scratch, half_flops,
    )
    return tuple(
        call(
            functools.partial(unpack_kernel, head_count, group), "unpack",
            [((rows, width), bf16)] * 3,
            [place, *swap(near_send)],
            [((group, rows + half, PAIR), bf16)],
        )
    )


def solution(mesh):
    return jax.shard_map(
        body,
        mesh=mesh,
        in_specs=(
            P(("context", "heads"), None),
            P("heads", None),
            P("context", "heads"),
            P("context", "heads"),
            P("context", "heads"),
            P(),
        ),
        out_specs=(P("context", "heads"), P("context", "heads"), P("context", "heads")),
        check_vma=False,
    )
```

```python
import functools
import math

import jax
import jax.numpy as jnp
from jax import lax
from jax.experimental import pallas as pl
from jax.experimental.pallas import tpu as pltpu
from jax.sharding import PartitionSpec as P

HEAD_SIZE = 64
PAIR = 2 * HEAD_SIZE
DILATION_RATE = 16
FIRST_SEGMENT = 2048
SCALE = 1.0 / math.sqrt(HEAD_SIZE)
LOG2E = math.log2(math.e)
SCORE_FACTOR = SCALE * LOG2E
STRIP = 64
STAT_ROWS = 16

SMEM = pl.BlockSpec(memory_space=pltpu.SMEM)
VMEM = pl.BlockSpec(memory_space=pltpu.VMEM)
ANY = pl.BlockSpec(memory_space=pl.ANY)


def dot_nt(left, right):
    return lax.dot_general(
        left, right, (((1,), (1,)), ((), ())), preferred_element_type=jnp.float32
    )


def dot_nn(left, right):
    return jnp.dot(left, right, preferred_element_type=jnp.float32)


def head_columns(ref, head):
    return ref[:, head * HEAD_SIZE : (head + 1) * HEAD_SIZE]


def pick_matrix(offset, picked, rows):
    source = lax.broadcasted_iota(jnp.int32, (picked, rows), 1)
    index = lax.broadcasted_iota(jnp.int32, (picked, rows), 0)
    return (source == index * DILATION_RATE + offset).astype(jnp.bfloat16)


def spread_matrix(offset, first, picked, rows, axis):
    shape = (picked, rows) if axis == 0 else (rows, picked)
    index = lax.broadcasted_iota(jnp.int32, shape, axis)
    source = lax.broadcasted_iota(jnp.int32, shape, 1 - axis)
    return (source == (index - first) * DILATION_RATE + offset).astype(jnp.bfloat16)


def split_two(value):
    high = value.astype(jnp.bfloat16)
    low = (value - high.astype(jnp.float32)).astype(jnp.bfloat16)
    return high, low


def split_three(value):
    high = value.astype(jnp.bfloat16)
    rest = value - high.astype(jnp.float32)
    middle = rest.astype(jnp.bfloat16)
    low = (rest - middle.astype(jnp.float32)).astype(jnp.bfloat16)
    return high, middle, low


def fold(value, combine):
    parts = [value[start : start + 8] for start in range(0, value.shape[0], 8)]
    while len(parts) > 1:
        merged = [combine(parts[i], parts[i + 1]) for i in range(0, len(parts) - 1, 2)]
        parts = merged + parts[len(merged) * 2 :]
    return parts[0]


def left_half(shape):
    return lax.broadcasted_iota(jnp.int32, shape, 1) < HEAD_SIZE


def side_by_side(block):
    half = block.shape[0] // 2
    return jnp.concatenate([block[:half], block[half:]], 1)


def swap_steps(group):
    if group == 8:
        return [(6, 6), (2, 4), (7, 1), (4, 2), (1, 7), (3, 5), (5, 3)]
    return [(bits, bits) for bits in range(1, group)]


def target_of(place, step):
    return lax.bitwise_xor(place, jnp.where(lax.rem(place, 2) == 1, step[1], step[0]))


def source_of(place, step):
    odd = lax.rem(place + step[0], 2) == 1
    return lax.bitwise_xor(place, jnp.where(odd, step[1], step[0]))


def send_out(place, head_count, stage_ref, out_refs):
    out_refs[0][...] = stage_ref[lax.rem(place, head_count)]
    for step, out_ref in zip(swap_steps(len(out_refs)), out_refs[1:]):
        out_ref[...] = stage_ref[lax.rem(target_of(place, step), head_count)]


def places_of(place, group):
    return [place] + [source_of(place, step) for step in swap_steps(group)]


def pack_kernel(head_count, group, place_ref, query_hbm, key_hbm, value_hbm, *refs):
    out_refs, (query_ref, key_ref, value_ref, stage_ref, sems) = refs[:group], refs[group:]
    rows = query_ref.shape[0]
    copies = [
        pltpu.make_async_copy(source, target, sems.at[index])
        for index, (source, target) in enumerate(
            [(key_hbm, key_ref), (value_hbm, value_ref), (query_hbm, query_ref)]
        )
    ]
    for copy in copies:
        copy.start()
    for copy in copies:
        copy.wait()
    for head in range(head_count):
        stage_ref[head, :rows, :] = jnp.concatenate(
            [head_columns(key_ref, head), head_columns(value_ref, head)], 1
        )
        stage_ref[head, rows:, :] = side_by_side(head_columns(query_ref, head))
    send_out(place_ref[0], head_count, stage_ref, out_refs)


def project_kernel(head_count, group, shards, place_ref, weight_ref, *refs):
    upstream_refs, refs = refs[:shards], refs[shards:]
    out_refs, grad_ref, stage_ref = refs[:group], refs[group], refs[group + 1]
    shard_rows = upstream_refs[0].shape[0]
    for step, upstream_ref in enumerate(upstream_refs):
        owner = lax.rem(place_ref[1] + (shards - step), shards)
        start = pl.multiple_of(owner * shard_rows, shard_rows)
        grad_ref[pl.ds(start, shard_rows), :] = dot_nt(
            upstream_ref[...], weight_ref[...]
        ).astype(jnp.bfloat16)
    for head in range(head_count):
        stage_ref[head] = side_by_side(head_columns(grad_ref, head))
    send_out(place_ref[0], head_count, stage_ref, out_refs)


def own_offset(head_count, place_ref, offset_ref):
    return offset_ref[place_ref[1] * head_count + lax.rem(place_ref[0], head_count)]


def gather_kernel(head_count, group, place_ref, offset_ref, *refs):
    sent_refs, refs = refs[:group], refs[group + 1 :]
    keys_out, key_t_out, queries_out, picks_out = refs
    rows = keys_out.shape[0] // group
    picked = rows // DILATION_RATE
    pick = pick_matrix(own_offset(head_count, place_ref, offset_ref), picked, rows)
    for place, sent_ref in zip(places_of(place_ref[0], group), sent_refs):
        pair = sent_ref[:rows, :]
        keys_out[pl.ds(pl.multiple_of(place * rows, rows), rows), :] = pair
        picks_out[pl.ds(pl.multiple_of(place * picked, picked), picked), :] = dot_nn(
            pick, pair
        ).astype(jnp.bfloat16)
        queries_out[place] = sent_ref[rows:, :]
    key_t_out[...] = keys_out[...].astype(jnp.float32).T[:HEAD_SIZE].astype(jnp.bfloat16)


def query_and_grad(query_ref, grad_ref):
    query, grad = query_ref[...], grad_ref[...]
    zero = jnp.zeros((query.shape[0], HEAD_SIZE), query.dtype)
    return (
        jnp.concatenate(
            [
                jnp.concatenate([query[:, :HEAD_SIZE], zero], 1),
                jnp.concatenate([query[:, HEAD_SIZE:], zero], 1),
            ], 0,
        ),
        jnp.concatenate(
            [
                jnp.concatenate([zero, grad[:, :HEAD_SIZE]], 1),
                jnp.concatenate([zero, grad[:, HEAD_SIZE:]], 1),
            ], 0,
        ),
    )


def far_kernel(
    head_count, group, others, place_ref, offset_ref, near_ref, queries_ref, picks_ref, *refs
):
    other_refs, refs = refs[:others], refs[others:]
    grad_refs, refs = refs[:group], refs[group:]
    extra_out, own_out, other_out, grads_out, keys_ref, query_ref, grad_ref = refs
    near = near_ref.shape[0]
    rows = near // group
    picked = rows // DILATION_RATE
    count = group * picked
    far = count * (1 + others)
    pick = pick_matrix(own_offset(head_count, place_ref, offset_ref), picked, rows)
    keys_ref[:near, :] = near_ref[...]
    for index, ref in enumerate([picks_ref, *other_refs]):
        keys_ref[near + index * count : near + (index + 1) * count, :] = ref[...]
    for place, ref in zip(places_of(place_ref[0], group), grad_refs):
        grads_out[place] = ref[...]
    for step in range(group):
        query, grad = query_and_grad(queries_ref.at[step], grads_out.at[step])
        span = slice(step * picked, (step + 1) * picked)
        query_ref[span, :] = dot_nn(pick, query).astype(jnp.bfloat16)
        grad_ref[span, :] = dot_nn(pick, grad).astype(jnp.bfloat16)
    far_t = keys_ref[near:, :].astype(jnp.float32).T[:HEAD_SIZE].astype(jnp.bfloat16)
    query, grad = query_ref[...], grad_ref[...]
    score = dot_nt(keys_ref[...], query)
    dprob = dot_nt(keys_ref[...], grad)
    top = jnp.max(score, 0, keepdims=True)
    prob = jnp.exp2((score - top) * SCORE_FACTOR)
    total = jnp.sum(prob, 0, keepdims=True)
    inverse = 1.0 / total
    delta = jnp.sum(prob * dprob, 0, keepdims=True) * inverse
    prob_far = prob[near:] * inverse
    dscore = (prob_far * (dprob[near:] - delta)).astype(jnp.bfloat16)
    terms = dot_nn(
        jnp.concatenate([dscore, prob_far.astype(jnp.bfloat16)], 1),
        jnp.concatenate([query, grad], 0),
    ) * jnp.where(left_half((far, PAIR)), SCALE, 1.0)
    own_out[...] = terms[:count]
    other_out[...] = terms[count:]
    query_grad = dot_nn(far_t, dscore)
    lse = top * SCORE_FACTOR + jnp.log2(total)
    extra_out[:PAIR, :] = jnp.concatenate(split_two(query_grad), 0)
    blank = jnp.zeros((STAT_ROWS - 6, count), jnp.bfloat16)
    extra_out[PAIR:, :] = jnp.concatenate([*split_three(lse), *split_three(delta), blank], 0)


def near_block(
    first, offset, keys_ref, key_t_ref, query_ref, grad_ref, extra_ref, score_ref, dprob_ref,
    work_ref, acc_ref,
):
    near = keys_ref.shape[0]
    rows = score_ref.shape[1]
    count = extra_ref.shape[1]
    query, grad = query_and_grad(query_ref, grad_ref)
    score_ref[...] = dot_nt(keys_ref[...], query)
    dprob_ref[...] = dot_nt(keys_ref[...], grad)
    extra = dot_nn(extra_ref[...], spread_matrix(offset, first, count, rows, 0))
    row_lane = lax.broadcasted_iota(jnp.int32, (1, rows), 1)
    picked = lax.rem(row_lane, DILATION_RATE) == offset
    lse_picked = extra[PAIR : PAIR + 1] + extra[PAIR + 1 : PAIR + 2] + extra[PAIR + 2 : PAIR + 3]
    delta_picked = (
        extra[PAIR + 3 : PAIR + 4] + extra[PAIR + 4 : PAIR + 5] + extra[PAIR + 5 : PAIR + 6]
    )
    strips = [slice(start, start + STRIP) for start in range(0, near, STRIP)]
    top = None
    for strip in strips:
        part = fold(score_ref[strip, :], jnp.maximum)
        top = part if top is None else jnp.maximum(top, part)
    top = jnp.max(top, 0, keepdims=True) * SCORE_FACTOR
    top = jnp.where(picked, lse_picked, top)
    total = jnp.zeros((8, rows), jnp.float32)
    delta = jnp.zeros((8, rows), jnp.float32)
    for strip in strips:
        prob = jnp.exp2(score_ref[strip, :] * SCORE_FACTOR - top)
        total = total + fold(prob, jnp.add)
        delta = delta + fold(prob * dprob_ref[strip, :], jnp.add)
        score_ref[strip, :] = prob
    inverse = jnp.where(picked, 1.0, 1.0 / jnp.sum(total, 0, keepdims=True))
    delta = jnp.where(picked, delta_picked, jnp.sum(delta, 0, keepdims=True) * inverse)
    for strip in strips:
        prob = score_ref[strip, :] * inverse
        work_ref[strip, :rows] = (prob * (dprob_ref[strip, :] - delta)).astype(jnp.bfloat16)
        work_ref[strip, rows:] = prob.astype(jnp.bfloat16)
    acc_ref[...] += dot_nn(work_ref[...], jnp.concatenate([query, grad], 0))
    query_grad = dot_nn(key_t_ref[...], work_ref[:, :rows])
    query_grad = query_grad + extra[:HEAD_SIZE] + extra[HEAD_SIZE:PAIR]
    query_grad = (query_grad * SCALE).T.astype(jnp.bfloat16)
    half = rows // 2
    return jnp.concatenate([query_grad[:half], query_grad[half:]], 1)


def first_kernel(
    head_count, steps, place_ref, offset_ref, keys_ref, key_t_ref, queries_ref, grads_ref,
    extra_ref, acc_ref, query_out, *scratch,
):
    rows = scratch[0].shape[2]
    offset = own_offset(head_count, place_ref, offset_ref)
    acc_ref[...] = jnp.zeros_like(acc_ref)
    for step in range(steps):
        query_out[step] = near_block(
            step * (rows // DILATION_RATE), offset, keys_ref, key_t_ref,
            queries_ref.at[step], grads_ref.at[step], extra_ref,
            *[ref.at[step % 2] for ref in scratch], acc_ref,
        )


def second_kernel(
    head_count, steps, others, place_ref, offset_ref, keys_ref, key_t_ref, queries_ref, grads_ref,
    extra_ref, start_ref, query_ref, own_ref, *refs,
):
    back_refs, refs = refs[:others], refs[others:]
    rows = query_ref.shape[1] * 2
    group = keys_ref.shape[0] // rows
    out_refs, refs = refs[:group], refs[group:]
    acc_ref, stage_ref, *scratch = refs
    count = extra_ref.shape[1]
    picked = count // group
    offset = own_offset(head_count, place_ref, offset_ref)
    acc_ref[...] = start_ref[...]
    for place in range(group - steps, group):
        stage_ref[place, rows:, :] = near_block(
            place * picked, offset, keys_ref, key_t_ref,
            queries_ref.at[place], grads_ref.at[place], extra_ref,
            *[ref.at[place % 2] for ref in scratch], acc_ref,
        )
    terms = own_ref[...]
    for back_ref in back_refs:
        terms = terms + back_ref[...]
    terms = jnp.concatenate(split_two(terms), 0)
    factor = jnp.where(left_half((rows, PAIR)), SCALE, 1.0)
    for place in range(group):
        spread = spread_matrix(offset, place * picked, count, rows, 1)
        placed = dot_nn(jnp.concatenate([spread, spread], 1), terms)
        summed = acc_ref[place * rows : (place + 1) * rows, :] * factor + placed
        stage_ref[place, :rows, :] = summed.astype(jnp.bfloat16)
        if place < group - steps:
            stage_ref[place, rows:, :] = query_ref[place]
    send_out(place_ref[0], group, stage_ref, out_refs)


def unpack_kernel(head_count, group, place_ref, *refs):
    near_refs, refs = refs[:group], refs[group:]
    query_out, key_out, value_out, stage_ref = refs
    rows = query_out.shape[0]
    half = rows // 2
    for place, near_ref in zip(places_of(place_ref[0], group), near_refs):
        stage_ref[place] = near_ref[...]
    for head in range(head_count):
        columns = slice(head * HEAD_SIZE, (head + 1) * HEAD_SIZE)
        key_out[:, columns] = stage_ref[head, :rows, :HEAD_SIZE]
        value_out[:, columns] = stage_ref[head, :rows, HEAD_SIZE:]
        query_out[:half, columns] = stage_ref[head, rows:, :HEAD_SIZE]
        query_out[half:, columns] = stage_ref[head, rows:, HEAD_SIZE:]


def call(kernel, name, out_shape, scalars, operands, scratch=(), flops=0, space=VMEM, limit=40):
    return pl.pallas_call(
        kernel,
        out_shape=tuple(jax.ShapeDtypeStruct(*shape) for shape in out_shape),
        in_specs=[SMEM] * len(scalars) + [space] * len(operands),
        out_specs=tuple(VMEM for _ in out_shape),
        scratch_shapes=[
            pltpu.VMEM(*shape) if isinstance(shape, tuple) else shape for shape in scratch
        ],
        compiler_params=pltpu.CompilerParams(vmem_limit_bytes=limit * 1024 * 1024),
        cost_estimate=pl.CostEstimate(flops=flops, bytes_accessed=2**21, transcendentals=0),
        name=name,
    )(*scalars, *operands)


def body(upstream, out_weight, query_rows, key_rows, value_rows, head_offsets):
    rows, width = query_rows.shape
    head_count = width // HEAD_SIZE
    devices = lax.axis_size("context")
    shards = lax.axis_size("heads")
    group = FIRST_SEGMENT // rows
    others = devices // group - 1
    half = rows // 2
    picked = rows // DILATION_RATE
    count = group * picked
    near = group * rows
    place = jnp.stack(
        [lax.rem(lax.axis_index("context"), group), lax.axis_index("heads")]
    ).astype(jnp.int32)
    scalars = [place, head_offsets]

    def swap(values):
        result = [values[0]]
        for step, value in zip(swap_steps(group), values[1:]):
            pairs = [(source, source ^ step[source % 2]) for source in range(devices)]
            result.append(lax.ppermute(value, "context", pairs))
        return result

    def segment_shift(value, shift):
        pairs = [(source, (source + shift * group) % devices) for source in range(devices)]
        return lax.ppermute(value, "context", pairs)

    upstreams = [upstream]
    for step in range(1, shards):
        pairs = [(source, (source + step) % shards) for source in range(shards)]
        upstreams.append(lax.ppermute(upstream, "heads", pairs))

    bf16, f32 = jnp.bfloat16, jnp.float32
    sent = swap(
        call(
            functools.partial(pack_kernel, head_count, group), "pack_rows",
            [((rows + half, PAIR), bf16)] * group,
            [place], [query_rows, key_rows, value_rows],
            [((rows, width), bf16)] * 3
            + [((head_count, rows + half, PAIR), bf16), pltpu.SemaphoreType.DMA((3,))],
            space=ANY, limit=60,
        )
    )
    grads = swap(
        call(
            functools.partial(project_kernel, head_count, group, shards), "project_pack",
            [((half, PAIR), bf16)] * group,
            [place], [out_weight, *upstreams],
            [((rows, width), bf16), ((head_count, half, PAIR), bf16)],
            flops=2 * rows * width * upstream.shape[1],
        )
    )
    keys, key_t, queries, picks = call(
        functools.partial(gather_kernel, head_count, group), "gather_keys",
        [
            ((near, PAIR), bf16), ((HEAD_SIZE, near), bf16), ((group, half, PAIR), bf16),
            ((count, PAIR), bf16),
        ],
        scalars, [*sent, grads[0]],
    )
    other_picks = [segment_shift(picks, shift) for shift in range(1, others + 1)]
    extra, own_terms, other_terms, grads = call(
        functools.partial(far_kernel, head_count, group, others), "picked_rows",
        [
            ((PAIR + STAT_ROWS, count), bf16), ((count, PAIR), f32),
            ((others * count, PAIR), f32), ((group, half, PAIR), bf16),
        ],
        scalars, [keys, queries, picks, *other_picks, *grads],
        [((near + count * (1 + others), PAIR), bf16)] + [((count, PAIR), bf16)] * 2,
        flops=8 * near * count * PAIR,
    )
    back = [
        segment_shift(other_terms[(shift - 1) * count : shift * count], -shift)
        for shift in range(1, others + 1)
    ]
    steps = group // 2
    scratch = [
        ((2, near, rows), f32), ((2, near, rows), f32), ((2, near, 2 * rows), bf16),
    ]
    half_flops = 10 * near * near // 2 * PAIR
    acc, query_half = call(
        functools.partial(first_kernel, head_count, steps), "first_rows",
        [((near, PAIR), f32), ((steps, half, PAIR), bf16)],
        scalars, [keys, key_t, queries, grads, extra], scratch, half_flops,
    )
    near_send = call(
        functools.partial(second_kernel, head_count, group - steps, others), "second_rows",
        [((rows + half, PAIR), bf16)] * group,
        scalars, [keys, key_t, queries, grads, extra, acc, query_half, own_terms, *back],
        [((near, PAIR), f32), ((group, rows + half, PAIR), bf16)] + scratch, half_flops,
    )
    return tuple(
        call(
            functools.partial(unpack_kernel, head_count, group), "unpack",
            [((rows, width), bf16)] * 3,
            [place], swap(near_send),
            [((group, rows + half, PAIR), bf16)],
        )
    )


def solution(mesh):
    return jax.shard_map(
        body,
        mesh=mesh,
        in_specs=(
            P(("context", "heads"), None),
            P("heads", None),
            P("context", "heads"),
            P("context", "heads"),
            P("context", "heads"),
            P(),
        ),
        out_specs=(P("context", "heads"), P("context", "heads"), P("context", "heads")),
        check_vma=False,
    )
```

```python
import functools
import math

import jax
import jax.numpy as jnp
from jax import lax
from jax.experimental import pallas as pl
from jax.experimental.pallas import tpu as pltpu
from jax.sharding import PartitionSpec as P

HEAD_SIZE = 64
PAIR = 2 * HEAD_SIZE
DILATION_RATE = 16
FIRST_SEGMENT = 2048
SCALE = 1.0 / math.sqrt(HEAD_SIZE)
LOG2E = math.log2(math.e)
SCORE_FACTOR = SCALE * LOG2E
STRIP = 64
STAT_ROWS = 16

SMEM = pl.BlockSpec(memory_space=pltpu.SMEM)
VMEM = pl.BlockSpec(memory_space=pltpu.VMEM)
ANY = pl.BlockSpec(memory_space=pl.ANY)


def dot_nt(left, right):
    return lax.dot_general(
        left, right, (((1,), (1,)), ((), ())), preferred_element_type=jnp.float32
    )


def dot_nn(left, right):
    return jnp.dot(left, right, preferred_element_type=jnp.float32)


def head_columns(ref, head):
    return ref[:, head * HEAD_SIZE : (head + 1) * HEAD_SIZE]


def pick_matrix(offset, picked, rows):
    source = lax.broadcasted_iota(jnp.int32, (picked, rows), 1)
    index = lax.broadcasted_iota(jnp.int32, (picked, rows), 0)
    return (source == index * DILATION_RATE + offset).astype(jnp.bfloat16)


def spread_matrix(offset, first, picked, rows, axis):
    shape = (picked, rows) if axis == 0 else (rows, picked)
    index = lax.broadcasted_iota(jnp.int32, shape, axis)
    source = lax.broadcasted_iota(jnp.int32, shape, 1 - axis)
    return (source == (index - first) * DILATION_RATE + offset).astype(jnp.bfloat16)


def split_two(value):
    high = value.astype(jnp.bfloat16)
    low = (value - high.astype(jnp.float32)).astype(jnp.bfloat16)
    return high, low


def split_three(value):
    high = value.astype(jnp.bfloat16)
    rest = value - high.astype(jnp.float32)
    middle = rest.astype(jnp.bfloat16)
    low = (rest - middle.astype(jnp.float32)).astype(jnp.bfloat16)
    return high, middle, low


def fold(value, combine):
    parts = [value[start : start + 8] for start in range(0, value.shape[0], 8)]
    while len(parts) > 1:
        merged = [combine(parts[i], parts[i + 1]) for i in range(0, len(parts) - 1, 2)]
        parts = merged + parts[len(merged) * 2 :]
    return parts[0]


def left_half(shape):
    return lax.broadcasted_iota(jnp.int32, shape, 1) < HEAD_SIZE


def side_by_side(block):
    half = block.shape[0] // 2
    return jnp.concatenate([block[:half], block[half:]], 1)


def send_out(place, stage_ref, out_refs):
    for bits, out_ref in enumerate(out_refs):
        out_ref[...] = stage_ref[lax.bitwise_xor(place, bits)]


def pack_kernel(head_count, query_hbm, key_hbm, value_hbm, *refs):
    out_ref, query_ref, key_ref, value_ref, sems = refs
    rows = query_ref.shape[0]
    copies = [
        pltpu.make_async_copy(source, target, sems.at[index])
        for index, (source, target) in enumerate(
            [(key_hbm, key_ref), (value_hbm, value_ref), (query_hbm, query_ref)]
        )
    ]
    for copy in copies:
        copy.start()
    for copy in copies:
        copy.wait()
    for head in range(head_count):
        pair = jnp.concatenate([head_columns(key_ref, head), head_columns(value_ref, head)], 1)
        query = side_by_side(head_columns(query_ref, head))
        for place in range(head, out_ref.shape[0], head_count):
            out_ref[place, :rows, :] = pair
            out_ref[place, rows:, :] = query


def project_kernel(head_count, shards, place_ref, weight_ref, *refs):
    upstream_refs, (out_ref, grad_ref) = refs[:shards], refs[shards:]
    shard_rows = upstream_refs[0].shape[0]
    for step, upstream_ref in enumerate(upstream_refs):
        owner = lax.rem(place_ref[1] + (shards - step), shards)
        start = pl.multiple_of(owner * shard_rows, shard_rows)
        grad_ref[pl.ds(start, shard_rows), :] = dot_nt(
            upstream_ref[...], weight_ref[...]
        ).astype(jnp.bfloat16)
    for head in range(head_count):
        grad = side_by_side(head_columns(grad_ref, head))
        for place in range(head, out_ref.shape[0], head_count):
            out_ref[place] = grad


def own_offset(head_count, place_ref, offset_ref):
    return offset_ref[place_ref[1] * head_count + lax.rem(place_ref[0], head_count)]


def gather_kernel(
    head_count, place_ref, offset_ref, sent_ref, after_ref, keys_out, key_t_out, queries_out,
    picks_out,
):
    group = sent_ref.shape[0]
    rows = keys_out.shape[0] // group
    picked = rows // DILATION_RATE
    pick = pick_matrix(own_offset(head_count, place_ref, offset_ref), picked, rows)
    for place in range(group):
        pair = sent_ref[place, :rows, :]
        keys_out[place * rows : (place + 1) * rows, :] = pair
        picks_out[place * picked : (place + 1) * picked, :] = dot_nn(pick, pair).astype(
            jnp.bfloat16
        )
        queries_out[place] = sent_ref[place, rows:, :]
    key_t_out[...] = keys_out[...].astype(jnp.float32).T[:HEAD_SIZE].astype(jnp.bfloat16)


def query_and_grad(query_ref, grad_ref):
    query, grad = query_ref[...], grad_ref[...]
    zero = jnp.zeros((query.shape[0], HEAD_SIZE), query.dtype)
    return (
        jnp.concatenate(
            [
                jnp.concatenate([query[:, :HEAD_SIZE], zero], 1),
                jnp.concatenate([query[:, HEAD_SIZE:], zero], 1),
            ], 0,
        ),
        jnp.concatenate(
            [
                jnp.concatenate([zero, grad[:, :HEAD_SIZE]], 1),
                jnp.concatenate([zero, grad[:, HEAD_SIZE:]], 1),
            ], 0,
        ),
    )


def far_kernel(
    head_count, group, others, place_ref, offset_ref, near_ref, queries_ref, grads_ref, picks_ref,
    *refs,
):
    other_refs, refs = refs[:others], refs[others:]
    extra_out, own_out, other_out, keys_ref, query_ref, grad_ref = refs
    near = near_ref.shape[0]
    rows = near // group
    picked = rows // DILATION_RATE
    count = group * picked
    far = count * (1 + others)
    pick = pick_matrix(own_offset(head_count, place_ref, offset_ref), picked, rows)
    keys_ref[:near, :] = near_ref[...]
    for index, ref in enumerate([picks_ref, *other_refs]):
        keys_ref[near + index * count : near + (index + 1) * count, :] = ref[...]
    for step in range(group):
        query, grad = query_and_grad(queries_ref.at[step], grads_ref.at[step])
        span = slice(step * picked, (step + 1) * picked)
        query_ref[span, :] = dot_nn(pick, query).astype(jnp.bfloat16)
        grad_ref[span, :] = dot_nn(pick, grad).astype(jnp.bfloat16)
    far_t = keys_ref[near:, :].astype(jnp.float32).T[:HEAD_SIZE].astype(jnp.bfloat16)
    query, grad = query_ref[...], grad_ref[...]
    score = dot_nt(keys_ref[...], query)
    dprob = dot_nt(keys_ref[...], grad)
    top = jnp.max(score, 0, keepdims=True)
    prob = jnp.exp2((score - top) * SCORE_FACTOR)
    total = jnp.sum(prob, 0, keepdims=True)
    inverse = 1.0 / total
    delta = jnp.sum(prob * dprob, 0, keepdims=True) * inverse
    prob_far = prob[near:] * inverse
    dscore = (prob_far * (dprob[near:] - delta)).astype(jnp.bfloat16)
    terms = dot_nn(
        jnp.concatenate([dscore, prob_far.astype(jnp.bfloat16)], 1),
        jnp.concatenate([query, grad], 0),
    ) * jnp.where(left_half((far, PAIR)), SCALE, 1.0)
    own_out[...] = terms[:count]
    other_out[...] = terms[count:]
    query_grad = dot_nn(far_t, dscore)
    lse = top * SCORE_FACTOR + jnp.log2(total)
    extra_out[:PAIR, :] = jnp.concatenate(split_two(query_grad), 0)
    blank = jnp.zeros((STAT_ROWS - 6, count), jnp.bfloat16)
    extra_out[PAIR:, :] = jnp.concatenate([*split_three(lse), *split_three(delta), blank], 0)


def near_block(
    first, offset, keys_ref, key_t_ref, query_ref, grad_ref, extra_ref, score_ref, dprob_ref,
    work_ref, acc_ref,
):
    near = keys_ref.shape[0]
    rows = score_ref.shape[1]
    count = extra_ref.shape[1]
    query, grad = query_and_grad(query_ref, grad_ref)
    score_ref[...] = dot_nt(keys_ref[...], query)
    dprob_ref[...] = dot_nt(keys_ref[...], grad)
    extra = dot_nn(extra_ref[...], spread_matrix(offset, first, count, rows, 0))
    row_lane = lax.broadcasted_iota(jnp.int32, (1, rows), 1)
    picked = lax.rem(row_lane, DILATION_RATE) == offset
    lse_picked = extra[PAIR : PAIR + 1] + extra[PAIR + 1 : PAIR + 2] + extra[PAIR + 2 : PAIR + 3]
    delta_picked = (
        extra[PAIR + 3 : PAIR + 4] + extra[PAIR + 4 : PAIR + 5] + extra[PAIR + 5 : PAIR + 6]
    )
    strips = [slice(start, start + STRIP) for start in range(0, near, STRIP)]
    top = None
    for strip in strips:
        part = fold(score_ref[strip, :], jnp.maximum)
        top = part if top is None else jnp.maximum(top, part)
    top = jnp.max(top, 0, keepdims=True) * SCORE_FACTOR
    top = jnp.where(picked, lse_picked, top)
    total = jnp.zeros((8, rows), jnp.float32)
    delta = jnp.zeros((8, rows), jnp.float32)
    for strip in strips:
        prob = jnp.exp2(score_ref[strip, :] * SCORE_FACTOR - top)
        total = total + fold(prob, jnp.add)
        delta = delta + fold(prob * dprob_ref[strip, :], jnp.add)
        score_ref[strip, :] = prob
    inverse = jnp.where(picked, 1.0, 1.0 / jnp.sum(total, 0, keepdims=True))
    delta = jnp.where(picked, delta_picked, jnp.sum(delta, 0, keepdims=True) * inverse)
    for strip in strips:
        prob = score_ref[strip, :] * inverse
        work_ref[strip, :rows] = (prob * (dprob_ref[strip, :] - delta)).astype(jnp.bfloat16)
        work_ref[strip, rows:] = prob.astype(jnp.bfloat16)
    acc_ref[...] += dot_nn(work_ref[...], jnp.concatenate([query, grad], 0))
    query_grad = dot_nn(key_t_ref[...], work_ref[:, :rows])
    query_grad = query_grad + extra[:HEAD_SIZE] + extra[HEAD_SIZE:PAIR]
    query_grad = (query_grad * SCALE).T.astype(jnp.bfloat16)
    half = rows // 2
    return jnp.concatenate([query_grad[:half], query_grad[half:]], 1)


def first_kernel(
    head_count, steps, place_ref, offset_ref, keys_ref, key_t_ref, queries_ref, grads_ref,
    extra_ref, acc_ref, query_out, *scratch,
):
    rows = scratch[0].shape[2]
    offset = own_offset(head_count, place_ref, offset_ref)
    acc_ref[...] = jnp.zeros_like(acc_ref)
    for step in range(steps):
        query_out[step] = near_block(
            step * (rows // DILATION_RATE), offset, keys_ref, key_t_ref,
            queries_ref.at[step], grads_ref.at[step], extra_ref,
            *[ref.at[step % 2] for ref in scratch], acc_ref,
        )


def second_kernel(
    head_count, steps, others, place_ref, offset_ref, keys_ref, key_t_ref, queries_ref, grads_ref,
    extra_ref, start_ref, query_ref, own_ref, *refs,
):
    back_refs, refs = refs[:others], refs[others:]
    rows = query_ref.shape[1] * 2
    group = keys_ref.shape[0] // rows
    out_refs, refs = refs[:group], refs[group:]
    acc_ref, stage_ref, *scratch = refs
    count = extra_ref.shape[1]
    picked = count // group
    offset = own_offset(head_count, place_ref, offset_ref)
    acc_ref[...] = start_ref[...]
    for place in range(group - steps, group):
        stage_ref[place, rows:, :] = near_block(
            place * picked, offset, keys_ref, key_t_ref,
            queries_ref.at[place], grads_ref.at[place], extra_ref,
            *[ref.at[place % 2] for ref in scratch], acc_ref,
        )
    terms = own_ref[...]
    for back_ref in back_refs:
        terms = terms + back_ref[...]
    terms = jnp.concatenate(split_two(terms), 0)
    factor = jnp.where(left_half((rows, PAIR)), SCALE, 1.0)
    for place in range(group):
        spread = spread_matrix(offset, place * picked, count, rows, 1)
        placed = dot_nn(jnp.concatenate([spread, spread], 1), terms)
        summed = acc_ref[place * rows : (place + 1) * rows, :] * factor + placed
        stage_ref[place, :rows, :] = summed.astype(jnp.bfloat16)
        if place < group - steps:
            stage_ref[place, rows:, :] = query_ref[place]
    send_out(place_ref[0], stage_ref, out_refs)


def unpack_kernel(head_count, group, place_ref, *refs):
    near_refs, refs = refs[:group], refs[group:]
    query_out, key_out, value_out, stage_ref = refs
    rows = query_out.shape[0]
    half = rows // 2
    for bits, near_ref in enumerate(near_refs):
        stage_ref[lax.bitwise_xor(place_ref[0], bits)] = near_ref[...]
    for head in range(head_count):
        columns = slice(head * HEAD_SIZE, (head + 1) * HEAD_SIZE)
        key_out[:, columns] = stage_ref[head, :rows, :HEAD_SIZE]
        value_out[:, columns] = stage_ref[head, :rows, HEAD_SIZE:]
        query_out[:half, columns] = stage_ref[head, rows:, :HEAD_SIZE]
        query_out[half:, columns] = stage_ref[head, rows:, HEAD_SIZE:]


def call(kernel, name, out_shape, scalars, operands, scratch=(), flops=0, space=VMEM, limit=40):
    return pl.pallas_call(
        kernel,
        out_shape=tuple(jax.ShapeDtypeStruct(*shape) for shape in out_shape),
        in_specs=[SMEM] * len(scalars) + [space] * len(operands),
        out_specs=tuple(VMEM for _ in out_shape),
        scratch_shapes=[
            pltpu.VMEM(*shape) if isinstance(shape, tuple) else shape for shape in scratch
        ],
        compiler_params=pltpu.CompilerParams(vmem_limit_bytes=limit * 1024 * 1024),
        cost_estimate=pl.CostEstimate(flops=flops, bytes_accessed=2**21, transcendentals=0),
        name=name,
    )(*scalars, *operands)


def body(upstream, out_weight, query_rows, key_rows, value_rows, head_offsets):
    rows, width = query_rows.shape
    head_count = width // HEAD_SIZE
    devices = lax.axis_size("context")
    shards = lax.axis_size("heads")
    group = FIRST_SEGMENT // rows
    others = devices // group - 1
    half = rows // 2
    picked = rows // DILATION_RATE
    count = group * picked
    near = group * rows
    place = jnp.stack(
        [lax.rem(lax.axis_index("context"), group), lax.axis_index("heads")]
    ).astype(jnp.int32)
    scalars = [place, head_offsets]

    def swap(values):
        pairs = [[(source, source ^ bits) for source in range(devices)] for bits in range(group)]
        return [values[0]] + [
            lax.ppermute(values[bits], "context", pairs[bits]) for bits in range(1, group)
        ]

    def exchange(value):
        groups = [list(range(first, first + group)) for first in range(0, devices, group)]
        return lax.all_to_all(value, "context", 0, 0, axis_index_groups=groups)

    def segment_shift(value, shift):
        pairs = [(source, (source + shift * group) % devices) for source in range(devices)]
        return lax.ppermute(value, "context", pairs)

    upstreams = [upstream]
    for step in range(1, shards):
        pairs = [(source, (source + step) % shards) for source in range(shards)]
        upstreams.append(lax.ppermute(upstream, "heads", pairs))

    bf16, f32 = jnp.bfloat16, jnp.float32
    (sent,) = call(
        functools.partial(pack_kernel, head_count), "pack_rows",
        [((group, rows + half, PAIR), bf16)],
        [], [query_rows, key_rows, value_rows],
        [((rows, width), bf16)] * 3 + [pltpu.SemaphoreType.DMA((3,))],
        flops=2**31, space=ANY, limit=60,
    )
    sent = exchange(sent)
    (grads_send,) = call(
        functools.partial(project_kernel, head_count, shards), "project_pack",
        [((group, half, PAIR), bf16)],
        [place], [out_weight, *upstreams],
        [((rows, width), bf16)],
        flops=2 * rows * width * upstream.shape[1],
    )
    grads = exchange(grads_send)
    keys, key_t, queries, picks = call(
        functools.partial(gather_kernel, head_count), "gather_keys",
        [
            ((near, PAIR), bf16), ((HEAD_SIZE, near), bf16), ((group, half, PAIR), bf16),
            ((count, PAIR), bf16),
        ],
        scalars, [sent, grads_send],
    )
    other_picks = [segment_shift(picks, shift) for shift in range(1, others + 1)]
    extra, own_terms, other_terms = call(
        functools.partial(far_kernel, head_count, group, others), "picked_rows",
        [
            ((PAIR + STAT_ROWS, count), bf16), ((count, PAIR), f32),
            ((others * count, PAIR), f32),
        ],
        scalars, [keys, queries, grads, picks, *other_picks],
        [((near + count * (1 + others), PAIR), bf16)] + [((count, PAIR), bf16)] * 2,
        flops=8 * near * count * PAIR,
    )
    back = [
        segment_shift(other_terms[(shift - 1) * count : shift * count], -shift)
        for shift in range(1, others + 1)
    ]
    steps = group // 2
    scratch = [
        ((2, near, rows), f32), ((2, near, rows), f32), ((2, near, 2 * rows), bf16),
    ]
    half_flops = 10 * near * near // 2 * PAIR
    acc, query_half = call(
        functools.partial(first_kernel, head_count, steps), "first_rows",
        [((near, PAIR), f32), ((steps, half, PAIR), bf16)],
        scalars, [keys, key_t, queries, grads, extra], scratch, half_flops,
    )
    near_send = call(
        functools.partial(second_kernel, head_count, group - steps, others), "second_rows",
        [((rows + half, PAIR), bf16)] * group,
        scalars, [keys, key_t, queries, grads, extra, acc, query_half, own_terms, *back],
        [((near, PAIR), f32), ((group, rows + half, PAIR), bf16)] + scratch, half_flops,
    )
    return tuple(
        call(
            functools.partial(unpack_kernel, head_count, group), "unpack",
            [((rows, width), bf16)] * 3,
            [place], swap(near_send),
            [((group, rows + half, PAIR), bf16)],
        )
    )


def solution(mesh):
    return jax.shard_map(
        body,
        mesh=mesh,
        in_specs=(
            P(("context", "heads"), None),
            P("heads", None),
            P("context", "heads"),
            P("context", "heads"),
            P("context", "heads"),
            P(),
        ),
        out_specs=(P("context", "heads"), P("context", "heads"), P("context", "heads")),
        check_vma=False,
    )
```

```python
import functools
import math

import jax
import jax.numpy as jnp
from jax import lax
from jax.experimental import pallas as pl
from jax.experimental.pallas import tpu as pltpu
from jax.sharding import PartitionSpec as P

HEAD_SIZE = 64
PAIR = 2 * HEAD_SIZE
DILATION_RATE = 16
FIRST_SEGMENT = 2048
SCALE = 1.0 / math.sqrt(HEAD_SIZE)
LOG2E = math.log2(math.e)
SCORE_FACTOR = SCALE * LOG2E
STRIP = 64
PIECE = 512
BUSY = 2**35
STAT_ROWS = 16

SMEM = pl.BlockSpec(memory_space=pltpu.SMEM)
VMEM = pl.BlockSpec(memory_space=pltpu.VMEM)
ANY = pl.BlockSpec(memory_space=pl.ANY)


def dot_nt(left, right):
    return lax.dot_general(
        left, right, (((1,), (1,)), ((), ())), preferred_element_type=jnp.float32
    )


def dot_nn(left, right):
    return jnp.dot(left, right, preferred_element_type=jnp.float32)


def head_columns(ref, head):
    return ref[:, head * HEAD_SIZE : (head + 1) * HEAD_SIZE]


def pick_matrix(offset, picked, rows):
    source = lax.broadcasted_iota(jnp.int32, (picked, rows), 1)
    index = lax.broadcasted_iota(jnp.int32, (picked, rows), 0)
    return (source == index * DILATION_RATE + offset).astype(jnp.bfloat16)


def spread_matrix(offset, first, picked, rows, axis):
    shape = (picked, rows) if axis == 0 else (rows, picked)
    index = lax.broadcasted_iota(jnp.int32, shape, axis)
    source = lax.broadcasted_iota(jnp.int32, shape, 1 - axis)
    return (source == (index - first) * DILATION_RATE + offset).astype(jnp.bfloat16)


def split_two(value):
    high = value.astype(jnp.bfloat16)
    low = (value - high.astype(jnp.float32)).astype(jnp.bfloat16)
    return high, low


def split_three(value):
    high = value.astype(jnp.bfloat16)
    rest = value - high.astype(jnp.float32)
    middle = rest.astype(jnp.bfloat16)
    low = (rest - middle.astype(jnp.float32)).astype(jnp.bfloat16)
    return high, middle, low


def fold(value, combine):
    parts = [value[start : start + 8] for start in range(0, value.shape[0], 8)]
    while len(parts) > 1:
        merged = [combine(parts[i], parts[i + 1]) for i in range(0, len(parts) - 1, 2)]
        parts = merged + parts[len(merged) * 2 :]
    return parts[0]


def left_half(shape):
    return lax.broadcasted_iota(jnp.int32, shape, 1) < HEAD_SIZE


def side_by_side(block):
    half = block.shape[0] // 2
    return jnp.concatenate([block[:half], block[half:]], 1)


def send_out(place, stage_ref, out_refs):
    for bits, out_ref in enumerate(out_refs):
        out_ref[...] = stage_ref[lax.bitwise_xor(place, bits)]


def pack_kernel(head_count, query_hbm, key_hbm, value_hbm, *refs):
    out_ref, query_ref, key_ref, value_ref, sems = refs
    rows = query_ref.shape[0]
    copies = [
        pltpu.make_async_copy(source, target, sems.at[index])
        for index, (source, target) in enumerate(
            [(key_hbm, key_ref), (value_hbm, value_ref), (query_hbm, query_ref)]
        )
    ]
    for copy in copies:
        copy.start()
    for copy in copies:
        copy.wait()
    for head in range(head_count):
        pair = jnp.concatenate([head_columns(key_ref, head), head_columns(value_ref, head)], 1)
        query = side_by_side(head_columns(query_ref, head))
        for place in range(head, out_ref.shape[0], head_count):
            out_ref[place, :rows, :] = pair
            out_ref[place, rows:, :] = query


def project_kernel(head_count, shards, place_ref, weight_ref, *refs):
    upstream_refs, (out_ref, grad_ref) = refs[:shards], refs[shards:]
    shard_rows = upstream_refs[0].shape[0]
    for step, upstream_ref in enumerate(upstream_refs):
        owner = lax.rem(place_ref[1] + (shards - step), shards)
        start = pl.multiple_of(owner * shard_rows, shard_rows)
        grad_ref[pl.ds(start, shard_rows), :] = dot_nt(
            upstream_ref[...], weight_ref[...]
        ).astype(jnp.bfloat16)
    for head in range(head_count):
        grad = side_by_side(head_columns(grad_ref, head))
        for place in range(head, out_ref.shape[0], head_count):
            out_ref[place] = grad


def own_offset(head_count, place_ref, offset_ref):
    return offset_ref[place_ref[1] * head_count + lax.rem(place_ref[0], head_count)]


def gather_kernel(
    head_count, place_ref, offset_ref, sent_ref, after_ref, keys_out, key_t_out, queries_out,
    picks_out,
):
    group = sent_ref.shape[0]
    rows = keys_out.shape[0] // group
    picked = rows // DILATION_RATE
    pick = pick_matrix(own_offset(head_count, place_ref, offset_ref), picked, rows)
    for place in range(group):
        pair = sent_ref[place, :rows, :]
        keys_out[place * rows : (place + 1) * rows, :] = pair
        picks_out[place * picked : (place + 1) * picked, :] = dot_nn(pick, pair).astype(
            jnp.bfloat16
        )
        queries_out[place] = sent_ref[place, rows:, :]
    key_t_out[...] = keys_out[...].astype(jnp.float32).T[:HEAD_SIZE].astype(jnp.bfloat16)


def query_and_grad(query_ref, grad_ref):
    query, grad = query_ref[...], grad_ref[...]
    zero = jnp.zeros((query.shape[0], HEAD_SIZE), query.dtype)
    return (
        jnp.concatenate(
            [
                jnp.concatenate([query[:, :HEAD_SIZE], zero], 1),
                jnp.concatenate([query[:, HEAD_SIZE:], zero], 1),
            ], 0,
        ),
        jnp.concatenate(
            [
                jnp.concatenate([zero, grad[:, :HEAD_SIZE]], 1),
                jnp.concatenate([zero, grad[:, HEAD_SIZE:]], 1),
            ], 0,
        ),
    )


def far_kernel(
    head_count, group, others, place_ref, offset_ref, near_ref, queries_ref, grads_ref, picks_ref,
    *refs,
):
    other_refs, refs = refs[:others], refs[others:]
    extra_out, own_out, other_out, keys_ref, query_ref, grad_ref = refs
    near = near_ref.shape[0]
    rows = near // group
    picked = rows // DILATION_RATE
    count = group * picked
    far = count * (1 + others)
    pick = pick_matrix(own_offset(head_count, place_ref, offset_ref), picked, rows)
    keys_ref[:near, :] = near_ref[...]
    for index, ref in enumerate([picks_ref, *other_refs]):
        keys_ref[near + index * count : near + (index + 1) * count, :] = ref[...]
    for step in range(group):
        query, grad = query_and_grad(queries_ref.at[step], grads_ref.at[step])
        span = slice(step * picked, (step + 1) * picked)
        query_ref[span, :] = dot_nn(pick, query).astype(jnp.bfloat16)
        grad_ref[span, :] = dot_nn(pick, grad).astype(jnp.bfloat16)
    far_t = keys_ref[near:, :].astype(jnp.float32).T[:HEAD_SIZE].astype(jnp.bfloat16)
    query, grad = query_ref[...], grad_ref[...]
    score = dot_nt(keys_ref[...], query)
    dprob = dot_nt(keys_ref[...], grad)
    top = jnp.max(score, 0, keepdims=True)
    prob = jnp.exp2((score - top) * SCORE_FACTOR)
    total = jnp.sum(prob, 0, keepdims=True)
    inverse = 1.0 / total
    delta = jnp.sum(prob * dprob, 0, keepdims=True) * inverse
    prob_far = prob[near:] * inverse
    dscore = (prob_far * (dprob[near:] - delta)).astype(jnp.bfloat16)
    terms = dot_nn(
        jnp.concatenate([dscore, prob_far.astype(jnp.bfloat16)], 1),
        jnp.concatenate([query, grad], 0),
    ) * jnp.where(left_half((far, PAIR)), SCALE, 1.0)
    own_out[...] = terms[:count]
    other_out[...] = terms[count:]
    query_grad = dot_nn(far_t, dscore)
    lse = top * SCORE_FACTOR + jnp.log2(total)
    extra_out[:PAIR, :] = jnp.concatenate(split_two(query_grad), 0)
    blank = jnp.zeros((STAT_ROWS - 6, count), jnp.bfloat16)
    extra_out[PAIR:, :] = jnp.concatenate([*split_three(lse), *split_three(delta), blank], 0)


def near_blocks(
    places, offset, keys_ref, key_t_ref, queries_ref, grads_ref, extra_ref,
    score_ref, dprob_ref, work_ref, acc_ref, emit,
):
    near = keys_ref.shape[0]
    rows = score_ref.shape[2]
    half = rows // 2
    count = extra_ref.shape[1]
    pieces = [slice(start, start + PIECE) for start in range(0, near, PIECE)]
    row_lane = lax.broadcasted_iota(jnp.int32, (1, rows), 1)
    picked = lax.rem(row_lane, DILATION_RATE) == offset

    def strips(piece):
        return [slice(start, start + STRIP) for start in range(piece.start, piece.stop, STRIP)]

    def first_matmuls(index, weights, piece):
        query, grad = weights
        score_ref[index % 2, piece, :] = dot_nt(keys_ref[piece, :], query)
        dprob_ref[index % 2, piece, :] = dot_nt(keys_ref[piece, :], grad)

    def maximum(index, top, piece):
        for strip in strips(piece):
            part = fold(score_ref[index % 2, strip, :], jnp.maximum)
            top = part if top is None else jnp.maximum(top, part)
        return top

    def weights_of(index):
        return query_and_grad(queries_ref.at[places[index]], grads_ref.at[places[index]])

    weights = weights_of(0)
    top = None
    for piece in pieces:
        first_matmuls(0, weights, piece)
        top = maximum(0, top, piece)
    for index, place in enumerate(places):
        slot = index % 2
        last = index + 1 == len(places)
        first = place * (rows // DILATION_RATE)
        extra = dot_nn(extra_ref[...], spread_matrix(offset, first, count, rows, 0))
        stats = [extra[PAIR + row : PAIR + row + 1] for row in range(6)]
        top = jnp.max(top, 0, keepdims=True) * SCORE_FACTOR
        top = jnp.where(picked, stats[0] + stats[1] + stats[2], top)
        total = jnp.zeros((8, rows), jnp.float32)
        delta = jnp.zeros((8, rows), jnp.float32)
        after = None if last else weights_of(index + 1)
        for piece in pieces:
            if not last:
                first_matmuls(index + 1, after, piece)
            for strip in strips(piece):
                prob = jnp.exp2(score_ref[slot, strip, :] * SCORE_FACTOR - top)
                total = total + fold(prob, jnp.add)
                delta = delta + fold(prob * dprob_ref[slot, strip, :], jnp.add)
                score_ref[slot, strip, :] = prob
        inverse = jnp.where(picked, 1.0, 1.0 / jnp.sum(total, 0, keepdims=True))
        delta = jnp.sum(delta, 0, keepdims=True) * inverse
        delta = jnp.where(picked, stats[3] + stats[4] + stats[5], delta)
        both = jnp.concatenate(weights, 0)
        query_grad = extra[:HEAD_SIZE] + extra[HEAD_SIZE:PAIR]
        top = None
        for piece in pieces:
            for strip in strips(piece):
                prob = score_ref[slot, strip, :] * inverse
                dscore = prob * (dprob_ref[slot, strip, :] - delta)
                work_ref[slot, strip, :rows] = dscore.astype(jnp.bfloat16)
                work_ref[slot, strip, rows:] = prob.astype(jnp.bfloat16)
            acc_ref[piece, :] += dot_nn(work_ref[slot, piece, :], both)
            query_grad = query_grad + dot_nn(key_t_ref[:, piece], work_ref[slot, piece, :rows])
            if not last:
                top = maximum(index + 1, top, piece)
        query_grad = (query_grad * SCALE).T.astype(jnp.bfloat16)
        emit(place, jnp.concatenate([query_grad[:half], query_grad[half:]], 1))
        weights = after


def first_kernel(
    head_count, steps, place_ref, offset_ref, keys_ref, key_t_ref, queries_ref, grads_ref,
    extra_ref, acc_ref, query_out, *scratch,
):
    offset = own_offset(head_count, place_ref, offset_ref)
    acc_ref[...] = jnp.zeros_like(acc_ref)

    def emit(place, query_grad):
        query_out[place] = query_grad

    near_blocks(
        range(steps), offset, keys_ref, key_t_ref, queries_ref, grads_ref, extra_ref,
        *scratch, acc_ref, emit,
    )


def second_kernel(
    head_count, steps, others, place_ref, offset_ref, keys_ref, key_t_ref, queries_ref, grads_ref,
    extra_ref, start_ref, query_ref, own_ref, *refs,
):
    back_refs, refs = refs[:others], refs[others:]
    rows = query_ref.shape[1] * 2
    group = keys_ref.shape[0] // rows
    out_refs, refs = refs[:group], refs[group:]
    acc_ref, stage_ref, *scratch = refs
    count = extra_ref.shape[1]
    picked = count // group
    offset = own_offset(head_count, place_ref, offset_ref)
    acc_ref[...] = start_ref[...]

    def emit(place, query_grad):
        stage_ref[place, rows:, :] = query_grad

    near_blocks(
        range(group - steps, group), offset, keys_ref, key_t_ref, queries_ref, grads_ref, extra_ref,
        *scratch, acc_ref, emit,
    )
    terms = own_ref[...]
    for back_ref in back_refs:
        terms = terms + back_ref[...]
    terms = jnp.concatenate(split_two(terms), 0)
    factor = jnp.where(left_half((rows, PAIR)), SCALE, 1.0)
    for place in range(group):
        spread = spread_matrix(offset, place * picked, count, rows, 1)
        placed = dot_nn(jnp.concatenate([spread, spread], 1), terms)
        summed = acc_ref[place * rows : (place + 1) * rows, :] * factor + placed
        stage_ref[place, :rows, :] = summed.astype(jnp.bfloat16)
        if place < group - steps:
            stage_ref[place, rows:, :] = query_ref[place]
    send_out(place_ref[0], stage_ref, out_refs)


def unpack_kernel(head_count, group, place_ref, *refs):
    near_refs, refs = refs[:group], refs[group:]
    query_out, key_out, value_out, stage_ref = refs
    rows = query_out.shape[0]
    half = rows // 2
    for bits, near_ref in enumerate(near_refs):
        stage_ref[lax.bitwise_xor(place_ref[0], bits)] = near_ref[...]
    for head in range(head_count):
        columns = slice(head * HEAD_SIZE, (head + 1) * HEAD_SIZE)
        key_out[:, columns] = stage_ref[head, :rows, :HEAD_SIZE]
        value_out[:, columns] = stage_ref[head, :rows, HEAD_SIZE:]
        query_out[:half, columns] = stage_ref[head, rows:, :HEAD_SIZE]
        query_out[half:, columns] = stage_ref[head, rows:, HEAD_SIZE:]


def call(kernel, name, out_shape, scalars, operands, scratch=(), flops=0, space=VMEM, limit=40):
    return pl.pallas_call(
        kernel,
        out_shape=tuple(jax.ShapeDtypeStruct(*shape) for shape in out_shape),
        in_specs=[SMEM] * len(scalars) + [space] * len(operands),
        out_specs=tuple(VMEM for _ in out_shape),
        scratch_shapes=[
            pltpu.VMEM(*shape) if isinstance(shape, tuple) else shape for shape in scratch
        ],
        compiler_params=pltpu.CompilerParams(vmem_limit_bytes=limit * 1024 * 1024),
        cost_estimate=pl.CostEstimate(flops=flops, bytes_accessed=2**21, transcendentals=0),
        name=name,
    )(*scalars, *operands)


def body(upstream, out_weight, query_rows, key_rows, value_rows, head_offsets):
    rows, width = query_rows.shape
    head_count = width // HEAD_SIZE
    devices = lax.axis_size("context")
    shards = lax.axis_size("heads")
    group = FIRST_SEGMENT // rows
    others = devices // group - 1
    half = rows // 2
    picked = rows // DILATION_RATE
    count = group * picked
    near = group * rows
    place = jnp.stack(
        [lax.rem(lax.axis_index("context"), group), lax.axis_index("heads")]
    ).astype(jnp.int32)
    scalars = [place, head_offsets]

    def swap(values):
        pairs = [[(source, source ^ bits) for source in range(devices)] for bits in range(group)]
        return [values[0]] + [
            lax.ppermute(values[bits], "context", pairs[bits]) for bits in range(1, group)
        ]

    def exchange(value):
        groups = [list(range(first, first + group)) for first in range(0, devices, group)]
        return lax.all_to_all(value, "context", 0, 0, axis_index_groups=groups)

    def segment_shift(value, shift):
        pairs = [(source, (source + shift * group) % devices) for source in range(devices)]
        return lax.ppermute(value, "context", pairs)

    upstreams = [upstream]
    for step in range(1, shards):
        pairs = [(source, (source + step) % shards) for source in range(shards)]
        upstreams.append(lax.ppermute(upstream, "heads", pairs))

    bf16, f32 = jnp.bfloat16, jnp.float32
    (sent,) = call(
        functools.partial(pack_kernel, head_count), "pack_rows",
        [((group, rows + half, PAIR), bf16)],
        [], [query_rows, key_rows, value_rows],
        [((rows, width), bf16)] * 3 + [pltpu.SemaphoreType.DMA((3,))],
        flops=2**31, space=ANY, limit=60,
    )
    sent = exchange(sent)
    (grads_send,) = call(
        functools.partial(project_kernel, head_count, shards), "project_pack",
        [((group, half, PAIR), bf16)],
        [place], [out_weight, *upstreams],
        [((rows, width), bf16)],
        flops=BUSY,
    )
    grads = exchange(grads_send)
    keys, key_t, queries, picks = call(
        functools.partial(gather_kernel, head_count), "gather_keys",
        [
            ((near, PAIR), bf16), ((HEAD_SIZE, near), bf16), ((group, half, PAIR), bf16),
            ((count, PAIR), bf16),
        ],
        scalars, [sent, grads_send],
    )
    other_picks = [segment_shift(picks, shift) for shift in range(1, others + 1)]
    extra, own_terms, other_terms = call(
        functools.partial(far_kernel, head_count, group, others), "picked_rows",
        [
            ((PAIR + STAT_ROWS, count), bf16), ((count, PAIR), f32),
            ((others * count, PAIR), f32),
        ],
        scalars, [keys, queries, grads, picks, *other_picks],
        [((near + count * (1 + others), PAIR), bf16)] + [((count, PAIR), bf16)] * 2,
        flops=8 * near * count * PAIR,
    )
    back = [
        segment_shift(other_terms[(shift - 1) * count : shift * count], -shift)
        for shift in range(1, others + 1)
    ]
    steps = group // 2
    scratch = [
        ((2, near, rows), f32), ((2, near, rows), f32), ((2, near, 2 * rows), bf16),
    ]
    half_flops = 10 * near * near // 2 * PAIR
    acc, query_half = call(
        functools.partial(first_kernel, head_count, steps), "first_rows",
        [((near, PAIR), f32), ((steps, half, PAIR), bf16)],
        scalars, [keys, key_t, queries, grads, extra], scratch, half_flops,
    )
    near_send = call(
        functools.partial(second_kernel, head_count, group - steps, others), "second_rows",
        [((rows + half, PAIR), bf16)] * group,
        scalars, [keys, key_t, queries, grads, extra, acc, query_half, own_terms, *back],
        [((near, PAIR), f32), ((group, rows + half, PAIR), bf16)] + scratch, half_flops,
    )
    return tuple(
        call(
            functools.partial(unpack_kernel, head_count, group), "unpack",
            [((rows, width), bf16)] * 3,
            [place], swap(near_send),
            [((group, rows + half, PAIR), bf16)],
        )
    )


def solution(mesh):
    return jax.shard_map(
        body,
        mesh=mesh,
        in_specs=(
            P(("context", "heads"), None),
            P("heads", None),
            P("context", "heads"),
            P("context", "heads"),
            P("context", "heads"),
            P(),
        ),
        out_specs=(P("context", "heads"), P("context", "heads"), P("context", "heads")),
        check_vma=False,
    )
```

```python
import functools
import math

import jax
import jax.numpy as jnp
from jax import lax
from jax.experimental import pallas as pl
from jax.experimental.pallas import tpu as pltpu
from jax.sharding import PartitionSpec as P

HEAD_SIZE = 64
PAIR = 2 * HEAD_SIZE
DILATION_RATE = 16
FIRST_SEGMENT = 2048
SCALE = 1.0 / math.sqrt(HEAD_SIZE)
LOG2E = math.log2(math.e)
SCORE_FACTOR = SCALE * LOG2E
STRIP = 64
PIECE = 256
BUSY = 2**35
STAT_ROWS = 16

SMEM = pl.BlockSpec(memory_space=pltpu.SMEM)
VMEM = pl.BlockSpec(memory_space=pltpu.VMEM)
ANY = pl.BlockSpec(memory_space=pl.ANY)


def dot_nt(left, right):
    return lax.dot_general(
        left, right, (((1,), (1,)), ((), ())), preferred_element_type=jnp.float32
    )


def dot_nn(left, right):
    return jnp.dot(left, right, preferred_element_type=jnp.float32)


def head_columns(ref, head):
    return ref[:, head * HEAD_SIZE : (head + 1) * HEAD_SIZE]


def pick_matrix(offset, picked, rows):
    source = lax.broadcasted_iota(jnp.int32, (picked, rows), 1)
    index = lax.broadcasted_iota(jnp.int32, (picked, rows), 0)
    return (source == index * DILATION_RATE + offset).astype(jnp.bfloat16)


def spread_matrix(offset, first, picked, rows, axis):
    shape = (picked, rows) if axis == 0 else (rows, picked)
    index = lax.broadcasted_iota(jnp.int32, shape, axis)
    source = lax.broadcasted_iota(jnp.int32, shape, 1 - axis)
    return (source == (index - first) * DILATION_RATE + offset).astype(jnp.bfloat16)


def split_two(value):
    high = value.astype(jnp.bfloat16)
    low = (value - high.astype(jnp.float32)).astype(jnp.bfloat16)
    return high, low


def split_three(value):
    high = value.astype(jnp.bfloat16)
    rest = value - high.astype(jnp.float32)
    middle = rest.astype(jnp.bfloat16)
    low = (rest - middle.astype(jnp.float32)).astype(jnp.bfloat16)
    return high, middle, low


def fold(value, combine):
    parts = [value[start : start + 8] for start in range(0, value.shape[0], 8)]
    while len(parts) > 1:
        merged = [combine(parts[i], parts[i + 1]) for i in range(0, len(parts) - 1, 2)]
        parts = merged + parts[len(merged) * 2 :]
    return parts[0]


def left_half(shape):
    return lax.broadcasted_iota(jnp.int32, shape, 1) < HEAD_SIZE


def side_by_side(block):
    half = block.shape[0] // 2
    return jnp.concatenate([block[:half], block[half:]], 1)


def send_out(place, stage_ref, out_refs):
    for bits, out_ref in enumerate(out_refs):
        out_ref[...] = stage_ref[lax.bitwise_xor(place, bits)]


def pack_kernel(head_count, query_hbm, key_hbm, value_hbm, *refs):
    out_ref, query_ref, key_ref, value_ref, sems = refs
    rows = query_ref.shape[0]
    copies = [
        pltpu.make_async_copy(source, target, sems.at[index])
        for index, (source, target) in enumerate(
            [(key_hbm, key_ref), (value_hbm, value_ref), (query_hbm, query_ref)]
        )
    ]
    for copy in copies:
        copy.start()
    for copy in copies:
        copy.wait()
    for head in range(head_count):
        pair = jnp.concatenate([head_columns(key_ref, head), head_columns(value_ref, head)], 1)
        query = side_by_side(head_columns(query_ref, head))
        for place in range(head, out_ref.shape[0], head_count):
            out_ref[place, :rows, :] = pair
            out_ref[place, rows:, :] = query


def project_kernel(head_count, group, shards, place_ref, weight_ref, *refs):
    upstream_refs, refs = refs[:shards], refs[shards:]
    out_refs, (grad_ref, stage_ref) = refs[:group], refs[group:]
    shard_rows = upstream_refs[0].shape[0]
    for step, upstream_ref in enumerate(upstream_refs):
        owner = lax.rem(place_ref[1] + (shards - step), shards)
        start = pl.multiple_of(owner * shard_rows, shard_rows)
        grad_ref[pl.ds(start, shard_rows), :] = dot_nt(
            upstream_ref[...], weight_ref[...]
        ).astype(jnp.bfloat16)
    for head in range(head_count):
        grad = side_by_side(head_columns(grad_ref, head))
        for place in range(head, group, head_count):
            stage_ref[place] = grad
    send_out(place_ref[0], stage_ref, out_refs)


def own_offset(head_count, place_ref, offset_ref):
    return offset_ref[place_ref[1] * head_count + lax.rem(place_ref[0], head_count)]


def gather_kernel(
    head_count, place_ref, offset_ref, sent_ref, after_ref, keys_out, key_t_out, queries_out,
    picks_out,
):
    group = sent_ref.shape[0]
    rows = keys_out.shape[0] // group
    picked = rows // DILATION_RATE
    pick = pick_matrix(own_offset(head_count, place_ref, offset_ref), picked, rows)
    for place in range(group):
        pair = sent_ref[place, :rows, :]
        keys_out[place * rows : (place + 1) * rows, :] = pair
        picks_out[place * picked : (place + 1) * picked, :] = dot_nn(pick, pair).astype(
            jnp.bfloat16
        )
        queries_out[place] = sent_ref[place, rows:, :]
    key_t_out[...] = keys_out[...].astype(jnp.float32).T[:HEAD_SIZE].astype(jnp.bfloat16)


def query_and_grad(query_ref, grad_ref):
    query, grad = query_ref[...], grad_ref[...]
    zero = jnp.zeros((query.shape[0], HEAD_SIZE), query.dtype)
    return (
        jnp.concatenate(
            [
                jnp.concatenate([query[:, :HEAD_SIZE], zero], 1),
                jnp.concatenate([query[:, HEAD_SIZE:], zero], 1),
            ], 0,
        ),
        jnp.concatenate(
            [
                jnp.concatenate([zero, grad[:, :HEAD_SIZE]], 1),
                jnp.concatenate([zero, grad[:, HEAD_SIZE:]], 1),
            ], 0,
        ),
    )


def far_kernel(
    head_count, group, others, place_ref, offset_ref, near_ref, queries_ref, picks_ref, *refs
):
    other_refs, refs = refs[:others], refs[others:]
    grad_refs, refs = refs[:group], refs[group:]
    extra_out, own_out, other_out, grads_out, keys_ref, query_ref, grad_ref = refs
    near = near_ref.shape[0]
    rows = near // group
    picked = rows // DILATION_RATE
    count = group * picked
    far = count * (1 + others)
    pick = pick_matrix(own_offset(head_count, place_ref, offset_ref), picked, rows)
    keys_ref[:near, :] = near_ref[...]
    for index, ref in enumerate([picks_ref, *other_refs]):
        keys_ref[near + index * count : near + (index + 1) * count, :] = ref[...]
    for bits, ref in enumerate(grad_refs):
        grads_out[lax.bitwise_xor(place_ref[0], bits)] = ref[...]
    for step in range(group):
        query, grad = query_and_grad(queries_ref.at[step], grads_out.at[step])
        span = slice(step * picked, (step + 1) * picked)
        query_ref[span, :] = dot_nn(pick, query).astype(jnp.bfloat16)
        grad_ref[span, :] = dot_nn(pick, grad).astype(jnp.bfloat16)
    far_t = keys_ref[near:, :].astype(jnp.float32).T[:HEAD_SIZE].astype(jnp.bfloat16)
    query, grad = query_ref[...], grad_ref[...]
    score = dot_nt(keys_ref[...], query)
    dprob = dot_nt(keys_ref[...], grad)
    top = jnp.max(score, 0, keepdims=True)
    prob = jnp.exp2((score - top) * SCORE_FACTOR)
    total = jnp.sum(prob, 0, keepdims=True)
    inverse = 1.0 / total
    delta = jnp.sum(prob * dprob, 0, keepdims=True) * inverse
    prob_far = prob[near:] * inverse
    dscore = (prob_far * (dprob[near:] - delta)).astype(jnp.bfloat16)
    terms = dot_nn(
        jnp.concatenate([dscore, prob_far.astype(jnp.bfloat16)], 1),
        jnp.concatenate([query, grad], 0),
    ) * jnp.where(left_half((far, PAIR)), SCALE, 1.0)
    own_out[...] = terms[:count]
    other_out[...] = terms[count:]
    query_grad = dot_nn(far_t, dscore)
    lse = top * SCORE_FACTOR + jnp.log2(total)
    extra_out[:PAIR, :] = jnp.concatenate(split_two(query_grad), 0)
    blank = jnp.zeros((STAT_ROWS - 6, count), jnp.bfloat16)
    extra_out[PAIR:, :] = jnp.concatenate([*split_three(lse), *split_three(delta), blank], 0)


def near_blocks(
    places, offset, keys_ref, key_t_ref, queries_ref, grads_ref, extra_ref,
    prob_ref, dprob_ref, work_ref, top_ref, acc_ref, emit,
):
    near = keys_ref.shape[0]
    rows = prob_ref.shape[2]
    half = rows // 2
    count = extra_ref.shape[1]
    row_lane = lax.broadcasted_iota(jnp.int32, (1, rows), 1)
    picked = lax.rem(row_lane, DILATION_RATE) == offset

    def by_eight(value):
        return value.reshape(value.shape[0] // 8, 8, rows)

    def weights_of(index):
        return query_and_grad(queries_ref.at[places[index]], grads_ref.at[places[index]])

    def first_pass(index, weights, start, state):
        top, total, delta = state
        slot = index % 2
        query, grad = weights
        keys = keys_ref[start : start + PIECE, :]
        scores, dprobs = dot_nt(keys, query), dot_nt(keys, grad)
        for inner in range(0, PIECE, STRIP):
            strip = slice(start + inner, start + inner + STRIP)
            score, dprob = scores[inner : inner + STRIP], dprobs[inner : inner + STRIP]
            part = fold(score, jnp.maximum) * SCORE_FACTOR
            raised = part if top is None else jnp.maximum(top, part)
            prob = jnp.exp2(by_eight(score) * SCORE_FACTOR - raised[None])
            part_total = jnp.sum(prob, 0)
            part_delta = jnp.sum(prob * by_eight(dprob), 0)
            if top is None:
                total, delta = part_total, part_delta
            else:
                shrink = jnp.exp2(top - raised)
                total, delta = total * shrink + part_total, delta * shrink + part_delta
            top = raised
            prob_ref[slot, strip, :] = prob.reshape(STRIP, rows)
            dprob_ref[slot, strip, :] = dprob
            top_ref[slot, strip.start // STRIP] = raised
        return top, total, delta

    def last_pass(index, lse, delta, both, start, query_grad):
        slot = index % 2
        piece = slice(start, start + PIECE)
        for inner in range(0, PIECE, STRIP):
            strip = slice(start + inner, start + inner + STRIP)
            factor = jnp.exp2(top_ref[slot, strip.start // STRIP] - lse)
            prob = by_eight(prob_ref[slot, strip, :]) * factor[None]
            dscore = prob * (by_eight(dprob_ref[slot, strip, :]) - delta)
            work_ref[slot, strip, :rows] = dscore.reshape(STRIP, rows).astype(jnp.bfloat16)
            work_ref[slot, strip, rows:] = prob.reshape(STRIP, rows).astype(jnp.bfloat16)
        acc_ref[piece, :] += dot_nn(work_ref[slot, piece, :], both)
        return query_grad + dot_nn(key_t_ref[:, piece], work_ref[slot, piece, :rows])

    starts = range(0, near, PIECE)
    weights = weights_of(0)
    state = (None, None, None)
    for start in starts:
        state = first_pass(0, weights, start, state)
    for index, place in enumerate(places):
        last = index + 1 == len(places)
        first = place * (rows // DILATION_RATE)
        extra = dot_nn(extra_ref[...], spread_matrix(offset, first, count, rows, 0))
        stats = [extra[PAIR + row : PAIR + row + 1] for row in range(6)]
        top, total, delta = state
        highest = jnp.max(top, 0, keepdims=True)
        shrink = jnp.exp2(top - highest)
        total = jnp.sum(total * shrink, 0, keepdims=True)
        delta = jnp.sum(delta * shrink, 0, keepdims=True) / total
        lse = jnp.where(picked, stats[0] + stats[1] + stats[2], highest + jnp.log2(total))
        delta = jnp.where(picked, stats[3] + stats[4] + stats[5], delta)
        both = jnp.concatenate(weights, 0)
        query_grad = extra[:HEAD_SIZE] + extra[HEAD_SIZE:PAIR]
        weights = None if last else weights_of(index + 1)
        state = (None, None, None)
        for start in starts:
            if not last:
                state = first_pass(index + 1, weights, start, state)
            query_grad = last_pass(index, lse, delta, both, start, query_grad)
        query_grad = (query_grad * SCALE).T.astype(jnp.bfloat16)
        emit(place, jnp.concatenate([query_grad[:half], query_grad[half:]], 1))


def first_kernel(
    head_count, steps, place_ref, offset_ref, keys_ref, key_t_ref, queries_ref, grads_ref,
    extra_ref, acc_ref, query_out, *scratch,
):
    offset = own_offset(head_count, place_ref, offset_ref)
    acc_ref[...] = jnp.zeros_like(acc_ref)

    def emit(place, query_grad):
        query_out[place] = query_grad

    near_blocks(
        range(steps), offset, keys_ref, key_t_ref, queries_ref, grads_ref, extra_ref,
        *scratch, acc_ref, emit,
    )


def second_kernel(
    head_count, steps, others, place_ref, offset_ref, keys_ref, key_t_ref, queries_ref, grads_ref,
    extra_ref, start_ref, query_ref, own_ref, *refs,
):
    back_refs, refs = refs[:others], refs[others:]
    rows = query_ref.shape[1] * 2
    group = keys_ref.shape[0] // rows
    out_refs, refs = refs[:group], refs[group:]
    acc_ref, stage_ref, *scratch = refs
    count = extra_ref.shape[1]
    picked = count // group
    offset = own_offset(head_count, place_ref, offset_ref)
    acc_ref[...] = start_ref[...]

    def emit(place, query_grad):
        stage_ref[place, rows:, :] = query_grad

    near_blocks(
        range(group - steps, group), offset, keys_ref, key_t_ref, queries_ref, grads_ref, extra_ref,
        *scratch, acc_ref, emit,
    )
    terms = own_ref[...]
    for back_ref in back_refs:
        terms = terms + back_ref[...]
    terms = jnp.concatenate(split_two(terms), 0)
    factor = jnp.where(left_half((rows, PAIR)), SCALE, 1.0)
    for place in range(group):
        spread = spread_matrix(offset, place * picked, count, rows, 1)
        placed = dot_nn(jnp.concatenate([spread, spread], 1), terms)
        summed = acc_ref[place * rows : (place + 1) * rows, :] * factor + placed
        stage_ref[place, :rows, :] = summed.astype(jnp.bfloat16)
        if place < group - steps:
            stage_ref[place, rows:, :] = query_ref[place]
    send_out(place_ref[0], stage_ref, out_refs)


def unpack_kernel(head_count, group, place_ref, *refs):
    near_refs, refs = refs[:group], refs[group:]
    query_out, key_out, value_out, stage_ref = refs
    rows = query_out.shape[0]
    half = rows // 2
    for bits, near_ref in enumerate(near_refs):
        stage_ref[lax.bitwise_xor(place_ref[0], bits)] = near_ref[...]
    for head in range(head_count):
        columns = slice(head * HEAD_SIZE, (head + 1) * HEAD_SIZE)
        key_out[:, columns] = stage_ref[head, :rows, :HEAD_SIZE]
        value_out[:, columns] = stage_ref[head, :rows, HEAD_SIZE:]
        query_out[:half, columns] = stage_ref[head, rows:, :HEAD_SIZE]
        query_out[half:, columns] = stage_ref[head, rows:, HEAD_SIZE:]


def call(kernel, name, out_shape, scalars, operands, scratch=(), flops=0, space=VMEM, limit=40):
    return pl.pallas_call(
        kernel,
        out_shape=tuple(jax.ShapeDtypeStruct(*shape) for shape in out_shape),
        in_specs=[SMEM] * len(scalars) + [space] * len(operands),
        out_specs=tuple(VMEM for _ in out_shape),
        scratch_shapes=[
            pltpu.VMEM(*shape) if isinstance(shape, tuple) else shape for shape in scratch
        ],
        compiler_params=pltpu.CompilerParams(vmem_limit_bytes=limit * 1024 * 1024),
        cost_estimate=pl.CostEstimate(flops=flops, bytes_accessed=2**21, transcendentals=0),
        name=name,
    )(*scalars, *operands)


def body(upstream, out_weight, query_rows, key_rows, value_rows, head_offsets):
    rows, width = query_rows.shape
    head_count = width // HEAD_SIZE
    devices = lax.axis_size("context")
    shards = lax.axis_size("heads")
    group = FIRST_SEGMENT // rows
    others = devices // group - 1
    half = rows // 2
    picked = rows // DILATION_RATE
    count = group * picked
    near = group * rows
    place = jnp.stack(
        [lax.rem(lax.axis_index("context"), group), lax.axis_index("heads")]
    ).astype(jnp.int32)
    scalars = [place, head_offsets]

    def swap(values):
        pairs = [[(source, source ^ bits) for source in range(devices)] for bits in range(group)]
        return [values[0]] + [
            lax.ppermute(values[bits], "context", pairs[bits]) for bits in range(1, group)
        ]

    def exchange(value):
        groups = [list(range(first, first + group)) for first in range(0, devices, group)]
        return lax.all_to_all(value, "context", 0, 0, axis_index_groups=groups)

    def segment_shift(value, shift):
        pairs = [(source, (source + shift * group) % devices) for source in range(devices)]
        return lax.ppermute(value, "context", pairs)

    upstreams = [upstream]
    for step in range(1, shards):
        pairs = [(source, (source + step) % shards) for source in range(shards)]
        upstreams.append(lax.ppermute(upstream, "heads", pairs))

    bf16, f32 = jnp.bfloat16, jnp.float32
    (sent,) = call(
        functools.partial(pack_kernel, head_count), "pack_rows",
        [((group, rows + half, PAIR), bf16)],
        [], [query_rows, key_rows, value_rows],
        [((rows, width), bf16)] * 3 + [pltpu.SemaphoreType.DMA((3,))],
        flops=2**31, space=ANY, limit=60,
    )
    sent = exchange(sent)
    grads_send = call(
        functools.partial(project_kernel, head_count, group, shards), "project_pack",
        [((half, PAIR), bf16)] * group,
        [place], [out_weight, *upstreams],
        [((rows, width), bf16), ((group, half, PAIR), bf16)],
        flops=BUSY,
    )
    grads = swap(grads_send)
    keys, key_t, queries, picks = call(
        functools.partial(gather_kernel, head_count), "gather_keys",
        [
            ((near, PAIR), bf16), ((HEAD_SIZE, near), bf16), ((group, half, PAIR), bf16),
            ((count, PAIR), bf16),
        ],
        scalars, [sent, grads_send[0]],
    )
    other_picks = [segment_shift(picks, shift) for shift in range(1, others + 1)]
    extra, own_terms, other_terms, grads = call(
        functools.partial(far_kernel, head_count, group, others), "picked_rows",
        [
            ((PAIR + STAT_ROWS, count), bf16), ((count, PAIR), f32),
            ((others * count, PAIR), f32), ((group, half, PAIR), bf16),
        ],
        scalars, [keys, queries, picks, *other_picks, *grads],
        [((near + count * (1 + others), PAIR), bf16)] + [((count, PAIR), bf16)] * 2,
        flops=8 * near * count * PAIR,
    )
    back = [
        segment_shift(other_terms[(shift - 1) * count : shift * count], -shift)
        for shift in range(1, others + 1)
    ]
    steps = group // 2
    scratch = [
        ((2, near, rows), f32), ((2, near, rows), f32), ((2, near, 2 * rows), bf16),
        ((2, near // STRIP, 8, rows), f32),
    ]
    half_flops = 10 * near * near // 2 * PAIR
    acc, query_half = call(
        functools.partial(first_kernel, head_count, steps), "first_rows",
        [((near, PAIR), f32), ((steps, half, PAIR), bf16)],
        scalars, [keys, key_t, queries, grads, extra], scratch, half_flops,
    )
    near_send = call(
        functools.partial(second_kernel, head_count, group - steps, others), "second_rows",
        [((rows + half, PAIR), bf16)] * group,
        scalars, [keys, key_t, queries, grads, extra, acc, query_half, own_terms, *back],
        [((near, PAIR), f32), ((group, rows + half, PAIR), bf16)] + scratch, half_flops,
    )
    return tuple(
        call(
            functools.partial(unpack_kernel, head_count, group), "unpack",
            [((rows, width), bf16)] * 3,
            [place], swap(near_send),
            [((group, rows + half, PAIR), bf16)],
        )
    )


def solution(mesh):
    return jax.shard_map(
        body,
        mesh=mesh,
        in_specs=(
            P(("context", "heads"), None),
            P("heads", None),
            P("context", "heads"),
            P("context", "heads"),
            P("context", "heads"),
            P(),
        ),
        out_specs=(P("context", "heads"), P("context", "heads"), P("context", "heads")),
        check_vma=False,
    )
```

```python
import functools
import math

import jax
import jax.numpy as jnp
from jax import lax
from jax.experimental import pallas as pl
from jax.experimental.pallas import tpu as pltpu
from jax.sharding import PartitionSpec as P

HEAD_SIZE = 64
PAIR = 2 * HEAD_SIZE
DILATION_RATE = 16
FIRST_SEGMENT = 2048
SCALE = 1.0 / math.sqrt(HEAD_SIZE)
LOG2E = math.log2(math.e)
SCORE_FACTOR = SCALE * LOG2E
STRIP = 64
PIECE = 256
BUSY = 2**35
STAT_ROWS = 16

SMEM = pl.BlockSpec(memory_space=pltpu.SMEM)
VMEM = pl.BlockSpec(memory_space=pltpu.VMEM)
ANY = pl.BlockSpec(memory_space=pl.ANY)


def dot_nt(left, right):
    return lax.dot_general(
        left, right, (((1,), (1,)), ((), ())), preferred_element_type=jnp.float32
    )


def dot_nn(left, right):
    return jnp.dot(left, right, preferred_element_type=jnp.float32)


def head_columns(ref, head):
    return ref[:, head * HEAD_SIZE : (head + 1) * HEAD_SIZE]


def pick_matrix(offset, picked, rows):
    source = lax.broadcasted_iota(jnp.int32, (picked, rows), 1)
    index = lax.broadcasted_iota(jnp.int32, (picked, rows), 0)
    return (source == index * DILATION_RATE + offset).astype(jnp.bfloat16)


def spread_matrix(offset, first, picked, rows, axis):
    shape = (picked, rows) if axis == 0 else (rows, picked)
    index = lax.broadcasted_iota(jnp.int32, shape, axis)
    source = lax.broadcasted_iota(jnp.int32, shape, 1 - axis)
    return (source == (index - first) * DILATION_RATE + offset).astype(jnp.bfloat16)


def split_two(value):
    high = value.astype(jnp.bfloat16)
    low = (value - high.astype(jnp.float32)).astype(jnp.bfloat16)
    return high, low


def split_three(value):
    high = value.astype(jnp.bfloat16)
    rest = value - high.astype(jnp.float32)
    middle = rest.astype(jnp.bfloat16)
    low = (rest - middle.astype(jnp.float32)).astype(jnp.bfloat16)
    return high, middle, low


def fold(value, combine):
    parts = [value[start : start + 8] for start in range(0, value.shape[0], 8)]
    while len(parts) > 1:
        merged = [combine(parts[i], parts[i + 1]) for i in range(0, len(parts) - 1, 2)]
        parts = merged + parts[len(merged) * 2 :]
    return parts[0]


def left_half(shape):
    return lax.broadcasted_iota(jnp.int32, shape, 1) < HEAD_SIZE


def side_by_side(block):
    half = block.shape[0] // 2
    return jnp.concatenate([block[:half], block[half:]], 1)


def send_out(place, stage_ref, out_refs):
    for bits, out_ref in enumerate(out_refs):
        out_ref[...] = stage_ref[lax.bitwise_xor(place, bits)]


def pack_kernel(head_count, query_hbm, key_hbm, value_hbm, offset_hbm, *refs):
    out_ref, picks_ref, query_ref, key_ref, value_ref, offset_ref, sems = refs
    rows = query_ref.shape[0]
    picked = picks_ref.shape[1]
    shard = lax.axis_index("heads")
    loads = [
        (offset_hbm, offset_ref), (key_hbm, key_ref), (value_hbm, value_ref),
        (query_hbm, query_ref),
    ]
    copies = [
        pltpu.make_async_copy(source, target, sems.at[index])
        for index, (source, target) in enumerate(loads)
    ]
    for copy in copies:
        copy.start()
    for copy in copies:
        copy.wait()
    for head in range(head_count):
        pair = jnp.concatenate([head_columns(key_ref, head), head_columns(value_ref, head)], 1)
        query = side_by_side(head_columns(query_ref, head))
        for place in range(head, out_ref.shape[0], head_count):
            out_ref[place, :rows, :] = pair
            out_ref[place, rows:, :] = query
        pick = pick_matrix(offset_ref[shard * head_count + head], picked, rows)
        picks_ref[head] = dot_nn(pick, pair).astype(jnp.bfloat16)


def project_kernel(head_count, group, shards, place_ref, weight_ref, *refs):
    upstream_refs, refs = refs[:shards], refs[shards:]
    far_refs, refs = refs[: -group - 2], refs[-group - 2 :]
    out_refs, (grad_ref, stage_ref) = refs[:group], refs[group:]
    shard_rows = upstream_refs[0].shape[0]
    for step, upstream_ref in enumerate(upstream_refs):
        owner = lax.rem(place_ref[1] + (shards - step), shards)
        start = pl.multiple_of(owner * shard_rows, shard_rows)
        grad_ref[pl.ds(start, shard_rows), :] = dot_nt(
            upstream_ref[...], weight_ref[...]
        ).astype(jnp.bfloat16)
    for head in range(head_count):
        grad = side_by_side(head_columns(grad_ref, head))
        for place in range(head, group, head_count):
            stage_ref[place, : grad.shape[0], :] = grad
            for other, far_ref in enumerate(far_refs):
                first = grad.shape[0] + other * far_ref.shape[1]
                stage_ref[place, first : first + far_ref.shape[1], :] = far_ref[head]
    send_out(place_ref[0], stage_ref, out_refs)


def own_offset(head_count, place_ref, offset_ref):
    return offset_ref[place_ref[1] * head_count + lax.rem(place_ref[0], head_count)]


def query_and_grad(query_ref, grad_ref):
    query, grad = query_ref[...], grad_ref[...]
    zero = jnp.zeros((query.shape[0], HEAD_SIZE), query.dtype)
    return (
        jnp.concatenate(
            [
                jnp.concatenate([query[:, :HEAD_SIZE], zero], 1),
                jnp.concatenate([query[:, HEAD_SIZE:], zero], 1),
            ], 0,
        ),
        jnp.concatenate(
            [
                jnp.concatenate([zero, grad[:, :HEAD_SIZE]], 1),
                jnp.concatenate([zero, grad[:, HEAD_SIZE:]], 1),
            ], 0,
        ),
    )


def far_kernel(head_count, others, place_ref, offset_ref, sent_ref, *refs):
    group = sent_ref.shape[0]
    grad_refs, refs = refs[:group], refs[group:]
    keys_out, key_t_out, queries_out, grads_out, *refs = refs
    extra_out, own_out, other_out, keys_ref, query_ref, grad_ref = refs
    near = keys_out.shape[0]
    rows = near // group
    half = rows // 2
    picked = rows // DILATION_RATE
    count = group * picked
    far = count * (1 + others)
    pick = pick_matrix(own_offset(head_count, place_ref, offset_ref), picked, rows)
    for bits, ref in enumerate(grad_refs):
        place = lax.bitwise_xor(place_ref[0], bits)
        grads_out[place] = ref[:half, :]
        for other in range(others):
            start = pl.multiple_of(near + (1 + other) * count + place * picked, picked)
            source = half + other * picked
            keys_ref[pl.ds(start, picked), :] = ref[source : source + picked, :]
    for place in range(group):
        pair = sent_ref[place, :rows, :]
        span = slice(place * picked, (place + 1) * picked)
        keys_ref[place * rows : (place + 1) * rows, :] = pair
        keys_ref[near + span.start : near + span.stop, :] = dot_nn(pick, pair).astype(jnp.bfloat16)
        queries_out[place] = sent_ref[place, rows:, :]
        query, grad = query_and_grad(queries_out.at[place], grads_out.at[place])
        query_ref[span, :] = dot_nn(pick, query).astype(jnp.bfloat16)
        grad_ref[span, :] = dot_nn(pick, grad).astype(jnp.bfloat16)
    keys_out[...] = keys_ref[:near, :]
    key_t_out[...] = keys_out[...].astype(jnp.float32).T[:HEAD_SIZE].astype(jnp.bfloat16)
    far_t = keys_ref[near:, :].astype(jnp.float32).T[:HEAD_SIZE].astype(jnp.bfloat16)
    query, grad = query_ref[...], grad_ref[...]
    score = dot_nt(keys_ref[...], query)
    dprob = dot_nt(keys_ref[...], grad)
    top = jnp.max(score, 0, keepdims=True)
    prob = jnp.exp2((score - top) * SCORE_FACTOR)
    total = jnp.sum(prob, 0, keepdims=True)
    inverse = 1.0 / total
    delta = jnp.sum(prob * dprob, 0, keepdims=True) * inverse
    prob_far = prob[near:] * inverse
    dscore = (prob_far * (dprob[near:] - delta)).astype(jnp.bfloat16)
    terms = dot_nn(
        jnp.concatenate([dscore, prob_far.astype(jnp.bfloat16)], 1),
        jnp.concatenate([query, grad], 0),
    ) * jnp.where(left_half((far, PAIR)), SCALE, 1.0)
    own_out[...] = terms[:count]
    other_out[...] = terms[count:]
    query_grad = dot_nn(far_t, dscore)
    lse = top * SCORE_FACTOR + jnp.log2(total)
    extra_out[:PAIR, :] = jnp.concatenate(split_two(query_grad), 0)
    blank = jnp.zeros((STAT_ROWS - 6, count), jnp.bfloat16)
    extra_out[PAIR:, :] = jnp.concatenate([*split_three(lse), *split_three(delta), blank], 0)


def near_blocks(
    places, offset, keys_ref, key_t_ref, queries_ref, grads_ref, extra_ref,
    prob_ref, dprob_ref, work_ref, top_ref, acc_ref, emit,
):
    near = keys_ref.shape[0]
    rows = prob_ref.shape[2]
    half = rows // 2
    count = extra_ref.shape[1]
    row_lane = lax.broadcasted_iota(jnp.int32, (1, rows), 1)
    picked = lax.rem(row_lane, DILATION_RATE) == offset

    def by_eight(value):
        return value.reshape(value.shape[0] // 8, 8, rows)

    def weights_of(index):
        return query_and_grad(queries_ref.at[places[index]], grads_ref.at[places[index]])

    def first_pass(index, weights, start, state):
        top, total, delta = state
        slot = index % 2
        query, grad = weights
        keys = keys_ref[start : start + PIECE, :]
        scores, dprobs = dot_nt(keys, query), dot_nt(keys, grad)
        for inner in range(0, PIECE, STRIP):
            strip = slice(start + inner, start + inner + STRIP)
            score, dprob = scores[inner : inner + STRIP], dprobs[inner : inner + STRIP]
            part = fold(score, jnp.maximum) * SCORE_FACTOR
            raised = part if top is None else jnp.maximum(top, part)
            prob = jnp.exp2(by_eight(score) * SCORE_FACTOR - raised[None])
            part_total = jnp.sum(prob, 0)
            part_delta = jnp.sum(prob * by_eight(dprob), 0)
            if top is None:
                total, delta = part_total, part_delta
            else:
                shrink = jnp.exp2(top - raised)
                total, delta = total * shrink + part_total, delta * shrink + part_delta
            top = raised
            prob_ref[slot, strip, :] = prob.reshape(STRIP, rows)
            dprob_ref[slot, strip, :] = dprob
            top_ref[slot, strip.start // STRIP] = raised
        return top, total, delta

    def last_pass(index, lse, delta, both, start, query_grad):
        slot = index % 2
        piece = slice(start, start + PIECE)
        for inner in range(0, PIECE, STRIP):
            strip = slice(start + inner, start + inner + STRIP)
            factor = jnp.exp2(top_ref[slot, strip.start // STRIP] - lse)
            prob = by_eight(prob_ref[slot, strip, :]) * factor[None]
            dscore = prob * (by_eight(dprob_ref[slot, strip, :]) - delta)
            work_ref[slot, strip, :rows] = dscore.reshape(STRIP, rows).astype(jnp.bfloat16)
            work_ref[slot, strip, rows:] = prob.reshape(STRIP, rows).astype(jnp.bfloat16)
        acc_ref[piece, :] += dot_nn(work_ref[slot, piece, :], both)
        return query_grad + dot_nn(key_t_ref[:, piece], work_ref[slot, piece, :rows])

    starts = range(0, near, PIECE)
    weights = weights_of(0)
    state = (None, None, None)
    for start in starts:
        state = first_pass(0, weights, start, state)
    for index, place in enumerate(places):
        last = index + 1 == len(places)
        first = place * (rows // DILATION_RATE)
        extra = dot_nn(extra_ref[...], spread_matrix(offset, first, count, rows, 0))
        stats = [extra[PAIR + row : PAIR + row + 1] for row in range(6)]
        top, total, delta = state
        highest = jnp.max(top, 0, keepdims=True)
        shrink = jnp.exp2(top - highest)
        total = jnp.sum(total * shrink, 0, keepdims=True)
        delta = jnp.sum(delta * shrink, 0, keepdims=True) / total
        lse = jnp.where(picked, stats[0] + stats[1] + stats[2], highest + jnp.log2(total))
        delta = jnp.where(picked, stats[3] + stats[4] + stats[5], delta)
        both = jnp.concatenate(weights, 0)
        query_grad = extra[:HEAD_SIZE] + extra[HEAD_SIZE:PAIR]
        weights = None if last else weights_of(index + 1)
        state = (None, None, None)
        for start in starts:
            if not last:
                state = first_pass(index + 1, weights, start, state)
            query_grad = last_pass(index, lse, delta, both, start, query_grad)
        query_grad = (query_grad * SCALE).T.astype(jnp.bfloat16)
        emit(place, jnp.concatenate([query_grad[:half], query_grad[half:]], 1))


def first_kernel(
    head_count, steps, place_ref, offset_ref, keys_ref, key_t_ref, queries_ref, grads_ref,
    extra_ref, acc_ref, query_out, *scratch,
):
    offset = own_offset(head_count, place_ref, offset_ref)
    acc_ref[...] = jnp.zeros_like(acc_ref)

    def emit(place, query_grad):
        query_out[place] = query_grad

    near_blocks(
        range(steps), offset, keys_ref, key_t_ref, queries_ref, grads_ref, extra_ref,
        *scratch, acc_ref, emit,
    )


def second_kernel(
    head_count, steps, others, place_ref, offset_ref, keys_ref, key_t_ref, queries_ref, grads_ref,
    extra_ref, start_ref, query_ref, own_ref, *refs,
):
    back_refs, refs = refs[:others], refs[others:]
    rows = query_ref.shape[1] * 2
    group = keys_ref.shape[0] // rows
    out_refs, refs = refs[:group], refs[group:]
    acc_ref, stage_ref, *scratch = refs
    count = extra_ref.shape[1]
    picked = count // group
    offset = own_offset(head_count, place_ref, offset_ref)
    acc_ref[...] = start_ref[...]

    def emit(place, query_grad):
        stage_ref[place, rows:, :] = query_grad

    near_blocks(
        range(group - steps, group), offset, keys_ref, key_t_ref, queries_ref, grads_ref, extra_ref,
        *scratch, acc_ref, emit,
    )
    terms = own_ref[...]
    for back_ref in back_refs:
        terms = terms + back_ref[...]
    terms = jnp.concatenate(split_two(terms), 0)
    factor = jnp.where(left_half((rows, PAIR)), SCALE, 1.0)
    for place in range(group):
        spread = spread_matrix(offset, place * picked, count, rows, 1)
        placed = dot_nn(jnp.concatenate([spread, spread], 1), terms)
        summed = acc_ref[place * rows : (place + 1) * rows, :] * factor + placed
        stage_ref[place, :rows, :] = summed.astype(jnp.bfloat16)
        if place < group - steps:
            stage_ref[place, rows:, :] = query_ref[place]
    send_out(place_ref[0], stage_ref, out_refs)


def unpack_kernel(head_count, group, place_ref, *refs):
    near_refs, refs = refs[:group], refs[group:]
    query_out, key_out, value_out, stage_ref = refs
    rows = query_out.shape[0]
    half = rows // 2
    for bits, near_ref in enumerate(near_refs):
        stage_ref[lax.bitwise_xor(place_ref[0], bits)] = near_ref[...]
    for head in range(head_count):
        columns = slice(head * HEAD_SIZE, (head + 1) * HEAD_SIZE)
        key_out[:, columns] = stage_ref[head, :rows, :HEAD_SIZE]
        value_out[:, columns] = stage_ref[head, :rows, HEAD_SIZE:]
        query_out[:half, columns] = stage_ref[head, rows:, :HEAD_SIZE]
        query_out[half:, columns] = stage_ref[head, rows:, HEAD_SIZE:]


def call(kernel, name, out_shape, scalars, operands, scratch=(), flops=0, space=VMEM, limit=40):
    return pl.pallas_call(
        kernel,
        out_shape=tuple(jax.ShapeDtypeStruct(*shape) for shape in out_shape),
        in_specs=[SMEM] * len(scalars) + [space] * len(operands),
        out_specs=tuple(VMEM for _ in out_shape),
        scratch_shapes=[
            pltpu.VMEM(*shape) if isinstance(shape, tuple) else shape for shape in scratch
        ],
        compiler_params=pltpu.CompilerParams(vmem_limit_bytes=limit * 1024 * 1024),
        cost_estimate=pl.CostEstimate(flops=flops, bytes_accessed=2**21, transcendentals=0),
        name=name,
    )(*scalars, *operands)


def body(upstream, out_weight, query_rows, key_rows, value_rows, head_offsets):
    rows, width = query_rows.shape
    head_count = width // HEAD_SIZE
    devices = lax.axis_size("context")
    shards = lax.axis_size("heads")
    group = FIRST_SEGMENT // rows
    others = devices // group - 1
    half = rows // 2
    picked = rows // DILATION_RATE
    count = group * picked
    near = group * rows
    place = jnp.stack(
        [lax.rem(lax.axis_index("context"), group), lax.axis_index("heads")]
    ).astype(jnp.int32)
    scalars = [place, head_offsets]

    def swap(values):
        pairs = [[(source, source ^ bits) for source in range(devices)] for bits in range(group)]
        return [values[0]] + [
            lax.ppermute(values[bits], "context", pairs[bits]) for bits in range(1, group)
        ]

    def segment_shift(value, shift):
        pairs = [(source, (source + shift * group) % devices) for source in range(devices)]
        return lax.ppermute(value, "context", pairs)

    upstreams = [upstream]
    for step in range(1, shards):
        pairs = [(source, (source + step) % shards) for source in range(shards)]
        upstreams.append(lax.ppermute(upstream, "heads", pairs))

    bf16, f32 = jnp.bfloat16, jnp.float32
    sent, far_send = call(
        functools.partial(pack_kernel, head_count), "pack_rows",
        [((group, rows + half, PAIR), bf16), ((head_count, picked, PAIR), bf16)],
        [], [query_rows, key_rows, value_rows, head_offsets],
        [((rows, width), bf16)] * 3
        + [pltpu.SMEM(head_offsets.shape, jnp.int32), pltpu.SemaphoreType.DMA((4,))],
        flops=2**31, space=ANY, limit=60,
    )
    groups = [list(range(first, first + group)) for first in range(0, devices, group)]
    sent = lax.all_to_all(sent, "context", 0, 0, axis_index_groups=groups)
    far_in = [segment_shift(far_send, shift) for shift in range(1, others + 1)]
    sent_rows = half + others * picked
    grads = swap(
        call(
            functools.partial(project_kernel, head_count, group, shards), "project_pack",
            [((sent_rows, PAIR), bf16)] * group,
            [place], [out_weight, *upstreams, *far_in],
            [((rows, width), bf16), ((group, sent_rows, PAIR), bf16)],
            flops=BUSY,
        )
    )
    keys, key_t, queries, grads, extra, own_terms, other_terms = call(
        functools.partial(far_kernel, head_count, others), "picked_rows",
        [
            ((near, PAIR), bf16), ((HEAD_SIZE, near), bf16), ((group, half, PAIR), bf16),
            ((group, half, PAIR), bf16), ((PAIR + STAT_ROWS, count), bf16),
            ((count, PAIR), f32), ((others * count, PAIR), f32),
        ],
        scalars, [sent, *grads],
        [((near + count * (1 + others), PAIR), bf16)] + [((count, PAIR), bf16)] * 2,
        flops=8 * near * count * PAIR,
    )
    back = [
        segment_shift(other_terms[(shift - 1) * count : shift * count], -shift)
        for shift in range(1, others + 1)
    ]
    steps = group // 2
    scratch = [
        ((2, near, rows), f32), ((2, near, rows), f32), ((2, near, 2 * rows), bf16),
        ((2, near // STRIP, 8, rows), f32),
    ]
    half_flops = 10 * near * near // 2 * PAIR
    acc, query_half = call(
        functools.partial(first_kernel, head_count, steps), "first_rows",
        [((near, PAIR), f32), ((steps, half, PAIR), bf16)],
        scalars, [keys, key_t, queries, grads, extra], scratch, half_flops,
    )
    near_send = call(
        functools.partial(second_kernel, head_count, group - steps, others), "second_rows",
        [((rows + half, PAIR), bf16)] * group,
        scalars, [keys, key_t, queries, grads, extra, acc, query_half, own_terms, *back],
        [((near, PAIR), f32), ((group, rows + half, PAIR), bf16)] + scratch, half_flops,
    )
    return tuple(
        call(
            functools.partial(unpack_kernel, head_count, group), "unpack",
            [((rows, width), bf16)] * 3,
            [place], swap(near_send),
            [((group, rows + half, PAIR), bf16)],
        )
    )


def solution(mesh):
    return jax.shard_map(
        body,
        mesh=mesh,
        in_specs=(
            P(("context", "heads"), None),
            P("heads", None),
            P("context", "heads"),
            P("context", "heads"),
            P("context", "heads"),
            P(),
        ),
        out_specs=(P("context", "heads"), P("context", "heads"), P("context", "heads")),
        check_vma=False,
    )
```

```python
import functools
import math

import jax
import jax.numpy as jnp
from jax import lax
from jax.experimental import pallas as pl
from jax.experimental.pallas import tpu as pltpu
from jax.sharding import PartitionSpec as P

HEAD_SIZE = 64
PAIR = 2 * HEAD_SIZE
DILATION_RATE = 16
FIRST_SEGMENT = 2048
SCALE = 1.0 / math.sqrt(HEAD_SIZE)
LOG2E = math.log2(math.e)
SCORE_FACTOR = SCALE * LOG2E
STRIP = 64
PIECE = 1024
BUSY = 2**35
STAT_ROWS = 16

SMEM = pl.BlockSpec(memory_space=pltpu.SMEM)
VMEM = pl.BlockSpec(memory_space=pltpu.VMEM)
ANY = pl.BlockSpec(memory_space=pl.ANY)


def dot_nt(left, right):
    return lax.dot_general(
        left, right, (((1,), (1,)), ((), ())), preferred_element_type=jnp.float32
    )


def dot_nn(left, right):
    return jnp.dot(left, right, preferred_element_type=jnp.float32)


def head_columns(ref, head):
    return ref[:, head * HEAD_SIZE : (head + 1) * HEAD_SIZE]


def pick_matrix(offset, picked, rows):
    source = lax.broadcasted_iota(jnp.int32, (picked, rows), 1)
    index = lax.broadcasted_iota(jnp.int32, (picked, rows), 0)
    return (source == index * DILATION_RATE + offset).astype(jnp.bfloat16)


def spread_matrix(offset, first, picked, rows, axis):
    shape = (picked, rows) if axis == 0 else (rows, picked)
    index = lax.broadcasted_iota(jnp.int32, shape, axis)
    source = lax.broadcasted_iota(jnp.int32, shape, 1 - axis)
    return (source == (index - first) * DILATION_RATE + offset).astype(jnp.bfloat16)


def split_two(value):
    high = value.astype(jnp.bfloat16)
    low = (value - high.astype(jnp.float32)).astype(jnp.bfloat16)
    return high, low


def split_three(value):
    high = value.astype(jnp.bfloat16)
    rest = value - high.astype(jnp.float32)
    middle = rest.astype(jnp.bfloat16)
    low = (rest - middle.astype(jnp.float32)).astype(jnp.bfloat16)
    return high, middle, low


def fold(value, combine):
    parts = [value[start : start + 8] for start in range(0, value.shape[0], 8)]
    while len(parts) > 1:
        merged = [combine(parts[i], parts[i + 1]) for i in range(0, len(parts) - 1, 2)]
        parts = merged + parts[len(merged) * 2 :]
    return parts[0]


def left_half(shape):
    return lax.broadcasted_iota(jnp.int32, shape, 1) < HEAD_SIZE


def side_by_side(block):
    half = block.shape[0] // 2
    return jnp.concatenate([block[:half], block[half:]], 1)


def send_out(place, stage_ref, out_refs):
    for bits, out_ref in enumerate(out_refs):
        out_ref[...] = stage_ref[lax.bitwise_xor(place, bits)]


def pack_kernel(head_count, query_hbm, key_hbm, value_hbm, *refs):
    out_ref, query_ref, key_ref, value_ref, sems = refs
    rows = query_ref.shape[0]
    copies = [
        pltpu.make_async_copy(source, target, sems.at[index])
        for index, (source, target) in enumerate(
            [(key_hbm, key_ref), (value_hbm, value_ref), (query_hbm, query_ref)]
        )
    ]
    for copy in copies:
        copy.start()
    for copy in copies:
        copy.wait()
    for head in range(head_count):
        pair = jnp.concatenate([head_columns(key_ref, head), head_columns(value_ref, head)], 1)
        query = side_by_side(head_columns(query_ref, head))
        for place in range(head, out_ref.shape[0], head_count):
            out_ref[place, :rows, :] = pair
            out_ref[place, rows:, :] = query


def project_kernel(head_count, group, shards, place_ref, weight_ref, *refs):
    upstream_refs, refs = refs[:shards], refs[shards:]
    out_refs, (grad_ref, stage_ref) = refs[:group], refs[group:]
    shard_rows = upstream_refs[0].shape[0]
    for step, upstream_ref in enumerate(upstream_refs):
        owner = lax.rem(place_ref[1] + (shards - step), shards)
        start = pl.multiple_of(owner * shard_rows, shard_rows)
        grad_ref[pl.ds(start, shard_rows), :] = dot_nt(
            upstream_ref[...], weight_ref[...]
        ).astype(jnp.bfloat16)
    for head in range(head_count):
        grad = side_by_side(head_columns(grad_ref, head))
        for place in range(head, group, head_count):
            stage_ref[place] = grad
    send_out(place_ref[0], stage_ref, out_refs)


def own_offset(head_count, place_ref, offset_ref):
    return offset_ref[place_ref[1] * head_count + lax.rem(place_ref[0], head_count)]


def gather_kernel(
    head_count, place_ref, offset_ref, sent_ref, after_ref, keys_out, key_t_out, queries_out,
    picks_out,
):
    group = sent_ref.shape[0]
    rows = keys_out.shape[0] // group
    picked = rows // DILATION_RATE
    pick = pick_matrix(own_offset(head_count, place_ref, offset_ref), picked, rows)
    for place in range(group):
        pair = sent_ref[place, :rows, :]
        keys_out[place * rows : (place + 1) * rows, :] = pair
        picks_out[place * picked : (place + 1) * picked, :] = dot_nn(pick, pair).astype(
            jnp.bfloat16
        )
        queries_out[place] = sent_ref[place, rows:, :]
    key_t_out[...] = keys_out[...].astype(jnp.float32).T[:HEAD_SIZE].astype(jnp.bfloat16)


def query_and_grad(query_ref, grad_ref):
    query, grad = query_ref[...], grad_ref[...]
    zero = jnp.zeros((query.shape[0], HEAD_SIZE), query.dtype)
    return (
        jnp.concatenate(
            [
                jnp.concatenate([query[:, :HEAD_SIZE], zero], 1),
                jnp.concatenate([query[:, HEAD_SIZE:], zero], 1),
            ], 0,
        ),
        jnp.concatenate(
            [
                jnp.concatenate([zero, grad[:, :HEAD_SIZE]], 1),
                jnp.concatenate([zero, grad[:, HEAD_SIZE:]], 1),
            ], 0,
        ),
    )


def far_kernel(
    head_count, group, others, place_ref, offset_ref, near_ref, queries_ref, picks_ref, *refs
):
    other_refs, refs = refs[:others], refs[others:]
    grad_refs, refs = refs[:group], refs[group:]
    extra_out, own_out, other_out, grads_out, keys_ref, query_ref, grad_ref = refs
    near = near_ref.shape[0]
    rows = near // group
    picked = rows // DILATION_RATE
    count = group * picked
    far = count * (1 + others)
    pick = pick_matrix(own_offset(head_count, place_ref, offset_ref), picked, rows)
    keys_ref[:near, :] = near_ref[...]
    for index, ref in enumerate([picks_ref, *other_refs]):
        keys_ref[near + index * count : near + (index + 1) * count, :] = ref[...]
    for bits, ref in enumerate(grad_refs):
        grads_out[lax.bitwise_xor(place_ref[0], bits)] = ref[...]
    for step in range(group):
        query, grad = query_and_grad(queries_ref.at[step], grads_out.at[step])
        span = slice(step * picked, (step + 1) * picked)
        query_ref[span, :] = dot_nn(pick, query).astype(jnp.bfloat16)
        grad_ref[span, :] = dot_nn(pick, grad).astype(jnp.bfloat16)
    far_t = keys_ref[near:, :].astype(jnp.float32).T[:HEAD_SIZE].astype(jnp.bfloat16)
    query, grad = query_ref[...], grad_ref[...]
    score = dot_nt(keys_ref[...], query)
    dprob = dot_nt(keys_ref[...], grad)
    top = jnp.max(score, 0, keepdims=True)
    prob = jnp.exp2((score - top) * SCORE_FACTOR)
    total = jnp.sum(prob, 0, keepdims=True)
    inverse = 1.0 / total
    delta = jnp.sum(prob * dprob, 0, keepdims=True) * inverse
    prob_far = prob[near:] * inverse
    dscore = (prob_far * (dprob[near:] - delta)).astype(jnp.bfloat16)
    terms = dot_nn(
        jnp.concatenate([dscore, prob_far.astype(jnp.bfloat16)], 1),
        jnp.concatenate([query, grad], 0),
    ) * jnp.where(left_half((far, PAIR)), SCALE, 1.0)
    own_out[...] = terms[:count]
    other_out[...] = terms[count:]
    query_grad = dot_nn(far_t, dscore)
    lse = top * SCORE_FACTOR + jnp.log2(total)
    extra_out[:PAIR, :] = jnp.concatenate(split_two(query_grad), 0)
    blank = jnp.zeros((STAT_ROWS - 6, count), jnp.bfloat16)
    extra_out[PAIR:, :] = jnp.concatenate([*split_three(lse), *split_three(delta), blank], 0)


def near_blocks(
    places, offset, keys_ref, key_t_ref, queries_ref, grads_ref, extra_ref,
    prob_ref, dprob_ref, work_ref, top_ref, acc_ref, emit,
):
    near = keys_ref.shape[0]
    rows = prob_ref.shape[2]
    half = rows // 2
    count = extra_ref.shape[1]
    row_lane = lax.broadcasted_iota(jnp.int32, (1, rows), 1)
    picked = lax.rem(row_lane, DILATION_RATE) == offset

    def by_eight(value):
        return value.reshape(value.shape[0] // 8, 8, rows)

    def weights_of(index):
        return query_and_grad(queries_ref.at[places[index]], grads_ref.at[places[index]])

    def columns_of(ref):
        packed = ref[...].astype(jnp.float32).T
        return jnp.concatenate([packed[:HEAD_SIZE], packed[HEAD_SIZE:]], 1).astype(jnp.bfloat16)

    def transposed_of(index):
        zero = jnp.zeros((HEAD_SIZE, rows), jnp.bfloat16)
        query = columns_of(queries_ref.at[places[index]])
        grad = columns_of(grads_ref.at[places[index]])
        return jnp.concatenate([query, zero], 0), jnp.concatenate([zero, grad], 0)

    def first_pass(index, weights, start, state):
        top, total, delta = state
        slot = index % 2
        query, grad = weights
        keys = keys_ref[start : start + PIECE, :]
        scores, dprobs = dot_nn(keys, query), dot_nn(keys, grad)
        for inner in range(0, PIECE, STRIP):
            strip = slice(start + inner, start + inner + STRIP)
            score, dprob = scores[inner : inner + STRIP], dprobs[inner : inner + STRIP]
            part = fold(score, jnp.maximum) * SCORE_FACTOR
            raised = part if top is None else jnp.maximum(top, part)
            prob = jnp.exp2(by_eight(score) * SCORE_FACTOR - raised[None])
            part_total = jnp.sum(prob, 0)
            part_delta = jnp.sum(prob * by_eight(dprob), 0)
            if top is None:
                total, delta = part_total, part_delta
            else:
                shrink = jnp.exp2(top - raised)
                total, delta = total * shrink + part_total, delta * shrink + part_delta
            top = raised
            prob_ref[slot, strip, :] = prob.reshape(STRIP, rows)
            dprob_ref[slot, strip, :] = dprob
            top_ref[slot, strip.start // STRIP] = raised
        return top, total, delta

    def last_pass(index, lse, delta, both, start, query_grad):
        slot = index % 2
        piece = slice(start, start + PIECE)
        for inner in range(0, PIECE, STRIP):
            strip = slice(start + inner, start + inner + STRIP)
            factor = jnp.exp2(top_ref[slot, strip.start // STRIP] - lse)
            prob = by_eight(prob_ref[slot, strip, :]) * factor[None]
            dscore = prob * (by_eight(dprob_ref[slot, strip, :]) - delta)
            work_ref[slot, strip, :rows] = dscore.reshape(STRIP, rows).astype(jnp.bfloat16)
            work_ref[slot, strip, rows:] = prob.reshape(STRIP, rows).astype(jnp.bfloat16)
        acc_ref[piece, :] += dot_nn(work_ref[slot, piece, :], both)
        return query_grad + dot_nn(key_t_ref[:, piece], work_ref[slot, piece, :rows])

    starts = range(0, near, PIECE)
    weights = transposed_of(0)
    state = (None, None, None)
    for start in starts:
        state = first_pass(0, weights, start, state)
    for index, place in enumerate(places):
        last = index + 1 == len(places)
        first = place * (rows // DILATION_RATE)
        extra = dot_nn(extra_ref[...], spread_matrix(offset, first, count, rows, 0))
        stats = [extra[PAIR + row : PAIR + row + 1] for row in range(6)]
        top, total, delta = state
        highest = jnp.max(top, 0, keepdims=True)
        shrink = jnp.exp2(top - highest)
        total = jnp.sum(total * shrink, 0, keepdims=True)
        delta = jnp.sum(delta * shrink, 0, keepdims=True) / total
        lse = jnp.where(picked, stats[0] + stats[1] + stats[2], highest + jnp.log2(total))
        delta = jnp.where(picked, stats[3] + stats[4] + stats[5], delta)
        both = jnp.concatenate(weights_of(index), 0)
        query_grad = extra[:HEAD_SIZE] + extra[HEAD_SIZE:PAIR]
        weights = None if last else transposed_of(index + 1)
        state = (None, None, None)
        for start in starts:
            if not last:
                state = first_pass(index + 1, weights, start, state)
            query_grad = last_pass(index, lse, delta, both, start, query_grad)
        query_grad = (query_grad * SCALE).T.astype(jnp.bfloat16)
        emit(place, jnp.concatenate([query_grad[:half], query_grad[half:]], 1))


def first_kernel(
    head_count, steps, place_ref, offset_ref, keys_ref, key_t_ref, queries_ref, grads_ref,
    extra_ref, acc_ref, query_out, *scratch,
):
    offset = own_offset(head_count, place_ref, offset_ref)
    acc_ref[...] = jnp.zeros_like(acc_ref)

    def emit(place, query_grad):
        query_out[place] = query_grad

    near_blocks(
        range(steps), offset, keys_ref, key_t_ref, queries_ref, grads_ref, extra_ref,
        *scratch, acc_ref, emit,
    )


def second_kernel(
    head_count, steps, others, place_ref, offset_ref, keys_ref, key_t_ref, queries_ref, grads_ref,
    extra_ref, start_ref, query_ref, own_ref, *refs,
):
    back_refs, refs = refs[:others], refs[others:]
    rows = query_ref.shape[1] * 2
    group = keys_ref.shape[0] // rows
    out_refs, refs = refs[:group], refs[group:]
    acc_ref, stage_ref, *scratch = refs
    count = extra_ref.shape[1]
    picked = count // group
    offset = own_offset(head_count, place_ref, offset_ref)
    acc_ref[...] = start_ref[...]

    def emit(place, query_grad):
        stage_ref[place, rows:, :] = query_grad

    near_blocks(
        range(group - steps, group), offset, keys_ref, key_t_ref, queries_ref, grads_ref, extra_ref,
        *scratch, acc_ref, emit,
    )
    terms = own_ref[...]
    for back_ref in back_refs:
        terms = terms + back_ref[...]
    terms = jnp.concatenate(split_two(terms), 0)
    factor = jnp.where(left_half((rows, PAIR)), SCALE, 1.0)
    for place in range(group):
        spread = spread_matrix(offset, place * picked, count, rows, 1)
        placed = dot_nn(jnp.concatenate([spread, spread], 1), terms)
        summed = acc_ref[place * rows : (place + 1) * rows, :] * factor + placed
        stage_ref[place, :rows, :] = summed.astype(jnp.bfloat16)
        if place < group - steps:
            stage_ref[place, rows:, :] = query_ref[place]
    send_out(place_ref[0], stage_ref, out_refs)


def unpack_kernel(head_count, group, place_ref, *refs):
    near_refs, refs = refs[:group], refs[group:]
    query_out, key_out, value_out, stage_ref = refs
    rows = query_out.shape[0]
    half = rows // 2
    for bits, near_ref in enumerate(near_refs):
        stage_ref[lax.bitwise_xor(place_ref[0], bits)] = near_ref[...]
    for head in range(head_count):
        columns = slice(head * HEAD_SIZE, (head + 1) * HEAD_SIZE)
        key_out[:, columns] = stage_ref[head, :rows, :HEAD_SIZE]
        value_out[:, columns] = stage_ref[head, :rows, HEAD_SIZE:]
        query_out[:half, columns] = stage_ref[head, rows:, :HEAD_SIZE]
        query_out[half:, columns] = stage_ref[head, rows:, HEAD_SIZE:]


def call(kernel, name, out_shape, scalars, operands, scratch=(), flops=0, space=VMEM, limit=40):
    return pl.pallas_call(
        kernel,
        out_shape=tuple(jax.ShapeDtypeStruct(*shape) for shape in out_shape),
        in_specs=[SMEM] * len(scalars) + [space] * len(operands),
        out_specs=tuple(VMEM for _ in out_shape),
        scratch_shapes=[
            pltpu.VMEM(*shape) if isinstance(shape, tuple) else shape for shape in scratch
        ],
        compiler_params=pltpu.CompilerParams(vmem_limit_bytes=limit * 1024 * 1024),
        cost_estimate=pl.CostEstimate(flops=flops, bytes_accessed=2**21, transcendentals=0),
        name=name,
    )(*scalars, *operands)


def body(upstream, out_weight, query_rows, key_rows, value_rows, head_offsets):
    rows, width = query_rows.shape
    head_count = width // HEAD_SIZE
    devices = lax.axis_size("context")
    shards = lax.axis_size("heads")
    group = FIRST_SEGMENT // rows
    others = devices // group - 1
    half = rows // 2
    picked = rows // DILATION_RATE
    count = group * picked
    near = group * rows
    place = jnp.stack(
        [lax.rem(lax.axis_index("context"), group), lax.axis_index("heads")]
    ).astype(jnp.int32)
    scalars = [place, head_offsets]

    def swap(values):
        pairs = [[(source, source ^ bits) for source in range(devices)] for bits in range(group)]
        return [values[0]] + [
            lax.ppermute(values[bits], "context", pairs[bits]) for bits in range(1, group)
        ]

    def exchange(value):
        groups = [list(range(first, first + group)) for first in range(0, devices, group)]
        return lax.all_to_all(value, "context", 0, 0, axis_index_groups=groups)

    def segment_shift(value, shift):
        pairs = [(source, (source + shift * group) % devices) for source in range(devices)]
        return lax.ppermute(value, "context", pairs)

    upstreams = [upstream]
    for step in range(1, shards):
        pairs = [(source, (source + step) % shards) for source in range(shards)]
        upstreams.append(lax.ppermute(upstream, "heads", pairs))

    bf16, f32 = jnp.bfloat16, jnp.float32
    (sent,) = call(
        functools.partial(pack_kernel, head_count), "pack_rows",
        [((group, rows + half, PAIR), bf16)],
        [], [query_rows, key_rows, value_rows],
        [((rows, width), bf16)] * 3 + [pltpu.SemaphoreType.DMA((3,))],
        flops=2**31, space=ANY, limit=60,
    )
    sent = exchange(sent)
    grads_send = call(
        functools.partial(project_kernel, head_count, group, shards), "project_pack",
        [((half, PAIR), bf16)] * group,
        [place], [out_weight, *upstreams],
        [((rows, width), bf16), ((group, half, PAIR), bf16)],
        flops=BUSY,
    )
    grads = swap(grads_send)
    keys, key_t, queries, picks = call(
        functools.partial(gather_kernel, head_count), "gather_keys",
        [
            ((near, PAIR), bf16), ((HEAD_SIZE, near), bf16), ((group, half, PAIR), bf16),
            ((count, PAIR), bf16),
        ],
        scalars, [sent, grads_send[0]],
    )
    other_picks = [segment_shift(picks, shift) for shift in range(1, others + 1)]
    extra, own_terms, other_terms, grads = call(
        functools.partial(far_kernel, head_count, group, others), "picked_rows",
        [
            ((PAIR + STAT_ROWS, count), bf16), ((count, PAIR), f32),
            ((others * count, PAIR), f32), ((group, half, PAIR), bf16),
        ],
        scalars, [keys, queries, picks, *other_picks, *grads],
        [((near + count * (1 + others), PAIR), bf16)] + [((count, PAIR), bf16)] * 2,
        flops=8 * near * count * PAIR,
    )
    back = [
        segment_shift(other_terms[(shift - 1) * count : shift * count], -shift)
        for shift in range(1, others + 1)
    ]
    steps = group // 2
    scratch = [
        ((2, near, rows), f32), ((2, near, rows), f32), ((2, near, 2 * rows), bf16),
        ((2, near // STRIP, 8, rows), f32),
    ]
    half_flops = 10 * near * near // 2 * PAIR
    acc, query_half = call(
        functools.partial(first_kernel, head_count, steps), "first_rows",
        [((near, PAIR), f32), ((steps, half, PAIR), bf16)],
        scalars, [keys, key_t, queries, grads, extra], scratch, half_flops,
    )
    near_send = call(
        functools.partial(second_kernel, head_count, group - steps, others), "second_rows",
        [((rows + half, PAIR), bf16)] * group,
        scalars, [keys, key_t, queries, grads, extra, acc, query_half, own_terms, *back],
        [((near, PAIR), f32), ((group, rows + half, PAIR), bf16)] + scratch, half_flops,
    )
    return tuple(
        call(
            functools.partial(unpack_kernel, head_count, group), "unpack",
            [((rows, width), bf16)] * 3,
            [place], swap(near_send),
            [((group, rows + half, PAIR), bf16)],
        )
    )


def solution(mesh):
    return jax.shard_map(
        body,
        mesh=mesh,
        in_specs=(
            P(("context", "heads"), None),
            P("heads", None),
            P("context", "heads"),
            P("context", "heads"),
            P("context", "heads"),
            P(),
        ),
        out_specs=(P("context", "heads"), P("context", "heads"), P("context", "heads")),
        check_vma=False,
    )
```

```python
import functools
import math

import jax
import jax.numpy as jnp
from jax import lax
from jax.experimental import pallas as pl
from jax.experimental.pallas import tpu as pltpu
from jax.sharding import PartitionSpec as P

HEAD_SIZE = 64
PAIR = 2 * HEAD_SIZE
DILATION_RATE = 16
FIRST_SEGMENT = 2048
SCALE = 1.0 / math.sqrt(HEAD_SIZE)
LOG2E = math.log2(math.e)
SCORE_FACTOR = SCALE * LOG2E
STRIP = 64
PIECE = 128
BUSY = 2**35
STAT_ROWS = 16

SMEM = pl.BlockSpec(memory_space=pltpu.SMEM)
VMEM = pl.BlockSpec(memory_space=pltpu.VMEM)
ANY = pl.BlockSpec(memory_space=pl.ANY)


def dot_nt(left, right):
    return lax.dot_general(
        left, right, (((1,), (1,)), ((), ())), preferred_element_type=jnp.float32
    )


def dot_nn(left, right):
    return jnp.dot(left, right, preferred_element_type=jnp.float32)


def head_columns(ref, head):
    return ref[:, head * HEAD_SIZE : (head + 1) * HEAD_SIZE]


def pick_matrix(offset, picked, rows):
    source = lax.broadcasted_iota(jnp.int32, (picked, rows), 1)
    index = lax.broadcasted_iota(jnp.int32, (picked, rows), 0)
    return (source == index * DILATION_RATE + offset).astype(jnp.bfloat16)


def spread_matrix(offset, first, picked, rows, axis):
    shape = (picked, rows) if axis == 0 else (rows, picked)
    index = lax.broadcasted_iota(jnp.int32, shape, axis)
    source = lax.broadcasted_iota(jnp.int32, shape, 1 - axis)
    return (source == (index - first) * DILATION_RATE + offset).astype(jnp.bfloat16)


def split_two(value):
    high = value.astype(jnp.bfloat16)
    low = (value - high.astype(jnp.float32)).astype(jnp.bfloat16)
    return high, low


def split_three(value):
    high = value.astype(jnp.bfloat16)
    rest = value - high.astype(jnp.float32)
    middle = rest.astype(jnp.bfloat16)
    low = (rest - middle.astype(jnp.float32)).astype(jnp.bfloat16)
    return high, middle, low


def fold(value, combine):
    parts = [value[start : start + 8] for start in range(0, value.shape[0], 8)]
    while len(parts) > 1:
        merged = [combine(parts[i], parts[i + 1]) for i in range(0, len(parts) - 1, 2)]
        parts = merged + parts[len(merged) * 2 :]
    return parts[0]


def left_half(shape):
    return lax.broadcasted_iota(jnp.int32, shape, 1) < HEAD_SIZE


def side_by_side(block):
    half = block.shape[0] // 2
    return jnp.concatenate([block[:half], block[half:]], 1)


def send_out(place, stage_ref, out_refs):
    for bits, out_ref in enumerate(out_refs):
        out_ref[...] = stage_ref[lax.bitwise_xor(place, bits)]


def pack_kernel(head_count, query_hbm, key_hbm, value_hbm, *refs):
    out_ref, query_ref, key_ref, value_ref, sems = refs
    rows = query_ref.shape[0]
    copies = [
        pltpu.make_async_copy(source, target, sems.at[index])
        for index, (source, target) in enumerate(
            [(key_hbm, key_ref), (value_hbm, value_ref), (query_hbm, query_ref)]
        )
    ]
    for copy in copies:
        copy.start()
    for copy in copies:
        copy.wait()
    for head in range(head_count):
        pair = jnp.concatenate([head_columns(key_ref, head), head_columns(value_ref, head)], 1)
        query = side_by_side(head_columns(query_ref, head))
        for place in range(head, out_ref.shape[0], head_count):
            out_ref[place, :rows, :] = pair
            out_ref[place, rows:, :] = query


def project_kernel(head_count, group, shards, place_ref, weight_ref, *refs):
    upstream_refs, refs = refs[:shards], refs[shards:]
    out_refs, (grad_ref, stage_ref) = refs[:group], refs[group:]
    shard_rows = upstream_refs[0].shape[0]
    for step, upstream_ref in enumerate(upstream_refs):
        owner = lax.rem(place_ref[1] + (shards - step), shards)
        start = pl.multiple_of(owner * shard_rows, shard_rows)
        grad_ref[pl.ds(start, shard_rows), :] = dot_nt(
            upstream_ref[...], weight_ref[...]
        ).astype(jnp.bfloat16)
    for head in range(head_count):
        grad = side_by_side(head_columns(grad_ref, head))
        for place in range(head, group, head_count):
            stage_ref[place] = grad
    send_out(place_ref[0], stage_ref, out_refs)


def own_offset(head_count, place_ref, offset_ref):
    return offset_ref[place_ref[1] * head_count + lax.rem(place_ref[0], head_count)]


def gather_kernel(
    head_count, place_ref, offset_ref, sent_ref, after_ref, keys_out, key_t_out, queries_out,
    picks_out,
):
    group = sent_ref.shape[0]
    rows = keys_out.shape[0] // group
    picked = rows // DILATION_RATE
    pick = pick_matrix(own_offset(head_count, place_ref, offset_ref), picked, rows)
    for place in range(group):
        pair = sent_ref[place, :rows, :]
        keys_out[place * rows : (place + 1) * rows, :] = pair
        picks_out[place * picked : (place + 1) * picked, :] = dot_nn(pick, pair).astype(
            jnp.bfloat16
        )
        queries_out[place] = sent_ref[place, rows:, :]
    key_t_out[...] = keys_out[...].astype(jnp.float32).T[:HEAD_SIZE].astype(jnp.bfloat16)


def query_and_grad(query_ref, grad_ref):
    query, grad = query_ref[...], grad_ref[...]
    zero = jnp.zeros((query.shape[0], HEAD_SIZE), query.dtype)
    return (
        jnp.concatenate(
            [
                jnp.concatenate([query[:, :HEAD_SIZE], zero], 1),
                jnp.concatenate([query[:, HEAD_SIZE:], zero], 1),
            ], 0,
        ),
        jnp.concatenate(
            [
                jnp.concatenate([zero, grad[:, :HEAD_SIZE]], 1),
                jnp.concatenate([zero, grad[:, HEAD_SIZE:]], 1),
            ], 0,
        ),
    )


def far_kernel(
    head_count, group, others, place_ref, offset_ref, near_ref, queries_ref, picks_ref, *refs
):
    other_refs, refs = refs[:others], refs[others:]
    grad_refs, refs = refs[:group], refs[group:]
    extra_out, own_out, other_out, grads_out, keys_ref, query_ref, grad_ref = refs
    near = near_ref.shape[0]
    rows = near // group
    picked = rows // DILATION_RATE
    count = group * picked
    far = count * (1 + others)
    pick = pick_matrix(own_offset(head_count, place_ref, offset_ref), picked, rows)
    keys_ref[:near, :] = near_ref[...]
    for index, ref in enumerate([picks_ref, *other_refs]):
        keys_ref[near + index * count : near + (index + 1) * count, :] = ref[...]
    for bits, ref in enumerate(grad_refs):
        grads_out[lax.bitwise_xor(place_ref[0], bits)] = ref[...]
    for step in range(group):
        query, grad = query_and_grad(queries_ref.at[step], grads_out.at[step])
        span = slice(step * picked, (step + 1) * picked)
        query_ref[span, :] = dot_nn(pick, query).astype(jnp.bfloat16)
        grad_ref[span, :] = dot_nn(pick, grad).astype(jnp.bfloat16)
    far_t = keys_ref[near:, :].astype(jnp.float32).T[:HEAD_SIZE].astype(jnp.bfloat16)
    query, grad = query_ref[...], grad_ref[...]
    score = dot_nt(keys_ref[...], query)
    dprob = dot_nt(keys_ref[...], grad)
    top = jnp.max(score, 0, keepdims=True)
    prob = jnp.exp2((score - top) * SCORE_FACTOR)
    total = jnp.sum(prob, 0, keepdims=True)
    inverse = 1.0 / total
    delta = jnp.sum(prob * dprob, 0, keepdims=True) * inverse
    prob_far = prob[near:] * inverse
    dscore = (prob_far * (dprob[near:] - delta)).astype(jnp.bfloat16)
    terms = dot_nn(
        jnp.concatenate([dscore, prob_far.astype(jnp.bfloat16)], 1),
        jnp.concatenate([query, grad], 0),
    ) * jnp.where(left_half((far, PAIR)), SCALE, 1.0)
    own_out[...] = terms[:count]
    other_out[...] = terms[count:]
    query_grad = dot_nn(far_t, dscore)
    lse = top * SCORE_FACTOR + jnp.log2(total)
    extra_out[:PAIR, :] = jnp.concatenate(split_two(query_grad), 0)
    blank = jnp.zeros((STAT_ROWS - 6, count), jnp.bfloat16)
    extra_out[PAIR:, :] = jnp.concatenate([*split_three(lse), *split_three(delta), blank], 0)


def near_blocks(
    places, offset, keys_ref, key_t_ref, queries_ref, grads_ref, extra_ref,
    prob_ref, dprob_ref, work_ref, top_ref, acc_ref, emit,
):
    near = keys_ref.shape[0]
    rows = prob_ref.shape[2]
    half = rows // 2
    count = extra_ref.shape[1]
    row_lane = lax.broadcasted_iota(jnp.int32, (1, rows), 1)
    picked = lax.rem(row_lane, DILATION_RATE) == offset

    def by_eight(value):
        return value.reshape(value.shape[0] // 8, 8, rows)

    def weights_of(index):
        return query_and_grad(queries_ref.at[places[index]], grads_ref.at[places[index]])

    def columns_of(ref):
        packed = ref[...].astype(jnp.float32).T
        return jnp.concatenate([packed[:HEAD_SIZE], packed[HEAD_SIZE:]], 1).astype(jnp.bfloat16)

    def transposed_of(index):
        zero = jnp.zeros((HEAD_SIZE, rows), jnp.bfloat16)
        query = columns_of(queries_ref.at[places[index]])
        grad = columns_of(grads_ref.at[places[index]])
        return jnp.concatenate([query, zero], 0), jnp.concatenate([zero, grad], 0)

    def first_pass(index, weights, start, state):
        top, total, delta = state
        slot = index % 2
        query, grad = weights
        keys = keys_ref[start : start + PIECE, :]
        scores, dprobs = dot_nn(keys, query), dot_nn(keys, grad)
        for inner in range(0, PIECE, STRIP):
            strip = slice(start + inner, start + inner + STRIP)
            score, dprob = scores[inner : inner + STRIP], dprobs[inner : inner + STRIP]
            part = fold(score, jnp.maximum) * SCORE_FACTOR
            raised = part if top is None else jnp.maximum(top, part)
            prob = jnp.exp2(by_eight(score) * SCORE_FACTOR - raised[None])
            part_total = jnp.sum(prob, 0)
            part_delta = jnp.sum(prob * by_eight(dprob), 0)
            if top is None:
                total, delta = part_total, part_delta
            else:
                shrink = jnp.exp2(top - raised)
                total, delta = total * shrink + part_total, delta * shrink + part_delta
            top = raised
            prob_ref[slot, strip, :] = prob.reshape(STRIP, rows)
            dprob_ref[slot, strip, :] = dprob
            top_ref[slot, strip.start // STRIP] = raised
        return top, total, delta

    def last_pass(index, lse, delta, both, start, query_grad):
        slot = index % 2
        piece = slice(start, start + PIECE)
        for inner in range(0, PIECE, STRIP):
            strip = slice(start + inner, start + inner + STRIP)
            factor = jnp.exp2(top_ref[slot, strip.start // STRIP] - lse)
            prob = by_eight(prob_ref[slot, strip, :]) * factor[None]
            dscore = prob * (by_eight(dprob_ref[slot, strip, :]) - delta)
            work_ref[slot, strip, :rows] = dscore.reshape(STRIP, rows).astype(jnp.bfloat16)
            work_ref[slot, strip, rows:] = prob.reshape(STRIP, rows).astype(jnp.bfloat16)
        acc_ref[piece, :] += dot_nn(work_ref[slot, piece, :], both)
        return query_grad + dot_nn(key_t_ref[:, piece], work_ref[slot, piece, :rows])

    starts = range(0, near, PIECE)
    weights = transposed_of(0)
    state = (None, None, None)
    for start in starts:
        state = first_pass(0, weights, start, state)
    for index, place in enumerate(places):
        last = index + 1 == len(places)
        first = place * (rows // DILATION_RATE)
        extra = dot_nn(extra_ref[...], spread_matrix(offset, first, count, rows, 0))
        stats = [extra[PAIR + row : PAIR + row + 1] for row in range(6)]
        top, total, delta = state
        highest = jnp.max(top, 0, keepdims=True)
        shrink = jnp.exp2(top - highest)
        total = jnp.sum(total * shrink, 0, keepdims=True)
        delta = jnp.sum(delta * shrink, 0, keepdims=True) / total
        lse = jnp.where(picked, stats[0] + stats[1] + stats[2], highest + jnp.log2(total))
        delta = jnp.where(picked, stats[3] + stats[4] + stats[5], delta)
        both = jnp.concatenate(weights_of(index), 0)
        query_grad = extra[:HEAD_SIZE] + extra[HEAD_SIZE:PAIR]
        weights = None if last else transposed_of(index + 1)
        state = (None, None, None)
        for start in starts:
            if not last:
                state = first_pass(index + 1, weights, start, state)
            query_grad = last_pass(index, lse, delta, both, start, query_grad)
        query_grad = (query_grad * SCALE).T.astype(jnp.bfloat16)
        emit(place, jnp.concatenate([query_grad[:half], query_grad[half:]], 1))


def first_kernel(
    head_count, steps, place_ref, offset_ref, keys_ref, key_t_ref, queries_ref, grads_ref,
    extra_ref, acc_ref, query_out, *scratch,
):
    offset = own_offset(head_count, place_ref, offset_ref)
    acc_ref[...] = jnp.zeros_like(acc_ref)

    def emit(place, query_grad):
        query_out[place] = query_grad

    near_blocks(
        range(steps), offset, keys_ref, key_t_ref, queries_ref, grads_ref, extra_ref,
        *scratch, acc_ref, emit,
    )


def second_kernel(
    head_count, steps, others, place_ref, offset_ref, keys_ref, key_t_ref, queries_ref, grads_ref,
    extra_ref, start_ref, query_ref, own_ref, *refs,
):
    back_refs, refs = refs[:others], refs[others:]
    rows = query_ref.shape[1] * 2
    group = keys_ref.shape[0] // rows
    out_refs, refs = refs[:group], refs[group:]
    acc_ref, stage_ref, *scratch = refs
    count = extra_ref.shape[1]
    picked = count // group
    offset = own_offset(head_count, place_ref, offset_ref)
    acc_ref[...] = start_ref[...]

    def emit(place, query_grad):
        stage_ref[place, rows:, :] = query_grad

    near_blocks(
        range(group - steps, group), offset, keys_ref, key_t_ref, queries_ref, grads_ref, extra_ref,
        *scratch, acc_ref, emit,
    )
    terms = own_ref[...]
    for back_ref in back_refs:
        terms = terms + back_ref[...]
    terms = jnp.concatenate(split_two(terms), 0)
    factor = jnp.where(left_half((rows, PAIR)), SCALE, 1.0)
    for place in range(group):
        spread = spread_matrix(offset, place * picked, count, rows, 1)
        placed = dot_nn(jnp.concatenate([spread, spread], 1), terms)
        summed = acc_ref[place * rows : (place + 1) * rows, :] * factor + placed
        stage_ref[place, :rows, :] = summed.astype(jnp.bfloat16)
        if place < group - steps:
            stage_ref[place, rows:, :] = query_ref[place]
    send_out(place_ref[0], stage_ref, out_refs)


def unpack_kernel(head_count, group, place_ref, *refs):
    near_refs, refs = refs[:group], refs[group:]
    query_out, key_out, value_out, stage_ref = refs
    rows = query_out.shape[0]
    half = rows // 2
    for bits, near_ref in enumerate(near_refs):
        stage_ref[lax.bitwise_xor(place_ref[0], bits)] = near_ref[...]
    for head in range(head_count):
        columns = slice(head * HEAD_SIZE, (head + 1) * HEAD_SIZE)
        key_out[:, columns] = stage_ref[head, :rows, :HEAD_SIZE]
        value_out[:, columns] = stage_ref[head, :rows, HEAD_SIZE:]
        query_out[:half, columns] = stage_ref[head, rows:, :HEAD_SIZE]
        query_out[half:, columns] = stage_ref[head, rows:, HEAD_SIZE:]


def call(kernel, name, out_shape, scalars, operands, scratch=(), flops=0, space=VMEM, limit=40):
    return pl.pallas_call(
        kernel,
        out_shape=tuple(jax.ShapeDtypeStruct(*shape) for shape in out_shape),
        in_specs=[SMEM] * len(scalars) + [space] * len(operands),
        out_specs=tuple(VMEM for _ in out_shape),
        scratch_shapes=[
            pltpu.VMEM(*shape) if isinstance(shape, tuple) else shape for shape in scratch
        ],
        compiler_params=pltpu.CompilerParams(vmem_limit_bytes=limit * 1024 * 1024),
        cost_estimate=pl.CostEstimate(flops=flops, bytes_accessed=2**21, transcendentals=0),
        name=name,
    )(*scalars, *operands)


def body(upstream, out_weight, query_rows, key_rows, value_rows, head_offsets):
    rows, width = query_rows.shape
    head_count = width // HEAD_SIZE
    devices = lax.axis_size("context")
    shards = lax.axis_size("heads")
    group = FIRST_SEGMENT // rows
    others = devices // group - 1
    half = rows // 2
    picked = rows // DILATION_RATE
    count = group * picked
    near = group * rows
    place = jnp.stack(
        [lax.rem(lax.axis_index("context"), group), lax.axis_index("heads")]
    ).astype(jnp.int32)
    scalars = [place, head_offsets]

    def swap(values):
        pairs = [[(source, source ^ bits) for source in range(devices)] for bits in range(group)]
        return [values[0]] + [
            lax.ppermute(values[bits], "context", pairs[bits]) for bits in range(1, group)
        ]

    def exchange(value):
        groups = [list(range(first, first + group)) for first in range(0, devices, group)]
        return lax.all_to_all(value, "context", 0, 0, axis_index_groups=groups)

    def segment_shift(value, shift):
        pairs = [(source, (source + shift * group) % devices) for source in range(devices)]
        return lax.ppermute(value, "context", pairs)

    upstreams = [upstream]
    for step in range(1, shards):
        pairs = [(source, (source + step) % shards) for source in range(shards)]
        upstreams.append(lax.ppermute(upstream, "heads", pairs))

    bf16, f32 = jnp.bfloat16, jnp.float32
    (sent,) = call(
        functools.partial(pack_kernel, head_count), "pack_rows",
        [((group, rows + half, PAIR), bf16)],
        [], [query_rows, key_rows, value_rows],
        [((rows, width), bf16)] * 3 + [pltpu.SemaphoreType.DMA((3,))],
        flops=2**31, space=ANY, limit=60,
    )
    sent = exchange(sent)
    grads_send = call(
        functools.partial(project_kernel, head_count, group, shards), "project_pack",
        [((half, PAIR), bf16)] * group,
        [place], [out_weight, *upstreams],
        [((rows, width), bf16), ((group, half, PAIR), bf16)],
        flops=BUSY,
    )
    grads = swap(grads_send)
    keys, key_t, queries, picks = call(
        functools.partial(gather_kernel, head_count), "gather_keys",
        [
            ((near, PAIR), bf16), ((HEAD_SIZE, near), bf16), ((group, half, PAIR), bf16),
            ((count, PAIR), bf16),
        ],
        scalars, [sent, grads_send[0]],
    )
    other_picks = [segment_shift(picks, shift) for shift in range(1, others + 1)]
    extra, own_terms, other_terms, grads = call(
        functools.partial(far_kernel, head_count, group, others), "picked_rows",
        [
            ((PAIR + STAT_ROWS, count), bf16), ((count, PAIR), f32),
            ((others * count, PAIR), f32), ((group, half, PAIR), bf16),
        ],
        scalars, [keys, queries, picks, *other_picks, *grads],
        [((near + count * (1 + others), PAIR), bf16)] + [((count, PAIR), bf16)] * 2,
        flops=8 * near * count * PAIR,
    )
    back = [
        segment_shift(other_terms[(shift - 1) * count : shift * count], -shift)
        for shift in range(1, others + 1)
    ]
    steps = group // 2
    scratch = [
        ((2, near, rows), f32), ((2, near, rows), f32), ((2, near, 2 * rows), bf16),
        ((2, near // STRIP, 8, rows), f32),
    ]
    half_flops = 10 * near * near // 2 * PAIR
    acc, query_half = call(
        functools.partial(first_kernel, head_count, steps), "first_rows",
        [((near, PAIR), f32), ((steps, half, PAIR), bf16)],
        scalars, [keys, key_t, queries, grads, extra], scratch, half_flops,
    )
    near_send = call(
        functools.partial(second_kernel, head_count, group - steps, others), "second_rows",
        [((rows + half, PAIR), bf16)] * group,
        scalars, [keys, key_t, queries, grads, extra, acc, query_half, own_terms, *back],
        [((near, PAIR), f32), ((group, rows + half, PAIR), bf16)] + scratch, half_flops,
    )
    return tuple(
        call(
            functools.partial(unpack_kernel, head_count, group), "unpack",
            [((rows, width), bf16)] * 3,
            [place], swap(near_send),
            [((group, rows + half, PAIR), bf16)],
        )
    )


def solution(mesh):
    return jax.shard_map(
        body,
        mesh=mesh,
        in_specs=(
            P(("context", "heads"), None),
            P("heads", None),
            P("context", "heads"),
            P("context", "heads"),
            P("context", "heads"),
            P(),
        ),
        out_specs=(P("context", "heads"), P("context", "heads"), P("context", "heads")),
        check_vma=False,
    )
```

```python
import functools
import math

import jax
import jax.numpy as jnp
from jax import lax
from jax.experimental import pallas as pl
from jax.experimental.pallas import tpu as pltpu
from jax.sharding import PartitionSpec as P

HEAD_SIZE = 64
PAIR = 2 * HEAD_SIZE
DILATION_RATE = 16
FIRST_SEGMENT = 2048
SCALE = 1.0 / math.sqrt(HEAD_SIZE)
LOG2E = math.log2(math.e)
SCORE_FACTOR = SCALE * LOG2E
STRIP = 64
PIECE = 256
BUSY = 2**35
STAT_ROWS = 16

SMEM = pl.BlockSpec(memory_space=pltpu.SMEM)
VMEM = pl.BlockSpec(memory_space=pltpu.VMEM)
ANY = pl.BlockSpec(memory_space=pl.ANY)


def dot_nt(left, right):
    return lax.dot_general(
        left, right, (((1,), (1,)), ((), ())), preferred_element_type=jnp.float32
    )


def dot_nn(left, right):
    return jnp.dot(left, right, preferred_element_type=jnp.float32)


def head_columns(ref, head):
    return ref[:, head * HEAD_SIZE : (head + 1) * HEAD_SIZE]


def pick_matrix(offset, picked, rows):
    source = lax.broadcasted_iota(jnp.int32, (picked, rows), 1)
    index = lax.broadcasted_iota(jnp.int32, (picked, rows), 0)
    return (source == index * DILATION_RATE + offset).astype(jnp.bfloat16)


def spread_matrix(offset, first, picked, rows, axis):
    shape = (picked, rows) if axis == 0 else (rows, picked)
    index = lax.broadcasted_iota(jnp.int32, shape, axis)
    source = lax.broadcasted_iota(jnp.int32, shape, 1 - axis)
    return (source == (index - first) * DILATION_RATE + offset).astype(jnp.bfloat16)


def split_two(value):
    high = value.astype(jnp.bfloat16)
    low = (value - high.astype(jnp.float32)).astype(jnp.bfloat16)
    return high, low


def split_three(value):
    high = value.astype(jnp.bfloat16)
    rest = value - high.astype(jnp.float32)
    middle = rest.astype(jnp.bfloat16)
    low = (rest - middle.astype(jnp.float32)).astype(jnp.bfloat16)
    return high, middle, low


def fold(value, combine):
    parts = [value[start : start + 8] for start in range(0, value.shape[0], 8)]
    while len(parts) > 1:
        merged = [combine(parts[i], parts[i + 1]) for i in range(0, len(parts) - 1, 2)]
        parts = merged + parts[len(merged) * 2 :]
    return parts[0]


def left_half(shape):
    return lax.broadcasted_iota(jnp.int32, shape, 1) < HEAD_SIZE


def side_by_side(block):
    half = block.shape[0] // 2
    return jnp.concatenate([block[:half], block[half:]], 1)


def send_out(place, stage_ref, out_refs):
    for bits, out_ref in enumerate(out_refs):
        out_ref[...] = stage_ref[lax.bitwise_xor(place, bits)]


def pack_kernel(head_count, query_hbm, key_hbm, value_hbm, *refs):
    out_ref, query_ref, key_ref, value_ref, sems = refs
    rows = query_ref.shape[0]
    copies = [
        pltpu.make_async_copy(source, target, sems.at[index])
        for index, (source, target) in enumerate(
            [(key_hbm, key_ref), (value_hbm, value_ref), (query_hbm, query_ref)]
        )
    ]
    for copy in copies:
        copy.start()
    for copy in copies:
        copy.wait()
    for head in range(head_count):
        pair = jnp.concatenate([head_columns(key_ref, head), head_columns(value_ref, head)], 1)
        query = side_by_side(head_columns(query_ref, head))
        for place in range(head, out_ref.shape[0], head_count):
            out_ref[place, :rows, :] = pair
            out_ref[place, rows:, :] = query


def project_kernel(head_count, group, shards, place_ref, weight_ref, *refs):
    upstream_refs, refs = refs[:shards], refs[shards:]
    out_refs, (grad_ref, stage_ref) = refs[:group], refs[group:]
    shard_rows = upstream_refs[0].shape[0]
    for step, upstream_ref in enumerate(upstream_refs):
        owner = lax.rem(place_ref[1] + (shards - step), shards)
        start = pl.multiple_of(owner * shard_rows, shard_rows)
        grad_ref[pl.ds(start, shard_rows), :] = dot_nt(
            upstream_ref[...], weight_ref[...]
        ).astype(jnp.bfloat16)
    for head in range(head_count):
        grad = side_by_side(head_columns(grad_ref, head))
        for place in range(head, group, head_count):
            stage_ref[place] = grad
    send_out(place_ref[0], stage_ref, out_refs)


def own_offset(head_count, place_ref, offset_ref):
    return offset_ref[place_ref[1] * head_count + lax.rem(place_ref[0], head_count)]


def gather_kernel(
    head_count, place_ref, offset_ref, sent_ref, after_ref, keys_out, key_t_out, queries_out,
    picks_out,
):
    group = sent_ref.shape[0]
    rows = keys_out.shape[0] // group
    picked = rows // DILATION_RATE
    pick = pick_matrix(own_offset(head_count, place_ref, offset_ref), picked, rows)
    for place in range(group):
        pair = sent_ref[place, :rows, :]
        keys_out[place * rows : (place + 1) * rows, :] = pair
        picks_out[place * picked : (place + 1) * picked, :] = dot_nn(pick, pair).astype(
            jnp.bfloat16
        )
        queries_out[place] = sent_ref[place, rows:, :]
    key_t_out[:PAIR, :] = keys_out[...].astype(jnp.float32).T.astype(jnp.bfloat16)
    key_t_out[PAIR:, :] = jnp.ones((STAT_ROWS, keys_out.shape[0]), jnp.bfloat16)


def query_and_grad(query_ref, grad_ref):
    query, grad = query_ref[...], grad_ref[...]
    zero = jnp.zeros((query.shape[0], HEAD_SIZE), query.dtype)
    return (
        jnp.concatenate(
            [
                jnp.concatenate([query[:, :HEAD_SIZE], zero], 1),
                jnp.concatenate([query[:, HEAD_SIZE:], zero], 1),
            ], 0,
        ),
        jnp.concatenate(
            [
                jnp.concatenate([zero, grad[:, :HEAD_SIZE]], 1),
                jnp.concatenate([zero, grad[:, HEAD_SIZE:]], 1),
            ], 0,
        ),
    )


def far_kernel(
    head_count, group, others, place_ref, offset_ref, near_ref, queries_ref, picks_ref, *refs
):
    other_refs, refs = refs[:others], refs[others:]
    grad_refs, refs = refs[:group], refs[group:]
    extra_out, own_out, other_out, grads_out, keys_ref, query_ref, grad_ref = refs
    near = near_ref.shape[0]
    rows = near // group
    picked = rows // DILATION_RATE
    count = group * picked
    far = count * (1 + others)
    pick = pick_matrix(own_offset(head_count, place_ref, offset_ref), picked, rows)
    keys_ref[:near, :] = near_ref[...]
    for index, ref in enumerate([picks_ref, *other_refs]):
        keys_ref[near + index * count : near + (index + 1) * count, :] = ref[...]
    for bits, ref in enumerate(grad_refs):
        grads_out[lax.bitwise_xor(place_ref[0], bits)] = ref[...]
    for step in range(group):
        query, grad = query_and_grad(queries_ref.at[step], grads_out.at[step])
        span = slice(step * picked, (step + 1) * picked)
        query_ref[span, :] = dot_nn(pick, query).astype(jnp.bfloat16)
        grad_ref[span, :] = dot_nn(pick, grad).astype(jnp.bfloat16)
    far_t = keys_ref[near:, :].astype(jnp.float32).T[:HEAD_SIZE].astype(jnp.bfloat16)
    query, grad = query_ref[...], grad_ref[...]
    score = dot_nt(keys_ref[...], query)
    dprob = dot_nt(keys_ref[...], grad)
    top = jnp.max(score, 0, keepdims=True)
    prob = jnp.exp2((score - top) * SCORE_FACTOR)
    total = jnp.sum(prob, 0, keepdims=True)
    inverse = 1.0 / total
    delta = jnp.sum(prob * dprob, 0, keepdims=True) * inverse
    prob_far = prob[near:] * inverse
    dscore = (prob_far * (dprob[near:] - delta)).astype(jnp.bfloat16)
    terms = dot_nn(
        jnp.concatenate([dscore, prob_far.astype(jnp.bfloat16)], 1),
        jnp.concatenate([query, grad], 0),
    ) * jnp.where(left_half((far, PAIR)), SCALE, 1.0)
    own_out[...] = terms[:count]
    other_out[...] = terms[count:]
    query_grad = dot_nn(far_t, dscore)
    lse = top * SCORE_FACTOR + jnp.log2(total)
    extra_out[:PAIR, :] = jnp.concatenate(split_two(query_grad), 0)
    blank = jnp.zeros((STAT_ROWS - 6, count), jnp.bfloat16)
    extra_out[PAIR:, :] = jnp.concatenate([*split_three(lse), *split_three(delta), blank], 0)


def near_blocks(
    places, offset, keys_ref, key_t_ref, queries_ref, grads_ref, extra_ref,
    prob_ref, dprob_ref, work_ref, top_ref, acc_ref, emit,
):
    near = keys_ref.shape[0]
    rows = prob_ref.shape[2]
    half = rows // 2
    count = extra_ref.shape[1]
    row_lane = lax.broadcasted_iota(jnp.int32, (1, rows), 1)
    picked = lax.rem(row_lane, DILATION_RATE) == offset

    def weights_of(index):
        return query_and_grad(queries_ref.at[places[index]], grads_ref.at[places[index]])

    def columns_of(ref):
        packed = ref[...].astype(jnp.float32).T
        return jnp.concatenate([packed[:HEAD_SIZE], packed[HEAD_SIZE:]], 1).astype(jnp.bfloat16)

    def transposed_of(index):
        return columns_of(queries_ref.at[places[index]]), columns_of(grads_ref.at[places[index]])

    def first_pass(index, columns, start, state):
        slot = index % 2
        piece = slice(start, start + PIECE)
        query, grad = columns
        zero = jnp.zeros_like(query)
        keys = keys_ref[piece, :]
        score = dot_nn(keys, jnp.concatenate([query, zero], 0))
        dprob_ref[slot, piece, :] = dot_nn(keys, jnp.concatenate([zero, grad], 0))
        raised = jnp.max(fold(score, jnp.maximum), 0, keepdims=True) * SCORE_FACTOR
        if state is not None:
            raised = jnp.maximum(raised, state[0])
        for inner in range(0, PIECE, STRIP):
            prob = jnp.exp2(score[inner : inner + STRIP] * SCORE_FACTOR - raised)
            prob_ref[slot, start + inner : start + inner + STRIP, :] = prob.astype(jnp.bfloat16)
        sums = dot_nn(key_t_ref[HEAD_SIZE:, piece], prob_ref[slot, piece, :])
        if state is not None:
            sums = sums + state[1] * jnp.exp2(state[0] - raised)
        top_ref[slot, start // PIECE] = raised
        return raised, sums

    def last_pass(index, lse, delta, both, start, query_grad):
        slot = index % 2
        piece = slice(start, start + PIECE)
        factor = jnp.exp2(top_ref[slot, start // PIECE] - lse)
        factor = jnp.broadcast_to(factor, (16, rows)).astype(jnp.bfloat16)[None]
        for inner in range(0, PIECE, STRIP):
            strip = slice(start + inner, start + inner + STRIP)
            prob = prob_ref[slot, strip, :].reshape(STRIP // 16, 16, rows) * factor
            prob = prob.reshape(STRIP, rows)
            centred = (dprob_ref[slot, strip, :] - delta).astype(jnp.bfloat16)
            work_ref[slot, strip, :rows] = prob * centred
            work_ref[slot, strip, rows:] = prob
        acc_ref[piece, :] += dot_nn(work_ref[slot, piece, :], both)
        return query_grad + dot_nn(key_t_ref[:HEAD_SIZE, piece], work_ref[slot, piece, :rows])

    starts = range(0, near, PIECE)
    columns = transposed_of(0)
    state = None
    for start in starts:
        state = first_pass(0, columns, start, state)
    for index, place in enumerate(places):
        last = index + 1 == len(places)
        first = place * (rows // DILATION_RATE)
        extra = dot_nn(extra_ref[...], spread_matrix(offset, first, count, rows, 0))
        stats = [extra[PAIR + row : PAIR + row + 1] for row in range(6)]
        top, sums = state
        total = sums[HEAD_SIZE : HEAD_SIZE + 1]
        delta = jnp.sum(sums[:HEAD_SIZE] * columns[1].astype(jnp.float32), 0, keepdims=True) / total
        lse = jnp.where(picked, stats[0] + stats[1] + stats[2], top + jnp.log2(total))
        delta = jnp.where(picked, stats[3] + stats[4] + stats[5], delta)
        both = jnp.concatenate(weights_of(index), 0)
        query_grad = extra[:HEAD_SIZE] + extra[HEAD_SIZE:PAIR]
        state = None
        columns = None if last else transposed_of(index + 1)
        for start in starts:
            if not last:
                state = first_pass(index + 1, columns, start, state)
            query_grad = last_pass(index, lse, delta, both, start, query_grad)
        query_grad = (query_grad * SCALE).T.astype(jnp.bfloat16)
        emit(place, jnp.concatenate([query_grad[:half], query_grad[half:]], 1))


def first_kernel(
    head_count, steps, place_ref, offset_ref, keys_ref, key_t_ref, queries_ref, grads_ref,
    extra_ref, acc_ref, query_out, *scratch,
):
    offset = own_offset(head_count, place_ref, offset_ref)
    acc_ref[...] = jnp.zeros_like(acc_ref)

    def emit(place, query_grad):
        query_out[place] = query_grad

    near_blocks(
        range(steps), offset, keys_ref, key_t_ref, queries_ref, grads_ref, extra_ref,
        *scratch, acc_ref, emit,
    )


def second_kernel(
    head_count, steps, others, place_ref, offset_ref, keys_ref, key_t_ref, queries_ref, grads_ref,
    extra_ref, start_ref, query_ref, own_ref, *refs,
):
    back_refs, refs = refs[:others], refs[others:]
    rows = query_ref.shape[1] * 2
    group = keys_ref.shape[0] // rows
    out_refs, refs = refs[:group], refs[group:]
    acc_ref, stage_ref, *scratch = refs
    count = extra_ref.shape[1]
    picked = count // group
    offset = own_offset(head_count, place_ref, offset_ref)
    acc_ref[...] = start_ref[...]

    def emit(place, query_grad):
        stage_ref[place, rows:, :] = query_grad

    near_blocks(
        range(group - steps, group), offset, keys_ref, key_t_ref, queries_ref, grads_ref, extra_ref,
        *scratch, acc_ref, emit,
    )
    terms = own_ref[...]
    for back_ref in back_refs:
        terms = terms + back_ref[...]
    terms = jnp.concatenate(split_two(terms), 0)
    factor = jnp.where(left_half((rows, PAIR)), SCALE, 1.0)
    for place in range(group):
        spread = spread_matrix(offset, place * picked, count, rows, 1)
        placed = dot_nn(jnp.concatenate([spread, spread], 1), terms)
        summed = acc_ref[place * rows : (place + 1) * rows, :] * factor + placed
        stage_ref[place, :rows, :] = summed.astype(jnp.bfloat16)
        if place < group - steps:
            stage_ref[place, rows:, :] = query_ref[place]
    send_out(place_ref[0], stage_ref, out_refs)


def unpack_kernel(head_count, group, place_ref, *refs):
    near_refs, refs = refs[:group], refs[group:]
    query_out, key_out, value_out, stage_ref = refs
    rows = query_out.shape[0]
    half = rows // 2
    for bits, near_ref in enumerate(near_refs):
        stage_ref[lax.bitwise_xor(place_ref[0], bits)] = near_ref[...]
    for head in range(head_count):
        columns = slice(head * HEAD_SIZE, (head + 1) * HEAD_SIZE)
        key_out[:, columns] = stage_ref[head, :rows, :HEAD_SIZE]
        value_out[:, columns] = stage_ref[head, :rows, HEAD_SIZE:]
        query_out[:half, columns] = stage_ref[head, rows:, :HEAD_SIZE]
        query_out[half:, columns] = stage_ref[head, rows:, HEAD_SIZE:]


def call(kernel, name, out_shape, scalars, operands, scratch=(), flops=0, space=VMEM, limit=40):
    return pl.pallas_call(
        kernel,
        out_shape=tuple(jax.ShapeDtypeStruct(*shape) for shape in out_shape),
        in_specs=[SMEM] * len(scalars) + [space] * len(operands),
        out_specs=tuple(VMEM for _ in out_shape),
        scratch_shapes=[
            pltpu.VMEM(*shape) if isinstance(shape, tuple) else shape for shape in scratch
        ],
        compiler_params=pltpu.CompilerParams(vmem_limit_bytes=limit * 1024 * 1024),
        cost_estimate=pl.CostEstimate(flops=flops, bytes_accessed=2**21, transcendentals=0),
        name=name,
    )(*scalars, *operands)


def body(upstream, out_weight, query_rows, key_rows, value_rows, head_offsets):
    rows, width = query_rows.shape
    head_count = width // HEAD_SIZE
    devices = lax.axis_size("context")
    shards = lax.axis_size("heads")
    group = FIRST_SEGMENT // rows
    others = devices // group - 1
    half = rows // 2
    picked = rows // DILATION_RATE
    count = group * picked
    near = group * rows
    place = jnp.stack(
        [lax.rem(lax.axis_index("context"), group), lax.axis_index("heads")]
    ).astype(jnp.int32)
    scalars = [place, head_offsets]

    def swap(values):
        pairs = [[(source, source ^ bits) for source in range(devices)] for bits in range(group)]
        return [values[0]] + [
            lax.ppermute(values[bits], "context", pairs[bits]) for bits in range(1, group)
        ]

    def exchange(value):
        groups = [list(range(first, first + group)) for first in range(0, devices, group)]
        return lax.all_to_all(value, "context", 0, 0, axis_index_groups=groups)

    def segment_shift(value, shift):
        pairs = [(source, (source + shift * group) % devices) for source in range(devices)]
        return lax.ppermute(value, "context", pairs)

    upstreams = [upstream]
    for step in range(1, shards):
        pairs = [(source, (source + step) % shards) for source in range(shards)]
        upstreams.append(lax.ppermute(upstream, "heads", pairs))

    bf16, f32 = jnp.bfloat16, jnp.float32
    (sent,) = call(
        functools.partial(pack_kernel, head_count), "pack_rows",
        [((group, rows + half, PAIR), bf16)],
        [], [query_rows, key_rows, value_rows],
        [((rows, width), bf16)] * 3 + [pltpu.SemaphoreType.DMA((3,))],
        flops=2**31, space=ANY, limit=60,
    )
    sent = exchange(sent)
    grads_send = call(
        functools.partial(project_kernel, head_count, group, shards), "project_pack",
        [((half, PAIR), bf16)] * group,
        [place], [out_weight, *upstreams],
        [((rows, width), bf16), ((group, half, PAIR), bf16)],
        flops=BUSY,
    )
    grads = swap(grads_send)
    keys, key_t, queries, picks = call(
        functools.partial(gather_kernel, head_count), "gather_keys",
        [
            ((near, PAIR), bf16), ((PAIR + STAT_ROWS, near), bf16), ((group, half, PAIR), bf16),
            ((count, PAIR), bf16),
        ],
        scalars, [sent, grads_send[0]],
    )
    other_picks = [segment_shift(picks, shift) for shift in range(1, others + 1)]
    extra, own_terms, other_terms, grads = call(
        functools.partial(far_kernel, head_count, group, others), "picked_rows",
        [
            ((PAIR + STAT_ROWS, count), bf16), ((count, PAIR), f32),
            ((others * count, PAIR), f32), ((group, half, PAIR), bf16),
        ],
        scalars, [keys, queries, picks, *other_picks, *grads],
        [((near + count * (1 + others), PAIR), bf16)] + [((count, PAIR), bf16)] * 2,
        flops=8 * near * count * PAIR,
    )
    back = [
        segment_shift(other_terms[(shift - 1) * count : shift * count], -shift)
        for shift in range(1, others + 1)
    ]
    steps = group // 2
    scratch = [
        ((2, near, rows), bf16), ((2, near, rows), f32), ((2, near, 2 * rows), bf16),
        ((2, near // PIECE, 1, rows), f32),
    ]
    half_flops = 10 * near * near // 2 * PAIR
    acc, query_half = call(
        functools.partial(first_kernel, head_count, steps), "first_rows",
        [((near, PAIR), f32), ((steps, half, PAIR), bf16)],
        scalars, [keys, key_t, queries, grads, extra], scratch, half_flops,
    )
    near_send = call(
        functools.partial(second_kernel, head_count, group - steps, others), "second_rows",
        [((rows + half, PAIR), bf16)] * group,
        scalars, [keys, key_t, queries, grads, extra, acc, query_half, own_terms, *back],
        [((near, PAIR), f32), ((group, rows + half, PAIR), bf16)] + scratch, half_flops,
    )
    return tuple(
        call(
            functools.partial(unpack_kernel, head_count, group), "unpack",
            [((rows, width), bf16)] * 3,
            [place], swap(near_send),
            [((group, rows + half, PAIR), bf16)],
        )
    )


def solution(mesh):
    return jax.shard_map(
        body,
        mesh=mesh,
        in_specs=(
            P(("context", "heads"), None),
            P("heads", None),
            P("context", "heads"),
            P("context", "heads"),
            P("context", "heads"),
            P(),
        ),
        out_specs=(P("context", "heads"), P("context", "heads"), P("context", "heads")),
        check_vma=False,
    )
```

```python
import functools
import math

import jax
import jax.numpy as jnp
from jax import lax
from jax.experimental import pallas as pl
from jax.experimental.pallas import tpu as pltpu
from jax.sharding import PartitionSpec as P

HEAD_SIZE = 64
PAIR = 2 * HEAD_SIZE
DILATION_RATE = 16
FIRST_SEGMENT = 2048
SCALE = 1.0 / math.sqrt(HEAD_SIZE)
LOG2E = math.log2(math.e)
SCORE_FACTOR = SCALE * LOG2E
STRIP = 64
PIECE = 256
BUSY = 2**35
STAT_ROWS = 16

SMEM = pl.BlockSpec(memory_space=pltpu.SMEM)
VMEM = pl.BlockSpec(memory_space=pltpu.VMEM)
ANY = pl.BlockSpec(memory_space=pl.ANY)


def dot_nt(left, right):
    return lax.dot_general(
        left, right, (((1,), (1,)), ((), ())), preferred_element_type=jnp.float32
    )


def dot_nn(left, right):
    return jnp.dot(left, right, preferred_element_type=jnp.float32)


def dot_tn(left, right):
    return lax.dot_general(
        left, right, (((0,), (0,)), ((), ())), preferred_element_type=jnp.float32
    )


def head_columns(ref, head):
    return ref[:, head * HEAD_SIZE : (head + 1) * HEAD_SIZE]


def pick_matrix(offset, picked, rows):
    source = lax.broadcasted_iota(jnp.int32, (picked, rows), 1)
    index = lax.broadcasted_iota(jnp.int32, (picked, rows), 0)
    return (source == index * DILATION_RATE + offset).astype(jnp.bfloat16)


def spread_matrix(offset, first, picked, rows, axis):
    shape = (picked, rows) if axis == 0 else (rows, picked)
    index = lax.broadcasted_iota(jnp.int32, shape, axis)
    source = lax.broadcasted_iota(jnp.int32, shape, 1 - axis)
    return (source == (index - first) * DILATION_RATE + offset).astype(jnp.bfloat16)


def split_two(value):
    high = value.astype(jnp.bfloat16)
    low = (value - high.astype(jnp.float32)).astype(jnp.bfloat16)
    return high, low


def split_three(value):
    high = value.astype(jnp.bfloat16)
    rest = value - high.astype(jnp.float32)
    middle = rest.astype(jnp.bfloat16)
    low = (rest - middle.astype(jnp.float32)).astype(jnp.bfloat16)
    return high, middle, low


def fold(value, combine):
    parts = [value[start : start + 8] for start in range(0, value.shape[0], 8)]
    while len(parts) > 1:
        merged = [combine(parts[i], parts[i + 1]) for i in range(0, len(parts) - 1, 2)]
        parts = merged + parts[len(merged) * 2 :]
    return parts[0]


def left_half(shape):
    return lax.broadcasted_iota(jnp.int32, shape, 1) < HEAD_SIZE


def side_by_side(block):
    half = block.shape[0] // 2
    return jnp.concatenate([block[:half], block[half:]], 1)


def send_out(place, stage_ref, out_refs):
    for bits, out_ref in enumerate(out_refs):
        out_ref[...] = stage_ref[lax.bitwise_xor(place, bits)]


def pack_kernel(head_count, query_hbm, key_hbm, value_hbm, *refs):
    out_ref, query_ref, key_ref, value_ref, sems = refs
    rows = query_ref.shape[0]
    copies = [
        pltpu.make_async_copy(source, target, sems.at[index])
        for index, (source, target) in enumerate(
            [(key_hbm, key_ref), (value_hbm, value_ref), (query_hbm, query_ref)]
        )
    ]
    for copy in copies:
        copy.start()
    for copy in copies:
        copy.wait()
    for head in range(head_count):
        pair = jnp.concatenate([head_columns(key_ref, head), head_columns(value_ref, head)], 1)
        query = side_by_side(head_columns(query_ref, head))
        for place in range(head, out_ref.shape[0], head_count):
            out_ref[place, :rows, :] = pair
            out_ref[place, rows:, :] = query


def project_kernel(head_count, group, shards, place_ref, weight_ref, *refs):
    upstream_refs, refs = refs[:shards], refs[shards:]
    out_refs, (grad_ref, stage_ref) = refs[:group], refs[group:]
    shard_rows = upstream_refs[0].shape[0]
    for step, upstream_ref in enumerate(upstream_refs):
        owner = lax.rem(place_ref[1] + (shards - step), shards)
        start = pl.multiple_of(owner * shard_rows, shard_rows)
        grad_ref[pl.ds(start, shard_rows), :] = dot_nt(
            upstream_ref[...], weight_ref[...]
        ).astype(jnp.bfloat16)
    for head in range(head_count):
        grad = side_by_side(head_columns(grad_ref, head))
        for place in range(head, group, head_count):
            stage_ref[place] = grad
    send_out(place_ref[0], stage_ref, out_refs)


def own_offset(head_count, place_ref, offset_ref):
    return offset_ref[place_ref[1] * head_count + lax.rem(place_ref[0], head_count)]


def gather_kernel(
    head_count, place_ref, offset_ref, sent_ref, after_ref, keys_out, key_t_out, queries_out,
    picks_out,
):
    group = sent_ref.shape[0]
    rows = keys_out.shape[0] // group
    picked = rows // DILATION_RATE
    pick = pick_matrix(own_offset(head_count, place_ref, offset_ref), picked, rows)
    for place in range(group):
        pair = sent_ref[place, :rows, :]
        keys_out[place * rows : (place + 1) * rows, :] = pair
        picks_out[place * picked : (place + 1) * picked, :] = dot_nn(pick, pair).astype(
            jnp.bfloat16
        )
        queries_out[place] = sent_ref[place, rows:, :]
    key_t_out[...] = keys_out[...].astype(jnp.float32).T[:HEAD_SIZE].astype(jnp.bfloat16)


def query_and_grad(query_ref, grad_ref):
    query, grad = query_ref[...], grad_ref[...]
    zero = jnp.zeros((query.shape[0], HEAD_SIZE), query.dtype)
    return (
        jnp.concatenate(
            [
                jnp.concatenate([query[:, :HEAD_SIZE], zero], 1),
                jnp.concatenate([query[:, HEAD_SIZE:], zero], 1),
            ], 0,
        ),
        jnp.concatenate(
            [
                jnp.concatenate([zero, grad[:, :HEAD_SIZE]], 1),
                jnp.concatenate([zero, grad[:, HEAD_SIZE:]], 1),
            ], 0,
        ),
    )


def far_kernel(
    head_count, group, others, place_ref, offset_ref, near_ref, queries_ref, picks_ref, *refs
):
    other_refs, refs = refs[:others], refs[others:]
    grad_refs, refs = refs[:group], refs[group:]
    extra_out, own_out, other_out, grads_out, keys_ref, query_ref, grad_ref = refs
    near = near_ref.shape[0]
    rows = near // group
    picked = rows // DILATION_RATE
    count = group * picked
    far = count * (1 + others)
    pick = pick_matrix(own_offset(head_count, place_ref, offset_ref), picked, rows)
    keys_ref[:near, :] = near_ref[...]
    for index, ref in enumerate([picks_ref, *other_refs]):
        keys_ref[near + index * count : near + (index + 1) * count, :] = ref[...]
    for bits, ref in enumerate(grad_refs):
        grads_out[lax.bitwise_xor(place_ref[0], bits)] = ref[...]
    for step in range(group):
        query, grad = query_and_grad(queries_ref.at[step], grads_out.at[step])
        span = slice(step * picked, (step + 1) * picked)
        query_ref[span, :] = dot_nn(pick, query).astype(jnp.bfloat16)
        grad_ref[span, :] = dot_nn(pick, grad).astype(jnp.bfloat16)
    far_t = keys_ref[near:, :].astype(jnp.float32).T[:HEAD_SIZE].astype(jnp.bfloat16)
    query, grad = query_ref[...], grad_ref[...]
    score = dot_nt(keys_ref[...], query)
    dprob = dot_nt(keys_ref[...], grad)
    top = jnp.max(score, 0, keepdims=True)
    prob = jnp.exp2((score - top) * SCORE_FACTOR)
    total = jnp.sum(prob, 0, keepdims=True)
    inverse = 1.0 / total
    delta = jnp.sum(prob * dprob, 0, keepdims=True) * inverse
    prob_far = prob[near:] * inverse
    dscore = (prob_far * (dprob[near:] - delta)).astype(jnp.bfloat16)
    terms = dot_nn(
        jnp.concatenate([dscore, prob_far.astype(jnp.bfloat16)], 1),
        jnp.concatenate([query, grad], 0),
    ) * jnp.where(left_half((far, PAIR)), SCALE, 1.0)
    own_out[...] = terms[:count]
    other_out[...] = terms[count:]
    query_grad = dot_nn(far_t, dscore)
    lse = top * SCORE_FACTOR + jnp.log2(total)
    extra_out[:PAIR, :] = jnp.concatenate(split_two(query_grad), 0)
    blank = jnp.zeros((STAT_ROWS - 6, count), jnp.bfloat16)
    extra_out[PAIR:, :] = jnp.concatenate([*split_three(lse), *split_three(delta), blank], 0)


def near_blocks(
    places, offset, keys_ref, key_t_ref, queries_ref, grads_ref, extra_ref,
    prob_ref, dprob_ref, work_ref, top_ref, acc_ref, emit,
):
    near = keys_ref.shape[0]
    rows = prob_ref.shape[2]
    half = rows // 2
    count = extra_ref.shape[1]
    row_lane = lax.broadcasted_iota(jnp.int32, (1, rows), 1)
    picked = lax.rem(row_lane, DILATION_RATE) == offset

    def by_eight(value):
        return value.reshape(value.shape[0] // 8, 8, rows)

    def weights_of(index):
        return query_and_grad(queries_ref.at[places[index]], grads_ref.at[places[index]])

    def columns_of(ref):
        packed = ref[...].astype(jnp.float32).T
        return jnp.concatenate([packed[:HEAD_SIZE], packed[HEAD_SIZE:]], 1).astype(jnp.bfloat16)

    def transposed_of(index):
        zero = jnp.zeros((HEAD_SIZE, rows), jnp.bfloat16)
        query = columns_of(queries_ref.at[places[index]])
        grad = columns_of(grads_ref.at[places[index]])
        return jnp.concatenate([query, zero], 0), jnp.concatenate([zero, grad], 0)

    def first_pass(index, weights, start, state):
        top, total, delta = state
        slot = index % 2
        query, grad = weights
        keys = keys_ref[start : start + PIECE, :]
        scores, dprobs = dot_nn(keys, query), dot_nn(keys, grad)
        for inner in range(0, PIECE, STRIP):
            strip = slice(start + inner, start + inner + STRIP)
            score, dprob = scores[inner : inner + STRIP], dprobs[inner : inner + STRIP]
            part = fold(score, jnp.maximum) * SCORE_FACTOR
            raised = part if top is None else jnp.maximum(top, part)
            prob = jnp.exp2(by_eight(score) * SCORE_FACTOR - raised[None])
            part_total = jnp.sum(prob, 0)
            part_delta = jnp.sum(prob * by_eight(dprob), 0)
            if top is None:
                total, delta = part_total, part_delta
            else:
                shrink = jnp.exp2(top - raised)
                total, delta = total * shrink + part_total, delta * shrink + part_delta
            top = raised
            prob_ref[slot, strip, :] = prob.reshape(STRIP, rows)
            dprob_ref[slot, strip, :] = dprob
            top_ref[slot, strip.start // STRIP] = raised
        return top, total, delta

    def last_pass(index, lse, delta, both, start, query_grad):
        slot = index % 2
        piece = slice(start, start + PIECE)
        for inner in range(0, PIECE, STRIP):
            strip = slice(start + inner, start + inner + STRIP)
            factor = jnp.exp2(top_ref[slot, strip.start // STRIP] - lse)
            prob = by_eight(prob_ref[slot, strip, :]) * factor[None]
            dscore = prob * (by_eight(dprob_ref[slot, strip, :]) - delta)
            work_ref[slot, strip, :rows] = dscore.reshape(STRIP, rows).astype(jnp.bfloat16)
            work_ref[slot, strip, rows:] = prob.reshape(STRIP, rows).astype(jnp.bfloat16)
        acc_ref[piece, :] += dot_nn(work_ref[slot, piece, :], both)
        return query_grad + dot_tn(work_ref[slot, piece, :rows], keys_ref[piece, :])

    starts = range(0, near, PIECE)
    weights = transposed_of(0)
    state = (None, None, None)
    for start in starts:
        state = first_pass(0, weights, start, state)
    for index, place in enumerate(places):
        last = index + 1 == len(places)
        first = place * (rows // DILATION_RATE)
        spread = spread_matrix(offset, first, count, rows, 0)
        extra = dot_nn(extra_ref[PAIR:, :], spread)
        stats = [extra[row : row + 1] for row in range(6)]
        top, total, delta = state
        highest = jnp.max(top, 0, keepdims=True)
        shrink = jnp.exp2(top - highest)
        total = jnp.sum(total * shrink, 0, keepdims=True)
        delta = jnp.sum(delta * shrink, 0, keepdims=True) / total
        lse = jnp.where(picked, stats[0] + stats[1] + stats[2], highest + jnp.log2(total))
        delta = jnp.where(picked, stats[3] + stats[4] + stats[5], delta)
        both = jnp.concatenate(weights_of(index), 0)
        spread = spread_matrix(offset, first, count, rows, 1)
        query_grad = dot_nt(spread, extra_ref[:PAIR, :])
        query_grad = query_grad + pltpu.roll(query_grad, HEAD_SIZE, 1)
        weights = None if last else transposed_of(index + 1)
        state = (None, None, None)
        for start in starts:
            if not last:
                state = first_pass(index + 1, weights, start, state)
            query_grad = last_pass(index, lse, delta, both, start, query_grad)
        query_grad = (query_grad[:, :HEAD_SIZE] * SCALE).astype(jnp.bfloat16)
        emit(place, jnp.concatenate([query_grad[:half], query_grad[half:]], 1))


def first_kernel(
    head_count, steps, place_ref, offset_ref, keys_ref, key_t_ref, queries_ref, grads_ref,
    extra_ref, acc_ref, query_out, *scratch,
):
    offset = own_offset(head_count, place_ref, offset_ref)
    acc_ref[...] = jnp.zeros_like(acc_ref)

    def emit(place, query_grad):
        query_out[place] = query_grad

    near_blocks(
        range(steps), offset, keys_ref, key_t_ref, queries_ref, grads_ref, extra_ref,
        *scratch, acc_ref, emit,
    )


def second_kernel(
    head_count, steps, others, place_ref, offset_ref, keys_ref, key_t_ref, queries_ref, grads_ref,
    extra_ref, start_ref, query_ref, own_ref, *refs,
):
    back_refs, refs = refs[:others], refs[others:]
    rows = query_ref.shape[1] * 2
    group = keys_ref.shape[0] // rows
    out_refs, refs = refs[:group], refs[group:]
    acc_ref, stage_ref, *scratch = refs
    count = extra_ref.shape[1]
    picked = count // group
    offset = own_offset(head_count, place_ref, offset_ref)
    acc_ref[...] = start_ref[...]

    def emit(place, query_grad):
        stage_ref[place, rows:, :] = query_grad

    near_blocks(
        range(group - steps, group), offset, keys_ref, key_t_ref, queries_ref, grads_ref, extra_ref,
        *scratch, acc_ref, emit,
    )
    terms = own_ref[...]
    for back_ref in back_refs:
        terms = terms + back_ref[...]
    terms = jnp.concatenate(split_two(terms), 0)
    factor = jnp.where(left_half((rows, PAIR)), SCALE, 1.0)
    for place in range(group):
        spread = spread_matrix(offset, place * picked, count, rows, 1)
        placed = dot_nn(jnp.concatenate([spread, spread], 1), terms)
        summed = acc_ref[place * rows : (place + 1) * rows, :] * factor + placed
        stage_ref[place, :rows, :] = summed.astype(jnp.bfloat16)
        if place < group - steps:
            stage_ref[place, rows:, :] = query_ref[place]
    send_out(place_ref[0], stage_ref, out_refs)


def unpack_kernel(head_count, group, place_ref, *refs):
    near_refs, refs = refs[:group], refs[group:]
    query_out, key_out, value_out, stage_ref = refs
    rows = query_out.shape[0]
    half = rows // 2
    for bits, near_ref in enumerate(near_refs):
        stage_ref[lax.bitwise_xor(place_ref[0], bits)] = near_ref[...]
    for head in range(head_count):
        columns = slice(head * HEAD_SIZE, (head + 1) * HEAD_SIZE)
        key_out[:, columns] = stage_ref[head, :rows, :HEAD_SIZE]
        value_out[:, columns] = stage_ref[head, :rows, HEAD_SIZE:]
        query_out[:half, columns] = stage_ref[head, rows:, :HEAD_SIZE]
        query_out[half:, columns] = stage_ref[head, rows:, HEAD_SIZE:]


def call(kernel, name, out_shape, scalars, operands, scratch=(), flops=0, space=VMEM, limit=40):
    return pl.pallas_call(
        kernel,
        out_shape=tuple(jax.ShapeDtypeStruct(*shape) for shape in out_shape),
        in_specs=[SMEM] * len(scalars) + [space] * len(operands),
        out_specs=tuple(VMEM for _ in out_shape),
        scratch_shapes=[
            pltpu.VMEM(*shape) if isinstance(shape, tuple) else shape for shape in scratch
        ],
        compiler_params=pltpu.CompilerParams(vmem_limit_bytes=limit * 1024 * 1024),
        cost_estimate=pl.CostEstimate(flops=flops, bytes_accessed=2**21, transcendentals=0),
        name=name,
    )(*scalars, *operands)


def body(upstream, out_weight, query_rows, key_rows, value_rows, head_offsets):
    rows, width = query_rows.shape
    head_count = width // HEAD_SIZE
    devices = lax.axis_size("context")
    shards = lax.axis_size("heads")
    group = FIRST_SEGMENT // rows
    others = devices // group - 1
    half = rows // 2
    picked = rows // DILATION_RATE
    count = group * picked
    near = group * rows
    place = jnp.stack(
        [lax.rem(lax.axis_index("context"), group), lax.axis_index("heads")]
    ).astype(jnp.int32)
    scalars = [place, head_offsets]

    def swap(values):
        pairs = [[(source, source ^ bits) for source in range(devices)] for bits in range(group)]
        return [values[0]] + [
            lax.ppermute(values[bits], "context", pairs[bits]) for bits in range(1, group)
        ]

    def exchange(value):
        groups = [list(range(first, first + group)) for first in range(0, devices, group)]
        return lax.all_to_all(value, "context", 0, 0, axis_index_groups=groups)

    def segment_shift(value, shift):
        pairs = [(source, (source + shift * group) % devices) for source in range(devices)]
        return lax.ppermute(value, "context", pairs)

    upstreams = [upstream]
    for step in range(1, shards):
        pairs = [(source, (source + step) % shards) for source in range(shards)]
        upstreams.append(lax.ppermute(upstream, "heads", pairs))

    bf16, f32 = jnp.bfloat16, jnp.float32
    (sent,) = call(
        functools.partial(pack_kernel, head_count), "pack_rows",
        [((group, rows + half, PAIR), bf16)],
        [], [query_rows, key_rows, value_rows],
        [((rows, width), bf16)] * 3 + [pltpu.SemaphoreType.DMA((3,))],
        flops=2**31, space=ANY, limit=60,
    )
    sent = exchange(sent)
    grads_send = call(
        functools.partial(project_kernel, head_count, group, shards), "project_pack",
        [((half, PAIR), bf16)] * group,
        [place], [out_weight, *upstreams],
        [((rows, width), bf16), ((group, half, PAIR), bf16)],
        flops=BUSY,
    )
    grads = swap(grads_send)
    keys, key_t, queries, picks = call(
        functools.partial(gather_kernel, head_count), "gather_keys",
        [
            ((near, PAIR), bf16), ((HEAD_SIZE, near), bf16), ((group, half, PAIR), bf16),
            ((count, PAIR), bf16),
        ],
        scalars, [sent, grads_send[0]],
    )
    other_picks = [segment_shift(picks, shift) for shift in range(1, others + 1)]
    extra, own_terms, other_terms, grads = call(
        functools.partial(far_kernel, head_count, group, others), "picked_rows",
        [
            ((PAIR + STAT_ROWS, count), bf16), ((count, PAIR), f32),
            ((others * count, PAIR), f32), ((group, half, PAIR), bf16),
        ],
        scalars, [keys, queries, picks, *other_picks, *grads],
        [((near + count * (1 + others), PAIR), bf16)] + [((count, PAIR), bf16)] * 2,
        flops=8 * near * count * PAIR,
    )
    back = [
        segment_shift(other_terms[(shift - 1) * count : shift * count], -shift)
        for shift in range(1, others + 1)
    ]
    steps = group // 2
    scratch = [
        ((2, near, rows), f32), ((2, near, rows), f32), ((2, near, 2 * rows), bf16),
        ((2, near // STRIP, 8, rows), f32),
    ]
    half_flops = 10 * near * near // 2 * PAIR
    acc, query_half = call(
        functools.partial(first_kernel, head_count, steps), "first_rows",
        [((near, PAIR), f32), ((steps, half, PAIR), bf16)],
        scalars, [keys, key_t, queries, grads, extra], scratch, half_flops,
    )
    near_send = call(
        functools.partial(second_kernel, head_count, group - steps, others), "second_rows",
        [((rows + half, PAIR), bf16)] * group,
        scalars, [keys, key_t, queries, grads, extra, acc, query_half, own_terms, *back],
        [((near, PAIR), f32), ((group, rows + half, PAIR), bf16)] + scratch, half_flops,
    )
    return tuple(
        call(
            functools.partial(unpack_kernel, head_count, group), "unpack",
            [((rows, width), bf16)] * 3,
            [place], swap(near_send),
            [((group, rows + half, PAIR), bf16)],
        )
    )


def solution(mesh):
    return jax.shard_map(
        body,
        mesh=mesh,
        in_specs=(
            P(("context", "heads"), None),
            P("heads", None),
            P("context", "heads"),
            P("context", "heads"),
            P("context", "heads"),
            P(),
        ),
        out_specs=(P("context", "heads"), P("context", "heads"), P("context", "heads")),
        check_vma=False,
    )
```

```python
import functools
import math

import jax
import jax.numpy as jnp
from jax import lax
from jax.experimental import pallas as pl
from jax.experimental.pallas import tpu as pltpu
from jax.sharding import PartitionSpec as P

HEAD_SIZE = 64
PAIR = 2 * HEAD_SIZE
DILATION_RATE = 16
FIRST_SEGMENT = 2048
SCALE = 1.0 / math.sqrt(HEAD_SIZE)
LOG2E = math.log2(math.e)
SCORE_FACTOR = SCALE * LOG2E
STRIP = 64
PIECE = 256
BUSY = 2**35
STAT_ROWS = 16

SMEM = pl.BlockSpec(memory_space=pltpu.SMEM)
VMEM = pl.BlockSpec(memory_space=pltpu.VMEM)
ANY = pl.BlockSpec(memory_space=pl.ANY)


def dot_nt(left, right):
    return lax.dot_general(
        left, right, (((1,), (1,)), ((), ())), preferred_element_type=jnp.float32
    )


def dot_nn(left, right):
    return jnp.dot(left, right, preferred_element_type=jnp.float32)


def head_columns(ref, head):
    return ref[:, head * HEAD_SIZE : (head + 1) * HEAD_SIZE]


def pick_matrix(offset, picked, rows):
    source = lax.broadcasted_iota(jnp.int32, (picked, rows), 1)
    index = lax.broadcasted_iota(jnp.int32, (picked, rows), 0)
    return (source == index * DILATION_RATE + offset).astype(jnp.bfloat16)


def spread_matrix(offset, first, picked, rows, axis):
    shape = (picked, rows) if axis == 0 else (rows, picked)
    index = lax.broadcasted_iota(jnp.int32, shape, axis)
    source = lax.broadcasted_iota(jnp.int32, shape, 1 - axis)
    return (source == (index - first) * DILATION_RATE + offset).astype(jnp.bfloat16)


def split_two(value):
    high = value.astype(jnp.bfloat16)
    low = (value - high.astype(jnp.float32)).astype(jnp.bfloat16)
    return high, low


def split_three(value):
    high = value.astype(jnp.bfloat16)
    rest = value - high.astype(jnp.float32)
    middle = rest.astype(jnp.bfloat16)
    low = (rest - middle.astype(jnp.float32)).astype(jnp.bfloat16)
    return high, middle, low


def fold(value, combine):
    parts = [value[start : start + 8] for start in range(0, value.shape[0], 8)]
    while len(parts) > 1:
        merged = [combine(parts[i], parts[i + 1]) for i in range(0, len(parts) - 1, 2)]
        parts = merged + parts[len(merged) * 2 :]
    return parts[0]


def left_half(shape):
    return lax.broadcasted_iota(jnp.int32, shape, 1) < HEAD_SIZE


def side_by_side(block):
    half = block.shape[0] // 2
    return jnp.concatenate([block[:half], block[half:]], 1)


def send_out(place, stage_ref, out_refs):
    for bits, out_ref in enumerate(out_refs):
        out_ref[...] = stage_ref[lax.bitwise_xor(place, bits)]


def pack_kernel(head_count, query_hbm, key_hbm, value_hbm, *refs):
    out_ref, query_ref, key_ref, value_ref, sems = refs
    rows = query_ref.shape[0]
    copies = [
        pltpu.make_async_copy(source, target, sems.at[index])
        for index, (source, target) in enumerate(
            [(key_hbm, key_ref), (value_hbm, value_ref), (query_hbm, query_ref)]
        )
    ]
    for copy in copies:
        copy.start()
    for copy in copies:
        copy.wait()
    for head in range(head_count):
        pair = jnp.concatenate([head_columns(key_ref, head), head_columns(value_ref, head)], 1)
        query = side_by_side(head_columns(query_ref, head))
        for place in range(head, out_ref.shape[0], head_count):
            out_ref[place, :rows, :] = pair
            out_ref[place, rows:, :] = query


def project_kernel(head_count, group, shards, place_ref, weight_ref, *refs):
    upstream_refs, refs = refs[:shards], refs[shards:]
    out_refs, (grad_ref, stage_ref) = refs[:group], refs[group:]
    shard_rows = upstream_refs[0].shape[0]
    for step, upstream_ref in enumerate(upstream_refs):
        owner = lax.rem(place_ref[1] + (shards - step), shards)
        start = pl.multiple_of(owner * shard_rows, shard_rows)
        grad_ref[pl.ds(start, shard_rows), :] = dot_nt(
            upstream_ref[...], weight_ref[...]
        ).astype(jnp.bfloat16)
    for head in range(head_count):
        grad = side_by_side(head_columns(grad_ref, head))
        for place in range(head, group, head_count):
            stage_ref[place] = grad
    send_out(place_ref[0], stage_ref, out_refs)


def own_offset(head_count, place_ref, offset_ref):
    return offset_ref[place_ref[1] * head_count + lax.rem(place_ref[0], head_count)]


def gather_kernel(
    head_count, place_ref, offset_ref, sent_ref, after_ref, keys_out, key_t_out, queries_out,
    picks_out,
):
    group = sent_ref.shape[0]
    rows = keys_out.shape[0] // group
    picked = rows // DILATION_RATE
    pick = pick_matrix(own_offset(head_count, place_ref, offset_ref), picked, rows)
    for place in range(group):
        pair = sent_ref[place, :rows, :]
        keys_out[place * rows : (place + 1) * rows, :] = pair
        picks_out[place * picked : (place + 1) * picked, :] = dot_nn(pick, pair).astype(
            jnp.bfloat16
        )
        queries_out[place] = sent_ref[place, rows:, :]
    key_t_out[...] = keys_out[...].astype(jnp.float32).T[:HEAD_SIZE].astype(jnp.bfloat16)


def query_and_grad(query_ref, grad_ref):
    query, grad = query_ref[...], grad_ref[...]
    zero = jnp.zeros((query.shape[0], HEAD_SIZE), query.dtype)
    return (
        jnp.concatenate(
            [
                jnp.concatenate([query[:, :HEAD_SIZE], zero], 1),
                jnp.concatenate([query[:, HEAD_SIZE:], zero], 1),
            ], 0,
        ),
        jnp.concatenate(
            [
                jnp.concatenate([zero, grad[:, :HEAD_SIZE]], 1),
                jnp.concatenate([zero, grad[:, HEAD_SIZE:]], 1),
            ], 0,
        ),
    )


def far_kernel(
    head_count, group, others, place_ref, offset_ref, near_ref, queries_ref, picks_ref, *refs
):
    other_refs, refs = refs[:others], refs[others:]
    grad_refs, refs = refs[:group], refs[group:]
    extra_out, own_out, other_out, grads_out, keys_ref, query_ref, grad_ref = refs
    near = near_ref.shape[0]
    rows = near // group
    picked = rows // DILATION_RATE
    count = group * picked
    far = count * (1 + others)
    pick = pick_matrix(own_offset(head_count, place_ref, offset_ref), picked, rows)
    keys_ref[:near, :] = near_ref[...]
    for index, ref in enumerate([picks_ref, *other_refs]):
        keys_ref[near + index * count : near + (index + 1) * count, :] = ref[...]
    for bits, ref in enumerate(grad_refs):
        grads_out[lax.bitwise_xor(place_ref[0], bits)] = ref[...]
    for step in range(group):
        query, grad = query_and_grad(queries_ref.at[step], grads_out.at[step])
        span = slice(step * picked, (step + 1) * picked)
        query_ref[span, :] = dot_nn(pick, query).astype(jnp.bfloat16)
        grad_ref[span, :] = dot_nn(pick, grad).astype(jnp.bfloat16)
    far_t = keys_ref[near:, :].astype(jnp.float32).T[:HEAD_SIZE].astype(jnp.bfloat16)
    query, grad = query_ref[...], grad_ref[...]
    score = dot_nt(keys_ref[...], query)
    dprob = dot_nt(keys_ref[...], grad)
    top = jnp.max(score, 0, keepdims=True)
    prob = jnp.exp2((score - top) * SCORE_FACTOR)
    total = jnp.sum(prob, 0, keepdims=True)
    inverse = 1.0 / total
    delta = jnp.sum(prob * dprob, 0, keepdims=True) * inverse
    prob_far = prob[near:] * inverse
    dscore = (prob_far * (dprob[near:] - delta)).astype(jnp.bfloat16)
    terms = dot_nn(
        jnp.concatenate([dscore, prob_far.astype(jnp.bfloat16)], 1),
        jnp.concatenate([query, grad], 0),
    ) * jnp.where(left_half((far, PAIR)), SCALE, 1.0)
    own_out[...] = terms[:count]
    other_out[...] = terms[count:]
    query_grad = dot_nn(far_t, dscore)
    lse = top * SCORE_FACTOR + jnp.log2(total)
    extra_out[:PAIR, :] = jnp.concatenate(split_two(query_grad), 0)
    blank = jnp.zeros((STAT_ROWS - 6, count), jnp.bfloat16)
    extra_out[PAIR:, :] = jnp.concatenate([*split_three(lse), *split_three(delta), blank], 0)


def near_blocks(
    places, offset, keys_ref, key_t_ref, queries_ref, grads_ref, extra_ref,
    work_ref, acc_ref, emit,
):
    near = keys_ref.shape[0]
    rows = work_ref.shape[2] // 2
    half = rows // 2
    count = extra_ref.shape[1]
    row_lane = lax.broadcasted_iota(jnp.int32, (1, rows), 1)
    picked = lax.rem(row_lane, DILATION_RATE) == offset

    def by_eight(value):
        return value.reshape(value.shape[0] // 8, 8, rows)

    def weights_of(index):
        return query_and_grad(queries_ref.at[places[index]], grads_ref.at[places[index]])

    def first_pass(index, weights, start, state):
        top, total, delta = state
        query, grad = weights
        keys = keys_ref[start : start + PIECE, :]
        scores, dprobs = dot_nt(keys, query), dot_nt(keys, grad)
        for inner in range(0, PIECE, STRIP):
            score, dprob = scores[inner : inner + STRIP], dprobs[inner : inner + STRIP]
            part = fold(score, jnp.maximum) * SCORE_FACTOR
            raised = part if top is None else jnp.maximum(top, part)
            prob = jnp.exp2(by_eight(score) * SCORE_FACTOR - raised[None])
            part_total = jnp.sum(prob, 0)
            part_delta = jnp.sum(prob * by_eight(dprob), 0)
            if top is None:
                total, delta = part_total, part_delta
            else:
                shrink = jnp.exp2(top - raised)
                total, delta = total * shrink + part_total, delta * shrink + part_delta
            top = raised
        return top, total, delta

    def last_pass(index, lse, delta, weights, both, start, query_grad):
        slot = index % 2
        piece = slice(start, start + PIECE)
        query, grad = weights
        keys = keys_ref[piece, :]
        scores, dprobs = dot_nt(keys, query), dot_nt(keys, grad)
        for inner in range(0, PIECE, STRIP):
            strip = slice(start + inner, start + inner + STRIP)
            prob = jnp.exp2(scores[inner : inner + STRIP] * SCORE_FACTOR - lse)
            dscore = prob * (dprobs[inner : inner + STRIP] - delta)
            work_ref[slot, strip, :rows] = dscore.astype(jnp.bfloat16)
            work_ref[slot, strip, rows:] = prob.astype(jnp.bfloat16)
        acc_ref[piece, :] += dot_nn(work_ref[slot, piece, :], both)
        return query_grad + dot_nn(key_t_ref[:, piece], work_ref[slot, piece, :rows])

    starts = range(0, near, PIECE)
    weights = weights_of(0)
    state = (None, None, None)
    for start in starts:
        state = first_pass(0, weights, start, state)
    for index, place in enumerate(places):
        last = index + 1 == len(places)
        first = place * (rows // DILATION_RATE)
        extra = dot_nn(extra_ref[...], spread_matrix(offset, first, count, rows, 0))
        stats = [extra[PAIR + row : PAIR + row + 1] for row in range(6)]
        top, total, delta = state
        highest = jnp.max(top, 0, keepdims=True)
        shrink = jnp.exp2(top - highest)
        total = jnp.sum(total * shrink, 0, keepdims=True)
        delta = jnp.sum(delta * shrink, 0, keepdims=True) / total
        lse = jnp.where(picked, stats[0] + stats[1] + stats[2], highest + jnp.log2(total))
        delta = jnp.where(picked, stats[3] + stats[4] + stats[5], delta)
        both = jnp.concatenate(weights, 0)
        query_grad = extra[:HEAD_SIZE] + extra[HEAD_SIZE:PAIR]
        now = weights
        weights = None if last else weights_of(index + 1)
        state = (None, None, None)
        for start in starts:
            if not last:
                state = first_pass(index + 1, weights, start, state)
            query_grad = last_pass(index, lse, delta, now, both, start, query_grad)
        query_grad = (query_grad * SCALE).T.astype(jnp.bfloat16)
        emit(place, jnp.concatenate([query_grad[:half], query_grad[half:]], 1))


def first_kernel(
    head_count, steps, place_ref, offset_ref, keys_ref, key_t_ref, queries_ref, grads_ref,
    extra_ref, acc_ref, query_out, *scratch,
):
    offset = own_offset(head_count, place_ref, offset_ref)
    acc_ref[...] = jnp.zeros_like(acc_ref)

    def emit(place, query_grad):
        query_out[place] = query_grad

    near_blocks(
        range(steps), offset, keys_ref, key_t_ref, queries_ref, grads_ref, extra_ref,
        *scratch, acc_ref, emit,
    )


def second_kernel(
    head_count, steps, others, place_ref, offset_ref, keys_ref, key_t_ref, queries_ref, grads_ref,
    extra_ref, start_ref, query_ref, own_ref, *refs,
):
    back_refs, refs = refs[:others], refs[others:]
    rows = query_ref.shape[1] * 2
    group = keys_ref.shape[0] // rows
    out_refs, refs = refs[:group], refs[group:]
    acc_ref, stage_ref, *scratch = refs
    count = extra_ref.shape[1]
    picked = count // group
    offset = own_offset(head_count, place_ref, offset_ref)
    acc_ref[...] = start_ref[...]

    def emit(place, query_grad):
        stage_ref[place, rows:, :] = query_grad

    near_blocks(
        range(group - steps, group), offset, keys_ref, key_t_ref, queries_ref, grads_ref, extra_ref,
        *scratch, acc_ref, emit,
    )
    terms = own_ref[...]
    for back_ref in back_refs:
        terms = terms + back_ref[...]
    terms = jnp.concatenate(split_two(terms), 0)
    factor = jnp.where(left_half((rows, PAIR)), SCALE, 1.0)
    for place in range(group):
        spread = spread_matrix(offset, place * picked, count, rows, 1)
        placed = dot_nn(jnp.concatenate([spread, spread], 1), terms)
        summed = acc_ref[place * rows : (place + 1) * rows, :] * factor + placed
        stage_ref[place, :rows, :] = summed.astype(jnp.bfloat16)
        if place < group - steps:
            stage_ref[place, rows:, :] = query_ref[place]
    send_out(place_ref[0], stage_ref, out_refs)


def unpack_kernel(head_count, group, place_ref, *refs):
    near_refs, refs = refs[:group], refs[group:]
    query_out, key_out, value_out, stage_ref = refs
    rows = query_out.shape[0]
    half = rows // 2
    for bits, near_ref in enumerate(near_refs):
        stage_ref[lax.bitwise_xor(place_ref[0], bits)] = near_ref[...]
    for head in range(head_count):
        columns = slice(head * HEAD_SIZE, (head + 1) * HEAD_SIZE)
        key_out[:, columns] = stage_ref[head, :rows, :HEAD_SIZE]
        value_out[:, columns] = stage_ref[head, :rows, HEAD_SIZE:]
        query_out[:half, columns] = stage_ref[head, rows:, :HEAD_SIZE]
        query_out[half:, columns] = stage_ref[head, rows:, HEAD_SIZE:]


def call(kernel, name, out_shape, scalars, operands, scratch=(), flops=0, space=VMEM, limit=40):
    return pl.pallas_call(
        kernel,
        out_shape=tuple(jax.ShapeDtypeStruct(*shape) for shape in out_shape),
        in_specs=[SMEM] * len(scalars) + [space] * len(operands),
        out_specs=tuple(VMEM for _ in out_shape),
        scratch_shapes=[
            pltpu.VMEM(*shape) if isinstance(shape, tuple) else shape for shape in scratch
        ],
        compiler_params=pltpu.CompilerParams(vmem_limit_bytes=limit * 1024 * 1024),
        cost_estimate=pl.CostEstimate(flops=flops, bytes_accessed=2**21, transcendentals=0),
        name=name,
    )(*scalars, *operands)


def body(upstream, out_weight, query_rows, key_rows, value_rows, head_offsets):
    rows, width = query_rows.shape
    head_count = width // HEAD_SIZE
    devices = lax.axis_size("context")
    shards = lax.axis_size("heads")
    group = FIRST_SEGMENT // rows
    others = devices // group - 1
    half = rows // 2
    picked = rows // DILATION_RATE
    count = group * picked
    near = group * rows
    place = jnp.stack(
        [lax.rem(lax.axis_index("context"), group), lax.axis_index("heads")]
    ).astype(jnp.int32)
    scalars = [place, head_offsets]

    def swap(values):
        pairs = [[(source, source ^ bits) for source in range(devices)] for bits in range(group)]
        return [values[0]] + [
            lax.ppermute(values[bits], "context", pairs[bits]) for bits in range(1, group)
        ]

    def exchange(value):
        groups = [list(range(first, first + group)) for first in range(0, devices, group)]
        return lax.all_to_all(value, "context", 0, 0, axis_index_groups=groups)

    def segment_shift(value, shift):
        pairs = [(source, (source + shift * group) % devices) for source in range(devices)]
        return lax.ppermute(value, "context", pairs)

    upstreams = [upstream]
    for step in range(1, shards):
        pairs = [(source, (source + step) % shards) for source in range(shards)]
        upstreams.append(lax.ppermute(upstream, "heads", pairs))

    bf16, f32 = jnp.bfloat16, jnp.float32
    (sent,) = call(
        functools.partial(pack_kernel, head_count), "pack_rows",
        [((group, rows + half, PAIR), bf16)],
        [], [query_rows, key_rows, value_rows],
        [((rows, width), bf16)] * 3 + [pltpu.SemaphoreType.DMA((3,))],
        flops=2**31, space=ANY, limit=60,
    )
    sent = exchange(sent)
    grads_send = call(
        functools.partial(project_kernel, head_count, group, shards), "project_pack",
        [((half, PAIR), bf16)] * group,
        [place], [out_weight, *upstreams],
        [((rows, width), bf16), ((group, half, PAIR), bf16)],
        flops=BUSY,
    )
    grads = swap(grads_send)
    keys, key_t, queries, picks = call(
        functools.partial(gather_kernel, head_count), "gather_keys",
        [
            ((near, PAIR), bf16), ((HEAD_SIZE, near), bf16), ((group, half, PAIR), bf16),
            ((count, PAIR), bf16),
        ],
        scalars, [sent, grads_send[0]],
    )
    other_picks = [segment_shift(picks, shift) for shift in range(1, others + 1)]
    extra, own_terms, other_terms, grads = call(
        functools.partial(far_kernel, head_count, group, others), "picked_rows",
        [
            ((PAIR + STAT_ROWS, count), bf16), ((count, PAIR), f32),
            ((others * count, PAIR), f32), ((group, half, PAIR), bf16),
        ],
        scalars, [keys, queries, picks, *other_picks, *grads],
        [((near + count * (1 + others), PAIR), bf16)] + [((count, PAIR), bf16)] * 2,
        flops=8 * near * count * PAIR,
    )
    back = [
        segment_shift(other_terms[(shift - 1) * count : shift * count], -shift)
        for shift in range(1, others + 1)
    ]
    steps = group // 2
    scratch = [((2, near, 2 * rows), bf16)]
    half_flops = 10 * near * near // 2 * PAIR
    acc, query_half = call(
        functools.partial(first_kernel, head_count, steps), "first_rows",
        [((near, PAIR), f32), ((steps, half, PAIR), bf16)],
        scalars, [keys, key_t, queries, grads, extra], scratch, half_flops,
    )
    near_send = call(
        functools.partial(second_kernel, head_count, group - steps, others), "second_rows",
        [((rows + half, PAIR), bf16)] * group,
        scalars, [keys, key_t, queries, grads, extra, acc, query_half, own_terms, *back],
        [((near, PAIR), f32), ((group, rows + half, PAIR), bf16)] + scratch, half_flops,
    )
    return tuple(
        call(
            functools.partial(unpack_kernel, head_count, group), "unpack",
            [((rows, width), bf16)] * 3,
            [place], swap(near_send),
            [((group, rows + half, PAIR), bf16)],
        )
    )


def solution(mesh):
    return jax.shard_map(
        body,
        mesh=mesh,
        in_specs=(
            P(("context", "heads"), None),
            P("heads", None),
            P("context", "heads"),
            P("context", "heads"),
            P("context", "heads"),
            P(),
        ),
        out_specs=(P("context", "heads"), P("context", "heads"), P("context", "heads")),
        check_vma=False,
    )
```

```python
import functools
import math

import jax
import jax.numpy as jnp
from jax import lax
from jax.experimental import pallas as pl
from jax.experimental.pallas import tpu as pltpu
from jax.sharding import PartitionSpec as P

HEAD_SIZE = 64
PAIR = 2 * HEAD_SIZE
DILATION_RATE = 16
FIRST_SEGMENT = 2048
SCALE = 1.0 / math.sqrt(HEAD_SIZE)
LOG2E = math.log2(math.e)
SCORE_FACTOR = SCALE * LOG2E
STRIP = 64
PIECE = 256
BUSY = 2**35
STAT_ROWS = 16

SMEM = pl.BlockSpec(memory_space=pltpu.SMEM)
VMEM = pl.BlockSpec(memory_space=pltpu.VMEM)
ANY = pl.BlockSpec(memory_space=pl.ANY)


def dot_nt(left, right):
    return lax.dot_general(
        left, right, (((1,), (1,)), ((), ())), preferred_element_type=jnp.float32
    )


def dot_nn(left, right):
    return jnp.dot(left, right, preferred_element_type=jnp.float32)


def head_columns(ref, head):
    return ref[:, head * HEAD_SIZE : (head + 1) * HEAD_SIZE]


def pick_matrix(offset, picked, rows):
    source = lax.broadcasted_iota(jnp.int32, (picked, rows), 1)
    index = lax.broadcasted_iota(jnp.int32, (picked, rows), 0)
    return (source == index * DILATION_RATE + offset).astype(jnp.bfloat16)


def spread_matrix(offset, first, picked, rows, axis):
    shape = (picked, rows) if axis == 0 else (rows, picked)
    index = lax.broadcasted_iota(jnp.int32, shape, axis)
    source = lax.broadcasted_iota(jnp.int32, shape, 1 - axis)
    return (source == (index - first) * DILATION_RATE + offset).astype(jnp.bfloat16)


def split_two(value):
    high = value.astype(jnp.bfloat16)
    low = (value - high.astype(jnp.float32)).astype(jnp.bfloat16)
    return high, low


def split_three(value):
    high = value.astype(jnp.bfloat16)
    rest = value - high.astype(jnp.float32)
    middle = rest.astype(jnp.bfloat16)
    low = (rest - middle.astype(jnp.float32)).astype(jnp.bfloat16)
    return high, middle, low


def fold(value, combine):
    parts = [value[start : start + 8] for start in range(0, value.shape[0], 8)]
    while len(parts) > 1:
        merged = [combine(parts[i], parts[i + 1]) for i in range(0, len(parts) - 1, 2)]
        parts = merged + parts[len(merged) * 2 :]
    return parts[0]


def left_half(shape):
    return lax.broadcasted_iota(jnp.int32, shape, 1) < HEAD_SIZE


def side_by_side(block):
    half = block.shape[0] // 2
    return jnp.concatenate([block[:half], block[half:]], 1)


def send_out(place, stage_ref, out_refs):
    for bits, out_ref in enumerate(out_refs):
        out_ref[...] = stage_ref[lax.bitwise_xor(place, bits)]


def pack_kernel(head_count, query_hbm, key_hbm, value_hbm, *refs):
    out_ref, query_ref, key_ref, value_ref, sems = refs
    rows = query_ref.shape[0]
    copies = [
        pltpu.make_async_copy(source, target, sems.at[index])
        for index, (source, target) in enumerate(
            [(key_hbm, key_ref), (value_hbm, value_ref), (query_hbm, query_ref)]
        )
    ]
    for copy in copies:
        copy.start()
    for copy in copies:
        copy.wait()
    for head in range(head_count):
        pair = jnp.concatenate([head_columns(key_ref, head), head_columns(value_ref, head)], 1)
        query = side_by_side(head_columns(query_ref, head))
        for place in range(head, out_ref.shape[0], head_count):
            out_ref[place, :rows, :] = pair
            out_ref[place, rows:, :] = query


def project_kernel(head_count, group, shards, place_ref, weight_ref, *refs):
    upstream_refs, refs = refs[:shards], refs[shards:]
    out_refs, (grad_ref, stage_ref) = refs[:group], refs[group:]
    shard_rows = upstream_refs[0].shape[0]
    for step, upstream_ref in enumerate(upstream_refs):
        owner = lax.rem(place_ref[1] + (shards - step), shards)
        start = pl.multiple_of(owner * shard_rows, shard_rows)
        grad_ref[pl.ds(start, shard_rows), :] = dot_nt(
            upstream_ref[...], weight_ref[...]
        ).astype(jnp.bfloat16)
    for head in range(head_count):
        grad = side_by_side(head_columns(grad_ref, head))
        for place in range(head, group, head_count):
            stage_ref[place] = grad
    send_out(place_ref[0], stage_ref, out_refs)


def own_offset(head_count, place_ref, offset_ref):
    return offset_ref[place_ref[1] * head_count + lax.rem(place_ref[0], head_count)]


def gather_kernel(
    head_count, place_ref, offset_ref, sent_ref, after_ref, keys_out, key_t_out, queries_out,
    picks_out,
):
    group = sent_ref.shape[0]
    rows = keys_out.shape[0] // group
    picked = rows // DILATION_RATE
    pick = pick_matrix(own_offset(head_count, place_ref, offset_ref), picked, rows)
    for place in range(group):
        pair = sent_ref[place, :rows, :]
        keys_out[place * rows : (place + 1) * rows, :] = pair
        picks_out[place * picked : (place + 1) * picked, :] = dot_nn(pick, pair).astype(
            jnp.bfloat16
        )
        queries_out[place] = sent_ref[place, rows:, :]
    key_t_out[...] = keys_out[...].astype(jnp.float32).T[:HEAD_SIZE].astype(jnp.bfloat16)


def query_and_grad(query_ref, grad_ref):
    query, grad = query_ref[...], grad_ref[...]
    zero = jnp.zeros((query.shape[0], HEAD_SIZE), query.dtype)
    return (
        jnp.concatenate(
            [
                jnp.concatenate([query[:, :HEAD_SIZE], zero], 1),
                jnp.concatenate([query[:, HEAD_SIZE:], zero], 1),
            ], 0,
        ),
        jnp.concatenate(
            [
                jnp.concatenate([zero, grad[:, :HEAD_SIZE]], 1),
                jnp.concatenate([zero, grad[:, HEAD_SIZE:]], 1),
            ], 0,
        ),
    )


def far_kernel(
    head_count, group, others, place_ref, offset_ref, near_ref, queries_ref, picks_ref, *refs
):
    other_refs, refs = refs[:others], refs[others:]
    grad_refs, refs = refs[:group], refs[group:]
    extra_out, own_out, other_out, grads_out, keys_ref, query_ref, grad_ref = refs
    near = near_ref.shape[0]
    rows = near // group
    picked = rows // DILATION_RATE
    count = group * picked
    far = count * (1 + others)
    pick = pick_matrix(own_offset(head_count, place_ref, offset_ref), picked, rows)
    keys_ref[:near, :] = near_ref[...]
    for index, ref in enumerate([picks_ref, *other_refs]):
        keys_ref[near + index * count : near + (index + 1) * count, :] = ref[...]
    for bits, ref in enumerate(grad_refs):
        grads_out[lax.bitwise_xor(place_ref[0], bits)] = ref[...]
    for step in range(group):
        query, grad = query_and_grad(queries_ref.at[step], grads_out.at[step])
        span = slice(step * picked, (step + 1) * picked)
        query_ref[span, :] = dot_nn(pick, query).astype(jnp.bfloat16)
        grad_ref[span, :] = dot_nn(pick, grad).astype(jnp.bfloat16)
    far_t = keys_ref[near:, :].astype(jnp.float32).T[:HEAD_SIZE].astype(jnp.bfloat16)
    query, grad = query_ref[...], grad_ref[...]
    score = dot_nt(keys_ref[...], query)
    dprob = dot_nt(keys_ref[...], grad)
    top = jnp.max(score, 0, keepdims=True)
    prob = jnp.exp2((score - top) * SCORE_FACTOR)
    total = jnp.sum(prob, 0, keepdims=True)
    inverse = 1.0 / total
    delta = jnp.sum(prob * dprob, 0, keepdims=True) * inverse
    prob_far = prob[near:] * inverse
    dscore = (prob_far * (dprob[near:] - delta)).astype(jnp.bfloat16)
    terms = dot_nn(
        jnp.concatenate([dscore, prob_far.astype(jnp.bfloat16)], 1),
        jnp.concatenate([query, grad], 0),
    ) * jnp.where(left_half((far, PAIR)), SCALE, 1.0)
    own_out[...] = terms[:count]
    other_out[...] = terms[count:]
    query_grad = dot_nn(far_t, dscore)
    lse = top * SCORE_FACTOR + jnp.log2(total)
    extra_out[:PAIR, :] = jnp.concatenate(split_two(query_grad), 0)
    blank = jnp.zeros((STAT_ROWS - 6, count), jnp.bfloat16)
    extra_out[PAIR:, :] = jnp.concatenate([*split_three(lse), *split_three(delta), blank], 0)


def near_blocks(
    places, offset, keys_ref, key_t_ref, queries_ref, grads_ref, extra_ref,
    prob_ref, dprob_ref, work_ref, top_ref, acc_ref, emit,
):
    near = keys_ref.shape[0]
    rows = prob_ref.shape[2]
    half = rows // 2
    count = extra_ref.shape[1]
    row_lane = lax.broadcasted_iota(jnp.int32, (1, rows), 1)
    picked = lax.rem(row_lane, DILATION_RATE) == offset

    def by_eight(value):
        return value.reshape(value.shape[0] // 8, 8, rows)

    def weights_of(index):
        return query_and_grad(queries_ref.at[places[index]], grads_ref.at[places[index]])

    def columns_of(ref):
        packed = ref[...].astype(jnp.float32).T
        return jnp.concatenate([packed[:HEAD_SIZE], packed[HEAD_SIZE:]], 1).astype(jnp.bfloat16)

    def transposed_of(index):
        zero = jnp.zeros((HEAD_SIZE, rows), jnp.bfloat16)
        query = columns_of(queries_ref.at[places[index]])
        grad = columns_of(grads_ref.at[places[index]])
        return jnp.concatenate(
            [jnp.concatenate([query, zero], 0), jnp.concatenate([zero, grad], 0)], 1
        )

    def first_pass(index, weights, start, state):
        top, total, delta = state
        slot = index % 2
        products = dot_nn(keys_ref[start : start + PIECE, :], weights)
        scores, dprobs = products[:, :rows], products[:, rows:]
        for inner in range(0, PIECE, STRIP):
            strip = slice(start + inner, start + inner + STRIP)
            score, dprob = scores[inner : inner + STRIP], dprobs[inner : inner + STRIP]
            part = fold(score, jnp.maximum) * SCORE_FACTOR
            raised = part if top is None else jnp.maximum(top, part)
            prob = jnp.exp2(by_eight(score) * SCORE_FACTOR - raised[None])
            part_total = jnp.sum(prob, 0)
            part_delta = jnp.sum(prob * by_eight(dprob), 0)
            if top is None:
                total, delta = part_total, part_delta
            else:
                shrink = jnp.exp2(top - raised)
                total, delta = total * shrink + part_total, delta * shrink + part_delta
            top = raised
            prob_ref[slot, strip, :] = prob.reshape(STRIP, rows)
            dprob_ref[slot, strip, :] = dprob
            top_ref[slot, strip.start // STRIP] = raised
        return top, total, delta

    def last_pass(index, lse, delta, both, start, query_grad):
        slot = index % 2
        piece = slice(start, start + PIECE)
        for inner in range(0, PIECE, STRIP):
            strip = slice(start + inner, start + inner + STRIP)
            factor = jnp.exp2(top_ref[slot, strip.start // STRIP] - lse)
            prob = by_eight(prob_ref[slot, strip, :]) * factor[None]
            dscore = prob * (by_eight(dprob_ref[slot, strip, :]) - delta)
            work_ref[slot, strip, :rows] = dscore.reshape(STRIP, rows).astype(jnp.bfloat16)
            work_ref[slot, strip, rows:] = prob.reshape(STRIP, rows).astype(jnp.bfloat16)
        acc_ref[piece, :] += dot_nn(work_ref[slot, piece, :], both)
        return query_grad + dot_nn(key_t_ref[:, piece], work_ref[slot, piece, :rows])

    starts = range(0, near, PIECE)
    weights = transposed_of(0)
    state = (None, None, None)
    for start in starts:
        state = first_pass(0, weights, start, state)
    for index, place in enumerate(places):
        last = index + 1 == len(places)
        first = place * (rows // DILATION_RATE)
        extra = dot_nn(extra_ref[...], spread_matrix(offset, first, count, rows, 0))
        stats = [extra[PAIR + row : PAIR + row + 1] for row in range(6)]
        top, total, delta = state
        highest = jnp.max(top, 0, keepdims=True)
        shrink = jnp.exp2(top - highest)
        total = jnp.sum(total * shrink, 0, keepdims=True)
        delta = jnp.sum(delta * shrink, 0, keepdims=True) / total
        lse = jnp.where(picked, stats[0] + stats[1] + stats[2], highest + jnp.log2(total))
        delta = jnp.where(picked, stats[3] + stats[4] + stats[5], delta)
        both = jnp.concatenate(weights_of(index), 0)
        query_grad = extra[:HEAD_SIZE] + extra[HEAD_SIZE:PAIR]
        weights = None if last else transposed_of(index + 1)
        state = (None, None, None)
        for start in starts:
            if not last:
                state = first_pass(index + 1, weights, start, state)
            query_grad = last_pass(index, lse, delta, both, start, query_grad)
        query_grad = (query_grad * SCALE).T.astype(jnp.bfloat16)
        emit(place, jnp.concatenate([query_grad[:half], query_grad[half:]], 1))


def first_kernel(
    head_count, steps, place_ref, offset_ref, keys_ref, key_t_ref, queries_ref, grads_ref,
    extra_ref, acc_ref, query_out, *scratch,
):
    offset = own_offset(head_count, place_ref, offset_ref)
    acc_ref[...] = jnp.zeros_like(acc_ref)

    def emit(place, query_grad):
        query_out[place] = query_grad

    near_blocks(
        range(steps), offset, keys_ref, key_t_ref, queries_ref, grads_ref, extra_ref,
        *scratch, acc_ref, emit,
    )


def second_kernel(
    head_count, steps, others, place_ref, offset_ref, keys_ref, key_t_ref, queries_ref, grads_ref,
    extra_ref, start_ref, query_ref, own_ref, *refs,
):
    back_refs, refs = refs[:others], refs[others:]
    rows = query_ref.shape[1] * 2
    group = keys_ref.shape[0] // rows
    out_refs, refs = refs[:group], refs[group:]
    acc_ref, stage_ref, *scratch = refs
    count = extra_ref.shape[1]
    picked = count // group
    offset = own_offset(head_count, place_ref, offset_ref)
    acc_ref[...] = start_ref[...]

    def emit(place, query_grad):
        stage_ref[place, rows:, :] = query_grad

    near_blocks(
        range(group - steps, group), offset, keys_ref, key_t_ref, queries_ref, grads_ref, extra_ref,
        *scratch, acc_ref, emit,
    )
    terms = own_ref[...]
    for back_ref in back_refs:
        terms = terms + back_ref[...]
    terms = jnp.concatenate(split_two(terms), 0)
    factor = jnp.where(left_half((rows, PAIR)), SCALE, 1.0)
    for place in range(group):
        spread = spread_matrix(offset, place * picked, count, rows, 1)
        placed = dot_nn(jnp.concatenate([spread, spread], 1), terms)
        summed = acc_ref[place * rows : (place + 1) * rows, :] * factor + placed
        stage_ref[place, :rows, :] = summed.astype(jnp.bfloat16)
        if place < group - steps:
            stage_ref[place, rows:, :] = query_ref[place]
    send_out(place_ref[0], stage_ref, out_refs)


def unpack_kernel(head_count, group, place_ref, *refs):
    near_refs, refs = refs[:group], refs[group:]
    query_out, key_out, value_out, stage_ref = refs
    rows = query_out.shape[0]
    half = rows // 2
    for bits, near_ref in enumerate(near_refs):
        stage_ref[lax.bitwise_xor(place_ref[0], bits)] = near_ref[...]
    for head in range(head_count):
        columns = slice(head * HEAD_SIZE, (head + 1) * HEAD_SIZE)
        key_out[:, columns] = stage_ref[head, :rows, :HEAD_SIZE]
        value_out[:, columns] = stage_ref[head, :rows, HEAD_SIZE:]
        query_out[:half, columns] = stage_ref[head, rows:, :HEAD_SIZE]
        query_out[half:, columns] = stage_ref[head, rows:, HEAD_SIZE:]


def call(kernel, name, out_shape, scalars, operands, scratch=(), flops=0, space=VMEM, limit=40):
    return pl.pallas_call(
        kernel,
        out_shape=tuple(jax.ShapeDtypeStruct(*shape) for shape in out_shape),
        in_specs=[SMEM] * len(scalars) + [space] * len(operands),
        out_specs=tuple(VMEM for _ in out_shape),
        scratch_shapes=[
            pltpu.VMEM(*shape) if isinstance(shape, tuple) else shape for shape in scratch
        ],
        compiler_params=pltpu.CompilerParams(vmem_limit_bytes=limit * 1024 * 1024),
        cost_estimate=pl.CostEstimate(flops=flops, bytes_accessed=2**21, transcendentals=0),
        name=name,
    )(*scalars, *operands)


def body(upstream, out_weight, query_rows, key_rows, value_rows, head_offsets):
    rows, width = query_rows.shape
    head_count = width // HEAD_SIZE
    devices = lax.axis_size("context")
    shards = lax.axis_size("heads")
    group = FIRST_SEGMENT // rows
    others = devices // group - 1
    half = rows // 2
    picked = rows // DILATION_RATE
    count = group * picked
    near = group * rows
    place = jnp.stack(
        [lax.rem(lax.axis_index("context"), group), lax.axis_index("heads")]
    ).astype(jnp.int32)
    scalars = [place, head_offsets]

    def swap(values):
        pairs = [[(source, source ^ bits) for source in range(devices)] for bits in range(group)]
        return [values[0]] + [
            lax.ppermute(values[bits], "context", pairs[bits]) for bits in range(1, group)
        ]

    def exchange(value):
        groups = [list(range(first, first + group)) for first in range(0, devices, group)]
        return lax.all_to_all(value, "context", 0, 0, axis_index_groups=groups)

    def segment_shift(value, shift):
        pairs = [(source, (source + shift * group) % devices) for source in range(devices)]
        return lax.ppermute(value, "context", pairs)

    upstreams = [upstream]
    for step in range(1, shards):
        pairs = [(source, (source + step) % shards) for source in range(shards)]
        upstreams.append(lax.ppermute(upstream, "heads", pairs))

    bf16, f32 = jnp.bfloat16, jnp.float32
    (sent,) = call(
        functools.partial(pack_kernel, head_count), "pack_rows",
        [((group, rows + half, PAIR), bf16)],
        [], [query_rows, key_rows, value_rows],
        [((rows, width), bf16)] * 3 + [pltpu.SemaphoreType.DMA((3,))],
        flops=2**31, space=ANY, limit=60,
    )
    sent = exchange(sent)
    grads_send = call(
        functools.partial(project_kernel, head_count, group, shards), "project_pack",
        [((half, PAIR), bf16)] * group,
        [place], [out_weight, *upstreams],
        [((rows, width), bf16), ((group, half, PAIR), bf16)],
        flops=BUSY,
    )
    grads = swap(grads_send)
    keys, key_t, queries, picks = call(
        functools.partial(gather_kernel, head_count), "gather_keys",
        [
            ((near, PAIR), bf16), ((HEAD_SIZE, near), bf16), ((group, half, PAIR), bf16),
            ((count, PAIR), bf16),
        ],
        scalars, [sent, grads_send[0]],
    )
    other_picks = [segment_shift(picks, shift) for shift in range(1, others + 1)]
    extra, own_terms, other_terms, grads = call(
        functools.partial(far_kernel, head_count, group, others), "picked_rows",
        [
            ((PAIR + STAT_ROWS, count), bf16), ((count, PAIR), f32),
            ((others * count, PAIR), f32), ((group, half, PAIR), bf16),
        ],
        scalars, [keys, queries, picks, *other_picks, *grads],
        [((near + count * (1 + others), PAIR), bf16)] + [((count, PAIR), bf16)] * 2,
        flops=8 * near * count * PAIR,
    )
    back = [
        segment_shift(other_terms[(shift - 1) * count : shift * count], -shift)
        for shift in range(1, others + 1)
    ]
    steps = group // 2
    scratch = [
        ((2, near, rows), f32), ((2, near, rows), f32), ((2, near, 2 * rows), bf16),
        ((2, near // STRIP, 8, rows), f32),
    ]
    half_flops = 10 * near * near // 2 * PAIR
    acc, query_half = call(
        functools.partial(first_kernel, head_count, steps), "first_rows",
        [((near, PAIR), f32), ((steps, half, PAIR), bf16)],
        scalars, [keys, key_t, queries, grads, extra], scratch, half_flops,
    )
    near_send = call(
        functools.partial(second_kernel, head_count, group - steps, others), "second_rows",
        [((rows + half, PAIR), bf16)] * group,
        scalars, [keys, key_t, queries, grads, extra, acc, query_half, own_terms, *back],
        [((near, PAIR), f32), ((group, rows + half, PAIR), bf16)] + scratch, half_flops,
    )
    return tuple(
        call(
            functools.partial(unpack_kernel, head_count, group), "unpack",
            [((rows, width), bf16)] * 3,
            [place], swap(near_send),
            [((group, rows + half, PAIR), bf16)],
        )
    )


def solution(mesh):
    return jax.shard_map(
        body,
        mesh=mesh,
        in_specs=(
            P(("context", "heads"), None),
            P("heads", None),
            P("context", "heads"),
            P("context", "heads"),
            P("context", "heads"),
            P(),
        ),
        out_specs=(P("context", "heads"), P("context", "heads"), P("context", "heads")),
        check_vma=False,
    )
```

```python
import functools
import math

import jax
import jax.numpy as jnp
from jax import lax
from jax.experimental import pallas as pl
from jax.experimental.pallas import tpu as pltpu
from jax.sharding import PartitionSpec as P

HEAD_SIZE = 64
PAIR = 2 * HEAD_SIZE
DILATION_RATE = 16
FIRST_SEGMENT = 2048
SCALE = 1.0 / math.sqrt(HEAD_SIZE)
LOG2E = math.log2(math.e)
SCORE_FACTOR = SCALE * LOG2E
STRIP = 64
PIECE = 256
BUSY = 2**35
NEVER = -1e30

SMEM = pl.BlockSpec(memory_space=pltpu.SMEM)
VMEM = pl.BlockSpec(memory_space=pltpu.VMEM)
ANY = pl.BlockSpec(memory_space=pl.ANY)


def dot_nt(left, right):
    return lax.dot_general(
        left, right, (((1,), (1,)), ((), ())), preferred_element_type=jnp.float32
    )


def dot_nn(left, right):
    return jnp.dot(left, right, preferred_element_type=jnp.float32)


def head_columns(ref, head):
    return ref[:, head * HEAD_SIZE : (head + 1) * HEAD_SIZE]


def pick_matrix(offset, picked, rows):
    source = lax.broadcasted_iota(jnp.int32, (picked, rows), 1)
    index = lax.broadcasted_iota(jnp.int32, (picked, rows), 0)
    return (source == index * DILATION_RATE + offset).astype(jnp.bfloat16)


def spread_matrix(offset, first, picked, rows, axis):
    shape = (picked, rows) if axis == 0 else (rows, picked)
    index = lax.broadcasted_iota(jnp.int32, shape, axis)
    source = lax.broadcasted_iota(jnp.int32, shape, 1 - axis)
    return (source == (index - first) * DILATION_RATE + offset).astype(jnp.bfloat16)


def split_two(value):
    high = value.astype(jnp.bfloat16)
    low = (value - high.astype(jnp.float32)).astype(jnp.bfloat16)
    return high, low


def fold(value, combine):
    parts = [value[start : start + 8] for start in range(0, value.shape[0], 8)]
    while len(parts) > 1:
        merged = [combine(parts[i], parts[i + 1]) for i in range(0, len(parts) - 1, 2)]
        parts = merged + parts[len(merged) * 2 :]
    return parts[0]


def left_half(shape):
    return lax.broadcasted_iota(jnp.int32, shape, 1) < HEAD_SIZE


def side_by_side(block):
    half = block.shape[0] // 2
    return jnp.concatenate([block[:half], block[half:]], 1)


def send_out(place, stage_ref, out_refs):
    for bits, out_ref in enumerate(out_refs):
        out_ref[...] = stage_ref[lax.bitwise_xor(place, bits)]


def pack_kernel(head_count, key_hbm, value_hbm, out_ref, key_ref, value_ref, sems):
    copies = [
        pltpu.make_async_copy(source, target, sems.at[index])
        for index, (source, target) in enumerate([(key_hbm, key_ref), (value_hbm, value_ref)])
    ]
    for copy in copies:
        copy.start()
    for copy in copies:
        copy.wait()
    for head in range(head_count):
        pair = jnp.concatenate([head_columns(key_ref, head), head_columns(value_ref, head)], 1)
        for place in range(head, out_ref.shape[0], head_count):
            out_ref[place] = pair


def project_kernel(head_count, group, shards, place_ref, weight_ref, query_ref, *refs):
    upstream_refs, refs = refs[:shards], refs[shards:]
    out_refs, (grad_ref, stage_ref) = refs[:group], refs[group:]
    shard_rows = upstream_refs[0].shape[0]
    for step, upstream_ref in enumerate(upstream_refs):
        owner = lax.rem(place_ref[1] + (shards - step), shards)
        start = pl.multiple_of(owner * shard_rows, shard_rows)
        grad_ref[pl.ds(start, shard_rows), :] = dot_nt(
            upstream_ref[...], weight_ref[...]
        ).astype(jnp.bfloat16)
    for head in range(head_count):
        pair = jnp.concatenate([head_columns(query_ref, head), head_columns(grad_ref, head)], 1)
        for place in range(head, group, head_count):
            stage_ref[place] = pair
    send_out(place_ref[0], stage_ref, out_refs)


def own_offset(head_count, place_ref, offset_ref):
    return offset_ref[place_ref[1] * head_count + lax.rem(place_ref[0], head_count)]


def gather_kernel(
    head_count, group, place_ref, offset_ref, keys_ref, after_ref, key_t_out, picks_out
):
    rows = keys_ref.shape[0] // group
    picked = rows // DILATION_RATE
    pick = pick_matrix(own_offset(head_count, place_ref, offset_ref), picked, rows)
    for place in range(group):
        picks_out[place * picked : (place + 1) * picked, :] = dot_nn(
            pick, keys_ref[place * rows : (place + 1) * rows, :]
        ).astype(jnp.bfloat16)
    key_t_out[...] = keys_ref[...].astype(jnp.float32).T[:HEAD_SIZE].astype(jnp.bfloat16)


def halves(both):
    left = left_half(both.shape)
    zero = jnp.zeros((), both.dtype)
    return jnp.where(left, both, zero), jnp.where(left, zero, both)


def far_kernel(
    head_count, group, others, place_ref, offset_ref, near_ref, start_ref, picks_ref, *refs
):
    other_refs, refs = refs[:others], refs[others:]
    block_refs, refs = refs[:group], refs[group:]
    acc_out, query_out, own_out, other_out, keys_ref, rows_ref = refs
    near = near_ref.shape[0]
    rows = near // group
    picked = rows // DILATION_RATE
    count = group * picked
    far = count * (1 + others)
    pick = pick_matrix(own_offset(head_count, place_ref, offset_ref), picked, rows)
    keys_ref[:near, :] = near_ref[...]
    for index, ref in enumerate([picks_ref, *other_refs]):
        keys_ref[near + index * count : near + (index + 1) * count, :] = ref[...]
    for bits, ref in enumerate(block_refs):
        rows_ref[bits * picked : (bits + 1) * picked, :] = dot_nn(pick, ref[...]).astype(
            jnp.bfloat16
        )
    key_t = keys_ref[...].astype(jnp.float32).T[:HEAD_SIZE].astype(jnp.bfloat16)
    query, grad = halves(rows_ref[...])
    score = dot_nt(keys_ref[...], query)
    dprob = dot_nt(keys_ref[...], grad)
    top = jnp.max(score, 0, keepdims=True)
    prob = jnp.exp2((score - top) * SCORE_FACTOR)
    inverse = 1.0 / jnp.sum(prob, 0, keepdims=True)
    delta = jnp.sum(prob * dprob, 0, keepdims=True) * inverse
    prob = prob * inverse
    dscore = (prob * (dprob - delta)).astype(jnp.bfloat16)
    terms = dot_nn(
        jnp.concatenate([dscore, prob.astype(jnp.bfloat16)], 1), jnp.concatenate([query, grad], 0)
    )
    acc_out[...] = start_ref[...] + terms[:near]
    terms = terms[near:] * jnp.where(left_half((far, PAIR)), SCALE, 1.0)
    own_out[...] = terms[:count]
    other_out[...] = terms[count:]
    query_grad = (dot_nn(key_t, dscore) * SCALE).T.astype(jnp.bfloat16)
    zero = jnp.zeros_like(query_grad)
    query_out[:count, :] = jnp.concatenate([query_grad, zero], 1)
    query_out[count:, :] = jnp.concatenate([zero, query_grad], 1)


def near_blocks(
    offset, keys_ref, key_t_ref, block_refs, prob_ref, dprob_ref, work_ref, top_ref, acc_ref, emit
):
    near = keys_ref.shape[0]
    rows = prob_ref.shape[2]
    half = rows // 2
    row_lane = lax.broadcasted_iota(jnp.int32, (1, rows), 1)
    picked = lax.rem(row_lane, DILATION_RATE) == offset

    def by_eight(value):
        return value.reshape(value.shape[0] // 8, 8, rows)

    def transposed_of(index):
        both = block_refs[index][...].astype(jnp.float32).T.astype(jnp.bfloat16)
        zero = jnp.zeros((HEAD_SIZE, rows), jnp.bfloat16)
        query, grad = both[:HEAD_SIZE], both[HEAD_SIZE:]
        return jnp.concatenate(
            [jnp.concatenate([query, zero], 0), jnp.concatenate([zero, grad], 0)], 1
        )

    def first_pass(index, weights, start, state):
        top, total, delta = state
        slot = index % 2
        products = dot_nn(keys_ref[start : start + PIECE, :], weights)
        scores, dprobs = products[:, :rows], products[:, rows:]
        for inner in range(0, PIECE, STRIP):
            strip = slice(start + inner, start + inner + STRIP)
            score, dprob = scores[inner : inner + STRIP], dprobs[inner : inner + STRIP]
            part = fold(score, jnp.maximum) * SCORE_FACTOR
            raised = part if top is None else jnp.maximum(top, part)
            prob = jnp.exp2(by_eight(score) * SCORE_FACTOR - raised[None])
            part_total = jnp.sum(prob, 0)
            part_delta = jnp.sum(prob * by_eight(dprob), 0)
            if top is None:
                total, delta = part_total, part_delta
            else:
                shrink = jnp.exp2(top - raised)
                total, delta = total * shrink + part_total, delta * shrink + part_delta
            top = raised
            prob_ref[slot, strip, :] = prob.reshape(STRIP, rows)
            dprob_ref[slot, strip, :] = dprob
            top_ref[slot, strip.start // STRIP] = raised
        return top, total, delta

    def last_pass(index, lse, delta, both, start, query_grad):
        slot = index % 2
        piece = slice(start, start + PIECE)
        for inner in range(0, PIECE, STRIP):
            strip = slice(start + inner, start + inner + STRIP)
            factor = jnp.exp2(top_ref[slot, strip.start // STRIP] - lse)
            prob = by_eight(prob_ref[slot, strip, :]) * factor[None]
            dscore = prob * (by_eight(dprob_ref[slot, strip, :]) - delta)
            work_ref[slot, strip, :rows] = dscore.reshape(STRIP, rows).astype(jnp.bfloat16)
            work_ref[slot, strip, rows:] = prob.reshape(STRIP, rows).astype(jnp.bfloat16)
        acc_ref[piece, :] += dot_nn(work_ref[slot, piece, :], both)
        return query_grad + dot_nn(key_t_ref[:, piece], work_ref[slot, piece, :rows])

    starts = range(0, near, PIECE)
    weights = transposed_of(0)
    state = (None, None, None)
    for start in starts:
        state = first_pass(0, weights, start, state)
    for index, block_ref in enumerate(block_refs):
        last = index + 1 == len(block_refs)
        top, total, delta = state
        highest = jnp.max(top, 0, keepdims=True)
        shrink = jnp.exp2(top - highest)
        total = jnp.sum(total * shrink, 0, keepdims=True)
        delta = jnp.sum(delta * shrink, 0, keepdims=True) / total
        lse = jnp.where(picked, -NEVER, highest + jnp.log2(total))
        both = jnp.concatenate(halves(block_ref[...]), 0)
        query_grad = jnp.zeros((HEAD_SIZE, rows), jnp.float32)
        weights = None if last else transposed_of(index + 1)
        state = (None, None, None)
        for start in starts:
            if not last:
                state = first_pass(index + 1, weights, start, state)
            query_grad = last_pass(index, lse, delta, both, start, query_grad)
        query_grad = (query_grad * SCALE).T.astype(jnp.bfloat16)
        emit(index, jnp.concatenate([query_grad[:half], query_grad[half:]], 1))


def some_kernel(head_count, steps, begin, place_ref, offset_ref, keys_ref, key_t_ref, *refs):
    if not begin:
        start_ref, refs = refs[0], refs[1:]
    block_refs, (acc_ref, query_out, *scratch) = refs[:steps], refs[steps:]
    acc_ref[...] = jnp.zeros_like(acc_ref) if begin else start_ref[...]

    def emit(index, query_grad):
        query_out[index] = query_grad

    near_blocks(
        own_offset(head_count, place_ref, offset_ref), keys_ref, key_t_ref, block_refs,
        *scratch, acc_ref, emit,
    )


def end_kernel(
    head_count, steps, others, place_ref, offset_ref, keys_ref, key_t_ref, start_ref, query_ref,
    later_query_ref, picked_query_ref, own_ref, *refs,
):
    back_refs, refs = refs[:others], refs[others:]
    block_refs, refs = refs[:steps], refs[steps:]
    half = query_ref.shape[1]
    rows = 2 * half
    group = keys_ref.shape[0] // rows
    out_refs, refs = refs[:group], refs[group:]
    acc_ref, *scratch = refs
    count = own_ref.shape[0]
    picked = count // group
    offset = own_offset(head_count, place_ref, offset_ref)
    acc_ref[...] = start_ref[...]

    def finish(bits, query_grad):
        spread = spread_matrix(offset, bits * picked, count, rows, 1)
        spread = jnp.concatenate([spread[:half], spread[half:]], 1)
        placed = dot_nn(spread, picked_query_ref[...])
        out_refs[bits][rows:, :] = (query_grad.astype(jnp.float32) + placed).astype(jnp.bfloat16)

    def emit(index, query_grad):
        finish(group - steps + index, query_grad)

    near_blocks(offset, keys_ref, key_t_ref, block_refs, *scratch, acc_ref, emit)
    terms = own_ref[...]
    for back_ref in back_refs:
        terms = terms + back_ref[...]
    terms = jnp.concatenate(split_two(terms), 0)
    factor = jnp.where(left_half((rows, PAIR)), SCALE, 1.0)
    for bits in range(group):
        place = lax.bitwise_xor(place_ref[0], bits)
        spread = spread_matrix(offset, place * picked, count, rows, 1)
        placed = dot_nn(jnp.concatenate([spread, spread], 1), terms)
        acc = acc_ref[pl.ds(pl.multiple_of(place * rows, rows), rows), :]
        out_refs[bits][:rows, :] = (acc * factor + placed).astype(jnp.bfloat16)
        done = query_ref.shape[0]
        if bits < done:
            finish(bits, query_ref[bits])
        elif bits < group - steps:
            finish(bits, later_query_ref[bits - done])


def unpack_kernel(head_count, group, place_ref, *refs):
    near_refs, refs = refs[:group], refs[group:]
    query_out, key_out, value_out, stage_ref = refs
    rows = query_out.shape[0]
    half = rows // 2
    for bits, near_ref in enumerate(near_refs):
        stage_ref[lax.bitwise_xor(place_ref[0], bits)] = near_ref[...]
    for head in range(head_count):
        columns = slice(head * HEAD_SIZE, (head + 1) * HEAD_SIZE)
        key_out[:, columns] = stage_ref[head, :rows, :HEAD_SIZE]
        value_out[:, columns] = stage_ref[head, :rows, HEAD_SIZE:]
        query_out[:half, columns] = stage_ref[head, rows:, :HEAD_SIZE]
        query_out[half:, columns] = stage_ref[head, rows:, HEAD_SIZE:]


def call(kernel, name, out_shape, scalars, operands, scratch=(), flops=0, space=VMEM, limit=40):
    return pl.pallas_call(
        kernel,
        out_shape=tuple(jax.ShapeDtypeStruct(*shape) for shape in out_shape),
        in_specs=[SMEM] * len(scalars) + [space] * len(operands),
        out_specs=tuple(VMEM for _ in out_shape),
        scratch_shapes=[
            pltpu.VMEM(*shape) if isinstance(shape, tuple) else shape for shape in scratch
        ],
        compiler_params=pltpu.CompilerParams(vmem_limit_bytes=limit * 1024 * 1024),
        cost_estimate=pl.CostEstimate(flops=flops, bytes_accessed=2**21, transcendentals=0),
        name=name,
    )(*scalars, *operands)


def body(upstream, out_weight, query_rows, key_rows, value_rows, head_offsets):
    rows, width = query_rows.shape
    head_count = width // HEAD_SIZE
    devices = lax.axis_size("context")
    shards = lax.axis_size("heads")
    group = FIRST_SEGMENT // rows
    others = devices // group - 1
    half = rows // 2
    picked = rows // DILATION_RATE
    count = group * picked
    near = group * rows
    place = jnp.stack(
        [lax.rem(lax.axis_index("context"), group), lax.axis_index("heads")]
    ).astype(jnp.int32)
    scalars = [place, head_offsets]

    def swap(values):
        pairs = [[(source, source ^ bits) for source in range(devices)] for bits in range(group)]
        return [values[0]] + [
            lax.ppermute(values[bits], "context", pairs[bits]) for bits in range(1, group)
        ]

    def exchange(value):
        groups = [list(range(first, first + group)) for first in range(0, devices, group)]
        return lax.all_to_all(value, "context", 0, 0, axis_index_groups=groups)

    def segment_shift(value, shift):
        pairs = [(source, (source + shift * group) % devices) for source in range(devices)]
        return lax.ppermute(value, "context", pairs)

    upstreams = [upstream]
    for step in range(1, shards):
        pairs = [(source, (source + step) % shards) for source in range(shards)]
        upstreams.append(lax.ppermute(upstream, "heads", pairs))

    bf16, f32 = jnp.bfloat16, jnp.float32
    (sent,) = call(
        functools.partial(pack_kernel, head_count), "pack_rows",
        [((group, rows, PAIR), bf16)],
        [], [key_rows, value_rows],
        [((rows, width), bf16)] * 2 + [pltpu.SemaphoreType.DMA((2,))],
        flops=2**31, space=ANY, limit=60,
    )
    groups = [list(range(first, first + group)) for first in range(0, devices, group)]
    sent = lax.all_to_all(sent, "context", 0, 0, axis_index_groups=groups)
    blocks_send = call(
        functools.partial(project_kernel, head_count, group, shards), "project_pack",
        [((rows, PAIR), bf16)] * group,
        [place], [out_weight, query_rows, *upstreams],
        [((rows, width), bf16), ((group, rows, PAIR), bf16)],
        flops=BUSY,
    )
    blocks = swap(blocks_send)
    keys = sent.reshape(near, PAIR)
    key_t, picks = call(
        functools.partial(gather_kernel, head_count, group), "gather_keys",
        [((HEAD_SIZE, near), bf16), ((count, PAIR), bf16)],
        scalars, [keys, blocks_send[0]],
    )
    other_picks = [segment_shift(picks, shift) for shift in range(1, others + 1)]
    steps = group // 2
    scratch = [
        ((2, near, rows), f32), ((2, near, rows), f32), ((2, near, 2 * rows), bf16),
        ((2, near // STRIP, 8, rows), f32),
    ]
    half_flops = 30 * near * near // 2 * PAIR
    early, late = blocks[:steps], blocks[steps:-1]
    acc, query_early = call(
        functools.partial(some_kernel, head_count, len(early), True), "first_rows",
        [((near, PAIR), f32), ((len(early), half, PAIR), bf16)],
        scalars, [keys, key_t, *early], scratch, half_flops,
    )
    acc, picked_query, own_terms, other_terms = call(
        functools.partial(far_kernel, head_count, group, others), "picked_rows",
        [
            ((near, PAIR), f32), ((2 * count, PAIR), bf16), ((count, PAIR), f32),
            ((others * count, PAIR), f32),
        ],
        scalars, [keys, acc, picks, *other_picks, *blocks],
        [((near + count * (1 + others), PAIR), bf16), ((count, PAIR), bf16)],
        flops=20 * near * count * PAIR,
    )
    back = [
        segment_shift(other_terms[(shift - 1) * count : shift * count], -shift)
        for shift in range(1, others + 1)
    ]
    acc, query_late = call(
        functools.partial(some_kernel, head_count, len(late), False), "second_rows",
        [((near, PAIR), f32), ((len(late), half, PAIR), bf16)],
        scalars, [keys, key_t, acc, *late], scratch, half_flops,
    )
    near_send = call(
        functools.partial(end_kernel, head_count, 1, others), "last_rows",
        [((rows + half, PAIR), bf16)] * group,
        scalars,
        [
            keys, key_t, acc, query_early, query_late, picked_query, own_terms, *back, blocks[-1],
        ],
        [((near, PAIR), f32)] + scratch, half_flops // steps,
    )
    return tuple(
        call(
            functools.partial(unpack_kernel, head_count, group), "unpack",
            [((rows, width), bf16)] * 3,
            [place], swap(near_send),
            [((group, rows + half, PAIR), bf16)],
        )
    )


def solution(mesh):
    return jax.shard_map(
        body,
        mesh=mesh,
        in_specs=(
            P(("context", "heads"), None),
            P("heads", None),
            P("context", "heads"),
            P("context", "heads"),
            P("context", "heads"),
            P(),
        ),
        out_specs=(P("context", "heads"), P("context", "heads"), P("context", "heads")),
        check_vma=False,
    )
```

```python
import functools
import math

import jax
import jax.numpy as jnp
from jax import lax
from jax.experimental import pallas as pl
from jax.experimental.pallas import tpu as pltpu
from jax.sharding import PartitionSpec as P

HEAD_SIZE = 64
PAIR = 2 * HEAD_SIZE
DILATION_RATE = 16
FIRST_SEGMENT = 2048
SCALE = 1.0 / math.sqrt(HEAD_SIZE)
LOG2E = math.log2(math.e)
SCORE_FACTOR = SCALE * LOG2E
STRIP = 64
PIECE = 256
BUSY = 2**35
NEVER = -1e30

SMEM = pl.BlockSpec(memory_space=pltpu.SMEM)
VMEM = pl.BlockSpec(memory_space=pltpu.VMEM)
ANY = pl.BlockSpec(memory_space=pl.ANY)


def dot_nt(left, right):
    return lax.dot_general(
        left, right, (((1,), (1,)), ((), ())), preferred_element_type=jnp.float32
    )


def dot_nn(left, right):
    return jnp.dot(left, right, preferred_element_type=jnp.float32)


def head_columns(ref, head):
    return ref[:, head * HEAD_SIZE : (head + 1) * HEAD_SIZE]


def pick_matrix(offset, picked, rows):
    source = lax.broadcasted_iota(jnp.int32, (picked, rows), 1)
    index = lax.broadcasted_iota(jnp.int32, (picked, rows), 0)
    return (source == index * DILATION_RATE + offset).astype(jnp.bfloat16)


def spread_matrix(offset, first, picked, rows, axis):
    shape = (picked, rows) if axis == 0 else (rows, picked)
    index = lax.broadcasted_iota(jnp.int32, shape, axis)
    source = lax.broadcasted_iota(jnp.int32, shape, 1 - axis)
    return (source == (index - first) * DILATION_RATE + offset).astype(jnp.bfloat16)


def split_two(value):
    high = value.astype(jnp.bfloat16)
    low = (value - high.astype(jnp.float32)).astype(jnp.bfloat16)
    return high, low


def fold(value, combine):
    parts = [value[start : start + 8] for start in range(0, value.shape[0], 8)]
    while len(parts) > 1:
        merged = [combine(parts[i], parts[i + 1]) for i in range(0, len(parts) - 1, 2)]
        parts = merged + parts[len(merged) * 2 :]
    return parts[0]


def left_half(shape):
    return lax.broadcasted_iota(jnp.int32, shape, 1) < HEAD_SIZE


def side_by_side(block):
    half = block.shape[0] // 2
    return jnp.concatenate([block[:half], block[half:]], 1)


def swap_steps(group):
    if group == 8:
        return [(2, 4), (4, 2), (7, 1), (1, 7), (3, 5), (5, 3), (6, 6)]
    return [(bits, bits) for bits in range(1, group)]


def mirrored(step):
    return (step[1], step[0]) if step[0] % 2 else step


def target_of(place, step):
    return lax.bitwise_xor(place, jnp.where(lax.rem(place, 2) == 1, step[1], step[0]))


def targets(place, group):
    return [place] + [target_of(place, step) for step in swap_steps(group)]


def sources(place, group):
    return [place] + [target_of(place, mirrored(step)) for step in swap_steps(group)]


def pack_kernel(head_count, key_hbm, value_hbm, out_ref, key_ref, value_ref, sems):
    copies = [
        pltpu.make_async_copy(source, target, sems.at[index])
        for index, (source, target) in enumerate([(key_hbm, key_ref), (value_hbm, value_ref)])
    ]
    for copy in copies:
        copy.start()
    for copy in copies:
        copy.wait()
    for head in range(head_count):
        pair = jnp.concatenate([head_columns(key_ref, head), head_columns(value_ref, head)], 1)
        for place in range(head, out_ref.shape[0], head_count):
            out_ref[place] = pair


def project_kernel(head_count, group, shards, place_ref, weight_ref, query_ref, *refs):
    upstream_refs, refs = refs[:shards], refs[shards:]
    out_refs, (grad_ref, stage_ref) = refs[:group], refs[group:]
    shard_rows = upstream_refs[0].shape[0]
    for step, upstream_ref in enumerate(upstream_refs):
        owner = lax.rem(place_ref[1] + (shards - step), shards)
        start = pl.multiple_of(owner * shard_rows, shard_rows)
        grad_ref[pl.ds(start, shard_rows), :] = dot_nt(
            upstream_ref[...], weight_ref[...]
        ).astype(jnp.bfloat16)
    for head in range(head_count):
        pair = jnp.concatenate([head_columns(query_ref, head), head_columns(grad_ref, head)], 1)
        for place in range(head, group, head_count):
            stage_ref[place] = pair
    for place, out_ref in zip(targets(place_ref[0], group), out_refs):
        out_ref[...] = stage_ref[place]


def own_offset(head_count, place_ref, offset_ref):
    return offset_ref[place_ref[1] * head_count + lax.rem(place_ref[0], head_count)]


def gather_kernel(
    head_count, group, place_ref, offset_ref, keys_ref, after_ref, key_t_out, picks_out
):
    rows = keys_ref.shape[0] // group
    picked = rows // DILATION_RATE
    pick = pick_matrix(own_offset(head_count, place_ref, offset_ref), picked, rows)
    for place in range(group):
        picks_out[place * picked : (place + 1) * picked, :] = dot_nn(
            pick, keys_ref[place * rows : (place + 1) * rows, :]
        ).astype(jnp.bfloat16)
    key_t_out[...] = keys_ref[...].astype(jnp.float32).T[:HEAD_SIZE].astype(jnp.bfloat16)


def halves(both):
    left = left_half(both.shape)
    zero = jnp.zeros((), both.dtype)
    return jnp.where(left, both, zero), jnp.where(left, zero, both)


def far_kernel(
    head_count, group, others, place_ref, offset_ref, near_ref, start_ref, picks_ref, *refs
):
    other_refs, refs = refs[:others], refs[others:]
    block_refs, refs = refs[:group], refs[group:]
    acc_out, query_out, own_out, other_out, keys_ref, rows_ref = refs
    near = near_ref.shape[0]
    rows = near // group
    picked = rows // DILATION_RATE
    count = group * picked
    far = count * (1 + others)
    pick = pick_matrix(own_offset(head_count, place_ref, offset_ref), picked, rows)
    keys_ref[:near, :] = near_ref[...]
    for index, ref in enumerate([picks_ref, *other_refs]):
        keys_ref[near + index * count : near + (index + 1) * count, :] = ref[...]
    for bits, ref in enumerate(block_refs):
        rows_ref[bits * picked : (bits + 1) * picked, :] = dot_nn(pick, ref[...]).astype(
            jnp.bfloat16
        )
    key_t = keys_ref[...].astype(jnp.float32).T[:HEAD_SIZE].astype(jnp.bfloat16)
    query, grad = halves(rows_ref[...])
    score = dot_nt(keys_ref[...], query)
    dprob = dot_nt(keys_ref[...], grad)
    top = jnp.max(score, 0, keepdims=True)
    prob = jnp.exp2((score - top) * SCORE_FACTOR)
    inverse = 1.0 / jnp.sum(prob, 0, keepdims=True)
    delta = jnp.sum(prob * dprob, 0, keepdims=True) * inverse
    prob = prob * inverse
    dscore = (prob * (dprob - delta)).astype(jnp.bfloat16)
    terms = dot_nn(
        jnp.concatenate([dscore, prob.astype(jnp.bfloat16)], 1), jnp.concatenate([query, grad], 0)
    )
    acc_out[...] = start_ref[...] + terms[:near]
    terms = terms[near:] * jnp.where(left_half((far, PAIR)), SCALE, 1.0)
    own_out[...] = terms[:count]
    other_out[...] = terms[count:]
    query_grad = (dot_nn(key_t, dscore) * SCALE).T.astype(jnp.bfloat16)
    zero = jnp.zeros_like(query_grad)
    query_out[:count, :] = jnp.concatenate([query_grad, zero], 1)
    query_out[count:, :] = jnp.concatenate([zero, query_grad], 1)


def near_blocks(
    offset, keys_ref, key_t_ref, block_refs, prob_ref, dprob_ref, work_ref, top_ref, acc_ref, emit
):
    near = keys_ref.shape[0]
    rows = prob_ref.shape[2]
    half = rows // 2
    row_lane = lax.broadcasted_iota(jnp.int32, (1, rows), 1)
    picked = lax.rem(row_lane, DILATION_RATE) == offset

    def by_eight(value):
        return value.reshape(value.shape[0] // 8, 8, rows)

    def transposed_of(index):
        both = block_refs[index][...].astype(jnp.float32).T.astype(jnp.bfloat16)
        zero = jnp.zeros((HEAD_SIZE, rows), jnp.bfloat16)
        query, grad = both[:HEAD_SIZE], both[HEAD_SIZE:]
        return jnp.concatenate(
            [jnp.concatenate([query, zero], 0), jnp.concatenate([zero, grad], 0)], 1
        )

    def first_pass(index, weights, start, state):
        top, total, delta = state
        slot = index % 2
        products = dot_nn(keys_ref[start : start + PIECE, :], weights)
        scores, dprobs = products[:, :rows], products[:, rows:]
        for inner in range(0, PIECE, STRIP):
            strip = slice(start + inner, start + inner + STRIP)
            score, dprob = scores[inner : inner + STRIP], dprobs[inner : inner + STRIP]
            part = fold(score, jnp.maximum) * SCORE_FACTOR
            raised = part if top is None else jnp.maximum(top, part)
            prob = jnp.exp2(by_eight(score) * SCORE_FACTOR - raised[None])
            part_total = jnp.sum(prob, 0)
            part_delta = jnp.sum(prob * by_eight(dprob), 0)
            if top is None:
                total, delta = part_total, part_delta
            else:
                shrink = jnp.exp2(top - raised)
                total, delta = total * shrink + part_total, delta * shrink + part_delta
            top = raised
            prob_ref[slot, strip, :] = prob.reshape(STRIP, rows)
            dprob_ref[slot, strip, :] = dprob
            top_ref[slot, strip.start // STRIP] = raised
        return top, total, delta

    def last_pass(index, lse, delta, both, start, query_grad):
        slot = index % 2
        piece = slice(start, start + PIECE)
        for inner in range(0, PIECE, STRIP):
            strip = slice(start + inner, start + inner + STRIP)
            factor = jnp.exp2(top_ref[slot, strip.start // STRIP] - lse)
            prob = by_eight(prob_ref[slot, strip, :]) * factor[None]
            dscore = prob * (by_eight(dprob_ref[slot, strip, :]) - delta)
            work_ref[slot, strip, :rows] = dscore.reshape(STRIP, rows).astype(jnp.bfloat16)
            work_ref[slot, strip, rows:] = prob.reshape(STRIP, rows).astype(jnp.bfloat16)
        acc_ref[piece, :] += dot_nn(work_ref[slot, piece, :], both)
        return query_grad + dot_nn(key_t_ref[:, piece], work_ref[slot, piece, :rows])

    starts = range(0, near, PIECE)
    weights = transposed_of(0)
    state = (None, None, None)
    for start in starts:
        state = first_pass(0, weights, start, state)
    for index, block_ref in enumerate(block_refs):
        last = index + 1 == len(block_refs)
        top, total, delta = state
        highest = jnp.max(top, 0, keepdims=True)
        shrink = jnp.exp2(top - highest)
        total = jnp.sum(total * shrink, 0, keepdims=True)
        delta = jnp.sum(delta * shrink, 0, keepdims=True) / total
        lse = jnp.where(picked, -NEVER, highest + jnp.log2(total))
        both = jnp.concatenate(halves(block_ref[...]), 0)
        query_grad = jnp.zeros((HEAD_SIZE, rows), jnp.float32)
        weights = None if last else transposed_of(index + 1)
        state = (None, None, None)
        for start in starts:
            if not last:
                state = first_pass(index + 1, weights, start, state)
            query_grad = last_pass(index, lse, delta, both, start, query_grad)
        query_grad = (query_grad * SCALE).T.astype(jnp.bfloat16)
        emit(index, jnp.concatenate([query_grad[:half], query_grad[half:]], 1))


def some_kernel(head_count, steps, begin, place_ref, offset_ref, keys_ref, key_t_ref, *refs):
    if not begin:
        start_ref, refs = refs[0], refs[1:]
    block_refs, (acc_ref, query_out, *scratch) = refs[:steps], refs[steps:]
    acc_ref[...] = jnp.zeros_like(acc_ref) if begin else start_ref[...]

    def emit(index, query_grad):
        query_out[index] = query_grad

    near_blocks(
        own_offset(head_count, place_ref, offset_ref), keys_ref, key_t_ref, block_refs,
        *scratch, acc_ref, emit,
    )


def end_kernel(
    head_count, steps, others, place_ref, offset_ref, keys_ref, key_t_ref, start_ref, query_ref,
    later_query_ref, picked_query_ref, own_ref, *refs,
):
    back_refs, refs = refs[:others], refs[others:]
    block_refs, refs = refs[:steps], refs[steps:]
    half = query_ref.shape[1]
    rows = 2 * half
    group = keys_ref.shape[0] // rows
    out_refs, refs = refs[:group], refs[group:]
    acc_ref, *scratch = refs
    count = own_ref.shape[0]
    picked = count // group
    offset = own_offset(head_count, place_ref, offset_ref)
    acc_ref[...] = start_ref[...]

    def finish(bits, query_grad):
        spread = spread_matrix(offset, bits * picked, count, rows, 1)
        spread = jnp.concatenate([spread[:half], spread[half:]], 1)
        placed = dot_nn(spread, picked_query_ref[...])
        out_refs[bits][rows:, :] = (query_grad.astype(jnp.float32) + placed).astype(jnp.bfloat16)

    def emit(index, query_grad):
        finish(group - steps + index, query_grad)

    near_blocks(offset, keys_ref, key_t_ref, block_refs, *scratch, acc_ref, emit)
    terms = own_ref[...]
    for back_ref in back_refs:
        terms = terms + back_ref[...]
    terms = jnp.concatenate(split_two(terms), 0)
    factor = jnp.where(left_half((rows, PAIR)), SCALE, 1.0)
    for bits, place in enumerate(sources(place_ref[0], group)):
        spread = spread_matrix(offset, place * picked, count, rows, 1)
        placed = dot_nn(jnp.concatenate([spread, spread], 1), terms)
        acc = acc_ref[pl.ds(pl.multiple_of(place * rows, rows), rows), :]
        out_refs[bits][:rows, :] = (acc * factor + placed).astype(jnp.bfloat16)
        done = query_ref.shape[0]
        if bits < done:
            finish(bits, query_ref[bits])
        elif bits < group - steps:
            finish(bits, later_query_ref[bits - done])


def unpack_kernel(head_count, group, place_ref, *refs):
    near_refs, refs = refs[:group], refs[group:]
    query_out, key_out, value_out, stage_ref = refs
    rows = query_out.shape[0]
    half = rows // 2
    for place, near_ref in zip(targets(place_ref[0], group), near_refs):
        stage_ref[place] = near_ref[...]
    for head in range(head_count):
        columns = slice(head * HEAD_SIZE, (head + 1) * HEAD_SIZE)
        key_out[:, columns] = stage_ref[head, :rows, :HEAD_SIZE]
        value_out[:, columns] = stage_ref[head, :rows, HEAD_SIZE:]
        query_out[:half, columns] = stage_ref[head, rows:, :HEAD_SIZE]
        query_out[half:, columns] = stage_ref[head, rows:, HEAD_SIZE:]


def call(kernel, name, out_shape, scalars, operands, scratch=(), flops=0, space=VMEM, limit=40):
    return pl.pallas_call(
        kernel,
        out_shape=tuple(jax.ShapeDtypeStruct(*shape) for shape in out_shape),
        in_specs=[SMEM] * len(scalars) + [space] * len(operands),
        out_specs=tuple(VMEM for _ in out_shape),
        scratch_shapes=[
            pltpu.VMEM(*shape) if isinstance(shape, tuple) else shape for shape in scratch
        ],
        compiler_params=pltpu.CompilerParams(vmem_limit_bytes=limit * 1024 * 1024),
        cost_estimate=pl.CostEstimate(flops=flops, bytes_accessed=2**21, transcendentals=0),
        name=name,
    )(*scalars, *operands)


def body(upstream, out_weight, query_rows, key_rows, value_rows, head_offsets):
    rows, width = query_rows.shape
    head_count = width // HEAD_SIZE
    devices = lax.axis_size("context")
    shards = lax.axis_size("heads")
    group = FIRST_SEGMENT // rows
    others = devices // group - 1
    half = rows // 2
    picked = rows // DILATION_RATE
    count = group * picked
    near = group * rows
    place = jnp.stack(
        [lax.rem(lax.axis_index("context"), group), lax.axis_index("heads")]
    ).astype(jnp.int32)
    scalars = [place, head_offsets]

    def swap(values, steps):
        result = [values[0]]
        for step, value in zip(steps, values[1:]):
            pairs = [(source, source ^ step[source % 2]) for source in range(devices)]
            result.append(lax.ppermute(value, "context", pairs))
        return result

    out_steps = swap_steps(group)
    back_steps = [mirrored(step) for step in out_steps]

    def segment_shift(value, shift):
        pairs = [(source, (source + shift * group) % devices) for source in range(devices)]
        return lax.ppermute(value, "context", pairs)

    upstreams = [upstream]
    for step in range(1, shards):
        pairs = [(source, (source + step) % shards) for source in range(shards)]
        upstreams.append(lax.ppermute(upstream, "heads", pairs))

    bf16, f32 = jnp.bfloat16, jnp.float32
    (sent,) = call(
        functools.partial(pack_kernel, head_count), "pack_rows",
        [((group, rows, PAIR), bf16)],
        [], [key_rows, value_rows],
        [((rows, width), bf16)] * 2 + [pltpu.SemaphoreType.DMA((2,))],
        flops=2**31, space=ANY, limit=60,
    )
    groups = [list(range(first, first + group)) for first in range(0, devices, group)]
    sent = lax.all_to_all(sent, "context", 0, 0, axis_index_groups=groups)
    blocks_send = call(
        functools.partial(project_kernel, head_count, group, shards), "project_pack",
        [((rows, PAIR), bf16)] * group,
        [place], [out_weight, query_rows, *upstreams],
        [((rows, width), bf16), ((group, rows, PAIR), bf16)],
        flops=BUSY,
    )
    blocks = swap(blocks_send, out_steps)
    keys = sent.reshape(near, PAIR)
    key_t, picks = call(
        functools.partial(gather_kernel, head_count, group), "gather_keys",
        [((HEAD_SIZE, near), bf16), ((count, PAIR), bf16)],
        scalars, [keys, blocks_send[0]],
    )
    other_picks = [segment_shift(picks, shift) for shift in range(1, others + 1)]
    steps = group // 2
    scratch = [
        ((2, near, rows), f32), ((2, near, rows), f32), ((2, near, 2 * rows), bf16),
        ((2, near // STRIP, 8, rows), f32),
    ]
    half_flops = 30 * near * near // 2 * PAIR
    early, late = blocks[:steps], blocks[steps:-1]
    acc, query_early = call(
        functools.partial(some_kernel, head_count, len(early), True), "first_rows",
        [((near, PAIR), f32), ((len(early), half, PAIR), bf16)],
        scalars, [keys, key_t, *early], scratch, half_flops,
    )
    acc, picked_query, own_terms, other_terms = call(
        functools.partial(far_kernel, head_count, group, others), "picked_rows",
        [
            ((near, PAIR), f32), ((2 * count, PAIR), bf16), ((count, PAIR), f32),
            ((others * count, PAIR), f32),
        ],
        scalars, [keys, acc, picks, *other_picks, *blocks],
        [((near + count * (1 + others), PAIR), bf16), ((count, PAIR), bf16)],
        flops=20 * near * count * PAIR,
    )
    back = [
        segment_shift(other_terms[(shift - 1) * count : shift * count], -shift)
        for shift in range(1, others + 1)
    ]
    acc, query_late = call(
        functools.partial(some_kernel, head_count, len(late), False), "second_rows",
        [((near, PAIR), f32), ((len(late), half, PAIR), bf16)],
        scalars, [keys, key_t, acc, *late], scratch, half_flops,
    )
    near_send = call(
        functools.partial(end_kernel, head_count, 1, others), "last_rows",
        [((rows + half, PAIR), bf16)] * group,
        scalars,
        [
            keys, key_t, acc, query_early, query_late, picked_query, own_terms, *back, blocks[-1],
        ],
        [((near, PAIR), f32)] + scratch, half_flops // steps,
    )
    return tuple(
        call(
            functools.partial(unpack_kernel, head_count, group), "unpack",
            [((rows, width), bf16)] * 3,
            [place], swap(near_send, back_steps),
            [((group, rows + half, PAIR), bf16)],
        )
    )


def solution(mesh):
    return jax.shard_map(
        body,
        mesh=mesh,
        in_specs=(
            P(("context", "heads"), None),
            P("heads", None),
            P("context", "heads"),
            P("context", "heads"),
            P("context", "heads"),
            P(),
        ),
        out_specs=(P("context", "heads"), P("context", "heads"), P("context", "heads")),
        check_vma=False,
    )
```

```python
import functools
import math

import jax
import jax.numpy as jnp
from jax import lax
from jax.experimental import pallas as pl
from jax.experimental.pallas import tpu as pltpu
from jax.sharding import PartitionSpec as P

HEAD_SIZE = 64
PAIR = 2 * HEAD_SIZE
DILATION_RATE = 16
FIRST_SEGMENT = 2048
SCALE = 1.0 / math.sqrt(HEAD_SIZE)
LOG2E = math.log2(math.e)
SCORE_FACTOR = SCALE * LOG2E
STRIP = 64
PIECE = 256
BUSY = 2**35
NEVER = -1e30

SMEM = pl.BlockSpec(memory_space=pltpu.SMEM)
VMEM = pl.BlockSpec(memory_space=pltpu.VMEM)
ANY = pl.BlockSpec(memory_space=pl.ANY)


def dot_nt(left, right):
    return lax.dot_general(
        left, right, (((1,), (1,)), ((), ())), preferred_element_type=jnp.float32
    )


def dot_nn(left, right):
    return jnp.dot(left, right, preferred_element_type=jnp.float32)


def head_columns(ref, head):
    return ref[:, head * HEAD_SIZE : (head + 1) * HEAD_SIZE]


def pick_matrix(offset, picked, rows):
    source = lax.broadcasted_iota(jnp.int32, (picked, rows), 1)
    index = lax.broadcasted_iota(jnp.int32, (picked, rows), 0)
    return (source == index * DILATION_RATE + offset).astype(jnp.bfloat16)


def spread_matrix(offset, first, picked, rows, axis):
    shape = (picked, rows) if axis == 0 else (rows, picked)
    index = lax.broadcasted_iota(jnp.int32, shape, axis)
    source = lax.broadcasted_iota(jnp.int32, shape, 1 - axis)
    return (source == (index - first) * DILATION_RATE + offset).astype(jnp.bfloat16)


def split_two(value):
    high = value.astype(jnp.bfloat16)
    low = (value - high.astype(jnp.float32)).astype(jnp.bfloat16)
    return high, low


def fold(value, combine):
    parts = [value[start : start + 8] for start in range(0, value.shape[0], 8)]
    while len(parts) > 1:
        merged = [combine(parts[i], parts[i + 1]) for i in range(0, len(parts) - 1, 2)]
        parts = merged + parts[len(merged) * 2 :]
    return parts[0]


def left_half(shape):
    return lax.broadcasted_iota(jnp.int32, shape, 1) < HEAD_SIZE


def side_by_side(block):
    half = block.shape[0] // 2
    return jnp.concatenate([block[:half], block[half:]], 1)


def swap_steps(group):
    if group == 8:
        return [(2, 4), (4, 2), (7, 1), (1, 7), (3, 5), (5, 3), (6, 6)]
    return [(bits, bits) for bits in range(1, group)]


def mirrored(step):
    return (step[1], step[0]) if step[0] % 2 else step


def target_of(place, step):
    return lax.bitwise_xor(place, jnp.where(lax.rem(place, 2) == 1, step[1], step[0]))


def targets(place, group):
    return [place] + [target_of(place, step) for step in swap_steps(group)]


def sources(place, group):
    return [place] + [target_of(place, mirrored(step)) for step in swap_steps(group)]


def pack_kernel(head_count, group, place_ref, key_hbm, value_hbm, offset_hbm, *refs):
    out_refs, refs = refs[:group], refs[group:]
    own_out, key_ref, value_ref, stage_ref, offset_ref, sems = refs
    loads = [(key_hbm, key_ref), (value_hbm, value_ref), (offset_hbm, offset_ref)]
    copies = [
        pltpu.make_async_copy(source, target, sems.at[index])
        for index, (source, target) in enumerate(loads)
    ]
    for copy in copies:
        copy.start()
    for copy in copies:
        copy.wait()
    own_out[0] = place_ref[0]
    own_out[1] = offset_ref[place_ref[1] * head_count + lax.rem(place_ref[0], head_count)]
    for head in range(head_count):
        pair = jnp.concatenate([head_columns(key_ref, head), head_columns(value_ref, head)], 1)
        for place in range(head, group, head_count):
            stage_ref[place] = pair
    for place, out_ref in zip(targets(place_ref[0], group), out_refs):
        out_ref[...] = stage_ref[place]


def project_kernel(head_count, group, shards, place_ref, weight_ref, query_ref, *refs):
    upstream_refs, refs = refs[:shards], refs[shards:]
    out_refs, (grad_ref, stage_ref) = refs[:group], refs[group:]
    shard_rows = upstream_refs[0].shape[0]
    for step, upstream_ref in enumerate(upstream_refs):
        owner = lax.rem(place_ref[1] + (shards - step), shards)
        start = pl.multiple_of(owner * shard_rows, shard_rows)
        grad_ref[pl.ds(start, shard_rows), :] = dot_nt(
            upstream_ref[...], weight_ref[...]
        ).astype(jnp.bfloat16)
    for head in range(head_count):
        pair = jnp.concatenate([head_columns(query_ref, head), head_columns(grad_ref, head)], 1)
        for place in range(head, group, head_count):
            stage_ref[place] = pair
    for place, out_ref in zip(targets(place_ref[0], group), out_refs):
        out_ref[...] = stage_ref[place]


def gather_kernel(group, place_ref, *refs):
    chunk_refs, (keys_out, key_t_out, picks_out) = refs[:group], refs[group + 1 :]
    rows = keys_out.shape[0] // group
    picked = rows // DILATION_RATE
    for place, ref in zip(sources(place_ref[0], group), chunk_refs):
        keys_out[pl.ds(pl.multiple_of(place * rows, rows), rows), :] = ref[...]
    key_t_out[...] = keys_out[...].astype(jnp.float32).T[:HEAD_SIZE].astype(jnp.bfloat16)
    pick = pick_matrix(place_ref[1], picked, rows)
    for place in range(group):
        picks_out[place * picked : (place + 1) * picked, :] = dot_nn(
            pick, keys_out[place * rows : (place + 1) * rows, :]
        ).astype(jnp.bfloat16)


def halves(both):
    left = left_half(both.shape)
    zero = jnp.zeros((), both.dtype)
    return jnp.where(left, both, zero), jnp.where(left, zero, both)


def far_kernel(
    group, others, place_ref, near_ref, start_ref, picks_ref, *refs
):
    other_refs, refs = refs[:others], refs[others:]
    block_refs, refs = refs[:group], refs[group:]
    acc_out, query_out, own_out, other_out, keys_ref, rows_ref = refs
    near = near_ref.shape[0]
    rows = near // group
    picked = rows // DILATION_RATE
    count = group * picked
    far = count * (1 + others)
    pick = pick_matrix(place_ref[1], picked, rows)
    keys_ref[:near, :] = near_ref[...]
    for index, ref in enumerate([picks_ref, *other_refs]):
        keys_ref[near + index * count : near + (index + 1) * count, :] = ref[...]
    for bits, ref in enumerate(block_refs):
        rows_ref[bits * picked : (bits + 1) * picked, :] = dot_nn(pick, ref[...]).astype(
            jnp.bfloat16
        )
    key_t = keys_ref[...].astype(jnp.float32).T[:HEAD_SIZE].astype(jnp.bfloat16)
    query, grad = halves(rows_ref[...])
    score = dot_nt(keys_ref[...], query)
    dprob = dot_nt(keys_ref[...], grad)
    top = jnp.max(score, 0, keepdims=True)
    prob = jnp.exp2((score - top) * SCORE_FACTOR)
    inverse = 1.0 / jnp.sum(prob, 0, keepdims=True)
    delta = jnp.sum(prob * dprob, 0, keepdims=True) * inverse
    prob = prob * inverse
    dscore = (prob * (dprob - delta)).astype(jnp.bfloat16)
    terms = dot_nn(
        jnp.concatenate([dscore, prob.astype(jnp.bfloat16)], 1), jnp.concatenate([query, grad], 0)
    )
    acc_out[...] = start_ref[...] + terms[:near]
    terms = terms[near:] * jnp.where(left_half((far, PAIR)), SCALE, 1.0)
    own_out[...] = terms[:count]
    other_out[...] = terms[count:]
    query_grad = (dot_nn(key_t, dscore) * SCALE).T.astype(jnp.bfloat16)
    zero = jnp.zeros_like(query_grad)
    query_out[:count, :] = jnp.concatenate([query_grad, zero], 1)
    query_out[count:, :] = jnp.concatenate([zero, query_grad], 1)


def near_blocks(
    offset, keys_ref, key_t_ref, block_refs, prob_ref, dprob_ref, work_ref, top_ref, acc_ref, emit
):
    near = keys_ref.shape[0]
    rows = prob_ref.shape[2]
    half = rows // 2
    row_lane = lax.broadcasted_iota(jnp.int32, (1, rows), 1)
    picked = lax.rem(row_lane, DILATION_RATE) == offset

    def by_eight(value):
        return value.reshape(value.shape[0] // 8, 8, rows)

    def transposed_of(index):
        both = block_refs[index][...].astype(jnp.float32).T.astype(jnp.bfloat16)
        zero = jnp.zeros((HEAD_SIZE, rows), jnp.bfloat16)
        query, grad = both[:HEAD_SIZE], both[HEAD_SIZE:]
        return jnp.concatenate(
            [jnp.concatenate([query, zero], 0), jnp.concatenate([zero, grad], 0)], 1
        )

    def first_pass(index, weights, start, state):
        top, total, delta = state
        slot = index % 2
        products = dot_nn(keys_ref[start : start + PIECE, :], weights)
        scores, dprobs = products[:, :rows], products[:, rows:]
        for inner in range(0, PIECE, STRIP):
            strip = slice(start + inner, start + inner + STRIP)
            score, dprob = scores[inner : inner + STRIP], dprobs[inner : inner + STRIP]
            part = fold(score, jnp.maximum) * SCORE_FACTOR
            raised = part if top is None else jnp.maximum(top, part)
            prob = jnp.exp2(by_eight(score) * SCORE_FACTOR - raised[None])
            part_total = jnp.sum(prob, 0)
            part_delta = jnp.sum(prob * by_eight(dprob), 0)
            if top is None:
                total, delta = part_total, part_delta
            else:
                shrink = jnp.exp2(top - raised)
                total, delta = total * shrink + part_total, delta * shrink + part_delta
            top = raised
            prob_ref[slot, strip, :] = prob.reshape(STRIP, rows)
            dprob_ref[slot, strip, :] = dprob
            top_ref[slot, strip.start // STRIP] = raised
        return top, total, delta

    def last_pass(index, lse, delta, both, start, query_grad):
        slot = index % 2
        piece = slice(start, start + PIECE)
        for inner in range(0, PIECE, STRIP):
            strip = slice(start + inner, start + inner + STRIP)
            factor = jnp.exp2(top_ref[slot, strip.start // STRIP] - lse)
            prob = by_eight(prob_ref[slot, strip, :]) * factor[None]
            dscore = prob * (by_eight(dprob_ref[slot, strip, :]) - delta)
            work_ref[slot, strip, :rows] = dscore.reshape(STRIP, rows).astype(jnp.bfloat16)
            work_ref[slot, strip, rows:] = prob.reshape(STRIP, rows).astype(jnp.bfloat16)
        acc_ref[piece, :] += dot_nn(work_ref[slot, piece, :], both)
        return query_grad + dot_nn(key_t_ref[:, piece], work_ref[slot, piece, :rows])

    starts = range(0, near, PIECE)
    weights = transposed_of(0)
    state = (None, None, None)
    for start in starts:
        state = first_pass(0, weights, start, state)
    for index, block_ref in enumerate(block_refs):
        last = index + 1 == len(block_refs)
        top, total, delta = state
        highest = jnp.max(top, 0, keepdims=True)
        shrink = jnp.exp2(top - highest)
        total = jnp.sum(total * shrink, 0, keepdims=True)
        delta = jnp.sum(delta * shrink, 0, keepdims=True) / total
        lse = jnp.where(picked, -NEVER, highest + jnp.log2(total))
        both = jnp.concatenate(halves(block_ref[...]), 0)
        query_grad = jnp.zeros((HEAD_SIZE, rows), jnp.float32)
        weights = None if last else transposed_of(index + 1)
        state = (None, None, None)
        for start in starts:
            if not last:
                state = first_pass(index + 1, weights, start, state)
            query_grad = last_pass(index, lse, delta, both, start, query_grad)
        query_grad = (query_grad * SCALE).T.astype(jnp.bfloat16)
        emit(index, jnp.concatenate([query_grad[:half], query_grad[half:]], 1))


def some_kernel(steps, begin, place_ref, keys_ref, key_t_ref, *refs):
    if not begin:
        start_ref, refs = refs[0], refs[1:]
    block_refs, (acc_ref, query_out, *scratch) = refs[:steps], refs[steps:]
    acc_ref[...] = jnp.zeros_like(acc_ref) if begin else start_ref[...]

    def emit(index, query_grad):
        query_out[index] = query_grad

    near_blocks(
        place_ref[1], keys_ref, key_t_ref, block_refs,
        *scratch, acc_ref, emit,
    )


def end_kernel(
    steps, others, place_ref, keys_ref, key_t_ref, start_ref, query_ref,
    later_query_ref, picked_query_ref, own_ref, *refs,
):
    back_refs, refs = refs[:others], refs[others:]
    block_refs, refs = refs[:steps], refs[steps:]
    half = query_ref.shape[1]
    rows = 2 * half
    group = keys_ref.shape[0] // rows
    out_refs, refs = refs[:group], refs[group:]
    acc_ref, *scratch = refs
    count = own_ref.shape[0]
    picked = count // group
    offset = place_ref[1]
    acc_ref[...] = start_ref[...]

    def finish(bits, query_grad):
        spread = spread_matrix(offset, bits * picked, count, rows, 1)
        spread = jnp.concatenate([spread[:half], spread[half:]], 1)
        placed = dot_nn(spread, picked_query_ref[...])
        out_refs[bits][rows:, :] = (query_grad.astype(jnp.float32) + placed).astype(jnp.bfloat16)

    def emit(index, query_grad):
        finish(group - steps + index, query_grad)

    near_blocks(offset, keys_ref, key_t_ref, block_refs, *scratch, acc_ref, emit)
    terms = own_ref[...]
    for back_ref in back_refs:
        terms = terms + back_ref[...]
    terms = jnp.concatenate(split_two(terms), 0)
    factor = jnp.where(left_half((rows, PAIR)), SCALE, 1.0)
    for bits, place in enumerate(sources(place_ref[0], group)):
        spread = spread_matrix(offset, place * picked, count, rows, 1)
        placed = dot_nn(jnp.concatenate([spread, spread], 1), terms)
        acc = acc_ref[pl.ds(pl.multiple_of(place * rows, rows), rows), :]
        out_refs[bits][:rows, :] = (acc * factor + placed).astype(jnp.bfloat16)
        done = query_ref.shape[0]
        if bits < done:
            finish(bits, query_ref[bits])
        elif bits < group - steps:
            finish(bits, later_query_ref[bits - done])


def unpack_kernel(head_count, group, place_ref, *refs):
    near_refs, refs = refs[:group], refs[group:]
    query_out, key_out, value_out, stage_ref = refs
    rows = query_out.shape[0]
    half = rows // 2
    for place, near_ref in zip(targets(place_ref[0], group), near_refs):
        stage_ref[place] = near_ref[...]
    for head in range(0, head_count, 2):
        columns = slice(head * HEAD_SIZE, (head + 2) * HEAD_SIZE)
        pairs = [stage_ref[head, :rows, :], stage_ref[head + 1, :rows, :]]
        packed = [stage_ref[head, rows:, :], stage_ref[head + 1, rows:, :]]
        key_out[:, columns] = jnp.concatenate([pair[:, :HEAD_SIZE] for pair in pairs], 1)
        value_out[:, columns] = jnp.concatenate([pair[:, HEAD_SIZE:] for pair in pairs], 1)
        query_out[:half, columns] = jnp.concatenate([pair[:, :HEAD_SIZE] for pair in packed], 1)
        query_out[half:, columns] = jnp.concatenate([pair[:, HEAD_SIZE:] for pair in packed], 1)


def call(
    kernel, name, out_shape, scalars, operands, scratch=(), flops=0, hbm=(), limit=40, scalars_out=0
):
    last = len(out_shape) - scalars_out
    return pl.pallas_call(
        kernel,
        out_shape=tuple(jax.ShapeDtypeStruct(*shape) for shape in out_shape),
        in_specs=[SMEM] * len(scalars) + [VMEM] * len(operands) + [ANY] * len(hbm),
        out_specs=tuple(VMEM if index < last else SMEM for index in range(len(out_shape))),
        scratch_shapes=[
            pltpu.VMEM(*shape) if isinstance(shape, tuple) else shape for shape in scratch
        ],
        compiler_params=pltpu.CompilerParams(vmem_limit_bytes=limit * 1024 * 1024),
        cost_estimate=pl.CostEstimate(flops=flops, bytes_accessed=2**21, transcendentals=0),
        name=name,
    )(*scalars, *operands, *hbm)


def body(upstream, out_weight, query_rows, key_rows, value_rows, head_offsets):
    rows, width = query_rows.shape
    head_count = width // HEAD_SIZE
    devices = lax.axis_size("context")
    shards = lax.axis_size("heads")
    group = FIRST_SEGMENT // rows
    others = devices // group - 1
    half = rows // 2
    picked = rows // DILATION_RATE
    count = group * picked
    near = group * rows
    place = jnp.stack(
        [lax.rem(lax.axis_index("context"), group), lax.axis_index("heads")]
    ).astype(jnp.int32)

    def swap(values, steps):
        result = [values[0]]
        for step, value in zip(steps, values[1:]):
            pairs = [(source, source ^ step[source % 2]) for source in range(devices)]
            result.append(lax.ppermute(value, "context", pairs))
        return result

    out_steps = swap_steps(group)
    back_steps = [mirrored(step) for step in out_steps]

    def segment_shift(value, shift):
        pairs = [(source, (source + shift * group) % devices) for source in range(devices)]
        return lax.ppermute(value, "context", pairs)

    upstreams = [upstream]
    for step in range(1, shards):
        pairs = [(source, (source + step) % shards) for source in range(shards)]
        upstreams.append(lax.ppermute(upstream, "heads", pairs))

    bf16, f32 = jnp.bfloat16, jnp.float32
    *sent, own = call(
        functools.partial(pack_kernel, head_count, group), "pack_rows",
        [((rows, PAIR), bf16)] * group + [((2,), jnp.int32)],
        [place], [],
        [((rows, width), bf16)] * 2
        + [
            ((group, rows, PAIR), bf16), pltpu.SMEM(head_offsets.shape, jnp.int32),
            pltpu.SemaphoreType.DMA((3,)),
        ],
        flops=2**31, hbm=[key_rows, value_rows, head_offsets], limit=60, scalars_out=1,
    )
    sent = swap(sent, out_steps)
    blocks_send = call(
        functools.partial(project_kernel, head_count, group, shards), "project_pack",
        [((rows, PAIR), bf16)] * group,
        [place], [out_weight, query_rows, *upstreams],
        [((rows, width), bf16), ((group, rows, PAIR), bf16)],
        flops=BUSY,
    )
    blocks = swap(blocks_send, out_steps)
    keys, key_t, picks = call(
        functools.partial(gather_kernel, group), "gather_keys",
        [((near, PAIR), bf16), ((HEAD_SIZE, near), bf16), ((count, PAIR), bf16)],
        [own], [*sent, blocks_send[0]],
    )
    other_picks = [segment_shift(picks, shift) for shift in range(1, others + 1)]
    steps = group // 2
    scratch = [
        ((2, near, rows), f32), ((2, near, rows), f32), ((2, near, 2 * rows), bf16),
        ((2, near // STRIP, 8, rows), f32),
    ]
    half_flops = 30 * near * near // 2 * PAIR
    early, late = blocks[:steps], blocks[steps:-1]
    acc, query_early = call(
        functools.partial(some_kernel, len(early), True), "first_rows",
        [((near, PAIR), f32), ((len(early), half, PAIR), bf16)],
        [own], [keys, key_t, *early], scratch, half_flops,
    )
    acc, picked_query, own_terms, other_terms = call(
        functools.partial(far_kernel, group, others), "picked_rows",
        [
            ((near, PAIR), f32), ((2 * count, PAIR), bf16), ((count, PAIR), f32),
            ((others * count, PAIR), f32),
        ],
        [own], [keys, acc, picks, *other_picks, *blocks],
        [((near + count * (1 + others), PAIR), bf16), ((count, PAIR), bf16)],
        flops=20 * near * count * PAIR,
    )
    back = [
        segment_shift(other_terms[(shift - 1) * count : shift * count], -shift)
        for shift in range(1, others + 1)
    ]
    acc, query_late = call(
        functools.partial(some_kernel, len(late), False), "second_rows",
        [((near, PAIR), f32), ((len(late), half, PAIR), bf16)],
        [own], [keys, key_t, acc, *late], scratch, half_flops,
    )
    near_send = call(
        functools.partial(end_kernel, 1, others), "last_rows",
        [((rows + half, PAIR), bf16)] * group,
        [own],
        [
            keys, key_t, acc, query_early, query_late, picked_query, own_terms, *back, blocks[-1],
        ],
        [((near, PAIR), f32)] + scratch, half_flops // steps,
    )
    return tuple(
        call(
            functools.partial(unpack_kernel, head_count, group), "unpack",
            [((rows, width), bf16)] * 3,
            [place], swap(near_send, back_steps),
            [((group, rows + half, PAIR), bf16)],
        )
    )


def solution(mesh):
    return jax.shard_map(
        body,
        mesh=mesh,
        in_specs=(
            P(("context", "heads"), None),
            P("heads", None),
            P("context", "heads"),
            P("context", "heads"),
            P("context", "heads"),
            P(),
        ),
        out_specs=(P("context", "heads"), P("context", "heads"), P("context", "heads")),
        check_vma=False,
    )
```

```python
import functools
import math

import jax
import jax.numpy as jnp
from jax import lax
from jax.experimental import pallas as pl
from jax.experimental.pallas import tpu as pltpu
from jax.sharding import PartitionSpec as P

HEAD_SIZE = 64
PAIR = 2 * HEAD_SIZE
DILATION_RATE = 16
FIRST_SEGMENT = 2048
SCALE = 1.0 / math.sqrt(HEAD_SIZE)
LOG2E = math.log2(math.e)
SCORE_FACTOR = SCALE * LOG2E
STRIP = 64
PIECE = 256
BUSY = 2**35
NEVER = -1e30

SMEM = pl.BlockSpec(memory_space=pltpu.SMEM)
VMEM = pl.BlockSpec(memory_space=pltpu.VMEM)
ANY = pl.BlockSpec(memory_space=pl.ANY)


def dot_nt(left, right):
    return lax.dot_general(
        left, right, (((1,), (1,)), ((), ())), preferred_element_type=jnp.float32
    )


def dot_nn(left, right):
    return jnp.dot(left, right, preferred_element_type=jnp.float32)


def head_columns(ref, head):
    return ref[:, head * HEAD_SIZE : (head + 1) * HEAD_SIZE]


def pick_matrix(offset, picked, rows):
    source = lax.broadcasted_iota(jnp.int32, (picked, rows), 1)
    index = lax.broadcasted_iota(jnp.int32, (picked, rows), 0)
    return (source == index * DILATION_RATE + offset).astype(jnp.bfloat16)


def spread_matrix(offset, first, picked, rows, axis):
    shape = (picked, rows) if axis == 0 else (rows, picked)
    index = lax.broadcasted_iota(jnp.int32, shape, axis)
    source = lax.broadcasted_iota(jnp.int32, shape, 1 - axis)
    return (source == (index - first) * DILATION_RATE + offset).astype(jnp.bfloat16)


def split_two(value):
    high = value.astype(jnp.bfloat16)
    low = (value - high.astype(jnp.float32)).astype(jnp.bfloat16)
    return high, low


def fold(value, combine):
    parts = [value[start : start + 8] for start in range(0, value.shape[0], 8)]
    while len(parts) > 1:
        merged = [combine(parts[i], parts[i + 1]) for i in range(0, len(parts) - 1, 2)]
        parts = merged + parts[len(merged) * 2 :]
    return parts[0]


def left_half(shape):
    return lax.broadcasted_iota(jnp.int32, shape, 1) < HEAD_SIZE


def side_by_side(block):
    half = block.shape[0] // 2
    return jnp.concatenate([block[:half], block[half:]], 1)


def swap_steps(group):
    if group == 8:
        return [(2, 4), (4, 2), (6, 6), (3, 5), (5, 3), (7, 1), (1, 7)]
    return [(bits, bits) for bits in range(1, group)]


def mirrored(step):
    return (step[1], step[0]) if step[0] % 2 else step


def target_of(place, step):
    return lax.bitwise_xor(place, jnp.where(lax.rem(place, 2) == 1, step[1], step[0]))


def targets(place, group):
    return [place] + [target_of(place, step) for step in swap_steps(group)]


def sources(place, group):
    return [place] + [target_of(place, mirrored(step)) for step in swap_steps(group)]


def pack_kernel(head_count, key_hbm, value_hbm, out_ref, key_ref, value_ref, sems):
    copies = [
        pltpu.make_async_copy(source, target, sems.at[index])
        for index, (source, target) in enumerate([(key_hbm, key_ref), (value_hbm, value_ref)])
    ]
    for copy in copies:
        copy.start()
    for copy in copies:
        copy.wait()
    for head in range(head_count):
        pair = jnp.concatenate([head_columns(key_ref, head), head_columns(value_ref, head)], 1)
        for place in range(head, out_ref.shape[0], head_count):
            out_ref[place] = pair


def project_kernel(head_count, group, shards, place_ref, weight_ref, query_ref, *refs):
    upstream_refs, refs = refs[:shards], refs[shards:]
    out_refs, (grad_ref, stage_ref) = refs[:group], refs[group:]
    shard_rows = upstream_refs[0].shape[0]
    for step, upstream_ref in enumerate(upstream_refs):
        owner = lax.rem(place_ref[1] + (shards - step), shards)
        start = pl.multiple_of(owner * shard_rows, shard_rows)
        grad_ref[pl.ds(start, shard_rows), :] = dot_nt(
            upstream_ref[...], weight_ref[...]
        ).astype(jnp.bfloat16)
    for head in range(head_count):
        pair = jnp.concatenate([head_columns(query_ref, head), head_columns(grad_ref, head)], 1)
        for place in range(head, group, head_count):
            stage_ref[place] = pair
    for place, out_ref in zip(targets(place_ref[0], group), out_refs):
        out_ref[...] = stage_ref[place]


def own_offset(head_count, place_ref):
    return place_ref[2 + place_ref[1] * head_count + lax.rem(place_ref[0], head_count)]


def gather_kernel(
    head_count, group, place_ref, keys_ref, after_ref, key_t_out, picks_out
):
    rows = keys_ref.shape[0] // group
    picked = rows // DILATION_RATE
    pick = pick_matrix(own_offset(head_count, place_ref), picked, rows)
    for place in range(group):
        picks_out[place * picked : (place + 1) * picked, :] = dot_nn(
            pick, keys_ref[place * rows : (place + 1) * rows, :]
        ).astype(jnp.bfloat16)
    key_t_out[...] = keys_ref[...].astype(jnp.float32).T[:HEAD_SIZE].astype(jnp.bfloat16)


def halves(both):
    left = left_half(both.shape)
    zero = jnp.zeros((), both.dtype)
    return jnp.where(left, both, zero), jnp.where(left, zero, both)


def far_kernel(
    head_count, group, others, place_ref, near_ref, start_ref, picks_ref, *refs
):
    other_refs, refs = refs[:others], refs[others:]
    block_refs, refs = refs[:group], refs[group:]
    acc_out, query_out, own_out, other_out, keys_ref, rows_ref = refs
    near = near_ref.shape[0]
    rows = near // group
    picked = rows // DILATION_RATE
    count = group * picked
    far = count * (1 + others)
    pick = pick_matrix(own_offset(head_count, place_ref), picked, rows)
    keys_ref[:near, :] = near_ref[...]
    for index, ref in enumerate([picks_ref, *other_refs]):
        keys_ref[near + index * count : near + (index + 1) * count, :] = ref[...]
    for bits, ref in enumerate(block_refs):
        rows_ref[bits * picked : (bits + 1) * picked, :] = dot_nn(pick, ref[...]).astype(
            jnp.bfloat16
        )
    key_t = keys_ref[...].astype(jnp.float32).T[:HEAD_SIZE].astype(jnp.bfloat16)
    query, grad = halves(rows_ref[...])
    score = dot_nt(keys_ref[...], query)
    dprob = dot_nt(keys_ref[...], grad)
    top = jnp.max(score, 0, keepdims=True)
    prob = jnp.exp2((score - top) * SCORE_FACTOR)
    inverse = 1.0 / jnp.sum(prob, 0, keepdims=True)
    delta = jnp.sum(prob * dprob, 0, keepdims=True) * inverse
    prob = prob * inverse
    dscore = (prob * (dprob - delta)).astype(jnp.bfloat16)
    terms = dot_nn(
        jnp.concatenate([dscore, prob.astype(jnp.bfloat16)], 1), jnp.concatenate([query, grad], 0)
    )
    acc_out[...] = start_ref[...] + terms[:near]
    terms = terms[near:] * jnp.where(left_half((far, PAIR)), SCALE, 1.0)
    own_out[...] = terms[:count]
    other_out[...] = terms[count:]
    query_grad = (dot_nn(key_t, dscore) * SCALE).T.astype(jnp.bfloat16)
    zero = jnp.zeros_like(query_grad)
    query_out[:count, :] = jnp.concatenate([query_grad, zero], 1)
    query_out[count:, :] = jnp.concatenate([zero, query_grad], 1)


def near_blocks(
    offset, keys_ref, key_t_ref, block_refs, prob_ref, dprob_ref, work_ref, top_ref, acc_ref, emit
):
    near = keys_ref.shape[0]
    rows = prob_ref.shape[2]
    half = rows // 2
    row_lane = lax.broadcasted_iota(jnp.int32, (1, rows), 1)
    picked = lax.rem(row_lane, DILATION_RATE) == offset

    def by_eight(value):
        return value.reshape(value.shape[0] // 8, 8, rows)

    def transposed_of(index):
        both = block_refs[index][...].astype(jnp.float32).T.astype(jnp.bfloat16)
        zero = jnp.zeros((HEAD_SIZE, rows), jnp.bfloat16)
        query, grad = both[:HEAD_SIZE], both[HEAD_SIZE:]
        return jnp.concatenate(
            [jnp.concatenate([query, zero], 0), jnp.concatenate([zero, grad], 0)], 1
        )

    def first_pass(index, weights, start, state):
        top, total, delta = state
        slot = index % 2
        products = dot_nn(keys_ref[start : start + PIECE, :], weights)
        scores, dprobs = products[:, :rows], products[:, rows:]
        for inner in range(0, PIECE, STRIP):
            strip = slice(start + inner, start + inner + STRIP)
            score, dprob = scores[inner : inner + STRIP], dprobs[inner : inner + STRIP]
            part = fold(score, jnp.maximum) * SCORE_FACTOR
            raised = part if top is None else jnp.maximum(top, part)
            prob = jnp.exp2(by_eight(score) * SCORE_FACTOR - raised[None])
            part_total = jnp.sum(prob, 0)
            part_delta = jnp.sum(prob * by_eight(dprob), 0)
            if top is None:
                total, delta = part_total, part_delta
            else:
                shrink = jnp.exp2(top - raised)
                total, delta = total * shrink + part_total, delta * shrink + part_delta
            top = raised
            prob_ref[slot, strip, :] = prob.reshape(STRIP, rows)
            dprob_ref[slot, strip, :] = dprob
            top_ref[slot, strip.start // STRIP] = raised
        return top, total, delta

    def last_pass(index, lse, delta, both, start, query_grad):
        slot = index % 2
        piece = slice(start, start + PIECE)
        for inner in range(0, PIECE, STRIP):
            strip = slice(start + inner, start + inner + STRIP)
            factor = jnp.exp2(top_ref[slot, strip.start // STRIP] - lse)
            prob = by_eight(prob_ref[slot, strip, :]) * factor[None]
            dscore = prob * (by_eight(dprob_ref[slot, strip, :]) - delta)
            work_ref[slot, strip, :rows] = dscore.reshape(STRIP, rows).astype(jnp.bfloat16)
            work_ref[slot, strip, rows:] = prob.reshape(STRIP, rows).astype(jnp.bfloat16)
        acc_ref[piece, :] += dot_nn(work_ref[slot, piece, :], both)
        return query_grad + dot_nn(key_t_ref[:, piece], work_ref[slot, piece, :rows])

    starts = range(0, near, PIECE)
    weights = transposed_of(0)
    state = (None, None, None)
    for start in starts:
        state = first_pass(0, weights, start, state)
    for index, block_ref in enumerate(block_refs):
        last = index + 1 == len(block_refs)
        top, total, delta = state
        highest = jnp.max(top, 0, keepdims=True)
        shrink = jnp.exp2(top - highest)
        total = jnp.sum(total * shrink, 0, keepdims=True)
        delta = jnp.sum(delta * shrink, 0, keepdims=True) / total
        lse = jnp.where(picked, -NEVER, highest + jnp.log2(total))
        both = jnp.concatenate(halves(block_ref[...]), 0)
        query_grad = jnp.zeros((HEAD_SIZE, rows), jnp.float32)
        weights = None if last else transposed_of(index + 1)
        state = (None, None, None)
        for start in starts:
            if not last:
                state = first_pass(index + 1, weights, start, state)
            query_grad = last_pass(index, lse, delta, both, start, query_grad)
        query_grad = (query_grad * SCALE).T.astype(jnp.bfloat16)
        emit(index, jnp.concatenate([query_grad[:half], query_grad[half:]], 1))


def some_kernel(head_count, steps, begin, place_ref, keys_ref, key_t_ref, *refs):
    if not begin:
        start_ref, refs = refs[0], refs[1:]
    block_refs, (acc_ref, query_out, *scratch) = refs[:steps], refs[steps:]
    acc_ref[...] = jnp.zeros_like(acc_ref) if begin else start_ref[...]

    def emit(index, query_grad):
        query_out[index] = query_grad

    near_blocks(
        own_offset(head_count, place_ref), keys_ref, key_t_ref, block_refs,
        *scratch, acc_ref, emit,
    )


def end_kernel(
    head_count, steps, others, place_ref, keys_ref, key_t_ref, start_ref, query_ref,
    later_query_ref, picked_query_ref, own_ref, *refs,
):
    back_refs, refs = refs[:others], refs[others:]
    block_refs, refs = refs[:steps], refs[steps:]
    half = query_ref.shape[1]
    rows = 2 * half
    group = keys_ref.shape[0] // rows
    out_refs, refs = refs[:group], refs[group:]
    acc_ref, *scratch = refs
    count = own_ref.shape[0]
    picked = count // group
    offset = own_offset(head_count, place_ref)
    acc_ref[...] = start_ref[...]

    def finish(bits, query_grad):
        spread = spread_matrix(offset, bits * picked, count, rows, 1)
        spread = jnp.concatenate([spread[:half], spread[half:]], 1)
        placed = dot_nn(spread, picked_query_ref[...])
        out_refs[bits][rows:, :] = (query_grad.astype(jnp.float32) + placed).astype(jnp.bfloat16)

    def emit(index, query_grad):
        finish(group - steps + index, query_grad)

    near_blocks(offset, keys_ref, key_t_ref, block_refs, *scratch, acc_ref, emit)
    terms = own_ref[...]
    for back_ref in back_refs:
        terms = terms + back_ref[...]
    terms = jnp.concatenate(split_two(terms), 0)
    factor = jnp.where(left_half((rows, PAIR)), SCALE, 1.0)
    for bits, place in enumerate(sources(place_ref[0], group)):
        spread = spread_matrix(offset, place * picked, count, rows, 1)
        placed = dot_nn(jnp.concatenate([spread, spread], 1), terms)
        acc = acc_ref[pl.ds(pl.multiple_of(place * rows, rows), rows), :]
        out_refs[bits][:rows, :] = (acc * factor + placed).astype(jnp.bfloat16)
        done = query_ref.shape[0]
        if bits < done:
            finish(bits, query_ref[bits])
        elif bits < group - steps:
            finish(bits, later_query_ref[bits - done])


def unpack_kernel(head_count, group, place_ref, *refs):
    near_refs, refs = refs[:group], refs[group:]
    query_out, key_out, value_out, stage_ref = refs
    rows = query_out.shape[0]
    half = rows // 2
    for place, near_ref in zip(targets(place_ref[0], group), near_refs):
        stage_ref[place] = near_ref[...]
    for head in range(0, head_count, 2):
        columns = slice(head * HEAD_SIZE, (head + 2) * HEAD_SIZE)
        pairs = [stage_ref[head, :rows, :], stage_ref[head + 1, :rows, :]]
        packed = [stage_ref[head, rows:, :], stage_ref[head + 1, rows:, :]]
        key_out[:, columns] = jnp.concatenate([pair[:, :HEAD_SIZE] for pair in pairs], 1)
        value_out[:, columns] = jnp.concatenate([pair[:, HEAD_SIZE:] for pair in pairs], 1)
        query_out[:half, columns] = jnp.concatenate([pair[:, :HEAD_SIZE] for pair in packed], 1)
        query_out[half:, columns] = jnp.concatenate([pair[:, HEAD_SIZE:] for pair in packed], 1)


def call(kernel, name, out_shape, scalars, operands, scratch=(), flops=0, space=VMEM, limit=40):
    return pl.pallas_call(
        kernel,
        out_shape=tuple(jax.ShapeDtypeStruct(*shape) for shape in out_shape),
        in_specs=[SMEM] * len(scalars) + [space] * len(operands),
        out_specs=tuple(VMEM for _ in out_shape),
        scratch_shapes=[
            pltpu.VMEM(*shape) if isinstance(shape, tuple) else shape for shape in scratch
        ],
        compiler_params=pltpu.CompilerParams(vmem_limit_bytes=limit * 1024 * 1024),
        cost_estimate=pl.CostEstimate(flops=flops, bytes_accessed=2**21, transcendentals=0),
        name=name,
    )(*scalars, *operands)


def body(upstream, out_weight, query_rows, key_rows, value_rows, head_offsets):
    rows, width = query_rows.shape
    head_count = width // HEAD_SIZE
    devices = lax.axis_size("context")
    shards = lax.axis_size("heads")
    group = FIRST_SEGMENT // rows
    others = devices // group - 1
    half = rows // 2
    picked = rows // DILATION_RATE
    count = group * picked
    near = group * rows
    place = jnp.stack(
        [lax.rem(lax.axis_index("context"), group), lax.axis_index("heads")]
    ).astype(jnp.int32)
    place = jnp.concatenate([place, head_offsets])
    scalars = [place]

    def swap(values, steps):
        result = [values[0]]
        for step, value in zip(steps, values[1:]):
            pairs = [(source, source ^ step[source % 2]) for source in range(devices)]
            result.append(lax.ppermute(value, "context", pairs))
        return result

    out_steps = swap_steps(group)
    back_steps = [mirrored(step) for step in out_steps]

    def segment_shift(value, shift):
        pairs = [(source, (source + shift * group) % devices) for source in range(devices)]
        return lax.ppermute(value, "context", pairs)

    upstreams = [upstream]
    for step in range(1, shards):
        pairs = [(source, (source + step) % shards) for source in range(shards)]
        upstreams.append(lax.ppermute(upstream, "heads", pairs))

    bf16, f32 = jnp.bfloat16, jnp.float32
    (sent,) = call(
        functools.partial(pack_kernel, head_count), "pack_rows",
        [((group, rows, PAIR), bf16)],
        [], [key_rows, value_rows],
        [((rows, width), bf16)] * 2 + [pltpu.SemaphoreType.DMA((2,))],
        flops=2**31, space=ANY, limit=60,
    )
    groups = [list(range(first, first + group)) for first in range(0, devices, group)]
    sent = lax.all_to_all(sent, "context", 0, 0, axis_index_groups=groups)
    blocks_send = call(
        functools.partial(project_kernel, head_count, group, shards), "project_pack",
        [((rows, PAIR), bf16)] * group,
        [place], [out_weight, query_rows, *upstreams],
        [((rows, width), bf16), ((group, rows, PAIR), bf16)],
        flops=BUSY,
    )
    blocks = swap(blocks_send, out_steps)
    keys = sent.reshape(near, PAIR)
    key_t, picks = call(
        functools.partial(gather_kernel, head_count, group), "gather_keys",
        [((HEAD_SIZE, near), bf16), ((count, PAIR), bf16)],
        scalars, [keys, blocks_send[0]],
    )
    other_picks = [segment_shift(picks, shift) for shift in range(1, others + 1)]
    steps = group // 2
    scratch = [
        ((2, near, rows), f32), ((2, near, rows), f32), ((2, near, 2 * rows), bf16),
        ((2, near // STRIP, 8, rows), f32),
    ]
    half_flops = 30 * near * near // 2 * PAIR
    early, late = blocks[:steps], blocks[steps:-1]
    acc, query_early = call(
        functools.partial(some_kernel, head_count, len(early), True), "first_rows",
        [((near, PAIR), f32), ((len(early), half, PAIR), bf16)],
        scalars, [keys, key_t, *early], scratch, half_flops,
    )
    acc, picked_query, own_terms, other_terms = call(
        functools.partial(far_kernel, head_count, group, others), "picked_rows",
        [
            ((near, PAIR), f32), ((2 * count, PAIR), bf16), ((count, PAIR), f32),
            ((others * count, PAIR), f32),
        ],
        scalars, [keys, acc, picks, *other_picks, *blocks],
        [((near + count * (1 + others), PAIR), bf16), ((count, PAIR), bf16)],
        flops=20 * near * count * PAIR,
    )
    back = [
        segment_shift(other_terms[(shift - 1) * count : shift * count], -shift)
        for shift in range(1, others + 1)
    ]
    acc, query_late = call(
        functools.partial(some_kernel, head_count, len(late), False), "second_rows",
        [((near, PAIR), f32), ((len(late), half, PAIR), bf16)],
        scalars, [keys, key_t, acc, *late], scratch, half_flops,
    )
    near_send = call(
        functools.partial(end_kernel, head_count, 1, others), "last_rows",
        [((rows + half, PAIR), bf16)] * group,
        scalars,
        [
            keys, key_t, acc, query_early, query_late, picked_query, own_terms, *back, blocks[-1],
        ],
        [((near, PAIR), f32)] + scratch, half_flops // steps,
    )
    return tuple(
        call(
            functools.partial(unpack_kernel, head_count, group), "unpack",
            [((rows, width), bf16)] * 3,
            [place], swap(near_send, back_steps),
            [((group, rows + half, PAIR), bf16)],
        )
    )


def solution(mesh):
    return jax.shard_map(
        body,
        mesh=mesh,
        in_specs=(
            P(("context", "heads"), None),
            P("heads", None),
            P("context", "heads"),
            P("context", "heads"),
            P("context", "heads"),
            P(),
        ),
        out_specs=(P("context", "heads"), P("context", "heads"), P("context", "heads")),
        check_vma=False,
    )
```

```python
import functools
import math

import jax
import jax.numpy as jnp
from jax import lax
from jax.experimental import pallas as pl
from jax.experimental.pallas import tpu as pltpu
from jax.sharding import PartitionSpec as P

HEAD_SIZE = 64
PAIR = 2 * HEAD_SIZE
DILATION_RATE = 16
FIRST_SEGMENT = 2048
SCALE = 1.0 / math.sqrt(HEAD_SIZE)
LOG2E = math.log2(math.e)
SCORE_FACTOR = SCALE * LOG2E
STRIP = 64
PIECE = 256
BUSY = 2**35
NEVER = -1e30

SMEM = pl.BlockSpec(memory_space=pltpu.SMEM)
VMEM = pl.BlockSpec(memory_space=pltpu.VMEM)
ANY = pl.BlockSpec(memory_space=pl.ANY)


def dot_nt(left, right):
    return lax.dot_general(
        left, right, (((1,), (1,)), ((), ())), preferred_element_type=jnp.float32
    )


def dot_nn(left, right):
    return jnp.dot(left, right, preferred_element_type=jnp.float32)


def head_columns(ref, head):
    return ref[:, head * HEAD_SIZE : (head + 1) * HEAD_SIZE]


def pick_matrix(offset, picked, rows):
    source = lax.broadcasted_iota(jnp.int32, (picked, rows), 1)
    index = lax.broadcasted_iota(jnp.int32, (picked, rows), 0)
    return (source == index * DILATION_RATE + offset).astype(jnp.bfloat16)


def spread_matrix(offset, first, picked, rows, axis):
    shape = (picked, rows) if axis == 0 else (rows, picked)
    index = lax.broadcasted_iota(jnp.int32, shape, axis)
    source = lax.broadcasted_iota(jnp.int32, shape, 1 - axis)
    return (source == (index - first) * DILATION_RATE + offset).astype(jnp.bfloat16)


def split_two(value):
    high = value.astype(jnp.bfloat16)
    low = (value - high.astype(jnp.float32)).astype(jnp.bfloat16)
    return high, low


def fold(value, combine):
    parts = [value[start : start + 8] for start in range(0, value.shape[0], 8)]
    while len(parts) > 1:
        merged = [combine(parts[i], parts[i + 1]) for i in range(0, len(parts) - 1, 2)]
        parts = merged + parts[len(merged) * 2 :]
    return parts[0]


def left_half(shape):
    return lax.broadcasted_iota(jnp.int32, shape, 1) < HEAD_SIZE


def side_by_side(block):
    half = block.shape[0] // 2
    return jnp.concatenate([block[:half], block[half:]], 1)


def swap_steps(group):
    if group == 8:
        return [(2, 4), (4, 2), (7, 1), (1, 7), (3, 5), (5, 3), (6, 6)]
    return [(bits, bits) for bits in range(1, group)]


def mirrored(step):
    return (step[1], step[0]) if step[0] % 2 else step


def target_of(place, step):
    return lax.bitwise_xor(place, jnp.where(lax.rem(place, 2) == 1, step[1], step[0]))


def targets(place, group):
    return [place] + [target_of(place, step) for step in swap_steps(group)]


def sources(place, group):
    return [place] + [target_of(place, mirrored(step)) for step in swap_steps(group)]


def pack_kernel(head_count, key_hbm, value_hbm, out_ref, key_ref, value_ref, sems):
    copies = [
        pltpu.make_async_copy(source, target, sems.at[index])
        for index, (source, target) in enumerate([(key_hbm, key_ref), (value_hbm, value_ref)])
    ]
    for copy in copies:
        copy.start()
    for copy in copies:
        copy.wait()
    for head in range(head_count):
        pair = jnp.concatenate([head_columns(key_ref, head), head_columns(value_ref, head)], 1)
        for place in range(head, out_ref.shape[0], head_count):
            out_ref[place] = pair


def project_kernel(head_count, group, shards, place_ref, weight_ref, query_ref, *refs):
    upstream_refs, refs = refs[:shards], refs[shards:]
    out_refs, (grad_ref, stage_ref) = refs[:group], refs[group:]
    shard_rows = upstream_refs[0].shape[0]
    for step, upstream_ref in enumerate(upstream_refs):
        owner = lax.rem(place_ref[1] + (shards - step), shards)
        start = pl.multiple_of(owner * shard_rows, shard_rows)
        grad_ref[pl.ds(start, shard_rows), :] = dot_nt(
            upstream_ref[...], weight_ref[...]
        ).astype(jnp.bfloat16)
    for head in range(head_count):
        pair = jnp.concatenate([head_columns(query_ref, head), head_columns(grad_ref, head)], 1)
        for place in range(head, group, head_count):
            stage_ref[place] = pair
    for place, out_ref in zip(targets(place_ref[0], group), out_refs):
        out_ref[...] = stage_ref[place]


def own_offset(head_count, place_ref):
    return place_ref[2 + place_ref[1] * head_count + lax.rem(place_ref[0], head_count)]


def gather_kernel(
    head_count, group, place_ref, keys_ref, after_ref, key_t_out, picks_out
):
    rows = keys_ref.shape[0] // group
    picked = rows // DILATION_RATE
    pick = pick_matrix(own_offset(head_count, place_ref), picked, rows)
    for place in range(group):
        picks_out[place * picked : (place + 1) * picked, :] = dot_nn(
            pick, keys_ref[place * rows : (place + 1) * rows, :]
        ).astype(jnp.bfloat16)
    key_t_out[...] = keys_ref[...].astype(jnp.float32).T[:HEAD_SIZE].astype(jnp.bfloat16)


def halves(both):
    left = left_half(both.shape)
    zero = jnp.zeros((), both.dtype)
    return jnp.where(left, both, zero), jnp.where(left, zero, both)


def far_kernel(
    head_count, group, others, place_ref, near_ref, start_ref, picks_ref, *refs
):
    other_refs, refs = refs[:others], refs[others:]
    block_refs, refs = refs[:group], refs[group:]
    acc_out, query_out, own_out, other_out, keys_ref, rows_ref = refs
    near = near_ref.shape[0]
    rows = near // group
    picked = rows // DILATION_RATE
    count = group * picked
    far = count * (1 + others)
    pick = pick_matrix(own_offset(head_count, place_ref), picked, rows)
    keys_ref[:near, :] = near_ref[...]
    for index, ref in enumerate([picks_ref, *other_refs]):
        keys_ref[near + index * count : near + (index + 1) * count, :] = ref[...]
    for bits, ref in enumerate(block_refs):
        rows_ref[bits * picked : (bits + 1) * picked, :] = dot_nn(pick, ref[...]).astype(
            jnp.bfloat16
        )
    key_t = keys_ref[...].astype(jnp.float32).T[:HEAD_SIZE].astype(jnp.bfloat16)
    query, grad = halves(rows_ref[...])
    score = dot_nt(keys_ref[...], query)
    dprob = dot_nt(keys_ref[...], grad)
    top = jnp.max(score, 0, keepdims=True)
    prob = jnp.exp2((score - top) * SCORE_FACTOR)
    inverse = 1.0 / jnp.sum(prob, 0, keepdims=True)
    delta = jnp.sum(prob * dprob, 0, keepdims=True) * inverse
    prob = prob * inverse
    dscore = (prob * (dprob - delta)).astype(jnp.bfloat16)
    terms = dot_nn(
        jnp.concatenate([dscore, prob.astype(jnp.bfloat16)], 1), jnp.concatenate([query, grad], 0)
    )
    acc_out[...] = start_ref[...] + terms[:near]
    terms = terms[near:] * jnp.where(left_half((far, PAIR)), SCALE, 1.0)
    own_out[...] = terms[:count]
    other_out[...] = terms[count:]
    query_grad = (dot_nn(key_t, dscore) * SCALE).T.astype(jnp.bfloat16)
    zero = jnp.zeros_like(query_grad)
    query_out[:count, :] = jnp.concatenate([query_grad, zero], 1)
    query_out[count:, :] = jnp.concatenate([zero, query_grad], 1)


def near_blocks(
    offset, keys_ref, key_t_ref, block_refs, prob_ref, dprob_ref, work_ref, top_ref, acc_ref, emit
):
    near = keys_ref.shape[0]
    rows = prob_ref.shape[2]
    half = rows // 2
    row_lane = lax.broadcasted_iota(jnp.int32, (1, rows), 1)
    picked = lax.rem(row_lane, DILATION_RATE) == offset

    def by_eight(value):
        return value.reshape(value.shape[0] // 8, 8, rows)

    def transposed_of(index):
        both = block_refs[index][...].astype(jnp.float32).T.astype(jnp.bfloat16)
        zero = jnp.zeros((HEAD_SIZE, rows), jnp.bfloat16)
        query, grad = both[:HEAD_SIZE], both[HEAD_SIZE:]
        return jnp.concatenate(
            [jnp.concatenate([query, zero], 0), jnp.concatenate([zero, grad], 0)], 1
        )

    def first_pass(index, weights, start, state):
        top, total, delta = state
        slot = index % 2
        products = dot_nn(keys_ref[start : start + PIECE, :], weights)
        scores, dprobs = products[:, :rows], products[:, rows:]
        for inner in range(0, PIECE, STRIP):
            strip = slice(start + inner, start + inner + STRIP)
            score, dprob = scores[inner : inner + STRIP], dprobs[inner : inner + STRIP]
            part = fold(score, jnp.maximum) * SCORE_FACTOR
            raised = part if top is None else jnp.maximum(top, part)
            prob = jnp.exp2(by_eight(score) * SCORE_FACTOR - raised[None])
            part_total = jnp.sum(prob, 0)
            part_delta = jnp.sum(prob * by_eight(dprob), 0)
            if top is None:
                total, delta = part_total, part_delta
            else:
                shrink = jnp.exp2(top - raised)
                total, delta = total * shrink + part_total, delta * shrink + part_delta
            top = raised
            prob_ref[slot, strip, :] = prob.reshape(STRIP, rows)
            dprob_ref[slot, strip, :] = dprob
            top_ref[slot, strip.start // STRIP] = raised
        return top, total, delta

    def last_pass(index, lse, delta, both, start, query_grad):
        slot = index % 2
        piece = slice(start, start + PIECE)
        for inner in range(0, PIECE, STRIP):
            strip = slice(start + inner, start + inner + STRIP)
            factor = jnp.exp2(top_ref[slot, strip.start // STRIP] - lse)
            prob = by_eight(prob_ref[slot, strip, :]) * factor[None]
            dscore = prob * (by_eight(dprob_ref[slot, strip, :]) - delta)
            work_ref[slot, strip, :rows] = dscore.reshape(STRIP, rows).astype(jnp.bfloat16)
            work_ref[slot, strip, rows:] = prob.reshape(STRIP, rows).astype(jnp.bfloat16)
        acc_ref[piece, :] += dot_nn(work_ref[slot, piece, :], both)
        return query_grad + dot_nn(key_t_ref[:, piece], work_ref[slot, piece, :rows])

    starts = range(0, near, PIECE)
    weights = transposed_of(0)
    state = (None, None, None)
    for start in starts:
        state = first_pass(0, weights, start, state)
    for index, block_ref in enumerate(block_refs):
        last = index + 1 == len(block_refs)
        top, total, delta = state
        highest = jnp.max(top, 0, keepdims=True)
        shrink = jnp.exp2(top - highest)
        total = jnp.sum(total * shrink, 0, keepdims=True)
        delta = jnp.sum(delta * shrink, 0, keepdims=True) / total
        lse = jnp.where(picked, -NEVER, highest + jnp.log2(total))
        both = jnp.concatenate(halves(block_ref[...]), 0)
        query_grad = jnp.zeros((HEAD_SIZE, rows), jnp.float32)
        weights = None if last else transposed_of(index + 1)
        state = (None, None, None)
        for start in starts:
            if not last:
                state = first_pass(index + 1, weights, start, state)
            query_grad = last_pass(index, lse, delta, both, start, query_grad)
        query_grad = (query_grad * SCALE).T.astype(jnp.bfloat16)
        emit(index, jnp.concatenate([query_grad[:half], query_grad[half:]], 1))


def some_kernel(head_count, steps, begin, place_ref, keys_ref, key_t_ref, *refs):
    if not begin:
        start_ref, refs = refs[0], refs[1:]
    block_refs, (acc_ref, query_out, *scratch) = refs[:steps], refs[steps:]
    acc_ref[...] = jnp.zeros_like(acc_ref) if begin else start_ref[...]

    def emit(index, query_grad):
        query_out[index] = query_grad

    near_blocks(
        own_offset(head_count, place_ref), keys_ref, key_t_ref, block_refs,
        *scratch, acc_ref, emit,
    )


def end_kernel(
    head_count, steps, others, place_ref, keys_ref, key_t_ref, start_ref, query_ref,
    later_query_ref, picked_query_ref, own_ref, *refs,
):
    back_refs, refs = refs[:others], refs[others:]
    block_refs, refs = refs[:steps], refs[steps:]
    half = query_ref.shape[1]
    rows = 2 * half
    group = keys_ref.shape[0] // rows
    out_refs, refs = refs[:group], refs[group:]
    acc_ref, *scratch = refs
    count = own_ref.shape[0]
    picked = count // group
    offset = own_offset(head_count, place_ref)
    acc_ref[...] = start_ref[...]

    def finish(bits, query_grad):
        spread = spread_matrix(offset, bits * picked, count, rows, 1)
        spread = jnp.concatenate([spread[:half], spread[half:]], 1)
        placed = dot_nn(spread, picked_query_ref[...])
        out_refs[bits][rows:, :] = (query_grad.astype(jnp.float32) + placed).astype(jnp.bfloat16)

    def emit(index, query_grad):
        finish(group - steps + index, query_grad)

    near_blocks(offset, keys_ref, key_t_ref, block_refs, *scratch, acc_ref, emit)
    terms = own_ref[...]
    for back_ref in back_refs:
        terms = terms + back_ref[...]
    terms = jnp.concatenate(split_two(terms), 0)
    factor = jnp.where(left_half((rows, PAIR)), SCALE, 1.0)
    for bits, place in enumerate(sources(place_ref[0], group)):
        spread = spread_matrix(offset, place * picked, count, rows, 1)
        placed = dot_nn(jnp.concatenate([spread, spread], 1), terms)
        acc = acc_ref[pl.ds(pl.multiple_of(place * rows, rows), rows), :]
        out_refs[bits][:rows, :] = (acc * factor + placed).astype(jnp.bfloat16)
        done = query_ref.shape[0]
        if bits < done:
            finish(bits, query_ref[bits])
        elif bits < group - steps:
            finish(bits, later_query_ref[bits - done])


def unpack_kernel(head_count, group, place_ref, *refs):
    near_refs, refs = refs[:group], refs[group:]
    query_out, key_out, value_out, stage_ref = refs
    rows = query_out.shape[0]
    half = rows // 2
    for place, near_ref in zip(targets(place_ref[0], group), near_refs):
        stage_ref[place] = near_ref[...]
    for head in range(0, head_count, 2):
        columns = slice(head * HEAD_SIZE, (head + 2) * HEAD_SIZE)
        pairs = [stage_ref[head, :rows, :], stage_ref[head + 1, :rows, :]]
        packed = [stage_ref[head, rows:, :], stage_ref[head + 1, rows:, :]]
        key_out[:, columns] = jnp.concatenate([pair[:, :HEAD_SIZE] for pair in pairs], 1)
        value_out[:, columns] = jnp.concatenate([pair[:, HEAD_SIZE:] for pair in pairs], 1)
        query_out[:half, columns] = jnp.concatenate([pair[:, :HEAD_SIZE] for pair in packed], 1)
        query_out[half:, columns] = jnp.concatenate([pair[:, HEAD_SIZE:] for pair in packed], 1)


def call(kernel, name, out_shape, scalars, operands, scratch=(), flops=0, space=VMEM, limit=40):
    return pl.pallas_call(
        kernel,
        out_shape=tuple(jax.ShapeDtypeStruct(*shape) for shape in out_shape),
        in_specs=[SMEM] * len(scalars) + [space] * len(operands),
        out_specs=tuple(VMEM for _ in out_shape),
        scratch_shapes=[
            pltpu.VMEM(*shape) if isinstance(shape, tuple) else shape for shape in scratch
        ],
        compiler_params=pltpu.CompilerParams(vmem_limit_bytes=limit * 1024 * 1024),
        cost_estimate=pl.CostEstimate(flops=flops, bytes_accessed=2**21, transcendentals=0),
        name=name,
    )(*scalars, *operands)


def body(upstream, out_weight, query_rows, key_rows, value_rows, head_offsets):
    rows, width = query_rows.shape
    head_count = width // HEAD_SIZE
    devices = lax.axis_size("context")
    shards = lax.axis_size("heads")
    group = FIRST_SEGMENT // rows
    others = devices // group - 1
    half = rows // 2
    picked = rows // DILATION_RATE
    count = group * picked
    near = group * rows
    place = jnp.stack(
        [lax.rem(lax.axis_index("context"), group), lax.axis_index("heads")]
    ).astype(jnp.int32)
    place = jnp.concatenate([place, head_offsets])
    scalars = [place]

    def swap(values, steps, order=None):
        result = list(values)
        for index in order or range(1, group):
            step = steps[index - 1]
            pairs = [(source, source ^ step[source % 2]) for source in range(devices)]
            result[index] = lax.ppermute(values[index], "context", pairs)
        return result

    out_steps = swap_steps(group)
    back_steps = [mirrored(step) for step in out_steps]
    back_order = [1, 2, 7, 5, 6, 3, 4] if group == 8 else None

    def segment_shift(value, shift):
        pairs = [(source, (source + shift * group) % devices) for source in range(devices)]
        return lax.ppermute(value, "context", pairs)

    upstreams = [upstream]
    for step in range(1, shards):
        pairs = [(source, (source + step) % shards) for source in range(shards)]
        upstreams.append(lax.ppermute(upstream, "heads", pairs))

    bf16, f32 = jnp.bfloat16, jnp.float32
    (sent,) = call(
        functools.partial(pack_kernel, head_count), "pack_rows",
        [((group, rows, PAIR), bf16)],
        [], [key_rows, value_rows],
        [((rows, width), bf16)] * 2 + [pltpu.SemaphoreType.DMA((2,))],
        flops=2**31, space=ANY, limit=60,
    )
    groups = [list(range(first, first + group)) for first in range(0, devices, group)]
    sent = lax.all_to_all(sent, "context", 0, 0, axis_index_groups=groups)
    blocks_send = call(
        functools.partial(project_kernel, head_count, group, shards), "project_pack",
        [((rows, PAIR), bf16)] * group,
        [place], [out_weight, query_rows, *upstreams],
        [((rows, width), bf16), ((group, rows, PAIR), bf16)],
        flops=BUSY,
    )
    blocks = swap(blocks_send, out_steps)
    keys = sent.reshape(near, PAIR)
    key_t, picks = call(
        functools.partial(gather_kernel, head_count, group), "gather_keys",
        [((HEAD_SIZE, near), bf16), ((count, PAIR), bf16)],
        scalars, [keys, blocks_send[0]],
    )
    other_picks = [segment_shift(picks, shift) for shift in range(1, others + 1)]
    steps = group // 2 - 1
    scratch = [
        ((2, near, rows), f32), ((2, near, rows), f32), ((2, near, 2 * rows), bf16),
        ((2, near // STRIP, 8, rows), f32),
    ]
    half_flops = 30 * near * near // 2 * PAIR
    early, late = blocks[:steps], blocks[steps:-1]
    acc, query_early = call(
        functools.partial(some_kernel, head_count, len(early), True), "first_rows",
        [((near, PAIR), f32), ((len(early), half, PAIR), bf16)],
        scalars, [keys, key_t, *early], scratch, half_flops,
    )
    acc, picked_query, own_terms, other_terms = call(
        functools.partial(far_kernel, head_count, group, others), "picked_rows",
        [
            ((near, PAIR), f32), ((2 * count, PAIR), bf16), ((count, PAIR), f32),
            ((others * count, PAIR), f32),
        ],
        scalars, [keys, acc, picks, *other_picks, *blocks],
        [((near + count * (1 + others), PAIR), bf16), ((count, PAIR), bf16)],
        flops=20 * near * count * PAIR,
    )
    back = [
        segment_shift(other_terms[(shift - 1) * count : shift * count], -shift)
        for shift in range(1, others + 1)
    ]
    acc, query_late = call(
        functools.partial(some_kernel, head_count, len(late), False), "second_rows",
        [((near, PAIR), f32), ((len(late), half, PAIR), bf16)],
        scalars, [keys, key_t, acc, *late], scratch, half_flops,
    )
    near_send = call(
        functools.partial(end_kernel, head_count, 1, others), "last_rows",
        [((rows + half, PAIR), bf16)] * group,
        scalars,
        [
            keys, key_t, acc, query_early, query_late, picked_query, own_terms, *back, blocks[-1],
        ],
        [((near, PAIR), f32)] + scratch, half_flops // 4,
    )
    return tuple(
        call(
            functools.partial(unpack_kernel, head_count, group), "unpack",
            [((rows, width), bf16)] * 3,
            [place], swap(near_send, back_steps, back_order),
            [((group, rows + half, PAIR), bf16)],
        )
    )


def solution(mesh):
    return jax.shard_map(
        body,
        mesh=mesh,
        in_specs=(
            P(("context", "heads"), None),
            P("heads", None),
            P("context", "heads"),
            P("context", "heads"),
            P("context", "heads"),
            P(),
        ),
        out_specs=(P("context", "heads"), P("context", "heads"), P("context", "heads")),
        check_vma=False,
    )
```

```python
import functools
import math

import jax
import jax.numpy as jnp
from jax import lax
from jax.experimental import pallas as pl
from jax.experimental.pallas import tpu as pltpu
from jax.sharding import PartitionSpec as P

HEAD_SIZE = 64
PAIR = 2 * HEAD_SIZE
DILATION_RATE = 16
FIRST_SEGMENT = 2048
SCALE = 1.0 / math.sqrt(HEAD_SIZE)
LOG2E = math.log2(math.e)
SCORE_FACTOR = SCALE * LOG2E
STRIP = 64
PIECE = 256
BUSY = 2**35
NEVER = -1e30

SMEM = pl.BlockSpec(memory_space=pltpu.SMEM)
VMEM = pl.BlockSpec(memory_space=pltpu.VMEM)
ANY = pl.BlockSpec(memory_space=pl.ANY)


def dot_nt(left, right):
    return lax.dot_general(
        left, right, (((1,), (1,)), ((), ())), preferred_element_type=jnp.float32
    )


def dot_nn(left, right):
    return jnp.dot(left, right, preferred_element_type=jnp.float32)


def head_columns(ref, head):
    return ref[:, head * HEAD_SIZE : (head + 1) * HEAD_SIZE]


def pick_matrix(offset, picked, rows):
    source = lax.broadcasted_iota(jnp.int32, (picked, rows), 1)
    index = lax.broadcasted_iota(jnp.int32, (picked, rows), 0)
    return (source == index * DILATION_RATE + offset).astype(jnp.bfloat16)


def spread_matrix(offset, first, picked, rows, axis):
    shape = (picked, rows) if axis == 0 else (rows, picked)
    index = lax.broadcasted_iota(jnp.int32, shape, axis)
    source = lax.broadcasted_iota(jnp.int32, shape, 1 - axis)
    return (source == (index - first) * DILATION_RATE + offset).astype(jnp.bfloat16)


def split_two(value):
    high = value.astype(jnp.bfloat16)
    low = (value - high.astype(jnp.float32)).astype(jnp.bfloat16)
    return high, low


def fold(value, combine):
    parts = [value[start : start + 8] for start in range(0, value.shape[0], 8)]
    while len(parts) > 1:
        merged = [combine(parts[i], parts[i + 1]) for i in range(0, len(parts) - 1, 2)]
        parts = merged + parts[len(merged) * 2 :]
    return parts[0]


def left_half(shape):
    return lax.broadcasted_iota(jnp.int32, shape, 1) < HEAD_SIZE


def side_by_side(block):
    half = block.shape[0] // 2
    return jnp.concatenate([block[:half], block[half:]], 1)


def swap_steps(group):
    if group == 8:
        return [(2, 4), (4, 2), (3, 5), (6, 6), (5, 3), (7, 1), (1, 7)]
    return [(bits, bits) for bits in range(1, group)]


def mirrored(step):
    return (step[1], step[0]) if step[0] % 2 else step


def target_of(place, step):
    return lax.bitwise_xor(place, jnp.where(lax.rem(place, 2) == 1, step[1], step[0]))


def targets(place, group):
    return [place] + [target_of(place, step) for step in swap_steps(group)]


def sources(place, group):
    return [place] + [target_of(place, mirrored(step)) for step in swap_steps(group)]


def pack_kernel(head_count, key_hbm, value_hbm, out_ref, key_ref, value_ref, sems):
    copies = [
        pltpu.make_async_copy(source, target, sems.at[index])
        for index, (source, target) in enumerate([(key_hbm, key_ref), (value_hbm, value_ref)])
    ]
    for copy in copies:
        copy.start()
    for copy in copies:
        copy.wait()
    for head in range(head_count):
        pair = jnp.concatenate([head_columns(key_ref, head), head_columns(value_ref, head)], 1)
        for place in range(head, out_ref.shape[0], head_count):
            out_ref[place] = pair


def project_kernel(head_count, group, shards, place_ref, weight_ref, query_ref, *refs):
    upstream_refs, refs = refs[:shards], refs[shards:]
    out_refs, (grad_ref, stage_ref) = refs[:group], refs[group:]
    shard_rows = upstream_refs[0].shape[0]
    for step, upstream_ref in enumerate(upstream_refs):
        owner = lax.rem(place_ref[1] + (shards - step), shards)
        start = pl.multiple_of(owner * shard_rows, shard_rows)
        grad_ref[pl.ds(start, shard_rows), :] = dot_nt(
            upstream_ref[...], weight_ref[...]
        ).astype(jnp.bfloat16)
    for head in range(head_count):
        pair = jnp.concatenate([head_columns(query_ref, head), head_columns(grad_ref, head)], 1)
        for place in range(head, group, head_count):
            stage_ref[place] = pair
    for place, out_ref in zip(targets(place_ref[0], group), out_refs):
        out_ref[...] = stage_ref[place]


def own_offset(head_count, place_ref):
    return place_ref[2 + place_ref[1] * head_count + lax.rem(place_ref[0], head_count)]


def gather_kernel(
    head_count, group, place_ref, keys_ref, after_ref, key_t_out, picks_out
):
    rows = keys_ref.shape[0] // group
    picked = rows // DILATION_RATE
    pick = pick_matrix(own_offset(head_count, place_ref), picked, rows)
    for place in range(group):
        picks_out[place * picked : (place + 1) * picked, :] = dot_nn(
            pick, keys_ref[place * rows : (place + 1) * rows, :]
        ).astype(jnp.bfloat16)
    key_t_out[...] = keys_ref[...].astype(jnp.float32).T[:HEAD_SIZE].astype(jnp.bfloat16)


def halves(both):
    left = left_half(both.shape)
    zero = jnp.zeros((), both.dtype)
    return jnp.where(left, both, zero), jnp.where(left, zero, both)


def far_kernel(
    head_count, group, others, place_ref, near_ref, start_ref, picks_ref, *refs
):
    other_refs, refs = refs[:others], refs[others:]
    block_refs, refs = refs[:group], refs[group:]
    acc_out, query_out, own_out, other_out, keys_ref, rows_ref = refs
    near = near_ref.shape[0]
    rows = near // group
    picked = rows // DILATION_RATE
    count = group * picked
    far = count * (1 + others)
    pick = pick_matrix(own_offset(head_count, place_ref), picked, rows)
    keys_ref[:near, :] = near_ref[...]
    for index, ref in enumerate([picks_ref, *other_refs]):
        keys_ref[near + index * count : near + (index + 1) * count, :] = ref[...]
    for bits, ref in enumerate(block_refs):
        rows_ref[bits * picked : (bits + 1) * picked, :] = dot_nn(pick, ref[...]).astype(
            jnp.bfloat16
        )
    key_t = keys_ref[...].astype(jnp.float32).T[:HEAD_SIZE].astype(jnp.bfloat16)
    query, grad = halves(rows_ref[...])
    score = dot_nt(keys_ref[...], query)
    dprob = dot_nt(keys_ref[...], grad)
    top = jnp.max(score, 0, keepdims=True)
    prob = jnp.exp2((score - top) * SCORE_FACTOR)
    inverse = 1.0 / jnp.sum(prob, 0, keepdims=True)
    delta = jnp.sum(prob * dprob, 0, keepdims=True) * inverse
    prob = prob * inverse
    dscore = (prob * (dprob - delta)).astype(jnp.bfloat16)
    terms = dot_nn(
        jnp.concatenate([dscore, prob.astype(jnp.bfloat16)], 1), jnp.concatenate([query, grad], 0)
    )
    acc_out[...] = start_ref[...] + terms[:near]
    terms = terms[near:] * jnp.where(left_half((far, PAIR)), SCALE, 1.0)
    own_out[...] = terms[:count]
    other_out[...] = terms[count:]
    query_grad = (dot_nn(key_t, dscore) * SCALE).T.astype(jnp.bfloat16)
    zero = jnp.zeros_like(query_grad)
    query_out[:count, :] = jnp.concatenate([query_grad, zero], 1)
    query_out[count:, :] = jnp.concatenate([zero, query_grad], 1)


def near_blocks(
    offset, keys_ref, key_t_ref, block_refs, prob_ref, dprob_ref, work_ref, top_ref, acc_ref, emit
):
    near = keys_ref.shape[0]
    rows = prob_ref.shape[2]
    half = rows // 2
    row_lane = lax.broadcasted_iota(jnp.int32, (1, rows), 1)
    picked = lax.rem(row_lane, DILATION_RATE) == offset

    def by_eight(value):
        return value.reshape(value.shape[0] // 8, 8, rows)

    def transposed_of(index):
        both = block_refs[index][...].astype(jnp.float32).T.astype(jnp.bfloat16)
        zero = jnp.zeros((HEAD_SIZE, rows), jnp.bfloat16)
        query, grad = both[:HEAD_SIZE], both[HEAD_SIZE:]
        return jnp.concatenate(
            [jnp.concatenate([query, zero], 0), jnp.concatenate([zero, grad], 0)], 1
        )

    def first_pass(index, weights, start, state):
        top, total, delta = state
        slot = index % 2
        products = dot_nn(keys_ref[start : start + PIECE, :], weights)
        scores, dprobs = products[:, :rows], products[:, rows:]
        for inner in range(0, PIECE, STRIP):
            strip = slice(start + inner, start + inner + STRIP)
            score, dprob = scores[inner : inner + STRIP], dprobs[inner : inner + STRIP]
            part = fold(score, jnp.maximum) * SCORE_FACTOR
            raised = part if top is None else jnp.maximum(top, part)
            prob = jnp.exp2(by_eight(score) * SCORE_FACTOR - raised[None])
            part_total = jnp.sum(prob, 0)
            part_delta = jnp.sum(prob * by_eight(dprob), 0)
            if top is None:
                total, delta = part_total, part_delta
            else:
                shrink = jnp.exp2(top - raised)
                total, delta = total * shrink + part_total, delta * shrink + part_delta
            top = raised
            prob_ref[slot, strip, :] = prob.reshape(STRIP, rows)
            dprob_ref[slot, strip, :] = dprob
            top_ref[slot, strip.start // STRIP] = raised
        return top, total, delta

    def last_pass(index, lse, delta, both, start, query_grad):
        slot = index % 2
        piece = slice(start, start + PIECE)
        for inner in range(0, PIECE, STRIP):
            strip = slice(start + inner, start + inner + STRIP)
            factor = jnp.exp2(top_ref[slot, strip.start // STRIP] - lse)
            prob = by_eight(prob_ref[slot, strip, :]) * factor[None]
            dscore = prob * (by_eight(dprob_ref[slot, strip, :]) - delta)
            work_ref[slot, strip, :rows] = dscore.reshape(STRIP, rows).astype(jnp.bfloat16)
            work_ref[slot, strip, rows:] = prob.reshape(STRIP, rows).astype(jnp.bfloat16)
        acc_ref[piece, :] += dot_nn(work_ref[slot, piece, :], both)
        return query_grad + dot_nn(key_t_ref[:, piece], work_ref[slot, piece, :rows])

    starts = range(0, near, PIECE)
    weights = transposed_of(0)
    state = (None, None, None)
    for start in starts:
        state = first_pass(0, weights, start, state)
    for index, block_ref in enumerate(block_refs):
        last = index + 1 == len(block_refs)
        top, total, delta = state
        highest = jnp.max(top, 0, keepdims=True)
        shrink = jnp.exp2(top - highest)
        total = jnp.sum(total * shrink, 0, keepdims=True)
        delta = jnp.sum(delta * shrink, 0, keepdims=True) / total
        lse = jnp.where(picked, -NEVER, highest + jnp.log2(total))
        both = jnp.concatenate(halves(block_ref[...]), 0)
        query_grad = jnp.zeros((HEAD_SIZE, rows), jnp.float32)
        weights = None if last else transposed_of(index + 1)
        state = (None, None, None)
        for start in starts:
            if not last:
                state = first_pass(index + 1, weights, start, state)
            query_grad = last_pass(index, lse, delta, both, start, query_grad)
        query_grad = (query_grad * SCALE).T.astype(jnp.bfloat16)
        emit(index, jnp.concatenate([query_grad[:half], query_grad[half:]], 1))


def some_kernel(head_count, steps, begin, place_ref, keys_ref, key_t_ref, *refs):
    if not begin:
        start_ref, refs = refs[0], refs[1:]
    block_refs, (acc_ref, query_out, *scratch) = refs[:steps], refs[steps:]
    acc_ref[...] = jnp.zeros_like(acc_ref) if begin else start_ref[...]

    def emit(index, query_grad):
        query_out[index] = query_grad

    near_blocks(
        own_offset(head_count, place_ref), keys_ref, key_t_ref, block_refs,
        *scratch, acc_ref, emit,
    )


def end_kernel(
    head_count, steps, others, place_ref, keys_ref, key_t_ref, start_ref, query_ref,
    later_query_ref, picked_query_ref, own_ref, *refs,
):
    back_refs, refs = refs[:others], refs[others:]
    block_refs, refs = refs[:steps], refs[steps:]
    half = query_ref.shape[1]
    rows = 2 * half
    group = keys_ref.shape[0] // rows
    out_refs, refs = refs[:group], refs[group:]
    acc_ref, *scratch = refs
    count = own_ref.shape[0]
    picked = count // group
    offset = own_offset(head_count, place_ref)
    acc_ref[...] = start_ref[...]

    def finish(bits, query_grad):
        spread = spread_matrix(offset, bits * picked, count, rows, 1)
        spread = jnp.concatenate([spread[:half], spread[half:]], 1)
        placed = dot_nn(spread, picked_query_ref[...])
        out_refs[bits][rows:, :] = (query_grad.astype(jnp.float32) + placed).astype(jnp.bfloat16)

    def emit(index, query_grad):
        finish(group - steps + index, query_grad)

    near_blocks(offset, keys_ref, key_t_ref, block_refs, *scratch, acc_ref, emit)
    terms = own_ref[...]
    for back_ref in back_refs:
        terms = terms + back_ref[...]
    terms = jnp.concatenate(split_two(terms), 0)
    factor = jnp.where(left_half((rows, PAIR)), SCALE, 1.0)
    for bits, place in enumerate(sources(place_ref[0], group)):
        spread = spread_matrix(offset, place * picked, count, rows, 1)
        placed = dot_nn(jnp.concatenate([spread, spread], 1), terms)
        acc = acc_ref[pl.ds(pl.multiple_of(place * rows, rows), rows), :]
        out_refs[bits][:rows, :] = (acc * factor + placed).astype(jnp.bfloat16)
        done = query_ref.shape[0]
        if bits < done:
            finish(bits, query_ref[bits])
        elif bits < group - steps:
            finish(bits, later_query_ref[bits - done])


def unpack_kernel(head_count, group, place_ref, *refs):
    near_refs, refs = refs[:group], refs[group:]
    query_out, key_out, value_out, stage_ref = refs
    rows = query_out.shape[0]
    half = rows // 2
    for place, near_ref in zip(targets(place_ref[0], group), near_refs):
        stage_ref[place] = near_ref[...]
    for head in range(0, head_count, 2):
        columns = slice(head * HEAD_SIZE, (head + 2) * HEAD_SIZE)
        pairs = [stage_ref[head, :rows, :], stage_ref[head + 1, :rows, :]]
        packed = [stage_ref[head, rows:, :], stage_ref[head + 1, rows:, :]]
        key_out[:, columns] = jnp.concatenate([pair[:, :HEAD_SIZE] for pair in pairs], 1)
        value_out[:, columns] = jnp.concatenate([pair[:, HEAD_SIZE:] for pair in pairs], 1)
        query_out[:half, columns] = jnp.concatenate([pair[:, :HEAD_SIZE] for pair in packed], 1)
        query_out[half:, columns] = jnp.concatenate([pair[:, HEAD_SIZE:] for pair in packed], 1)


def call(kernel, name, out_shape, scalars, operands, scratch=(), flops=0, space=VMEM, limit=40):
    return pl.pallas_call(
        kernel,
        out_shape=tuple(jax.ShapeDtypeStruct(*shape) for shape in out_shape),
        in_specs=[SMEM] * len(scalars) + [space] * len(operands),
        out_specs=tuple(VMEM for _ in out_shape),
        scratch_shapes=[
            pltpu.VMEM(*shape) if isinstance(shape, tuple) else shape for shape in scratch
        ],
        compiler_params=pltpu.CompilerParams(vmem_limit_bytes=limit * 1024 * 1024),
        cost_estimate=pl.CostEstimate(flops=flops, bytes_accessed=2**21, transcendentals=0),
        name=name,
    )(*scalars, *operands)


def body(upstream, out_weight, query_rows, key_rows, value_rows, head_offsets):
    rows, width = query_rows.shape
    head_count = width // HEAD_SIZE
    devices = lax.axis_size("context")
    shards = lax.axis_size("heads")
    group = FIRST_SEGMENT // rows
    others = devices // group - 1
    half = rows // 2
    picked = rows // DILATION_RATE
    count = group * picked
    near = group * rows
    place = jnp.stack(
        [lax.rem(lax.axis_index("context"), group), lax.axis_index("heads")]
    ).astype(jnp.int32)
    place = jnp.concatenate([place, head_offsets])
    scalars = [place]

    def swap(values, steps):
        result = [values[0]]
        for step, value in zip(steps, values[1:]):
            pairs = [(source, source ^ step[source % 2]) for source in range(devices)]
            result.append(lax.ppermute(value, "context", pairs))
        return result

    out_steps = swap_steps(group)
    back_steps = [mirrored(step) for step in out_steps]

    def segment_shift(value, shift):
        pairs = [(source, (source + shift * group) % devices) for source in range(devices)]
        return lax.ppermute(value, "context", pairs)

    upstreams = [upstream]
    for step in range(1, shards):
        pairs = [(source, (source + step) % shards) for source in range(shards)]
        upstreams.append(lax.ppermute(upstream, "heads", pairs))

    bf16, f32 = jnp.bfloat16, jnp.float32
    (sent,) = call(
        functools.partial(pack_kernel, head_count), "pack_rows",
        [((group, rows, PAIR), bf16)],
        [], [key_rows, value_rows],
        [((rows, width), bf16)] * 2 + [pltpu.SemaphoreType.DMA((2,))],
        flops=2**31, space=ANY, limit=60,
    )
    groups = [list(range(first, first + group)) for first in range(0, devices, group)]
    sent = lax.all_to_all(sent, "context", 0, 0, axis_index_groups=groups)
    blocks_send = call(
        functools.partial(project_kernel, head_count, group, shards), "project_pack",
        [((rows, PAIR), bf16)] * group,
        [place], [out_weight, query_rows, *upstreams],
        [((rows, width), bf16), ((group, rows, PAIR), bf16)],
        flops=BUSY,
    )
    blocks = swap(blocks_send, out_steps)
    keys = sent.reshape(near, PAIR)
    key_t, picks = call(
        functools.partial(gather_kernel, head_count, group), "gather_keys",
        [((HEAD_SIZE, near), bf16), ((count, PAIR), bf16)],
        scalars, [keys, blocks_send[0]],
    )
    other_picks = [segment_shift(picks, shift) for shift in range(1, others + 1)]
    steps = group // 2
    scratch = [
        ((2, near, rows), f32), ((2, near, rows), f32), ((2, near, 2 * rows), bf16),
        ((2, near // STRIP, 8, rows), f32),
    ]
    half_flops = 30 * near * near // 2 * PAIR
    early, late = blocks[:steps], blocks[steps:-1]
    acc, query_early = call(
        functools.partial(some_kernel, head_count, len(early), True), "first_rows",
        [((near, PAIR), f32), ((len(early), half, PAIR), bf16)],
        scalars, [keys, key_t, *early], scratch, half_flops,
    )
    acc, picked_query, own_terms, other_terms = call(
        functools.partial(far_kernel, head_count, group, others), "picked_rows",
        [
            ((near, PAIR), f32), ((2 * count, PAIR), bf16), ((count, PAIR), f32),
            ((others * count, PAIR), f32),
        ],
        scalars, [keys, acc, picks, *other_picks, *blocks],
        [((near + count * (1 + others), PAIR), bf16), ((count, PAIR), bf16)],
        flops=20 * near * count * PAIR,
    )
    back = [
        segment_shift(other_terms[(shift - 1) * count : shift * count], -shift)
        for shift in range(1, others + 1)
    ]
    acc, query_late = call(
        functools.partial(some_kernel, head_count, len(late), False), "second_rows",
        [((near, PAIR), f32), ((len(late), half, PAIR), bf16)],
        scalars, [keys, key_t, acc, *late], scratch, half_flops,
    )
    near_send = call(
        functools.partial(end_kernel, head_count, 1, others), "last_rows",
        [((rows + half, PAIR), bf16)] * group,
        scalars,
        [
            keys, key_t, acc, query_early, query_late, picked_query, own_terms, *back, blocks[-1],
        ],
        [((near, PAIR), f32)] + scratch, half_flops // steps,
    )
    return tuple(
        call(
            functools.partial(unpack_kernel, head_count, group), "unpack",
            [((rows, width), bf16)] * 3,
            [place], swap(near_send, back_steps),
            [((group, rows + half, PAIR), bf16)],
        )
    )


def solution(mesh):
    return jax.shard_map(
        body,
        mesh=mesh,
        in_specs=(
            P(("context", "heads"), None),
            P("heads", None),
            P("context", "heads"),
            P("context", "heads"),
            P("context", "heads"),
            P(),
        ),
        out_specs=(P("context", "heads"), P("context", "heads"), P("context", "heads")),
        check_vma=False,
    )
```
